32 devices in a mesh: slab: 8 (over z, x), pencil: 4 (over y, core).
Axes of the slice: x: 2, y: 2, z: 4, core: 2. Of those that a mesh axis runs over, the one named last changes fastest.
Arguments:
- vorticity: float32 [3, 64, 128, 256], P(None, 'slab', 'pencil')
- velocity: float32 [3, 64, 128, 256], P(None, 'slab', 'pencil'), may hold values from -6 to 6
- viscosity: float32 [64, 128, 256], P('slab', 'pencil'), may hold values from 0.02 to 0.4
- tile_weights: float32 [1024, 3, 128], P(('slab', 'pencil')), may hold values from -6 to 6
- tile_cells: int32 [1024, 128], P(('slab', 'pencil')), may hold values from 0 to 65535
- tile_dest: int32 [1024, 1], P(('slab', 'pencil')), may hold values from 0 to 7; in each aligned block of 32 rows (0 to 31, 32 to 63, ...) at most 8 rows name the same one
- tile_count: int32 [32], P(('slab', 'pencil')), may hold values from 8 to 32, as said below
Outputs:
- vorticity_out: float32 [3, 64, 128, 256], P(None, 'slab', 'pencil')
- far_velocity: float32 [3, 8, 4, 16], P(None, 'slab', 'pencil')
The draws below stay inside these ranges and needn't reach their ends.
Inputs may be any that keep to these rules, and one draw needn't show every extreme that they name: Tiles of device (s, p) go to device (tile_dest, p). Among the 32 tiles of one device, at most 8 name one slab, a bound that some block reaches. The live tiles of a device are its first tile_count ones; some device has all 32 live.
All inputs are finite; a program needn't handle non-finite values.
Results may differ from the reference program's by a relative error of at most 0.0003.
Values sent between devices are 32-bit elements; how exact they have to be, the bound alone decides.
No kernel may reach another device: no remote copies, remote signals or barrier semaphores. Data moves between devices by JAX's collectives and lax.ppermute only.
A program may use at most 128 MiB of HBM per device.

```python
import math
import jax
import jax.numpy as jnp
import numpy as np
from jax import lax

CX = 8
CY = 32
NZ = 256
TILES = 32
CB = 16
TC = 128
NX = 64
NY = 128
CELLS = 65536
NCL = 16
CAP = 8
TILES_ALL = 1024
SIGMA = 16
N_SLAB = 8
N_PENCIL = 4


def draw_vorticity(key, part):
    first = jax.random.fold_in(key, 0)
    shape = (3, NX, NY, NZ)
    return jax.random.normal(first, shape, jnp.float32)


def draw_tile_count(key, part):
    first, second = jax.random.split(jax.random.fold_in(key, 7))
    devices_all = N_SLAB * N_PENCIL
    counts = jax.random.randint(first, (devices_all,), TILES // 4, TILES + 1, jnp.int32)
    chosen = jax.random.randint(second, (), 0, devices_all, jnp.int32)
    return counts.at[chosen].set(TILES)


def touch_ends(drawn, stream_key, low, largest):
    place = [jax.random.randint(jax.random.fold_in(stream_key, axis), (), 0, length) for axis, length in enumerate(drawn.shape)]
    widest = drawn.shape.index(max(drawn.shape))
    next_to = place[:widest] + [(place[widest] + 1) % drawn.shape[widest]] + place[widest + 1:]
    return drawn.at[tuple(place)].set(low).at[tuple(next_to)].set(largest)


def shard_levels(rng, extent, cuts, low, high):
    def one(axis_at, blocks):
        steps = jax.random.uniform(jax.random.fold_in(jax.random.fold_in(rng, 6), axis_at), (blocks,), jnp.float32, low / len(cuts), high / len(cuts))
        return jnp.repeat(jnp.exp(steps), extent[axis_at] // blocks).reshape((-1,) + (1,) * (len(extent) - axis_at - 1))

    gain = one(*cuts[0])
    for cut in cuts[1:]:
        gain = gain * one(*cut)
    return gain


def assign_block(stream_key, own, number, rows, amount, top, reach, slope):
    ranking = jax.random.permutation(stream_key, amount)
    crowded, ordinary = load_shares(amount, rows * top, reach, slope, True), load_shares(amount, rows * top, reach, slope, False)
    places = jnp.arange(amount)

    def named(lengths, turn):
        used = int((lengths > 0).sum())
        fixed = max(1, used // 4)
        passed = fixed + (places - fixed + turn * (used - fixed)) % max(1, amount - fixed)
        return jnp.zeros((amount,), jnp.int32).at[ranking[jnp.where(places < fixed, places, passed)]].set(jnp.asarray(lengths, jnp.int32))

    lengths = jnp.where(number % 4 == 0, named(crowded, number // 4), named(ordinary, number - number // 4 - 1))
    mixed = jax.random.permutation(jax.random.fold_in(own, 3), amount)
    donor, taker = mixed[0:amount // 2 * 2:2], mixed[1:amount // 2 * 2:2]
    margin = jnp.minimum(lengths[donor] - 1, reach - lengths[taker]) // 2
    margin = jnp.where((donor == ranking[0]) | (taker == ranking[0]) | (lengths[taker] == 0), 0, jnp.maximum(margin, 0))
    passed = jax.random.randint(jax.random.fold_in(own, 4), (amount // 2,), 0, 1 << 20) % (margin + 1)
    lengths = lengths.at[donor].add(-passed).at[taker].add(passed)
    labels = jnp.searchsorted(jnp.cumsum(lengths), jnp.arange(rows * top), side="right").astype(jnp.int32)
    grid = labels.reshape(top, rows).T
    grid = grid[jax.random.permutation(jax.random.fold_in(own, 1), rows)]
    turn = jax.random.randint(jax.random.fold_in(own, 2), (rows, 1), 0, top)
    return jnp.take_along_axis(grid, (jnp.arange(top)[None, :] + turn) % top, axis=1)


def load_shares(amount, total, limit, skew, full):
    weights = [(1 << 20) // math.isqrt(standing ** skew) + 1 for standing in range(1, amount + 1)]
    largest = limit if full else min(limit, max(-(-total // amount), total * weights[0] // sum(weights)))
    least = 1 if total - largest >= amount - 1 else 0
    holding, surplus = [largest] + [least] * (amount - 1), total - largest - least * (amount - 1)
    while surplus > 0:
        free = [i for i in range(1, amount) if holding[i] < largest] or [i for i in range(1, amount) if holding[i] < limit]
        mass, budget = sum([weights[i] for i in free]), surplus
        for i in free:
            more = min(limit - holding[i], max(1, budget * weights[i] // mass), surplus)
            holding[i] = holding[i] + more
            surplus = surplus - more
    return np.array(holding)


def bell_draw(own_key, shape, spread, limit, cuts=(), kind=jnp.bfloat16):
    result = jax.random.normal(own_key, shape, jnp.float32) * spread
    if len(cuts) > 0:
        result = shard_levels(own_key, shape, cuts, -0.22, 0.18) * result
    return jnp.clip(result, min=-limit, max=limit).astype(kind)


def setup_inputs(seed: int = 0) -> dict:
    key_of = jax.random.split(jax.random.key(seed), 8)
    vorticity = draw_vorticity(jax.random.fold_in(key_of[7], 71), 0)
    velocity = bell_draw(key_of[1], (3, NX, NY, NZ), 1.0, 6.0, ((1, 8), (2, 4)), jnp.float32)
    viscosity = jnp.clip(jnp.exp(math.log(0.4) - 2.9957323 * jax.random.uniform(key_of[2], (NX, NY, NZ), jnp.float32) ** shard_levels(key_of[2], (NX, NY, NZ), ((0, 8), (1, 4)), -0.2, 0.2)), 0.02, 0.4)
    tile_weights = bell_draw(key_of[3], (TILES_ALL, 3, TC), 1.0, 6.0, ((0, 32),), jnp.float32)
    tile_cells = touch_ends(jax.random.randint(key_of[4], (TILES_ALL, TC), 0, CELLS), jax.random.fold_in(key_of[4], 1), 0, CELLS - 1).astype(jnp.int32)
    tile_dest_keys = jax.random.split(jax.random.fold_in(key_of[5], 1), TILES_ALL // TILES)
    tile_dest_turns = jax.random.permutation(jax.random.fold_in(key_of[5], 3), TILES_ALL // TILES)
    tile_dest = jax.vmap(lambda own, number: assign_block(jax.random.fold_in(key_of[5], 2), own, number, TILES, N_SLAB, 1, CAP, 2))(tile_dest_keys, tile_dest_turns).reshape((TILES_ALL, 1))
    tile_count = draw_tile_count(jax.random.fold_in(key_of[7], 71), 0)
    return {"vorticity": vorticity, "velocity": velocity, "viscosity": viscosity, "tile_weights": tile_weights, "tile_cells": tile_cells, "tile_dest": tile_dest, "tile_count": tile_count}


time_step = 0.1

def interior(a):
    return a[..., 1:-1, 1:-1, :]

def ahead_x(a):
    return a[..., 2:, 1:-1, :]

def behind_x(a):
    return a[..., :-2, 1:-1, :]

def ahead_y(a):
    return a[..., 1:-1, 2:, :]

def behind_y(a):
    return a[..., 1:-1, :-2, :]

def ahead_z(a):
    return jnp.roll(interior(a), -1, axis=-1)

def behind_z(a):
    return jnp.roll(interior(a), 1, axis=-1)

def advance(padded):
    vort_all = padded[0:3]
    velo_all = padded[3:6]
    visc_all = padded[6]
    stencil_pairs = ((ahead_x, behind_x), (ahead_y, behind_y), (ahead_z, behind_z))
    own_vort = interior(vort_all)
    own_visc = interior(visc_all)
    stretch = jnp.zeros_like(own_vort)
    diffuse = jnp.zeros_like(own_vort)
    for axis_num in range(3):
        forward, backward = stencil_pairs[axis_num]
        stretch = stretch + own_vort[axis_num] * (0.5 * (forward(velo_all) - backward(velo_all)))
        for neighbour in stencil_pairs[axis_num]:
            diffuse = diffuse + 0.5 * (own_visc + neighbour(visc_all)) * (neighbour(vort_all) - own_vort)
    return own_vort + time_step * (stretch + diffuse)

def centres(cols, cx, cy, cb, npencil, ncl):
    slab_idx = cols // (npencil * ncl)
    pencil_idx = cols // ncl % npencil
    level = cols % ncl
    xpos = (slab_idx * cx).astype(jnp.float32) + (cx - 1) * 0.5
    ypos = (pencil_idx * cy).astype(jnp.float32) + (cy - 1) * 0.5
    zpos = (level * cb).astype(jnp.float32) + (cb - 1) * 0.5
    return (xpos, ypos, zpos)

def far_terms(targets, sources, moments, sigma):
    high = lax.Precision.HIGHEST
    rel_x = targets[0][:, None] - sources[0][None, :]
    rel_y = targets[1][:, None] - sources[1][None, :]
    rel_z = targets[2][:, None] - sources[2][None, :]
    dist_sq = rel_x * rel_x + rel_y * rel_y + rel_z * rel_z + sigma * sigma
    inverse = lax.rsqrt(dist_sq)
    weight = inverse * inverse * inverse
    trans = moments.T
    along_x = jnp.dot(weight * rel_x, trans, precision=high)
    along_y = jnp.dot(weight * rel_y, trans, precision=high)
    along_z = jnp.dot(weight * rel_z, trans, precision=high)
    first = along_z[:, 1] - along_y[:, 2]
    second = along_x[:, 2] - along_z[:, 0]
    third = along_y[:, 0] - along_x[:, 1]
    return jnp.stack([first, second, third], 0)

def reference(vorticity, velocity, viscosity, tile_weights, tile_cells, tile_dest, tile_count):
    stacked = jnp.concatenate([vorticity, velocity, viscosity[None]], 0)
    padded = jnp.pad(stacked, ((0, 0), (1, 1), (1, 1), (0, 0)))
    advanced = advance(padded)
    rows = jnp.arange(TILES_ALL, dtype=jnp.int32)
    device = rows // TILES
    pencil_idx = device % N_PENCIL
    live = (rows % TILES < tile_count[device]).astype(jnp.float32)
    cells = tile_cells
    local_x = cells // (CY * NZ)
    local_y = cells // NZ % CY
    local_z = cells % NZ
    grid_x = tile_dest[:, 0:1] * CX + local_x
    grid_y = pencil_idx[:, None] * CY + local_y
    flat = ((grid_x * NY + grid_y) * NZ + local_z).astype(jnp.int32)
    values = tile_weights * live[:, None, None]
    values = jnp.transpose(values, (1, 0, 2)).reshape(3, -1)
    field = advanced.reshape(3, NX * NY * NZ)
    field = field.at[:, flat.reshape(-1)].add(values)
    vorticity_out = field.reshape(3, NX, NY, NZ)
    moment = vorticity_out.reshape(3, N_SLAB, CX, N_PENCIL, CY, NCL, CB).sum(axis=(2, 4, 6))
    moment = moment.reshape(3, N_SLAB * N_PENCIL * NCL)
    all_cols = jnp.arange(N_SLAB * N_PENCIL * NCL, dtype=jnp.int32)
    sources = centres(all_cols, CX, CY, CB, N_PENCIL, NCL)
    sigma = jnp.float32(SIGMA)

    def per_device(dev):
        cols = dev * NCL + jnp.arange(NCL, dtype=jnp.int32)
        return far_terms(centres(cols, CX, CY, CB, N_PENCIL, NCL), sources, moment, sigma)
    blocks = lax.map(per_device, jnp.arange(N_SLAB * N_PENCIL, dtype=jnp.int32))
    far_velocity = jnp.transpose(blocks, (1, 0, 2)).reshape(3, N_SLAB, N_PENCIL, NCL)
    return (vorticity_out, far_velocity)
```

```python
import functools

import jax
import jax.numpy as jnp
from jax import lax
from jax.experimental import pallas as pl
from jax.experimental.pallas import tpu as pltpu
from jax.sharding import PartitionSpec as P

CB = 16
TIME_STEP = 0.1
LANES = 128
GROUP = 4
VMEM_LIMIT = 48 * 1024 * 1024

VMEM = pl.BlockSpec(memory_space=pltpu.VMEM)
SMEM = pl.BlockSpec(memory_space=pltpu.SMEM)
PARAMS = pltpu.CompilerParams(vmem_limit_bytes=VMEM_LIMIT)


def shaped(*shape):
    return jax.ShapeDtypeStruct(shape, jnp.float32)


def pack_kernel(cap, vort, velo, visc, weights, cells, dest, count, xlo, xhi, ylo, yhi, packets, filled):
    cx, cy = visc.shape[0], visc.shape[1]
    for face, at in ((xlo, 0), (xhi, cx - 1)):
        face[0:3] = vort[:, at]
        face[3:6] = velo[:, at]
        face[6] = visc[at]
    for face, at in ((ylo, 0), (yhi, cy - 1)):
        for x in range(cx):
            for c in range(3):
                face[c, x : x + 1, :] = vort[c, x, at : at + 1, :]
                face[3 + c, x : x + 1, :] = velo[c, x, at : at + 1, :]
            face[6, x : x + 1, :] = visc[x, at : at + 1, :]
    packets[...] = jnp.zeros_like(packets)
    n_slab = packets.shape[0] // cap
    for d in range(n_slab):
        filled[d] = 0

    def place(r, carry):
        d = dest[r, 0]
        slot = filled[d]
        at = d * cap + slot
        packets[at, 0:3, :] = weights[r]
        packets[at, 3:4, :] = cells[pl.ds(r, 1), :].astype(jnp.float32)
        filled[d] = slot + 1
        return carry

    lax.fori_loop(0, count[0], place, 0)


def pack(vort, velo, visc, weights, cells, dest, count, n_slab):
    _, cx, cy, nz = vort.shape
    cap = 2 * weights.shape[0] // n_slab
    return pl.pallas_call(
        functools.partial(pack_kernel, cap),
        out_shape=(
            shaped(7, cy, nz),
            shaped(7, cy, nz),
            shaped(7, cx, nz),
            shaped(7, cx, nz),
            shaped(n_slab * cap, 4, weights.shape[2]),
        ),
        in_specs=[VMEM] * 5 + [SMEM] * 2,
        out_specs=(VMEM,) * 5,
        scratch_shapes=[pltpu.SMEM((n_slab,), jnp.int32)],
        compiler_params=PARAMS,
    )(vort, velo, visc, weights, cells, dest, count)


def ahead(a, axis):
    return pltpu.roll(a, a.shape[axis] - 1, axis)


def behind(a, axis):
    return pltpu.roll(a, 1, axis)


def interior_step(vort, velo, visc, out):
    cx, cy, nz = visc.shape
    row = lax.broadcasted_iota(jnp.int32, (cy, nz), 0)
    has_ahead = row < cy - 1
    has_behind = row > 0
    for x in range(cx):
        nu = visc[x]
        spin = [vort[c, x] for c in range(3)]
        mean_y = jnp.where(has_ahead, 0.5 * (nu + ahead(nu, 0)), 0.0)
        mean_z = 0.5 * (nu + ahead(nu, 1))
        if x < cx - 1:
            mean_next = 0.5 * (nu + visc[x + 1])
        if x > 0:
            mean_last = 0.5 * (nu + visc[x - 1])
        for c in range(3):
            w = spin[c]
            u = velo[c, x]
            flux_y = mean_y * (ahead(w, 0) - w)
            flux_z = mean_z * (ahead(w, 1) - w)
            change = (flux_y - behind(flux_y, 0)) + (flux_z - behind(flux_z, 1))
            slope_y = jnp.where(has_ahead, ahead(u, 0), 0.0) - jnp.where(has_behind, behind(u, 0), 0.0)
            slope_z = ahead(u, 1) - behind(u, 1)
            if x == 0:
                slope_x = velo[c, x + 1]
            elif x == cx - 1:
                slope_x = -velo[c, x - 1]
            else:
                slope_x = velo[c, x + 1] - velo[c, x - 1]
            stretch = 0.5 * (spin[0] * slope_x + spin[1] * slope_y + spin[2] * slope_z)
            if x < cx - 1:
                change = change + mean_next * (vort[c, x + 1] - w)
            if x > 0:
                change = change + mean_last * (vort[c, x - 1] - w)
            out[c, x] = w + TIME_STEP * (stretch + change)


def deposit(packets, out):
    _, cx, cy, nz = out.shape
    rows = cx * cy
    wide = GROUP * packets.shape[2]
    row_iota = lax.broadcasted_iota(jnp.int32, (rows, wide), 0)
    col_iota = row_iota if nz == rows else lax.broadcasted_iota(jnp.int32, (nz, wide), 0)

    def group(g, carry):
        tiles = [packets[g * GROUP + k] for k in range(GROUP)]
        block = jnp.concatenate(tiles, axis=1)
        cell = block[3:4, :].astype(jnp.int32)
        at_row = row_iota == cell // nz
        at_col = col_iota == cell % nz
        spots = at_col.astype(jnp.float32).astype(jnp.bfloat16)
        parts = []
        for c in range(3):
            w = block[c : c + 1, :]
            high = w.astype(jnp.bfloat16).astype(jnp.float32)
            low = w - high
            parts.append(
                jnp.concatenate(
                    [jnp.where(at_row, piece, 0.0).astype(jnp.bfloat16) for piece in (high, low)], axis=1
                )
            )
        left = jnp.concatenate(parts, axis=0)
        right = jnp.concatenate([spots, spots], axis=1)
        added = lax.dot_general(
            left, right, (((1,), (1,)), ((), ())), preferred_element_type=jnp.float32
        )
        out[...] += added.reshape(out.shape)
        return carry

    lax.fori_loop(0, packets.shape[0] // GROUP, group, 0)


def inner_kernel(vort, velo, visc, packets, out, sums):
    interior_step(vort, velo, visc, out)
    deposit(packets, out)
    for c in range(3):
        sums[c : c + 1, :] = jnp.sum(out[c].reshape(-1, out.shape[3]), axis=0, keepdims=True)


def inner(vort, velo, visc, packets):
    return pl.pallas_call(
        inner_kernel,
        out_shape=(shaped(*vort.shape), shaped(3, vort.shape[3])),
        in_specs=[VMEM] * 4,
        out_specs=(VMEM,) * 2,
        compiler_params=PARAMS,
    )(vort, velo, visc, packets)


def face_change(own, other, along, sign, c):
    stretch = (0.5 * sign) * own[along] * other[3 + c]
    diffuse = 0.5 * (own[6] + other[6]) * (other[c] - own[c])
    return TIME_STEP * (stretch + diffuse)


def edge_kernel(inside, sums, xlo, xhi, ylo, yhi, xlo_in, xhi_in, ylo_in, yhi_in, out, moments):
    _, cx, cy, nz = out.shape
    out[...] = inside[...]
    row = lax.broadcasted_iota(jnp.int32, (nz, LANES), 0)
    lane = lax.broadcasted_iota(jnp.int32, (nz, LANES), 1)
    packed = jnp.zeros((1, LANES), jnp.float32)
    for c in range(3):
        total = sums[c : c + 1, :]
        for own, other, at, sign in ((xlo, xlo_in, 0, -1.0), (xhi, xhi_in, cx - 1, 1.0)):
            change = face_change(own, other, 0, sign, c)
            out[c, at] = out[c, at] + change
            total = total + jnp.sum(change, axis=0, keepdims=True)
        for own, other, at, sign in ((ylo, ylo_in, 0, -1.0), (yhi, yhi_in, cy - 1, 1.0)):
            change = face_change(own, other, 1, sign, c)
            for x in range(cx):
                out[c, x, at : at + 1, :] = out[c, x, at : at + 1, :] + change[x : x + 1, :]
            total = total + jnp.sum(change, axis=0, keepdims=True)
        gather = (lane == row // CB + c * (nz // CB)).astype(jnp.float32)
        packed = packed + jnp.dot(total, gather, precision=lax.Precision.HIGHEST, preferred_element_type=jnp.float32)
    for k in range(moments.shape[0]):
        moments[k] = packed


def edges(inside, sums, faces, halos, n_all):
    return pl.pallas_call(
        edge_kernel,
        out_shape=(shaped(*inside.shape), shaped(n_all, 1, LANES)),
        in_specs=[VMEM] * 10,
        out_specs=(VMEM,) * 2,
        compiler_params=PARAMS,
    )(inside, sums, *faces, *halos)


def far_kernel(cx, cy, ncl, n_slab, n_pencil, moments, out):
    n_all = n_slab * n_pencil
    shape = (n_all, LANES)
    slab = lax.axis_index("slab")
    pencil = lax.axis_index("pencil")
    source = lax.broadcasted_iota(jnp.int32, shape, 0)
    lane = lax.broadcasted_iota(jnp.int32, shape, 1)
    level = lane % ncl
    sigma = jnp.float32(cx * n_slab // 4)
    rel_x = ((slab - source // n_pencil) * cx).astype(jnp.float32)
    rel_y = ((pencil - source % n_pencil) * cy).astype(jnp.float32)
    flat = rel_x * rel_x + rel_y * rel_y
    moment = moments[...].reshape(shape)
    along = ([], [], [])
    for i in range(ncl):
        rel_z = ((i - level) * CB).astype(jnp.float32)
        inverse = lax.rsqrt(flat + rel_z * rel_z + sigma * sigma)
        weighted = (inverse * inverse * inverse) * moment
        for rows, rel in zip(along, (rel_x, rel_y, rel_z)):
            rows.append(jnp.sum(rel * weighted, axis=0, keepdims=True))
    part = lax.broadcasted_iota(jnp.int32, (8, LANES), 0)
    pick = (lax.broadcasted_iota(jnp.int32, (8, LANES), 1) // ncl == part).astype(jnp.float32)
    by_x, by_y, by_z = [
        lax.dot_general(
            pick,
            jnp.concatenate(rows, axis=0),
            (((1,), (1,)), ((), ())),
            precision=lax.Precision.HIGHEST,
            preferred_element_type=jnp.float32,
        )
        for rows in along
    ]
    out[0, 0] = by_z[1:2] - by_y[2:3]
    out[1, 0] = by_x[2:3] - by_z[0:1]
    out[2, 0] = by_y[0:1] - by_x[1:2]


def far(moments, cx, cy, ncl, n_slab, n_pencil):
    return pl.pallas_call(
        functools.partial(far_kernel, cx, cy, ncl, n_slab, n_pencil),
        out_shape=shaped(3, 1, 1, ncl),
        in_specs=[VMEM],
        out_specs=VMEM,
        compiler_params=PARAMS,
    )(moments)


def shift(array, axis, step):
    n = lax.axis_size(axis)
    pairs = [(i, i + step) for i in range(n) if 0 <= i + step < n]
    return lax.ppermute(array, axis, pairs)


def per_device(vorticity, velocity, viscosity, tile_weights, tile_cells, tile_dest, tile_count):
    _, cx, cy, nz = vorticity.shape
    n_slab = lax.axis_size("slab")
    n_pencil = lax.axis_size("pencil")
    n_all = n_slab * n_pencil
    xlo, xhi, ylo, yhi, packets = pack(
        vorticity, velocity, viscosity, tile_weights, tile_cells, tile_dest, tile_count, n_slab
    )
    arrived = lax.all_to_all(packets, "slab", 0, 0, tiled=True)
    xlo_in = shift(xhi, "slab", 1)
    xhi_in = shift(xlo, "slab", -1)
    ylo_in = shift(yhi, "pencil", 1)
    yhi_in = shift(ylo, "pencil", -1)
    inside, sums = inner(vorticity, velocity, viscosity, arrived)
    vorticity_out, moments = edges(
        inside, sums, (xlo, xhi, ylo, yhi), (xlo_in, xhi_in, ylo_in, yhi_in), n_all
    )
    gathered = lax.all_to_all(moments, ("slab", "pencil"), 0, 0, tiled=True)
    far_velocity = far(gathered, cx, cy, nz // CB, n_slab, n_pencil)
    return (vorticity_out, far_velocity)


def solution(mesh):
    in_specs = (
        P(None, "slab", "pencil", None),
        P(None, "slab", "pencil", None),
        P("slab", "pencil", None),
        P(("slab", "pencil"), None, None),
        P(("slab", "pencil"), None),
        P(("slab", "pencil"), None),
        P(("slab", "pencil")),
    )
    out_specs = (P(None, "slab", "pencil", None), P(None, "slab", "pencil", None))
    return jax.shard_map(
        per_device, mesh=mesh, in_specs=in_specs, out_specs=out_specs, check_vma=False
    )
```

```python
import functools

import jax
import jax.numpy as jnp
from jax import lax
from jax.experimental import pallas as pl
from jax.experimental.pallas import tpu as pltpu
from jax.sharding import PartitionSpec as P

CB = 16
TIME_STEP = 0.1
LANES = 128
GROUP = 4
VMEM_LIMIT = 48 * 1024 * 1024

VMEM = pl.BlockSpec(memory_space=pltpu.VMEM)
HBM = pl.BlockSpec(memory_space=pltpu.HBM)
SMEM = pl.BlockSpec(memory_space=pltpu.SMEM)
PARAMS = pltpu.CompilerParams(vmem_limit_bytes=VMEM_LIMIT)


def shaped(*shape):
    return jax.ShapeDtypeStruct(shape, jnp.float32)


def faces_kernel(vort, velo, visc, xlo, xhi, ylo, yhi, spin_rows, velo_rows, visc_rows, sems):
    cx, cy = visc.shape[0], visc.shape[1]
    copies = []

    def copy(source, target):
        copies.append(pltpu.make_async_copy(source, target, sems.at[len(copies)]))
        copies[-1].start()

    for k, at in ((0, 0), (1, cy - 8)):
        copy(vort.at[:, :, pl.ds(at, 8), :], spin_rows.at[k])
        copy(velo.at[:, :, pl.ds(at, 8), :], velo_rows.at[k])
        copy(visc.at[:, pl.ds(at, 8), :], visc_rows.at[k])
    for face, at in ((xlo, 0), (xhi, cx - 1)):
        copy(vort.at[:, at], face.at[0:3])
        copy(velo.at[:, at], face.at[3:6])
        copy(visc.at[at], face.at[6])
    for k in range(6):
        copies[k].wait()
    for k, face, at in ((0, ylo, 0), (1, yhi, 7)):
        for x in range(cx):
            for c in range(3):
                face[c, x : x + 1, :] = spin_rows[k, c, x, at : at + 1, :]
                face[3 + c, x : x + 1, :] = velo_rows[k, c, x, at : at + 1, :]
            face[6, x : x + 1, :] = visc_rows[k, x, at : at + 1, :]
    for k in range(6, 12):
        copies[k].wait()


def faces_of(vort, velo, visc):
    _, cx, cy, nz = vort.shape
    return pl.pallas_call(
        faces_kernel,
        out_shape=(shaped(7, cy, nz), shaped(7, cy, nz), shaped(7, cx, nz), shaped(7, cx, nz)),
        in_specs=[HBM] * 3,
        out_specs=(VMEM,) * 4,
        scratch_shapes=[
            pltpu.VMEM((2, 3, cx, 8, nz), jnp.float32),
            pltpu.VMEM((2, 3, cx, 8, nz), jnp.float32),
            pltpu.VMEM((2, cx, 8, nz), jnp.float32),
            pltpu.SemaphoreType.DMA((12,)),
        ],
        compiler_params=PARAMS,
    )(vort, velo, visc)


def ahead(a, axis):
    return pltpu.roll(a, a.shape[axis] - 1, axis)


def behind(a, axis):
    return pltpu.roll(a, 1, axis)


def interior_step(vort, velo, visc, out):
    cx, cy, nz = visc.shape
    row = lax.broadcasted_iota(jnp.int32, (cy, nz), 0)
    has_ahead = row < cy - 1
    has_behind = row > 0
    for x in range(cx):
        nu = visc[x]
        spin = [vort[c, x] for c in range(3)]
        mean_y = jnp.where(has_ahead, 0.5 * (nu + ahead(nu, 0)), 0.0)
        mean_z = 0.5 * (nu + ahead(nu, 1))
        if x < cx - 1:
            mean_next = 0.5 * (nu + visc[x + 1])
        if x > 0:
            mean_last = 0.5 * (nu + visc[x - 1])
        for c in range(3):
            w = spin[c]
            u = velo[c, x]
            flux_y = mean_y * (ahead(w, 0) - w)
            flux_z = mean_z * (ahead(w, 1) - w)
            change = (flux_y - behind(flux_y, 0)) + (flux_z - behind(flux_z, 1))
            slope_y = jnp.where(has_ahead, ahead(u, 0), 0.0) - jnp.where(has_behind, behind(u, 0), 0.0)
            slope_z = ahead(u, 1) - behind(u, 1)
            if x == 0:
                slope_x = velo[c, x + 1]
            elif x == cx - 1:
                slope_x = -velo[c, x - 1]
            else:
                slope_x = velo[c, x + 1] - velo[c, x - 1]
            stretch = 0.5 * (spin[0] * slope_x + spin[1] * slope_y + spin[2] * slope_z)
            if x < cx - 1:
                change = change + mean_next * (vort[c, x + 1] - w)
            if x > 0:
                change = change + mean_last * (vort[c, x - 1] - w)
            out[c, x] = w + TIME_STEP * (stretch + change)


def split(w):
    high = w.astype(jnp.bfloat16).astype(jnp.float32)
    return high, w - high


def pack_tiles(cap, units, weights, cells, dest, count, packets, filled):
    n_slab = packets.shape[0] // (cap + units)
    packets[...] = jnp.zeros_like(packets)
    for d in range(n_slab):
        filled[d] = 0

    def place(r, carry):
        d = dest[0, r]
        slot = filled[d]
        at = d * (cap + units) + slot
        for c in range(3):
            packets[at, c : c + 1, :] = weights[c, pl.ds(r, 1), :]
        packets[at, 3:4, :] = cells[pl.ds(r, 1), :].astype(jnp.float32)
        filled[d] = slot + 1
        return carry

    lax.fori_loop(0, count[0], place, 0)
    for d in range(n_slab):
        held = filled[d].astype(jnp.float32)
        packets[d * (cap + units) + cap, 3:4, :] = jnp.full((1, LANES), held, jnp.float32)


def tile_moments(cap, units, nz, packets, moments):
    n_slab = packets.shape[0] // (cap + units)
    ncl = nz // CB
    wide = cap * packets.shape[2]
    level = lax.broadcasted_iota(jnp.int32, (ncl, wide), 0)
    found = []
    for d in range(n_slab):
        first = d * (cap + units)
        block = jnp.concatenate([packets[first + k] for k in range(cap)], axis=1)
        cell = block[3:4, :].astype(jnp.int32)
        spots = (level == cell % nz // CB).astype(jnp.float32).astype(jnp.bfloat16)
        high, low = split(block)
        left = jnp.concatenate([high, low], axis=0).astype(jnp.bfloat16)
        sums = lax.dot_general(left, spots, (((1,), (1,)), ((), ())), preferred_element_type=jnp.float32)
        found.append(sums[0:4] + sums[4:8])
    moments[...] = jnp.concatenate(found, axis=1)


def inner_kernel(
    cap, units, vort, velo, visc, weights, cells, dest, count, out, sums, packets, moments, filled
):
    pack_tiles(cap, units, weights, cells, dest, count, packets, filled)
    tile_moments(cap, units, out.shape[3], packets, moments)
    interior_step(vort, velo, visc, out)
    for c in range(3):
        sums[c : c + 1, :] = jnp.sum(out[c].reshape(-1, out.shape[3]), axis=0, keepdims=True)


def inner(vort, velo, visc, weights, cells, dest, count, n_slab, cap, units):
    nz = vort.shape[3]
    return pl.pallas_call(
        functools.partial(inner_kernel, cap, units),
        out_shape=(
            shaped(*vort.shape),
            shaped(3, nz),
            shaped(n_slab * (cap + units), 4, weights.shape[2]),
            shaped(4, n_slab * nz // CB),
        ),
        in_specs=[VMEM] * 5 + [SMEM] * 2,
        out_specs=(VMEM,) * 4,
        scratch_shapes=[pltpu.SMEM((n_slab,), jnp.int32)],
        compiler_params=PARAMS,
    )(vort, velo, visc, weights, cells, dest, count)


def face_change(own, other, along, sign, c):
    stretch = (0.5 * sign) * own[along] * other[3 + c]
    diffuse = 0.5 * (own[6] + other[6]) * (other[c] - own[c])
    return TIME_STEP * (stretch + diffuse)


def edge_kernel(
    cap, units, inside, sums, packets, tiles, xlo, xhi, ylo, yhi, xlo_in, xhi_in, ylo_in, yhi_in, out, load
):
    _, cx, cy, nz = out.shape
    n_slab = load.shape[0] // (cap + units)
    out[...] = inside[...]
    load[...] = packets[...]
    totals = []
    for c in range(3):
        total = sums[c : c + 1, :]
        for own, other, at, sign in ((xlo, xlo_in, 0, -1.0), (xhi, xhi_in, cx - 1, 1.0)):
            change = face_change(own, other, 0, sign, c)
            out[c, at] = out[c, at] + change
            total = total + jnp.sum(change, axis=0, keepdims=True)
        for own, other, at, sign in ((ylo, ylo_in, 0, -1.0), (yhi, yhi_in, cy - 1, 1.0)):
            change = face_change(own, other, 1, sign, c)
            for x in range(cx):
                out[c, x, at : at + 1, :] = out[c, x, at : at + 1, :] + change[x : x + 1, :]
            total = total + jnp.sum(change, axis=0, keepdims=True)
        totals.append(total)
    totals.append(jnp.zeros_like(totals[0]))
    shape = (nz, tiles.shape[1])
    level = lax.broadcasted_iota(jnp.int32, shape, 0) // CB
    lane = lax.broadcasted_iota(jnp.int32, shape, 1)
    own_slab = lax.axis_index("slab")
    pick = (lane == own_slab * (nz // CB) + level).astype(jnp.float32)
    moment = tiles[...] + jnp.dot(
        jnp.concatenate(totals, axis=0), pick, precision=lax.Precision.HIGHEST, preferred_element_type=jnp.float32
    )
    for d in range(n_slab):
        for k in range(units):
            at = d * (cap + units) + cap + k
            load[at, 0:3, :] = moment[0:3, k * LANES : (k + 1) * LANES]


def edges(inside, sums, packets, tiles, faces, halos, cap, units):
    return pl.pallas_call(
        functools.partial(edge_kernel, cap, units),
        out_shape=(shaped(*inside.shape), shaped(*packets.shape)),
        in_specs=[VMEM] * 12,
        out_specs=(VMEM,) * 2,
        compiler_params=PARAMS,
    )(inside, sums, packets, tiles, *faces, *halos)


def far_kernel(cap, units, cx, cy, ncl, load, out):
    n_pencil = out.shape[0]
    n_slab = load.shape[0] // (cap + units)
    slab = lax.axis_index("slab")
    pencil = lax.axis_index("pencil")
    moment = []
    for k in range(units):
        total = load[cap + k]
        for d in range(1, n_slab):
            total = total + load[d * (cap + units) + cap + k]
        moment.append(total)
    moment = jnp.concatenate(moment, axis=1)
    shape = (n_pencil * ncl, n_slab * ncl)
    target = lax.broadcasted_iota(jnp.int32, shape, 0)
    source = lax.broadcasted_iota(jnp.int32, shape, 1)
    sigma = jnp.float32(cx * n_slab // 4)
    rel_x = ((slab - source // ncl) * cx).astype(jnp.float32)
    rel_y = ((target // ncl - pencil) * cy).astype(jnp.float32)
    rel_z = ((target % ncl - source % ncl) * CB).astype(jnp.float32)
    inverse = lax.rsqrt(rel_x * rel_x + rel_y * rel_y + rel_z * rel_z + sigma * sigma)
    weight = inverse * inverse * inverse
    first, second, third = moment[0:1], moment[1:2], moment[2:3]
    turned = (
        weight * (rel_z * second - rel_y * third),
        weight * (rel_x * third - rel_z * first),
        weight * (rel_y * first - rel_x * second),
    )
    ones = jnp.ones((8, shape[1]), jnp.float32)
    out[...] = jnp.zeros_like(out)
    for c in range(3):
        row = lax.dot_general(
            ones,
            turned[c],
            (((1,), (1,)), ((), ())),
            precision=lax.Precision.HIGHEST,
            preferred_element_type=jnp.float32,
        )
        for p in range(n_pencil):
            out[p, c : c + 1, 0:ncl] = row[0:1, p * ncl : (p + 1) * ncl]


def far_parts(load, cx, cy, ncl, n_pencil, cap, units):
    return pl.pallas_call(
        functools.partial(far_kernel, cap, units, cx, cy, ncl),
        out_shape=shaped(n_pencil, 4, LANES),
        in_specs=[VMEM],
        out_specs=VMEM,
        compiler_params=PARAMS,
    )(load)


def total_kernel(parts, out):
    total = parts[0]
    for p in range(1, parts.shape[0]):
        total = total + parts[p]
    for c in range(3):
        out[c, 0] = total[c : c + 1, 0 : out.shape[3]]


def far_total(parts, ncl):
    return pl.pallas_call(
        total_kernel,
        out_shape=shaped(3, 1, 1, ncl),
        in_specs=[VMEM],
        out_specs=VMEM,
        compiler_params=PARAMS,
    )(parts)


def deposit_kernel(cap, units, inside, load, out, order):
    _, cx, cy, nz = out.shape
    rows = cx * cy
    n_slab = load.shape[0] // (cap + units)
    wide = GROUP * load.shape[2]
    out[...] = inside[...]
    listed = jnp.int32(0)
    for d in range(n_slab):
        first = d * (cap + units)
        held = jnp.max(load[first + cap, 3:4, :]).astype(jnp.int32)
        for k in range(cap):
            order[listed + k] = first + k
        listed = listed + held
    for k in range(GROUP):
        order[listed + k] = 0
    row_iota = lax.broadcasted_iota(jnp.int32, (rows, wide), 0)
    col_iota = lax.broadcasted_iota(jnp.int32, (nz, wide), 0)
    place = lax.broadcasted_iota(jnp.int32, (1, wide), 1) // load.shape[2]

    def group(g, carry):
        tiles = [load[order[g * GROUP + k]] for k in range(GROUP)]
        block = jnp.concatenate(tiles, axis=1)
        live = place < listed - g * GROUP
        cell = block[3:4, :].astype(jnp.int32)
        at_row = row_iota == jnp.where(live, cell // nz, -1)
        at_col = col_iota == cell % nz
        spots = at_col.astype(jnp.float32).astype(jnp.bfloat16)
        parts = []
        for c in range(3):
            pieces = [
                jnp.where(at_row, piece, 0.0).astype(jnp.bfloat16) for piece in split(block[c : c + 1, :])
            ]
            parts.append(jnp.concatenate(pieces, axis=1))
        left = jnp.concatenate(parts, axis=0)
        right = jnp.concatenate([spots, spots], axis=1)
        added = lax.dot_general(left, right, (((1,), (1,)), ((), ())), preferred_element_type=jnp.float32)
        out[...] += added.reshape(out.shape)
        return carry

    lax.fori_loop(0, (listed + GROUP - 1) // GROUP, group, 0)


def deposit(inside, load, cap, units):
    slots = load.shape[0] // (cap + units) * cap
    return pl.pallas_call(
        functools.partial(deposit_kernel, cap, units),
        out_shape=shaped(*inside.shape),
        in_specs=[VMEM] * 2,
        out_specs=VMEM,
        scratch_shapes=[pltpu.SMEM((slots + max(cap, GROUP),), jnp.int32)],
        compiler_params=PARAMS,
    )(inside, load)


def shift(array, axis, step):
    n = lax.axis_size(axis)
    pairs = [(i, i + step) for i in range(n) if 0 <= i + step < n]
    return lax.ppermute(array, axis, pairs)


def per_device(vorticity, velocity, viscosity, tile_weights, tile_cells, tile_dest, tile_count):
    _, cx, cy, nz = vorticity.shape
    ncl = nz // CB
    n_slab = lax.axis_size("slab")
    n_pencil = lax.axis_size("pencil")
    cap = 2 * tile_weights.shape[0] // n_slab
    units = n_slab * ncl // LANES
    faces = faces_of(vorticity, velocity, viscosity)
    xlo, xhi, ylo, yhi = faces
    halos = (
        shift(xhi, "slab", 1),
        shift(xlo, "slab", -1),
        shift(yhi, "pencil", 1),
        shift(ylo, "pencil", -1),
    )
    weights = jnp.transpose(tile_weights, (1, 0, 2))
    inside, sums, packets, tiles = inner(
        vorticity, velocity, viscosity, weights, tile_cells, tile_dest.T, tile_count, n_slab, cap, units
    )
    advanced, load = edges(inside, sums, packets, tiles, faces, halos, cap, units)
    load = lax.all_to_all(load, "slab", 0, 0, tiled=True)
    parts = far_parts(load, cx, cy, ncl, n_pencil, cap, units)
    parts = lax.all_to_all(parts, "pencil", 0, 0, tiled=True)
    vorticity_out = deposit(advanced, load, cap, units)
    return (vorticity_out, far_total(parts, ncl))


def solution(mesh):
    in_specs = (
        P(None, "slab", "pencil", None),
        P(None, "slab", "pencil", None),
        P("slab", "pencil", None),
        P(("slab", "pencil"), None, None),
        P(("slab", "pencil"), None),
        P(("slab", "pencil"), None),
        P(("slab", "pencil")),
    )
    out_specs = (P(None, "slab", "pencil", None), P(None, "slab", "pencil", None))
    return jax.shard_map(
        per_device, mesh=mesh, in_specs=in_specs, out_specs=out_specs, check_vma=False
    )
```

```python
import functools

import jax
import jax.numpy as jnp
from jax import lax
from jax.experimental import pallas as pl
from jax.experimental.pallas import tpu as pltpu
from jax.sharding import PartitionSpec as P

CB = 16
TIME_STEP = 0.1
LANES = 128
GROUP = 4
VMEM_LIMIT = 48 * 1024 * 1024

VMEM = pl.BlockSpec(memory_space=pltpu.VMEM)
ANY = pl.BlockSpec(memory_space=pl.ANY)
SMEM = pl.BlockSpec(memory_space=pltpu.SMEM)
FIRST_PARAMS = pltpu.CompilerParams(vmem_limit_bytes=60 * 1024 * 1024)
PARAMS = pltpu.CompilerParams(vmem_limit_bytes=VMEM_LIMIT)


def shaped(*shape):
    return jax.ShapeDtypeStruct(shape, jnp.float32)


def send_kernel(
    cap,
    vort,
    velo,
    visc,
    weights_in,
    cells_in,
    dest,
    count,
    xlo,
    xhi,
    ylo,
    yhi,
    packets,
    spin_rows,
    velo_rows,
    visc_rows,
    weights,
    cells,
    filled,
    sems,
):
    cx, cy, nz = visc.shape
    copies = []

    def copy(source, target):
        copies.append(pltpu.make_async_copy(source, target, sems.at[len(copies)]))
        copies[-1].start()

    copy(weights_in, weights)
    copy(cells_in, cells)
    for k, at in ((0, 0), (1, cy - 8)):
        copy(vort.at[:, :, pl.ds(at, 8), :], spin_rows.at[k])
        copy(velo.at[:, :, pl.ds(at, 8), :], velo_rows.at[k])
        copy(visc.at[:, pl.ds(at, 8), :], visc_rows.at[k])
    for face, at in ((xlo, 0), (xhi, cx - 1)):
        copy(vort.at[:, at], face.at[0:3])
        copy(velo.at[:, at], face.at[3:6])
        copy(visc.at[at], face.at[6])

    packets[...] = jnp.zeros_like(packets)
    n_slab = packets.shape[0] // cap
    for d in range(n_slab):
        filled[d] = 0
    copies[0].wait()
    copies[1].wait()

    def place(r, carry):
        d = dest[0, r]
        slot = filled[d]
        at = d * cap + slot
        for c in range(3):
            packets[at, c : c + 1, :] = weights[c, pl.ds(r, 1), :]
        packets[at, 3:4, :] = cells[pl.ds(r, 1), :].astype(jnp.float32)
        filled[d] = slot + 1
        return carry

    lax.fori_loop(0, count[0], place, 0)
    for d in range(n_slab):
        held = (filled[d] * (cx * cy * nz)).astype(jnp.float32)
        packets[d * cap, 3:4, :] = packets[d * cap, 3:4, :] + held
    for k in range(2, 8):
        copies[k].wait()
    for k, face, at in ((0, ylo, 0), (1, yhi, 7)):
        for x in range(cx):
            for c in range(3):
                face[c, x : x + 1, :] = spin_rows[k, c, x, at : at + 1, :]
                face[3 + c, x : x + 1, :] = velo_rows[k, c, x, at : at + 1, :]
            face[6, x : x + 1, :] = visc_rows[k, x, at : at + 1, :]
    for k in range(8, 14):
        copies[k].wait()


def to_send(vort, velo, visc, weights, cells, dest, count, n_slab, cap):
    _, cx, cy, nz = vort.shape
    return pl.pallas_call(
        functools.partial(send_kernel, cap),
        out_shape=(
            shaped(7, cy, nz),
            shaped(7, cy, nz),
            shaped(7, cx, nz),
            shaped(7, cx, nz),
            shaped(n_slab * cap, 4, weights.shape[2]),
        ),
        in_specs=[ANY] * 5 + [SMEM] * 2,
        out_specs=(ANY, ANY, VMEM, VMEM, VMEM),
        scratch_shapes=[
            pltpu.VMEM((2, 3, cx, 8, nz), jnp.float32),
            pltpu.VMEM((2, 3, cx, 8, nz), jnp.float32),
            pltpu.VMEM((2, cx, 8, nz), jnp.float32),
            pltpu.VMEM(weights.shape, jnp.float32),
            pltpu.VMEM(cells.shape, jnp.int32),
            pltpu.SMEM((n_slab,), jnp.int32),
            pltpu.SemaphoreType.DMA((14,)),
        ],
        compiler_params=FIRST_PARAMS,
    )(vort, velo, visc, weights, cells, dest, count)


def ahead(a, axis):
    return pltpu.roll(a, a.shape[axis] - 1, axis)


def behind(a, axis):
    return pltpu.roll(a, 1, axis)


def interior_step(vort, velo, visc, out):
    cx, cy, nz = visc.shape
    row = lax.broadcasted_iota(jnp.int32, (cy, nz), 0)
    has_ahead = row < cy - 1
    has_behind = row > 0
    for x in range(cx):
        nu = visc[x]
        spin = [vort[c, x] for c in range(3)]
        mean_y = jnp.where(has_ahead, 0.5 * (nu + ahead(nu, 0)), 0.0)
        mean_z = 0.5 * (nu + ahead(nu, 1))
        if x < cx - 1:
            mean_next = 0.5 * (nu + visc[x + 1])
        if x > 0:
            mean_last = 0.5 * (nu + visc[x - 1])
        for c in range(3):
            w = spin[c]
            u = velo[c, x]
            flux_y = mean_y * (ahead(w, 0) - w)
            flux_z = mean_z * (ahead(w, 1) - w)
            change = (flux_y - behind(flux_y, 0)) + (flux_z - behind(flux_z, 1))
            slope_y = jnp.where(has_ahead, ahead(u, 0), 0.0) - jnp.where(has_behind, behind(u, 0), 0.0)
            slope_z = ahead(u, 1) - behind(u, 1)
            if x == 0:
                slope_x = velo[c, x + 1]
            elif x == cx - 1:
                slope_x = -velo[c, x - 1]
            else:
                slope_x = velo[c, x + 1] - velo[c, x - 1]
            stretch = 0.5 * (spin[0] * slope_x + spin[1] * slope_y + spin[2] * slope_z)
            if x < cx - 1:
                change = change + mean_next * (vort[c, x + 1] - w)
            if x > 0:
                change = change + mean_last * (vort[c, x - 1] - w)
            out[c, x] = w + TIME_STEP * (stretch + change)


def split(w):
    high = w.astype(jnp.bfloat16).astype(jnp.float32)
    return high, w - high


def tile_moments(cap, nz, packets, moments):
    n_slab = packets.shape[0] // cap
    ncl = nz // CB
    wide = cap * packets.shape[2]
    level = lax.broadcasted_iota(jnp.int32, (ncl, wide), 0)
    found = []
    for d in range(n_slab):
        block = jnp.concatenate([packets[d * cap + k] for k in range(cap)], axis=1)
        cell = block[3:4, :].astype(jnp.int32)
        spots = (level == cell % nz // CB).astype(jnp.float32).astype(jnp.bfloat16)
        high, low = split(block)
        left = jnp.concatenate([high, low], axis=0).astype(jnp.bfloat16)
        sums = lax.dot_general(left, spots, (((1,), (1,)), ((), ())), preferred_element_type=jnp.float32)
        found.append(sums[0:4] + sums[4:8])
    moments[...] = jnp.concatenate(found, axis=1)


def inner_kernel(cap, vort, velo, visc, packets, out, sums, moments):
    tile_moments(cap, out.shape[3], packets, moments)
    interior_step(vort, velo, visc, out)
    for c in range(3):
        sums[c : c + 1, :] = jnp.sum(out[c].reshape(-1, out.shape[3]), axis=0, keepdims=True)


def inner(vort, velo, visc, packets, n_slab, cap):
    nz = vort.shape[3]
    return pl.pallas_call(
        functools.partial(inner_kernel, cap),
        out_shape=(shaped(*vort.shape), shaped(3, nz), shaped(4, n_slab * nz // CB)),
        in_specs=[VMEM] * 4,
        out_specs=(VMEM,) * 3,
        compiler_params=PARAMS,
    )(vort, velo, visc, packets)


def face_change(own, other, along, sign, c):
    stretch = (0.5 * sign) * own[along] * other[3 + c]
    diffuse = 0.5 * (own[6] + other[6]) * (other[c] - own[c])
    return TIME_STEP * (stretch + diffuse)


def edge_kernel(inside, sums, tiles, xlo, xhi, ylo, yhi, xlo_in, xhi_in, ylo_in, yhi_in, out, load):
    _, cx, cy, nz = out.shape
    out[...] = inside[...]
    totals = []
    for c in range(3):
        total = sums[c : c + 1, :]
        for own, other, at, sign in ((xlo, xlo_in, 0, -1.0), (xhi, xhi_in, cx - 1, 1.0)):
            change = face_change(own, other, 0, sign, c)
            out[c, at] = out[c, at] + change
            total = total + jnp.sum(change, axis=0, keepdims=True)
        for own, other, at, sign in ((ylo, ylo_in, 0, -1.0), (yhi, yhi_in, cy - 1, 1.0)):
            change = face_change(own, other, 1, sign, c)
            for x in range(cx):
                out[c, x, at : at + 1, :] = out[c, x, at : at + 1, :] + change[x : x + 1, :]
            total = total + jnp.sum(change, axis=0, keepdims=True)
        totals.append(total)
    totals.append(jnp.zeros_like(totals[0]))
    shape = (nz, tiles.shape[1])
    level = lax.broadcasted_iota(jnp.int32, shape, 0) // CB
    lane = lax.broadcasted_iota(jnp.int32, shape, 1)
    own_slab = lax.axis_index("slab")
    pick = (lane == own_slab * (nz // CB) + level).astype(jnp.float32)
    moment = tiles[...] + jnp.dot(
        jnp.concatenate(totals, axis=0), pick, precision=lax.Precision.HIGHEST, preferred_element_type=jnp.float32
    )
    for k in range(load.shape[1] // 4):
        part = moment[:, k * LANES : (k + 1) * LANES]
        for j in range(load.shape[0]):
            load[j, 4 * k : 4 * k + 4, :] = part


def edges(inside, sums, tiles, faces, halos, n_all):
    return pl.pallas_call(
        edge_kernel,
        out_shape=(shaped(*inside.shape), shaped(n_all, 4 * tiles.shape[1] // LANES, LANES)),
        in_specs=[VMEM] * 11,
        out_specs=(VMEM,) * 2,
        compiler_params=PARAMS,
    )(inside, sums, tiles, *faces, *halos)


def far_kernel(cx, cy, ncl, n_pencil, load, out):
    n_all = load.shape[0]
    n_slab = n_all // n_pencil
    slab = lax.axis_index("slab")
    pencil = lax.axis_index("pencil")
    shape = (ncl, n_slab * ncl)
    target = lax.broadcasted_iota(jnp.int32, shape, 0)
    source = lax.broadcasted_iota(jnp.int32, shape, 1)
    sigma = jnp.float32(cx * n_slab // 4)
    rel_x = ((slab - source // ncl) * cx).astype(jnp.float32)
    rel_z = ((target - source % ncl) * CB).astype(jnp.float32)
    flat = rel_x * rel_x + rel_z * rel_z + sigma * sigma
    turned = [jnp.zeros(shape, jnp.float32) for _ in range(3)]
    for p in range(n_pencil):
        total = load[p]
        for s in range(1, n_slab):
            total = total + load[s * n_pencil + p]
        moment = jnp.concatenate([total[4 * k : 4 * k + 4] for k in range(load.shape[1] // 4)], axis=1)
        first, second, third = moment[0:1], moment[1:2], moment[2:3]
        rel_y = ((pencil - p) * cy).astype(jnp.float32)
        inverse = lax.rsqrt(flat + rel_y * rel_y)
        weight = inverse * inverse * inverse
        turned[0] = turned[0] + weight * (rel_z * second - rel_y * third)
        turned[1] = turned[1] + weight * (rel_x * third - rel_z * first)
        turned[2] = turned[2] + weight * (rel_y * first - rel_x * second)
    ones = jnp.ones((8, shape[1]), jnp.float32)
    for c in range(3):
        row = lax.dot_general(
            ones,
            turned[c],
            (((1,), (1,)), ((), ())),
            precision=lax.Precision.HIGHEST,
            preferred_element_type=jnp.float32,
        )
        out[c, 0] = row[0:1]


def far(load, cx, cy, ncl, n_pencil):
    return pl.pallas_call(
        functools.partial(far_kernel, cx, cy, ncl, n_pencil),
        out_shape=shaped(3, 1, 1, ncl),
        in_specs=[VMEM],
        out_specs=VMEM,
        compiler_params=PARAMS,
    )(load)


def deposit_kernel(cap, inside, load, out, order):
    _, cx, cy, nz = out.shape
    rows = cx * cy
    cells = rows * nz
    n_slab = load.shape[0] // cap
    wide = GROUP * load.shape[2]
    out[...] = inside[...]
    listed = jnp.int32(0)
    for d in range(n_slab):
        first = d * cap
        held = jnp.max(load[first, 3:4, :]).astype(jnp.int32) // cells
        for k in range(cap):
            order[listed + k] = first + k
        listed = listed + held
    for k in range(GROUP):
        order[listed + k] = 0
    row_iota = lax.broadcasted_iota(jnp.int32, (rows, wide), 0)
    col_iota = lax.broadcasted_iota(jnp.int32, (nz, wide), 0)
    place = lax.broadcasted_iota(jnp.int32, (1, wide), 1) // load.shape[2]

    def group(g, carry):
        tiles = [load[order[g * GROUP + k]] for k in range(GROUP)]
        block = jnp.concatenate(tiles, axis=1)
        live = place < listed - g * GROUP
        cell = block[3:4, :].astype(jnp.int32) % cells
        at_row = row_iota == jnp.where(live, cell // nz, -1)
        at_col = col_iota == cell % nz
        spots = at_col.astype(jnp.float32).astype(jnp.bfloat16)
        parts = []
        for c in range(3):
            pieces = [
                jnp.where(at_row, piece, 0.0).astype(jnp.bfloat16) for piece in split(block[c : c + 1, :])
            ]
            parts.append(jnp.concatenate(pieces, axis=1))
        left = jnp.concatenate(parts, axis=0)
        right = jnp.concatenate([spots, spots], axis=1)
        added = lax.dot_general(left, right, (((1,), (1,)), ((), ())), preferred_element_type=jnp.float32)
        out[...] += added.reshape(out.shape)
        return carry

    lax.fori_loop(0, (listed + GROUP - 1) // GROUP, group, 0)


def deposit(inside, load, cap):
    return pl.pallas_call(
        functools.partial(deposit_kernel, cap),
        out_shape=shaped(*inside.shape),
        in_specs=[VMEM] * 2,
        out_specs=VMEM,
        scratch_shapes=[pltpu.SMEM((load.shape[0] + max(cap, GROUP),), jnp.int32)],
        compiler_params=PARAMS,
    )(inside, load)


def shift(array, axis, step):
    n = lax.axis_size(axis)
    pairs = [(i, i + step) for i in range(n) if 0 <= i + step < n]
    return lax.ppermute(array, axis, pairs)


def per_device(vorticity, velocity, viscosity, tile_weights, tile_cells, tile_dest, tile_count):
    _, cx, cy, nz = vorticity.shape
    ncl = nz // CB
    n_slab = lax.axis_size("slab")
    n_pencil = lax.axis_size("pencil")
    cap = 2 * tile_weights.shape[0] // n_slab
    weights = jnp.transpose(tile_weights, (1, 0, 2))
    *faces, packets = to_send(
        vorticity, velocity, viscosity, weights, tile_cells, tile_dest.T, tile_count, n_slab, cap
    )
    xlo, xhi, ylo, yhi = faces
    arrived = lax.all_to_all(packets, "slab", 0, 0, tiled=True)
    halos = (
        shift(xhi, "slab", 1),
        shift(xlo, "slab", -1),
        shift(yhi, "pencil", 1),
        shift(ylo, "pencil", -1),
    )
    inside, sums, tiles = inner(vorticity, velocity, viscosity, packets, n_slab, cap)
    advanced, load = edges(inside, sums, tiles, faces, halos, n_slab * n_pencil)
    load = lax.all_to_all(load, ("slab", "pencil"), 0, 0, tiled=True)
    vorticity_out = deposit(advanced, arrived, cap)
    return (vorticity_out, far(load, cx, cy, ncl, n_pencil))


def solution(mesh):
    in_specs = (
        P(None, "slab", "pencil", None),
        P(None, "slab", "pencil", None),
        P("slab", "pencil", None),
        P(("slab", "pencil"), None, None),
        P(("slab", "pencil"), None),
        P(("slab", "pencil"), None),
        P(("slab", "pencil")),
    )
    out_specs = (P(None, "slab", "pencil", None), P(None, "slab", "pencil", None))
    return jax.shard_map(
        per_device, mesh=mesh, in_specs=in_specs, out_specs=out_specs, check_vma=False
    )
```

```python
import functools

import jax
import jax.numpy as jnp
from jax import lax
from jax.experimental import pallas as pl
from jax.experimental.pallas import tpu as pltpu
from jax.sharding import PartitionSpec as P

CB = 16
TIME_STEP = 0.1
LANES = 128
GROUP = 4
VMEM_LIMIT = 48 * 1024 * 1024

VMEM = pl.BlockSpec(memory_space=pltpu.VMEM)
ANY = pl.BlockSpec(memory_space=pl.ANY)
SMEM = pl.BlockSpec(memory_space=pltpu.SMEM)
FIRST_PARAMS = pltpu.CompilerParams(vmem_limit_bytes=60 * 1024 * 1024)
PARAMS = pltpu.CompilerParams(vmem_limit_bytes=VMEM_LIMIT)


def shaped(*shape):
    return jax.ShapeDtypeStruct(shape, jnp.float32)


def send_kernel(
    cap,
    vort,
    velo,
    visc,
    weights_in,
    cells_in,
    dest_in,
    count_in,
    xlo,
    xhi,
    ylo,
    yhi,
    packets,
    spin_rows,
    velo_rows,
    visc_rows,
    weights,
    cells,
    dest,
    count,
    filled,
    sems,
):
    cx, cy, nz = visc.shape
    copies = []

    def copy(source, target):
        copies.append(pltpu.make_async_copy(source, target, sems.at[len(copies)]))
        copies[-1].start()

    copy(weights_in, weights)
    copy(cells_in, cells)
    copy(dest_in, dest)
    copy(count_in, count)
    for k, at in ((0, 0), (1, cy - 8)):
        copy(vort.at[:, :, pl.ds(at, 8), :], spin_rows.at[k])
        copy(velo.at[:, :, pl.ds(at, 8), :], velo_rows.at[k])
        copy(visc.at[:, pl.ds(at, 8), :], visc_rows.at[k])
    for face, at in ((xlo, 0), (xhi, cx - 1)):
        copy(vort.at[:, at], face.at[0:3])
        copy(velo.at[:, at], face.at[3:6])
        copy(visc.at[at], face.at[6])

    packets[...] = jnp.zeros_like(packets)
    n_slab = packets.shape[0] // cap
    for d in range(n_slab):
        filled[d] = 0
    for k in range(4):
        copies[k].wait()

    def place(r, carry):
        d = dest[0, r]
        slot = filled[d]
        at = d * cap + slot
        for c in range(3):
            packets[at, c : c + 1, :] = weights[c, pl.ds(r, 1), :]
        packets[at, 3:4, :] = cells[pl.ds(r, 1), :].astype(jnp.float32)
        filled[d] = slot + 1
        return carry

    lax.fori_loop(0, count[0], place, 0)
    for d in range(n_slab):
        held = (filled[d] * (cx * cy * nz)).astype(jnp.float32)
        packets[d * cap, 3:4, :] = packets[d * cap, 3:4, :] + held
    for k in range(4, 10):
        copies[k].wait()
    for k, face, at in ((0, ylo, 0), (1, yhi, 7)):
        for x in range(cx):
            for c in range(3):
                face[c, x : x + 1, :] = spin_rows[k, c, x, at : at + 1, :]
                face[3 + c, x : x + 1, :] = velo_rows[k, c, x, at : at + 1, :]
            face[6, x : x + 1, :] = visc_rows[k, x, at : at + 1, :]
    for k in range(10, 16):
        copies[k].wait()


def to_send(vort, velo, visc, weights, cells, dest, count, n_slab, cap):
    _, cx, cy, nz = vort.shape
    return pl.pallas_call(
        functools.partial(send_kernel, cap),
        out_shape=(
            shaped(7, cy, nz),
            shaped(7, cy, nz),
            shaped(7, cx, nz),
            shaped(7, cx, nz),
            shaped(n_slab * cap, 4, weights.shape[2]),
        ),
        in_specs=[ANY] * 7,
        out_specs=(VMEM,) * 5,
        scratch_shapes=[
            pltpu.VMEM((2, 3, cx, 8, nz), jnp.float32),
            pltpu.VMEM((2, 3, cx, 8, nz), jnp.float32),
            pltpu.VMEM((2, cx, 8, nz), jnp.float32),
            pltpu.VMEM(weights.shape, jnp.float32),
            pltpu.VMEM(cells.shape, jnp.int32),
            pltpu.SMEM(dest.shape, jnp.int32),
            pltpu.SMEM(count.shape, jnp.int32),
            pltpu.SMEM((n_slab,), jnp.int32),
            pltpu.SemaphoreType.DMA((16,)),
        ],
        compiler_params=FIRST_PARAMS,
    )(vort, velo, visc, weights, cells, dest, count)


def ahead(a, axis):
    return pltpu.roll(a, a.shape[axis] - 1, axis)


def behind(a, axis):
    return pltpu.roll(a, 1, axis)


def interior_step(vort, velo, visc, out):
    cx, cy, nz = visc.shape
    row = lax.broadcasted_iota(jnp.int32, (cy, nz), 0)
    has_ahead = row < cy - 1
    has_behind = row > 0
    for x in range(cx):
        nu = visc[x]
        spin = [vort[c, x] for c in range(3)]
        mean_y = jnp.where(has_ahead, 0.5 * (nu + ahead(nu, 0)), 0.0)
        mean_z = 0.5 * (nu + ahead(nu, 1))
        if x < cx - 1:
            mean_next = 0.5 * (nu + visc[x + 1])
        if x > 0:
            mean_last = 0.5 * (nu + visc[x - 1])
        for c in range(3):
            w = spin[c]
            u = velo[c, x]
            flux_y = mean_y * (ahead(w, 0) - w)
            flux_z = mean_z * (ahead(w, 1) - w)
            change = (flux_y - behind(flux_y, 0)) + (flux_z - behind(flux_z, 1))
            slope_y = jnp.where(has_ahead, ahead(u, 0), 0.0) - jnp.where(has_behind, behind(u, 0), 0.0)
            slope_z = ahead(u, 1) - behind(u, 1)
            if x == 0:
                slope_x = velo[c, x + 1]
            elif x == cx - 1:
                slope_x = -velo[c, x - 1]
            else:
                slope_x = velo[c, x + 1] - velo[c, x - 1]
            stretch = 0.5 * (spin[0] * slope_x + spin[1] * slope_y + spin[2] * slope_z)
            if x < cx - 1:
                change = change + mean_next * (vort[c, x + 1] - w)
            if x > 0:
                change = change + mean_last * (vort[c, x - 1] - w)
            out[c, x] = w + TIME_STEP * (stretch + change)


def split(w):
    high = w.astype(jnp.bfloat16).astype(jnp.float32)
    return high, w - high


def tile_moments(cap, nz, packets, moments):
    n_slab = packets.shape[0] // cap
    ncl = nz // CB
    wide = cap * packets.shape[2]
    level = lax.broadcasted_iota(jnp.int32, (ncl, wide), 0)
    found = []
    for d in range(n_slab):
        block = jnp.concatenate([packets[d * cap + k] for k in range(cap)], axis=1)
        cell = block[3:4, :].astype(jnp.int32)
        spots = (level == cell % nz // CB).astype(jnp.float32).astype(jnp.bfloat16)
        high, low = split(block)
        left = jnp.concatenate([high, low], axis=0).astype(jnp.bfloat16)
        sums = lax.dot_general(left, spots, (((1,), (1,)), ((), ())), preferred_element_type=jnp.float32)
        found.append(sums[0:4] + sums[4:8])
    moments[...] = jnp.concatenate(found, axis=1)


def inner_kernel(cap, vort, velo, visc, packets, out, sums, moments):
    tile_moments(cap, out.shape[3], packets, moments)
    interior_step(vort, velo, visc, out)
    for c in range(3):
        sums[c : c + 1, :] = jnp.sum(out[c].reshape(-1, out.shape[3]), axis=0, keepdims=True)


def inner(vort, velo, visc, packets, n_slab, cap):
    nz = vort.shape[3]
    return pl.pallas_call(
        functools.partial(inner_kernel, cap),
        out_shape=(shaped(*vort.shape), shaped(3, nz), shaped(4, n_slab * nz // CB)),
        in_specs=[VMEM] * 4,
        out_specs=(VMEM,) * 3,
        compiler_params=PARAMS,
    )(vort, velo, visc, packets)


def face_change(own, other, along, sign, c):
    stretch = (0.5 * sign) * own[along] * other[3 + c]
    diffuse = 0.5 * (own[6] + other[6]) * (other[c] - own[c])
    return TIME_STEP * (stretch + diffuse)


def edge_kernel(inside, sums, tiles, xlo, xhi, ylo, yhi, xlo_in, xhi_in, ylo_in, yhi_in, out, load):
    _, cx, cy, nz = out.shape
    out[...] = inside[...]
    totals = []
    for c in range(3):
        total = sums[c : c + 1, :]
        for own, other, at, sign in ((xlo, xlo_in, 0, -1.0), (xhi, xhi_in, cx - 1, 1.0)):
            change = face_change(own, other, 0, sign, c)
            out[c, at] = out[c, at] + change
            total = total + jnp.sum(change, axis=0, keepdims=True)
        for own, other, at, sign in ((ylo, ylo_in, 0, -1.0), (yhi, yhi_in, cy - 1, 1.0)):
            change = face_change(own, other, 1, sign, c)
            for x in range(cx):
                out[c, x, at : at + 1, :] = out[c, x, at : at + 1, :] + change[x : x + 1, :]
            total = total + jnp.sum(change, axis=0, keepdims=True)
        totals.append(total)
    totals.append(jnp.zeros_like(totals[0]))
    shape = (nz, tiles.shape[1])
    level = lax.broadcasted_iota(jnp.int32, shape, 0) // CB
    lane = lax.broadcasted_iota(jnp.int32, shape, 1)
    own_slab = lax.axis_index("slab")
    pick = (lane == own_slab * (nz // CB) + level).astype(jnp.float32)
    moment = tiles[...] + jnp.dot(
        jnp.concatenate(totals, axis=0), pick, precision=lax.Precision.HIGHEST, preferred_element_type=jnp.float32
    )
    for k in range(load.shape[1] // 4):
        part = moment[:, k * LANES : (k + 1) * LANES]
        for j in range(load.shape[0]):
            load[j, 4 * k : 4 * k + 4, :] = part


def edges(inside, sums, tiles, faces, halos, n_all):
    return pl.pallas_call(
        edge_kernel,
        out_shape=(shaped(*inside.shape), shaped(n_all, 4 * tiles.shape[1] // LANES, LANES)),
        in_specs=[VMEM] * 11,
        out_specs=(VMEM,) * 2,
        compiler_params=PARAMS,
    )(inside, sums, tiles, *faces, *halos)


def far_kernel(cx, cy, ncl, n_pencil, load, out):
    n_all = load.shape[0]
    n_slab = n_all // n_pencil
    slab = lax.axis_index("slab")
    pencil = lax.axis_index("pencil")
    shape = (ncl, n_slab * ncl)
    target = lax.broadcasted_iota(jnp.int32, shape, 0)
    source = lax.broadcasted_iota(jnp.int32, shape, 1)
    sigma = jnp.float32(cx * n_slab // 4)
    rel_x = ((slab - source // ncl) * cx).astype(jnp.float32)
    rel_z = ((target - source % ncl) * CB).astype(jnp.float32)
    flat = rel_x * rel_x + rel_z * rel_z + sigma * sigma
    turned = [jnp.zeros(shape, jnp.float32) for _ in range(3)]
    for p in range(n_pencil):
        total = load[p]
        for s in range(1, n_slab):
            total = total + load[s * n_pencil + p]
        moment = jnp.concatenate([total[4 * k : 4 * k + 4] for k in range(load.shape[1] // 4)], axis=1)
        first, second, third = moment[0:1], moment[1:2], moment[2:3]
        rel_y = ((pencil - p) * cy).astype(jnp.float32)
        inverse = lax.rsqrt(flat + rel_y * rel_y)
        weight = inverse * inverse * inverse
        turned[0] = turned[0] + weight * (rel_z * second - rel_y * third)
        turned[1] = turned[1] + weight * (rel_x * third - rel_z * first)
        turned[2] = turned[2] + weight * (rel_y * first - rel_x * second)
    ones = jnp.ones((8, shape[1]), jnp.float32)
    for c in range(3):
        row = lax.dot_general(
            ones,
            turned[c],
            (((1,), (1,)), ((), ())),
            precision=lax.Precision.HIGHEST,
            preferred_element_type=jnp.float32,
        )
        out[c, 0] = row[0:1]


def far(load, cx, cy, ncl, n_pencil):
    return pl.pallas_call(
        functools.partial(far_kernel, cx, cy, ncl, n_pencil),
        out_shape=shaped(3, 1, 1, ncl),
        in_specs=[VMEM],
        out_specs=VMEM,
        compiler_params=PARAMS,
    )(load)


def deposit_kernel(cap, inside, load, out, order):
    _, cx, cy, nz = out.shape
    rows = cx * cy
    cells = rows * nz
    n_slab = load.shape[0] // cap
    wide = GROUP * load.shape[2]
    out[...] = inside[...]
    listed = jnp.int32(0)
    for d in range(n_slab):
        first = d * cap
        held = jnp.max(load[first, 3:4, :]).astype(jnp.int32) // cells
        for k in range(cap):
            order[listed + k] = first + k
        listed = listed + held
    for k in range(GROUP):
        order[listed + k] = 0
    def numbers(length):
        shape = (length // 16, 16, wide)
        return (lax.broadcasted_iota(jnp.int32, shape, 0) * 16 + lax.broadcasted_iota(jnp.int32, shape, 1)).astype(
            jnp.float32
        ).astype(jnp.bfloat16)

    def spread(row):
        return jnp.broadcast_to(row, (16, wide)).astype(jnp.bfloat16)[None]

    row_numbers = numbers(rows)
    col_numbers = numbers(nz)
    place = lax.broadcasted_iota(jnp.int32, (1, wide), 1) // load.shape[2]
    zero = jnp.zeros((), jnp.bfloat16)

    def group(g, carry):
        tiles = [load[order[g * GROUP + k]] for k in range(GROUP)]
        block = jnp.concatenate(tiles, axis=1)
        live = place < listed - g * GROUP
        cell = block[3:4, :].astype(jnp.int32) % cells
        at_row = row_numbers == spread(jnp.where(live, cell // nz, -1).astype(jnp.float32))
        at_col = col_numbers == spread((cell % nz).astype(jnp.float32))
        spots = jnp.where(at_col, jnp.ones((), jnp.bfloat16), zero).reshape(nz, wide)
        parts = []
        for c in range(3):
            pieces = [
                jnp.where(at_row, spread(piece), zero).reshape(rows, wide) for piece in split(block[c : c + 1, :])
            ]
            parts.append(jnp.concatenate(pieces, axis=1))
        left = jnp.concatenate(parts, axis=0)
        right = jnp.concatenate([spots, spots], axis=1)
        added = lax.dot_general(left, right, (((1,), (1,)), ((), ())), preferred_element_type=jnp.float32)
        out[...] += added.reshape(out.shape)
        return carry

    lax.fori_loop(0, (listed + GROUP - 1) // GROUP, group, 0)


def deposit(inside, load, cap):
    return pl.pallas_call(
        functools.partial(deposit_kernel, cap),
        out_shape=shaped(*inside.shape),
        in_specs=[VMEM] * 2,
        out_specs=VMEM,
        scratch_shapes=[pltpu.SMEM((load.shape[0] + max(cap, GROUP),), jnp.int32)],
        compiler_params=PARAMS,
    )(inside, load)


def shift(array, axis, step):
    n = lax.axis_size(axis)
    pairs = [(i, i + step) for i in range(n) if 0 <= i + step < n]
    return lax.ppermute(array, axis, pairs)


def per_device(vorticity, velocity, viscosity, tile_weights, tile_cells, tile_dest, tile_count):
    _, cx, cy, nz = vorticity.shape
    ncl = nz // CB
    n_slab = lax.axis_size("slab")
    n_pencil = lax.axis_size("pencil")
    cap = 2 * tile_weights.shape[0] // n_slab
    weights = jnp.transpose(tile_weights, (1, 0, 2))
    *faces, packets = to_send(
        vorticity, velocity, viscosity, weights, tile_cells, tile_dest.T, tile_count, n_slab, cap
    )
    xlo, xhi, ylo, yhi = faces
    arrived = lax.all_to_all(packets, "slab", 0, 0, tiled=True)
    halos = (
        shift(xhi, "slab", 1),
        shift(xlo, "slab", -1),
        shift(yhi, "pencil", 1),
        shift(ylo, "pencil", -1),
    )
    inside, sums, tiles = inner(vorticity, velocity, viscosity, packets, n_slab, cap)
    advanced, load = edges(inside, sums, tiles, faces, halos, n_slab * n_pencil)
    load = lax.all_to_all(load, ("slab", "pencil"), 0, 0, tiled=True)
    vorticity_out = deposit(advanced, arrived, cap)
    return (vorticity_out, far(load, cx, cy, ncl, n_pencil))


def solution(mesh):
    in_specs = (
        P(None, "slab", "pencil", None),
        P(None, "slab", "pencil", None),
        P("slab", "pencil", None),
        P(("slab", "pencil"), None, None),
        P(("slab", "pencil"), None),
        P(("slab", "pencil"), None),
        P(("slab", "pencil")),
    )
    out_specs = (P(None, "slab", "pencil", None), P(None, "slab", "pencil", None))
    return jax.shard_map(
        per_device, mesh=mesh, in_specs=in_specs, out_specs=out_specs, check_vma=False
    )
```

```python
import functools

import jax
import jax.numpy as jnp
from jax import lax
from jax.experimental import pallas as pl
from jax.experimental.pallas import tpu as pltpu
from jax.sharding import PartitionSpec as P

CB = 16
TIME_STEP = 0.1
LANES = 128
GROUP = 4
VMEM_LIMIT = 48 * 1024 * 1024

VMEM = pl.BlockSpec(memory_space=pltpu.VMEM)
ANY = pl.BlockSpec(memory_space=pl.ANY)
SMEM = pl.BlockSpec(memory_space=pltpu.SMEM)
FIRST_PARAMS = pltpu.CompilerParams(vmem_limit_bytes=60 * 1024 * 1024)
PARAMS = pltpu.CompilerParams(vmem_limit_bytes=VMEM_LIMIT)


def shaped(*shape):
    return jax.ShapeDtypeStruct(shape, jnp.float32)


def split(w):
    high = w.astype(jnp.bfloat16).astype(jnp.float32)
    return high, w - high


def tile_moments(cap, nz, packets, moments):
    n_slab = packets.shape[0] // cap
    ncl = nz // CB
    wide = cap * packets.shape[2]
    level = lax.broadcasted_iota(jnp.int32, (ncl, wide), 0)
    found = []
    for d in range(n_slab):
        block = jnp.concatenate([packets[d * cap + k] for k in range(cap)], axis=1)
        cell = block[3:4, :].astype(jnp.int32)
        spots = (level == cell % nz // CB).astype(jnp.float32).astype(jnp.bfloat16)
        high, low = split(block)
        left = jnp.concatenate([high, low], axis=0).astype(jnp.bfloat16)
        sums = lax.dot_general(left, spots, (((1,), (1,)), ((), ())), preferred_element_type=jnp.float32)
        found.append(sums[0:4] + sums[4:8])
    moments[...] = jnp.concatenate(found, axis=1)


def send_kernel(
    cap,
    vort,
    velo,
    visc,
    weights_in,
    cells_in,
    dest_in,
    count_in,
    xlo,
    xhi,
    ylo,
    yhi,
    sides,
    packets,
    moments,
    spin_rows,
    velo_rows,
    visc_rows,
    weights,
    cells,
    dest,
    count,
    filled,
    sems,
):
    cx, cy, nz = visc.shape
    copies = []

    def copy(source, target):
        copies.append(pltpu.make_async_copy(source, target, sems.at[len(copies)]))
        copies[-1].start()

    copy(weights_in, weights)
    copy(cells_in, cells)
    copy(dest_in, dest)
    copy(count_in, count)
    for k, at in ((0, 0), (1, cy - 8)):
        copy(vort.at[:, :, pl.ds(at, 8), :], spin_rows.at[k])
        copy(velo.at[:, :, pl.ds(at, 8), :], velo_rows.at[k])
        copy(visc.at[:, pl.ds(at, 8), :], visc_rows.at[k])
    for face, at in ((xlo, 0), (xhi, cx - 1)):
        copy(vort.at[:, at], face.at[0:3])
        copy(velo.at[:, at], face.at[3:6])
        copy(visc.at[at], face.at[6])

    packets[...] = jnp.zeros_like(packets)
    n_slab = packets.shape[0] // cap
    for d in range(n_slab):
        filled[d] = 0
    for k in range(4):
        copies[k].wait()

    def place(r, carry):
        d = dest[0, r]
        slot = filled[d]
        at = d * cap + slot
        for c in range(3):
            packets[at, c : c + 1, :] = weights[c, pl.ds(r, 1), :]
        packets[at, 3:4, :] = cells[pl.ds(r, 1), :].astype(jnp.float32)
        filled[d] = slot + 1
        return carry

    lax.fori_loop(0, count[0], place, 0)
    for d in range(n_slab):
        held = (filled[d] * (cx * cy * nz)).astype(jnp.float32)
        packets[d * cap, 3:4, :] = packets[d * cap, 3:4, :] + held
    tile_moments(cap, nz, packets, moments)
    sides[...] = jnp.zeros_like(sides)
    for k in range(4, 10):
        copies[k].wait()
    for k, face, at in ((0, ylo, 0), (1, yhi, 7)):
        for x in range(cx):
            for c in range(3):
                face[c, x : x + 1, :] = spin_rows[k, c, x, at : at + 1, :]
                face[3 + c, x : x + 1, :] = velo_rows[k, c, x, at : at + 1, :]
            face[6, x : x + 1, :] = visc_rows[k, x, at : at + 1, :]
    pencil = lax.axis_index("pencil")

    @pl.when(pencil < sides.shape[0] - 1)
    def _():
        sides[pencil + 1, 0:7] = yhi[...]

    @pl.when(pencil > 0)
    def _():
        sides[pencil - 1, 7:14] = ylo[...]

    for k in range(10, 16):
        copies[k].wait()


def to_send(vort, velo, visc, weights, cells, dest, count, n_slab, n_pencil, cap):
    _, cx, cy, nz = vort.shape
    return pl.pallas_call(
        functools.partial(send_kernel, cap),
        out_shape=(
            shaped(7, cy, nz),
            shaped(7, cy, nz),
            shaped(7, cx, nz),
            shaped(7, cx, nz),
            shaped(n_pencil, 14, cx, nz),
            shaped(n_slab * cap, 4, weights.shape[2]),
            shaped(4, n_slab * nz // CB),
        ),
        in_specs=[ANY] * 7,
        out_specs=(VMEM,) * 7,
        scratch_shapes=[
            pltpu.VMEM((2, 3, cx, 8, nz), jnp.float32),
            pltpu.VMEM((2, 3, cx, 8, nz), jnp.float32),
            pltpu.VMEM((2, cx, 8, nz), jnp.float32),
            pltpu.VMEM(weights.shape, jnp.float32),
            pltpu.VMEM(cells.shape, jnp.int32),
            pltpu.SMEM(dest.shape, jnp.int32),
            pltpu.SMEM(count.shape, jnp.int32),
            pltpu.SMEM((n_slab,), jnp.int32),
            pltpu.SemaphoreType.DMA((16,)),
        ],
        compiler_params=FIRST_PARAMS,
    )(vort, velo, visc, weights, cells, dest, count)


def ahead(a, axis):
    return pltpu.roll(a, a.shape[axis] - 1, axis)


def behind(a, axis):
    return pltpu.roll(a, 1, axis)


def interior_step(vort, velo, visc, out):
    cx, cy, nz = visc.shape
    row = lax.broadcasted_iota(jnp.int32, (cy, nz), 0)
    has_ahead = row < cy - 1
    has_behind = row > 0
    for x in range(cx):
        nu = visc[x]
        spin = [vort[c, x] for c in range(3)]
        mean_y = jnp.where(has_ahead, 0.5 * (nu + ahead(nu, 0)), 0.0)
        mean_z = 0.5 * (nu + ahead(nu, 1))
        if x < cx - 1:
            mean_next = 0.5 * (nu + visc[x + 1])
        if x > 0:
            mean_last = 0.5 * (nu + visc[x - 1])
        for c in range(3):
            w = spin[c]
            u = velo[c, x]
            flux_y = mean_y * (ahead(w, 0) - w)
            flux_z = mean_z * (ahead(w, 1) - w)
            change = (flux_y - behind(flux_y, 0)) + (flux_z - behind(flux_z, 1))
            slope_y = jnp.where(has_ahead, ahead(u, 0), 0.0) - jnp.where(has_behind, behind(u, 0), 0.0)
            slope_z = ahead(u, 1) - behind(u, 1)
            if x == 0:
                slope_x = velo[c, x + 1]
            elif x == cx - 1:
                slope_x = -velo[c, x - 1]
            else:
                slope_x = velo[c, x + 1] - velo[c, x - 1]
            stretch = 0.5 * (spin[0] * slope_x + spin[1] * slope_y + spin[2] * slope_z)
            if x < cx - 1:
                change = change + mean_next * (vort[c, x + 1] - w)
            if x > 0:
                change = change + mean_last * (vort[c, x - 1] - w)
            out[c, x] = w + TIME_STEP * (stretch + change)


def inner_kernel(vort, velo, visc, out, sums):
    interior_step(vort, velo, visc, out)
    for c in range(3):
        sums[c : c + 1, :] = jnp.sum(out[c].reshape(-1, out.shape[3]), axis=0, keepdims=True)


def inner(vort, velo, visc):
    return pl.pallas_call(
        inner_kernel,
        out_shape=(shaped(*vort.shape), shaped(3, vort.shape[3])),
        in_specs=[VMEM] * 3,
        out_specs=(VMEM,) * 2,
        compiler_params=PARAMS,
    )(vort, velo, visc)


def face_change(own, other, along, sign, c):
    stretch = (0.5 * sign) * own[along] * other[3 + c]
    diffuse = 0.5 * (own[6] + other[6]) * (other[c] - own[c])
    return TIME_STEP * (stretch + diffuse)


def edge_kernel(inside, sums, tiles, xlo, xhi, ylo, yhi, xlo_in, xhi_in, sides, out, load):
    _, cx, cy, nz = out.shape
    out[...] = inside[...]
    ylo_in, yhi_in = sides.at[0, 0:7], sides.at[0, 7:14]
    totals = []
    for c in range(3):
        total = sums[c : c + 1, :]
        for own, other, at, sign in ((xlo, xlo_in, 0, -1.0), (xhi, xhi_in, cx - 1, 1.0)):
            change = face_change(own, other, 0, sign, c)
            out[c, at] = out[c, at] + change
            total = total + jnp.sum(change, axis=0, keepdims=True)
        for own, other, at, sign in ((ylo, ylo_in, 0, -1.0), (yhi, yhi_in, cy - 1, 1.0)):
            change = face_change(own, other, 1, sign, c)
            for x in range(cx):
                out[c, x, at : at + 1, :] = out[c, x, at : at + 1, :] + change[x : x + 1, :]
            total = total + jnp.sum(change, axis=0, keepdims=True)
        totals.append(total)
    totals.append(jnp.zeros_like(totals[0]))
    shape = (nz, tiles.shape[1])
    level = lax.broadcasted_iota(jnp.int32, shape, 0) // CB
    lane = lax.broadcasted_iota(jnp.int32, shape, 1)
    own_slab = lax.axis_index("slab")
    pick = (lane == own_slab * (nz // CB) + level).astype(jnp.float32)
    moment = tiles[...] + jnp.dot(
        jnp.concatenate(totals, axis=0), pick, precision=lax.Precision.HIGHEST, preferred_element_type=jnp.float32
    )
    for k in range(load.shape[1] // 4):
        part = moment[:, k * LANES : (k + 1) * LANES]
        for j in range(load.shape[0]):
            load[j, 4 * k : 4 * k + 4, :] = part


def edges(inside, sums, tiles, faces, halos, n_all):
    return pl.pallas_call(
        edge_kernel,
        out_shape=(shaped(*inside.shape), shaped(n_all, 4 * tiles.shape[1] // LANES, LANES)),
        in_specs=[VMEM] * 10,
        out_specs=(VMEM,) * 2,
        compiler_params=PARAMS,
    )(inside, sums, tiles, *faces, *halos)


def far_kernel(cx, cy, ncl, n_pencil, load, out):
    n_all = load.shape[0]
    n_slab = n_all // n_pencil
    slab = lax.axis_index("slab")
    pencil = lax.axis_index("pencil")
    shape = (ncl, n_slab * ncl)
    target = lax.broadcasted_iota(jnp.int32, shape, 0)
    source = lax.broadcasted_iota(jnp.int32, shape, 1)
    sigma = jnp.float32(cx * n_slab // 4)
    rel_x = ((slab - source // ncl) * cx).astype(jnp.float32)
    rel_z = ((target - source % ncl) * CB).astype(jnp.float32)
    flat = rel_x * rel_x + rel_z * rel_z + sigma * sigma
    turned = [jnp.zeros(shape, jnp.float32) for _ in range(3)]
    for p in range(n_pencil):
        total = load[p]
        for s in range(1, n_slab):
            total = total + load[s * n_pencil + p]
        moment = jnp.concatenate([total[4 * k : 4 * k + 4] for k in range(load.shape[1] // 4)], axis=1)
        first, second, third = moment[0:1], moment[1:2], moment[2:3]
        rel_y = ((pencil - p) * cy).astype(jnp.float32)
        inverse = lax.rsqrt(flat + rel_y * rel_y)
        weight = inverse * inverse * inverse
        turned[0] = turned[0] + weight * (rel_z * second - rel_y * third)
        turned[1] = turned[1] + weight * (rel_x * third - rel_z * first)
        turned[2] = turned[2] + weight * (rel_y * first - rel_x * second)
    ones = jnp.ones((8, shape[1]), jnp.float32)
    for c in range(3):
        row = lax.dot_general(
            ones,
            turned[c],
            (((1,), (1,)), ((), ())),
            precision=lax.Precision.HIGHEST,
            preferred_element_type=jnp.float32,
        )
        out[c, 0] = row[0:1]


def far(load, cx, cy, ncl, n_pencil):
    return pl.pallas_call(
        functools.partial(far_kernel, cx, cy, ncl, n_pencil),
        out_shape=shaped(3, 1, 1, ncl),
        in_specs=[VMEM],
        out_specs=VMEM,
        compiler_params=PARAMS,
    )(load)


def deposit_kernel(cap, inside, load, out, acc, order):
    _, cx, cy, nz = out.shape
    rows = cx * cy // 2
    cells = 2 * rows * nz
    n_slab = load.shape[0] // cap
    wide = GROUP * load.shape[2]
    acc[...] = jnp.zeros_like(acc)
    listed = jnp.int32(0)
    for d in range(n_slab):
        first = d * cap
        held = jnp.max(load[first, 3:4, :]).astype(jnp.int32) // cells
        for k in range(cap):
            order[listed + k] = first + k
        listed = listed + held
    for k in range(GROUP):
        order[listed + k] = 0
    def numbers(length):
        shape = (length // 16, 16, wide)
        return (lax.broadcasted_iota(jnp.int32, shape, 0) * 16 + lax.broadcasted_iota(jnp.int32, shape, 1)).astype(
            jnp.float32
        ).astype(jnp.bfloat16)

    def spread(row):
        return jnp.broadcast_to(row, (16, wide)).astype(jnp.bfloat16)[None]

    row_numbers = numbers(rows)
    col_numbers = numbers(nz)
    place = lax.broadcasted_iota(jnp.int32, (1, wide), 1) // load.shape[2]
    zero = jnp.zeros((), jnp.bfloat16)
    one = jnp.ones((), jnp.bfloat16)

    def group(g, carry):
        tiles = [load[order[g * GROUP + k]] for k in range(GROUP)]
        block = jnp.concatenate(tiles, axis=1)
        live = place < listed - g * GROUP
        cell = block[3:4, :].astype(jnp.int32) % cells
        row = cell // nz
        half = row // rows
        at_row = row_numbers == spread(jnp.where(live, row % rows, -1).astype(jnp.float32))
        right = []
        for h in range(2):
            at_col = col_numbers == spread(jnp.where(half == h, cell % nz, -1).astype(jnp.float32))
            right.append(jnp.where(at_col, one, zero).reshape(nz, wide))
        left = []
        for piece in split(block):
            for c in range(3):
                left.append(jnp.where(at_row, spread(piece[c : c + 1, :]), zero).reshape(rows, wide))
        added = lax.dot_general(
            jnp.concatenate(left, axis=0),
            jnp.concatenate(right, axis=0),
            (((1,), (1,)), ((), ())),
            preferred_element_type=jnp.float32,
        )
        acc[...] += added[: 3 * rows] + added[3 * rows :]
        return carry

    lax.fori_loop(0, (listed + GROUP - 1) // GROUP, group, 0)
    for h in range(2):
        span = slice(h * (cx // 2), (h + 1) * (cx // 2))
        change = acc[:, h * nz : (h + 1) * nz].reshape(3, cx // 2, cy, nz)
        out[:, span] = inside[:, span] + change


def deposit(inside, load, cap):
    return pl.pallas_call(
        functools.partial(deposit_kernel, cap),
        out_shape=shaped(*inside.shape),
        in_specs=[VMEM] * 2,
        out_specs=VMEM,
        scratch_shapes=[
            pltpu.VMEM((3 * inside.shape[1] * inside.shape[2] // 2, 2 * inside.shape[3]), jnp.float32),
            pltpu.SMEM((load.shape[0] + max(cap, GROUP),), jnp.int32),
        ],
        compiler_params=PARAMS,
    )(inside, load)


def shift(array, axis, step):
    n = lax.axis_size(axis)
    pairs = [(i, i + step) for i in range(n) if 0 <= i + step < n]
    return lax.ppermute(array, axis, pairs)


def per_device(vorticity, velocity, viscosity, tile_weights, tile_cells, tile_dest, tile_count):
    _, cx, cy, nz = vorticity.shape
    ncl = nz // CB
    n_slab = lax.axis_size("slab")
    n_pencil = lax.axis_size("pencil")
    cap = 2 * tile_weights.shape[0] // n_slab
    weights = jnp.transpose(tile_weights, (1, 0, 2))
    xlo, xhi, ylo, yhi, sides, packets, tiles = to_send(
        vorticity, velocity, viscosity, weights, tile_cells, tile_dest.T, tile_count, n_slab, n_pencil, cap
    )
    sides_in = lax.psum_scatter(sides, "pencil", scatter_dimension=0, tiled=True)
    arrived = lax.all_to_all(packets, "slab", 0, 0, tiled=True)
    xlo_in = shift(xhi, "slab", 1)
    xhi_in = shift(xlo, "slab", -1)
    inside, sums = inner(vorticity, velocity, viscosity)
    advanced, load = edges(
        inside, sums, tiles, (xlo, xhi, ylo, yhi), (xlo_in, xhi_in, sides_in), n_slab * n_pencil
    )
    load = lax.all_to_all(load, ("slab", "pencil"), 0, 0, tiled=True)
    vorticity_out = deposit(advanced, arrived, cap)
    return (vorticity_out, far(load, cx, cy, ncl, n_pencil))


def solution(mesh):
    in_specs = (
        P(None, "slab", "pencil", None),
        P(None, "slab", "pencil", None),
        P("slab", "pencil", None),
        P(("slab", "pencil"), None, None),
        P(("slab", "pencil"), None),
        P(("slab", "pencil"), None),
        P(("slab", "pencil")),
    )
    out_specs = (P(None, "slab", "pencil", None), P(None, "slab", "pencil", None))
    return jax.shard_map(
        per_device, mesh=mesh, in_specs=in_specs, out_specs=out_specs, check_vma=False
    )
```

```python
import functools

import jax
import jax.numpy as jnp
from jax import lax
from jax.experimental import pallas as pl
from jax.experimental.pallas import tpu as pltpu
from jax.sharding import PartitionSpec as P

CB = 16
TIME_STEP = 0.1
LANES = 128
GROUP = 4
VMEM_LIMIT = 48 * 1024 * 1024

VMEM = pl.BlockSpec(memory_space=pltpu.VMEM)
ANY = pl.BlockSpec(memory_space=pl.ANY)
SMEM = pl.BlockSpec(memory_space=pltpu.SMEM)
FIRST_PARAMS = pltpu.CompilerParams(vmem_limit_bytes=60 * 1024 * 1024)
PARAMS = pltpu.CompilerParams(vmem_limit_bytes=VMEM_LIMIT)


def shaped(*shape):
    return jax.ShapeDtypeStruct(shape, jnp.float32)


def split(w):
    high = w.astype(jnp.bfloat16).astype(jnp.float32)
    return high, w - high


def tile_moments(cap, nz, packets, moments):
    n_slab = packets.shape[0] // cap
    ncl = nz // CB
    wide = cap * packets.shape[2]
    level = lax.broadcasted_iota(jnp.int32, (ncl, wide), 0)
    found = []
    for d in range(n_slab):
        block = jnp.concatenate([packets[d * cap + k] for k in range(cap)], axis=1)
        cell = block[3:4, :].astype(jnp.int32)
        spots = (level == cell % nz // CB).astype(jnp.float32).astype(jnp.bfloat16)
        high, low = split(block)
        left = jnp.concatenate([high, low], axis=0).astype(jnp.bfloat16)
        sums = lax.dot_general(left, spots, (((1,), (1,)), ((), ())), preferred_element_type=jnp.float32)
        found.append(sums[0:4] + sums[4:8])
    moments[...] = jnp.concatenate(found, axis=1)


def send_kernel(
    cap,
    vort,
    velo,
    visc,
    weights_in,
    cells_in,
    dest_in,
    count_in,
    xlo,
    xhi,
    ylo,
    yhi,
    sides,
    packets,
    moments,
    spin_rows,
    velo_rows,
    visc_rows,
    weights,
    cells,
    dest,
    count,
    filled,
    sems,
):
    cx, cy, nz = visc.shape
    copies = []

    def copy(source, target):
        copies.append(pltpu.make_async_copy(source, target, sems.at[len(copies)]))
        copies[-1].start()

    copy(weights_in, weights)
    copy(cells_in, cells)
    copy(dest_in, dest)
    copy(count_in, count)
    for k, at in ((0, 0), (1, cy - 8)):
        copy(vort.at[:, :, pl.ds(at, 8), :], spin_rows.at[k])
        copy(velo.at[:, :, pl.ds(at, 8), :], velo_rows.at[k])
        copy(visc.at[:, pl.ds(at, 8), :], visc_rows.at[k])
    for face, at in ((xlo, 0), (xhi, cx - 1)):
        copy(vort.at[:, at], face.at[0:3])
        copy(velo.at[:, at], face.at[3:6])
        copy(visc.at[at], face.at[6])

    packets[...] = jnp.zeros_like(packets)
    n_slab = packets.shape[0] // cap
    for d in range(n_slab):
        filled[d] = 0
    for k in range(4):
        copies[k].wait()

    def place(r, carry):
        d = dest[0, r]
        slot = filled[d]
        at = d * cap + slot
        for c in range(3):
            packets[at, c : c + 1, :] = weights[c, pl.ds(r, 1), :]
        packets[at, 3:4, :] = cells[pl.ds(r, 1), :].astype(jnp.float32)
        filled[d] = slot + 1
        return carry

    lax.fori_loop(0, count[0], place, 0)
    for d in range(n_slab):
        held = (filled[d] * (cx * cy * nz)).astype(jnp.float32)
        packets[d * cap, 3:4, :] = packets[d * cap, 3:4, :] + held
    tile_moments(cap, nz, packets, moments)
    sides[...] = jnp.zeros_like(sides)
    for k in range(4, 10):
        copies[k].wait()
    for k, face, at in ((0, ylo, 0), (1, yhi, 7)):
        for x in range(cx):
            for c in range(3):
                face[c, x : x + 1, :] = spin_rows[k, c, x, at : at + 1, :]
                face[3 + c, x : x + 1, :] = velo_rows[k, c, x, at : at + 1, :]
            face[6, x : x + 1, :] = visc_rows[k, x, at : at + 1, :]
    pencil = lax.axis_index("pencil")

    @pl.when(pencil < sides.shape[0] - 1)
    def _():
        sides[pencil + 1] = yhi[...]

    @pl.when(pencil > 0)
    def _():
        sides[pencil - 1] = ylo[...]

    for k in range(10, 16):
        copies[k].wait()


def to_send(vort, velo, visc, weights, cells, dest, count, n_slab, n_pencil, cap):
    _, cx, cy, nz = vort.shape
    return pl.pallas_call(
        functools.partial(send_kernel, cap),
        out_shape=(
            shaped(7, cy, nz),
            shaped(7, cy, nz),
            shaped(7, cx, nz),
            shaped(7, cx, nz),
            shaped(n_pencil, 7, cx, nz),
            shaped(n_slab * cap, 4, weights.shape[2]),
            shaped(4, n_slab * nz // CB),
        ),
        in_specs=[ANY] * 7,
        out_specs=(VMEM,) * 7,
        scratch_shapes=[
            pltpu.VMEM((2, 3, cx, 8, nz), jnp.float32),
            pltpu.VMEM((2, 3, cx, 8, nz), jnp.float32),
            pltpu.VMEM((2, cx, 8, nz), jnp.float32),
            pltpu.VMEM(weights.shape, jnp.float32),
            pltpu.VMEM(cells.shape, jnp.int32),
            pltpu.SMEM(dest.shape, jnp.int32),
            pltpu.SMEM(count.shape, jnp.int32),
            pltpu.SMEM((n_slab,), jnp.int32),
            pltpu.SemaphoreType.DMA((16,)),
        ],
        compiler_params=FIRST_PARAMS,
    )(vort, velo, visc, weights, cells, dest, count)


def ahead(a, axis):
    return pltpu.roll(a, a.shape[axis] - 1, axis)


def behind(a, axis):
    return pltpu.roll(a, 1, axis)


def interior_step(vort, velo, visc, out):
    cx, cy, nz = visc.shape
    row = lax.broadcasted_iota(jnp.int32, (cy, nz), 0)
    has_ahead = row < cy - 1
    has_behind = row > 0
    for x in range(cx):
        nu = visc[x]
        spin = [vort[c, x] for c in range(3)]
        mean_y = jnp.where(has_ahead, 0.5 * (nu + ahead(nu, 0)), 0.0)
        mean_z = 0.5 * (nu + ahead(nu, 1))
        if x < cx - 1:
            mean_next = 0.5 * (nu + visc[x + 1])
        if x > 0:
            mean_last = 0.5 * (nu + visc[x - 1])
        for c in range(3):
            w = spin[c]
            u = velo[c, x]
            flux_y = mean_y * (ahead(w, 0) - w)
            flux_z = mean_z * (ahead(w, 1) - w)
            change = (flux_y - behind(flux_y, 0)) + (flux_z - behind(flux_z, 1))
            slope_y = jnp.where(has_ahead, ahead(u, 0), 0.0) - jnp.where(has_behind, behind(u, 0), 0.0)
            slope_z = ahead(u, 1) - behind(u, 1)
            if x == 0:
                slope_x = velo[c, x + 1]
            elif x == cx - 1:
                slope_x = -velo[c, x - 1]
            else:
                slope_x = velo[c, x + 1] - velo[c, x - 1]
            stretch = 0.5 * (spin[0] * slope_x + spin[1] * slope_y + spin[2] * slope_z)
            if x < cx - 1:
                change = change + mean_next * (vort[c, x + 1] - w)
            if x > 0:
                change = change + mean_last * (vort[c, x - 1] - w)
            out[c, x] = w + TIME_STEP * (stretch + change)


def inner_kernel(vort, velo, visc, out, sums):
    interior_step(vort, velo, visc, out)
    for c in range(3):
        sums[c : c + 1, :] = jnp.sum(out[c].reshape(-1, out.shape[3]), axis=0, keepdims=True)


def inner(vort, velo, visc):
    return pl.pallas_call(
        inner_kernel,
        out_shape=(shaped(*vort.shape), shaped(3, vort.shape[3])),
        in_specs=[VMEM] * 3,
        out_specs=(VMEM,) * 2,
        compiler_params=PARAMS,
    )(vort, velo, visc)


def face_change(own, other, along, sign, c):
    stretch = (0.5 * sign) * own[along] * other[3 + c]
    diffuse = 0.5 * (own[6] + other[6]) * (other[c] - own[c])
    return TIME_STEP * (stretch + diffuse)


def edge_kernel(inside, sums, tiles, xlo, xhi, ylo, yhi, xlo_in, xhi_in, sides, out, load):
    _, cx, cy, nz = out.shape
    out[...] = inside[...]
    pencil = lax.axis_index("pencil")
    ylo_in = sides.at[jnp.maximum(pencil - 1, 0)]
    yhi_in = sides.at[jnp.minimum(pencil + 1, sides.shape[0] - 1)]
    totals = []
    for c in range(3):
        total = sums[c : c + 1, :]
        for own, other, at, sign in ((xlo, xlo_in, 0, -1.0), (xhi, xhi_in, cx - 1, 1.0)):
            change = face_change(own, other, 0, sign, c)
            out[c, at] = out[c, at] + change
            total = total + jnp.sum(change, axis=0, keepdims=True)
        for own, other, at, sign in ((ylo, ylo_in, 0, -1.0), (yhi, yhi_in, cy - 1, 1.0)):
            change = face_change(own, other, 1, sign, c)
            for x in range(cx):
                out[c, x, at : at + 1, :] = out[c, x, at : at + 1, :] + change[x : x + 1, :]
            total = total + jnp.sum(change, axis=0, keepdims=True)
        totals.append(total)
    totals.append(jnp.zeros_like(totals[0]))
    shape = (nz, tiles.shape[1])
    level = lax.broadcasted_iota(jnp.int32, shape, 0) // CB
    lane = lax.broadcasted_iota(jnp.int32, shape, 1)
    own_slab = lax.axis_index("slab")
    pick = (lane == own_slab * (nz // CB) + level).astype(jnp.float32)
    moment = tiles[...] + jnp.dot(
        jnp.concatenate(totals, axis=0), pick, precision=lax.Precision.HIGHEST, preferred_element_type=jnp.float32
    )
    for k in range(load.shape[1] // 4):
        part = moment[:, k * LANES : (k + 1) * LANES]
        for j in range(load.shape[0]):
            load[j, 4 * k : 4 * k + 4, :] = part


def edges(inside, sums, tiles, faces, halos, n_all):
    return pl.pallas_call(
        edge_kernel,
        out_shape=(shaped(*inside.shape), shaped(n_all, 4 * tiles.shape[1] // LANES, LANES)),
        in_specs=[VMEM] * 10,
        out_specs=(VMEM,) * 2,
        compiler_params=PARAMS,
    )(inside, sums, tiles, *faces, *halos)


def far_kernel(cx, cy, ncl, n_pencil, load, out):
    n_all = load.shape[0]
    n_slab = n_all // n_pencil
    slab = lax.axis_index("slab")
    pencil = lax.axis_index("pencil")
    shape = (ncl, n_slab * ncl)
    target = lax.broadcasted_iota(jnp.int32, shape, 0)
    source = lax.broadcasted_iota(jnp.int32, shape, 1)
    sigma = jnp.float32(cx * n_slab // 4)
    rel_x = ((slab - source // ncl) * cx).astype(jnp.float32)
    rel_z = ((target - source % ncl) * CB).astype(jnp.float32)
    flat = rel_x * rel_x + rel_z * rel_z + sigma * sigma
    turned = [jnp.zeros(shape, jnp.float32) for _ in range(3)]
    for p in range(n_pencil):
        total = load[p]
        for s in range(1, n_slab):
            total = total + load[s * n_pencil + p]
        moment = jnp.concatenate([total[4 * k : 4 * k + 4] for k in range(load.shape[1] // 4)], axis=1)
        first, second, third = moment[0:1], moment[1:2], moment[2:3]
        rel_y = ((pencil - p) * cy).astype(jnp.float32)
        inverse = lax.rsqrt(flat + rel_y * rel_y)
        weight = inverse * inverse * inverse
        turned[0] = turned[0] + weight * (rel_z * second - rel_y * third)
        turned[1] = turned[1] + weight * (rel_x * third - rel_z * first)
        turned[2] = turned[2] + weight * (rel_y * first - rel_x * second)
    ones = jnp.ones((8, shape[1]), jnp.float32)
    for c in range(3):
        row = lax.dot_general(
            ones,
            turned[c],
            (((1,), (1,)), ((), ())),
            precision=lax.Precision.HIGHEST,
            preferred_element_type=jnp.float32,
        )
        out[c, 0] = row[0:1]


def far(load, cx, cy, ncl, n_pencil):
    return pl.pallas_call(
        functools.partial(far_kernel, cx, cy, ncl, n_pencil),
        out_shape=shaped(3, 1, 1, ncl),
        in_specs=[VMEM],
        out_specs=VMEM,
        compiler_params=PARAMS,
    )(load)


def deposit_kernel(cap, inside, load, out, order):
    _, cx, cy, nz = out.shape
    rows = cx * cy
    cells = rows * nz
    n_slab = load.shape[0] // cap
    wide = GROUP * load.shape[2]
    out[...] = inside[...]
    listed = jnp.int32(0)
    for d in range(n_slab):
        first = d * cap
        held = jnp.max(load[first, 3:4, :]).astype(jnp.int32) // cells
        for k in range(cap):
            order[listed + k] = first + k
        listed = listed + held
    for k in range(GROUP):
        order[listed + k] = 0
    shape = (rows // 16, 16, wide)
    row_numbers = lax.broadcasted_iota(jnp.int32, shape, 0) * 16 + lax.broadcasted_iota(jnp.int32, shape, 1)
    row_numbers = row_numbers.astype(jnp.float32).astype(jnp.bfloat16)
    col_numbers = lax.broadcasted_iota(jnp.int32, (wide, nz), 1).astype(jnp.float32).astype(jnp.bfloat16)
    place = lax.broadcasted_iota(jnp.int32, (1, wide), 1) // load.shape[2]
    zero = jnp.zeros((), jnp.bfloat16)
    one = jnp.ones((), jnp.bfloat16)

    def spread(row):
        return jnp.broadcast_to(row, (16, wide)).astype(jnp.bfloat16)[None]

    def group(g, carry):
        tiles = [load[order[g * GROUP + k]] for k in range(GROUP)]
        block = jnp.concatenate(tiles, axis=1)
        live = place < listed - g * GROUP
        cell = block[3:4, :].astype(jnp.int32) % cells
        at_row = row_numbers == spread(jnp.where(live, cell // nz, -1).astype(jnp.float32))
        columns = jnp.transpose(jnp.broadcast_to((cell % nz).astype(jnp.float32), (8, wide)))
        columns = jnp.broadcast_to(columns[:, 0:1], (wide, nz)).astype(jnp.bfloat16)
        right = jnp.where(col_numbers == columns, one, zero)
        left = []
        for piece in split(block):
            for c in range(3):
                left.append(jnp.where(at_row, spread(piece[c : c + 1, :]), zero).reshape(rows, wide))
        added = jnp.dot(jnp.concatenate(left, axis=0), right, preferred_element_type=jnp.float32)
        out[...] += (added[: 3 * rows] + added[3 * rows :]).reshape(out.shape)
        return carry

    lax.fori_loop(0, (listed + GROUP - 1) // GROUP, group, 0)


def deposit(inside, load, cap):
    return pl.pallas_call(
        functools.partial(deposit_kernel, cap),
        out_shape=shaped(*inside.shape),
        in_specs=[VMEM] * 2,
        out_specs=VMEM,
        scratch_shapes=[
            pltpu.SMEM((load.shape[0] + max(cap, GROUP),), jnp.int32),
        ],
        compiler_params=PARAMS,
    )(inside, load)


def shift(array, axis, step):
    n = lax.axis_size(axis)
    pairs = [(i, i + step) for i in range(n) if 0 <= i + step < n]
    return lax.ppermute(array, axis, pairs)


def per_device(vorticity, velocity, viscosity, tile_weights, tile_cells, tile_dest, tile_count):
    _, cx, cy, nz = vorticity.shape
    ncl = nz // CB
    n_slab = lax.axis_size("slab")
    n_pencil = lax.axis_size("pencil")
    cap = 2 * tile_weights.shape[0] // n_slab
    weights = jnp.transpose(tile_weights, (1, 0, 2))
    xlo, xhi, ylo, yhi, sides, packets, tiles = to_send(
        vorticity, velocity, viscosity, weights, tile_cells, tile_dest.T, tile_count, n_slab, n_pencil, cap
    )
    arrived = lax.all_to_all(packets, "slab", 0, 0, tiled=True)
    xlo_in = shift(xhi, "slab", 1)
    xhi_in = shift(xlo, "slab", -1)
    sides_in = lax.all_to_all(sides, "pencil", 0, 0, tiled=True)
    inside, sums = inner(vorticity, velocity, viscosity)
    advanced, load = edges(
        inside, sums, tiles, (xlo, xhi, ylo, yhi), (xlo_in, xhi_in, sides_in), n_slab * n_pencil
    )
    load = lax.all_to_all(load, ("slab", "pencil"), 0, 0, tiled=True)
    vorticity_out = deposit(advanced, arrived, cap)
    return (vorticity_out, far(load, cx, cy, ncl, n_pencil))


def solution(mesh):
    in_specs = (
        P(None, "slab", "pencil", None),
        P(None, "slab", "pencil", None),
        P("slab", "pencil", None),
        P(("slab", "pencil"), None, None),
        P(("slab", "pencil"), None),
        P(("slab", "pencil"), None),
        P(("slab", "pencil")),
    )
    out_specs = (P(None, "slab", "pencil", None), P(None, "slab", "pencil", None))
    return jax.shard_map(
        per_device, mesh=mesh, in_specs=in_specs, out_specs=out_specs, check_vma=False
    )
```

```python
import functools

import jax
import jax.numpy as jnp
from jax import lax
from jax.experimental import pallas as pl
from jax.experimental.pallas import tpu as pltpu
from jax.sharding import PartitionSpec as P

CB = 16
TIME_STEP = 0.1
LANES = 128
GROUP = 8
VMEM_LIMIT = 48 * 1024 * 1024

VMEM = pl.BlockSpec(memory_space=pltpu.VMEM)
ANY = pl.BlockSpec(memory_space=pl.ANY)
SMEM = pl.BlockSpec(memory_space=pltpu.SMEM)
FIRST_PARAMS = pltpu.CompilerParams(vmem_limit_bytes=60 * 1024 * 1024)
PARAMS = pltpu.CompilerParams(vmem_limit_bytes=VMEM_LIMIT)


def shaped(*shape):
    return jax.ShapeDtypeStruct(shape, jnp.float32)


def split(w):
    high = w.astype(jnp.bfloat16).astype(jnp.float32)
    return high, w - high


def tile_moments(cap, nz, packets, moments):
    n_slab = packets.shape[0] // cap
    ncl = nz // CB
    wide = cap * packets.shape[2]
    level = lax.broadcasted_iota(jnp.int32, (ncl, wide), 0)
    found = []
    for d in range(n_slab):
        block = jnp.concatenate([packets[d * cap + k] for k in range(cap)], axis=1)
        cell = block[3:4, :].astype(jnp.int32)
        spots = (level == cell % nz // CB).astype(jnp.float32).astype(jnp.bfloat16)
        high, low = split(block)
        left = jnp.concatenate([high, low], axis=0).astype(jnp.bfloat16)
        sums = lax.dot_general(left, spots, (((1,), (1,)), ((), ())), preferred_element_type=jnp.float32)
        found.append(sums[0:4] + sums[4:8])
    moments[...] = jnp.concatenate(found, axis=1)


class Copies:
    def __init__(self, sems):
        self.sems = sems
        self.made = []

    def start(self, source, target):
        self.made.append(pltpu.make_async_copy(source, target, self.sems.at[len(self.made)]))
        self.made[-1].start()

    def wait(self, first, last):
        for k in range(first, last):
            self.made[k].wait()


def slab_kernel(vort, velo, visc, xlo, xhi, sems):
    copies = Copies(sems)
    for face, at in ((xlo, 0), (xhi, visc.shape[0] - 1)):
        copies.start(vort.at[:, at], face.at[0:3])
        copies.start(velo.at[:, at], face.at[3:6])
        copies.start(visc.at[at], face.at[6])
    copies.wait(0, 6)


def slab_faces(vort, velo, visc):
    _, _, cy, nz = vort.shape
    return pl.pallas_call(
        slab_kernel,
        out_shape=(shaped(7, cy, nz), shaped(7, cy, nz)),
        in_specs=[ANY] * 3,
        out_specs=(VMEM,) * 2,
        scratch_shapes=[pltpu.SemaphoreType.DMA((6,))],
        compiler_params=FIRST_PARAMS,
    )(vort, velo, visc)


def send_kernel(
    cap,
    vort,
    velo,
    visc,
    weights_in,
    cells_in,
    dest_in,
    count_in,
    earlier,
    ylo,
    yhi,
    packets,
    moments,
    spin_rows,
    velo_rows,
    visc_rows,
    weights,
    cells,
    dest,
    count,
    filled,
    sems,
):
    cx, cy, nz = visc.shape
    copies = Copies(sems)
    copies.start(weights_in, weights)
    copies.start(cells_in, cells)
    copies.start(dest_in, dest)
    copies.start(count_in, count)
    for k, at in ((0, 0), (1, cy - 8)):
        copies.start(vort.at[:, :, pl.ds(at, 8), :], spin_rows.at[k])
        copies.start(velo.at[:, :, pl.ds(at, 8), :], velo_rows.at[k])
        copies.start(visc.at[:, pl.ds(at, 8), :], visc_rows.at[k])

    packets[...] = jnp.zeros_like(packets)
    n_slab = packets.shape[0] // cap
    for d in range(n_slab):
        filled[d] = 0
    copies.wait(0, 4)

    def place(r, carry):
        d = dest[0, r]
        slot = filled[d]
        at = d * cap + slot
        for c in range(3):
            packets[at, c : c + 1, :] = weights[c, pl.ds(r, 1), :]
        packets[at, 3:4, :] = cells[pl.ds(r, 1), :].astype(jnp.float32)
        filled[d] = slot + 1
        return carry

    lax.fori_loop(0, count[0], place, 0)
    for d in range(n_slab):
        held = (filled[d] * (cx * cy * nz)).astype(jnp.float32)
        packets[d * cap, 3:4, :] = packets[d * cap, 3:4, :] + held
    tile_moments(cap, nz, packets, moments)
    copies.wait(4, 10)
    for k, face, at in ((0, ylo, 0), (1, yhi, 7)):
        for x in range(cx):
            for c in range(3):
                face[c, x : x + 1, :] = spin_rows[k, c, x, at : at + 1, :]
                face[3 + c, x : x + 1, :] = velo_rows[k, c, x, at : at + 1, :]
            face[6, x : x + 1, :] = visc_rows[k, x, at : at + 1, :]


def to_send(vort, velo, visc, weights, cells, dest, count, earlier, n_slab, cap):
    _, cx, cy, nz = vort.shape
    return pl.pallas_call(
        functools.partial(send_kernel, cap),
        out_shape=(
            shaped(7, cx, nz),
            shaped(7, cx, nz),
            shaped(n_slab * cap, 4, weights.shape[2]),
            shaped(4, n_slab * nz // CB),
        ),
        in_specs=[ANY] * 8,
        out_specs=(VMEM,) * 4,
        scratch_shapes=[
            pltpu.VMEM((2, 3, cx, 8, nz), jnp.float32),
            pltpu.VMEM((2, 3, cx, 8, nz), jnp.float32),
            pltpu.VMEM((2, cx, 8, nz), jnp.float32),
            pltpu.VMEM(weights.shape, jnp.float32),
            pltpu.VMEM(cells.shape, jnp.int32),
            pltpu.SMEM(dest.shape, jnp.int32),
            pltpu.SMEM(count.shape, jnp.int32),
            pltpu.SMEM((n_slab,), jnp.int32),
            pltpu.SemaphoreType.DMA((10,)),
        ],
        compiler_params=FIRST_PARAMS,
    )(vort, velo, visc, weights, cells, dest, count, earlier)


def ahead(a, axis):
    return pltpu.roll(a, a.shape[axis] - 1, axis)


def behind(a, axis):
    return pltpu.roll(a, 1, axis)


def interior_step(vort, velo, visc, out):
    cx, cy, nz = visc.shape
    row = lax.broadcasted_iota(jnp.int32, (cy, nz), 0)
    has_ahead = row < cy - 1
    has_behind = row > 0
    for x in range(cx):
        nu = visc[x]
        spin = [vort[c, x] for c in range(3)]
        mean_y = jnp.where(has_ahead, 0.5 * (nu + ahead(nu, 0)), 0.0)
        mean_z = 0.5 * (nu + ahead(nu, 1))
        if x < cx - 1:
            mean_next = 0.5 * (nu + visc[x + 1])
        if x > 0:
            mean_last = 0.5 * (nu + visc[x - 1])
        for c in range(3):
            w = spin[c]
            u = velo[c, x]
            flux_y = mean_y * (ahead(w, 0) - w)
            flux_z = mean_z * (ahead(w, 1) - w)
            change = (flux_y - behind(flux_y, 0)) + (flux_z - behind(flux_z, 1))
            slope_y = jnp.where(has_ahead, ahead(u, 0), 0.0) - jnp.where(has_behind, behind(u, 0), 0.0)
            slope_z = ahead(u, 1) - behind(u, 1)
            if x == 0:
                slope_x = velo[c, x + 1]
            elif x == cx - 1:
                slope_x = -velo[c, x - 1]
            else:
                slope_x = velo[c, x + 1] - velo[c, x - 1]
            stretch = 0.5 * (spin[0] * slope_x + spin[1] * slope_y + spin[2] * slope_z)
            if x < cx - 1:
                change = change + mean_next * (vort[c, x + 1] - w)
            if x > 0:
                change = change + mean_last * (vort[c, x - 1] - w)
            out[c, x] = w + TIME_STEP * (stretch + change)


def by_level(totals, width):
    nz = totals[0].shape[1]
    shape = (nz, width)
    level = lax.broadcasted_iota(jnp.int32, shape, 0) // CB
    lane = lax.broadcasted_iota(jnp.int32, shape, 1)
    pick = (lane == lax.axis_index("slab") * (nz // CB) + level).astype(jnp.float32)
    rows = jnp.concatenate(totals + [jnp.zeros_like(totals[0])], axis=0)
    return jnp.dot(rows, pick, precision=lax.Precision.HIGHEST, preferred_element_type=jnp.float32)


def inner_kernel(vort, velo, visc, tiles_in, out, moments, tiles, sem):
    copy = pltpu.make_async_copy(tiles_in, tiles, sem)
    copy.start()
    interior_step(vort, velo, visc, out)
    totals = [jnp.sum(out[c].reshape(-1, out.shape[3]), axis=0, keepdims=True) for c in range(3)]
    own = by_level(totals, moments.shape[1])
    copy.wait()
    moments[...] = tiles[...] + own


def inner(vort, velo, visc, tiles):
    return pl.pallas_call(
        inner_kernel,
        out_shape=(shaped(*vort.shape), shaped(*tiles.shape)),
        in_specs=[VMEM] * 3 + [ANY],
        out_specs=(VMEM,) * 2,
        scratch_shapes=[pltpu.VMEM(tiles.shape, jnp.float32), pltpu.SemaphoreType.DMA],
        compiler_params=PARAMS,
    )(vort, velo, visc, tiles)


def face_change(own, other, along, sign, c):
    stretch = (0.5 * sign) * own[along] * other[3 + c]
    diffuse = 0.5 * (own[6] + other[6]) * (other[c] - own[c])
    return TIME_STEP * (stretch + diffuse)


def edge_kernel(inside, moments, xlo, xhi, ylo, yhi, xlo_in, xhi_in, ylo_in, yhi_in, out, load):
    _, cx, cy, nz = out.shape
    out[...] = inside[...]
    totals = []
    for c in range(3):
        total = jnp.zeros((1, nz), jnp.float32)
        for own, other, at, sign in ((xlo, xlo_in, 0, -1.0), (xhi, xhi_in, cx - 1, 1.0)):
            change = face_change(own, other, 0, sign, c)
            out[c, at] = out[c, at] + change
            total = total + jnp.sum(change, axis=0, keepdims=True)
        for own, other, at, sign in ((ylo, ylo_in, 0, -1.0), (yhi, yhi_in, cy - 1, 1.0)):
            change = face_change(own, other, 1, sign, c)
            for x in range(cx):
                out[c, x, at : at + 1, :] = out[c, x, at : at + 1, :] + change[x : x + 1, :]
            total = total + jnp.sum(change, axis=0, keepdims=True)
        totals.append(total)
    moment = moments[...] + by_level(totals, moments.shape[1])
    for k in range(load.shape[1] // 4):
        part = moment[:, k * LANES : (k + 1) * LANES]
        for j in range(load.shape[0]):
            load[j, 4 * k : 4 * k + 4, :] = part


def edges(inside, moments, faces, halos, n_all):
    return pl.pallas_call(
        edge_kernel,
        out_shape=(shaped(*inside.shape), shaped(n_all, 4 * moments.shape[1] // LANES, LANES)),
        in_specs=[VMEM] * 10,
        out_specs=(VMEM,) * 2,
        compiler_params=PARAMS,
    )(inside, moments, *faces, *halos)


def far_kernel(cx, cy, ncl, n_pencil, load, out):
    n_all = load.shape[0]
    n_slab = n_all // n_pencil
    slab = lax.axis_index("slab")
    pencil = lax.axis_index("pencil")
    shape = (ncl, n_slab * ncl)
    target = lax.broadcasted_iota(jnp.int32, shape, 0)
    source = lax.broadcasted_iota(jnp.int32, shape, 1)
    sigma = jnp.float32(cx * n_slab // 4)
    rel_x = ((slab - source // ncl) * cx).astype(jnp.float32)
    rel_z = ((target - source % ncl) * CB).astype(jnp.float32)
    flat = rel_x * rel_x + rel_z * rel_z + sigma * sigma
    turned = [jnp.zeros(shape, jnp.float32) for _ in range(3)]
    for p in range(n_pencil):
        total = load[p]
        for s in range(1, n_slab):
            total = total + load[s * n_pencil + p]
        moment = jnp.concatenate([total[4 * k : 4 * k + 4] for k in range(load.shape[1] // 4)], axis=1)
        first, second, third = moment[0:1], moment[1:2], moment[2:3]
        rel_y = ((pencil - p) * cy).astype(jnp.float32)
        inverse = lax.rsqrt(flat + rel_y * rel_y)
        weight = inverse * inverse * inverse
        turned[0] = turned[0] + weight * (rel_z * second - rel_y * third)
        turned[1] = turned[1] + weight * (rel_x * third - rel_z * first)
        turned[2] = turned[2] + weight * (rel_y * first - rel_x * second)
    ones = jnp.ones((8, shape[1]), jnp.float32)
    for c in range(3):
        row = lax.dot_general(
            ones,
            turned[c],
            (((1,), (1,)), ((), ())),
            precision=lax.Precision.HIGHEST,
            preferred_element_type=jnp.float32,
        )
        out[c, 0] = row[0:1]


def far(load, cx, cy, ncl, n_pencil):
    return pl.pallas_call(
        functools.partial(far_kernel, cx, cy, ncl, n_pencil),
        out_shape=shaped(3, 1, 1, ncl),
        in_specs=[VMEM],
        out_specs=VMEM,
        compiler_params=PARAMS,
    )(load)


def deposit_kernel(cap, inside, load, out, acc, order):
    _, cx, cy, nz = out.shape
    rows = cx * cy // 2
    cells = 2 * rows * nz
    n_slab = load.shape[0] // cap
    wide = GROUP * load.shape[2]
    acc[...] = jnp.zeros_like(acc)
    listed = jnp.int32(0)
    for d in range(n_slab):
        first = d * cap
        held = jnp.max(load[first, 3:4, :]).astype(jnp.int32) // cells
        for k in range(cap):
            order[listed + k] = first + k
        listed = listed + held
    for k in range(GROUP):
        order[listed + k] = 0
    def numbers(length):
        shape = (length // 16, 16, wide)
        return (lax.broadcasted_iota(jnp.int32, shape, 0) * 16 + lax.broadcasted_iota(jnp.int32, shape, 1)).astype(
            jnp.float32
        ).astype(jnp.bfloat16)

    def spread(row):
        return jnp.broadcast_to(row, (16, wide)).astype(jnp.bfloat16)[None]

    row_numbers = numbers(rows)
    col_numbers = numbers(nz)
    place = lax.broadcasted_iota(jnp.int32, (1, wide), 1) // load.shape[2]
    zero = jnp.zeros((), jnp.bfloat16)
    one = jnp.ones((), jnp.bfloat16)

    def group(g, carry):
        tiles = [load[order[g * GROUP + k]] for k in range(GROUP)]
        block = jnp.concatenate(tiles, axis=1)
        live = place < listed - g * GROUP
        cell = block[3:4, :].astype(jnp.int32) % cells
        row = cell // nz
        half = row // rows
        at_row = row_numbers == spread(jnp.where(live, row % rows, -1).astype(jnp.float32))
        right = []
        for h in range(2):
            at_col = col_numbers == spread(jnp.where(half == h, cell % nz, -1).astype(jnp.float32))
            right.append(jnp.where(at_col, one, zero).reshape(nz, wide))
        left = []
        for piece in split(block):
            for c in range(3):
                left.append(jnp.where(at_row, spread(piece[c : c + 1, :]), zero).reshape(rows, wide))
        added = lax.dot_general(
            jnp.concatenate(left, axis=0),
            jnp.concatenate(right, axis=0),
            (((1,), (1,)), ((), ())),
            preferred_element_type=jnp.float32,
        )
        acc[...] += added[: 3 * rows] + added[3 * rows :]
        return carry

    lax.fori_loop(0, (listed + GROUP - 1) // GROUP, group, 0)
    for h in range(2):
        span = slice(h * (cx // 2), (h + 1) * (cx // 2))
        change = acc[:, h * nz : (h + 1) * nz].reshape(3, cx // 2, cy, nz)
        out[:, span] = inside[:, span] + change


def deposit(inside, load, cap):
    return pl.pallas_call(
        functools.partial(deposit_kernel, cap),
        out_shape=shaped(*inside.shape),
        in_specs=[VMEM] * 2,
        out_specs=VMEM,
        scratch_shapes=[
            pltpu.VMEM((3 * inside.shape[1] * inside.shape[2] // 2, 2 * inside.shape[3]), jnp.float32),
            pltpu.SMEM((load.shape[0] + max(cap, GROUP),), jnp.int32),
        ],
        compiler_params=PARAMS,
    )(inside, load)


def shift(array, axis, step):
    n = lax.axis_size(axis)
    pairs = [(i, i + step) for i in range(n) if 0 <= i + step < n]
    return lax.ppermute(array, axis, pairs)


def per_device(vorticity, velocity, viscosity, tile_weights, tile_cells, tile_dest, tile_count):
    _, cx, cy, nz = vorticity.shape
    ncl = nz // CB
    n_slab = lax.axis_size("slab")
    n_pencil = lax.axis_size("pencil")
    cap = 2 * tile_weights.shape[0] // n_slab
    weights = jnp.transpose(tile_weights, (1, 0, 2))
    xlo, xhi = slab_faces(vorticity, velocity, viscosity)
    xhi_in = shift(xlo, "slab", -1)
    xlo_in = shift(xhi, "slab", 1)
    ylo, yhi, packets, tiles = to_send(
        vorticity, velocity, viscosity, weights, tile_cells, tile_dest.T, tile_count, xhi, n_slab, cap
    )
    arrived = lax.all_to_all(packets, "slab", 0, 0, tiled=True)
    ylo_in = shift(yhi, "pencil", 1)
    yhi_in = shift(ylo, "pencil", -1)
    inside, moments = inner(vorticity, velocity, viscosity, tiles)
    advanced, load = edges(
        inside, moments, (xlo, xhi, ylo, yhi), (xlo_in, xhi_in, ylo_in, yhi_in), n_slab * n_pencil
    )
    load = lax.all_to_all(load, ("slab", "pencil"), 0, 0, tiled=True)
    vorticity_out = deposit(advanced, arrived, cap)
    return (vorticity_out, far(load, cx, cy, ncl, n_pencil))


def solution(mesh):
    in_specs = (
        P(None, "slab", "pencil", None),
        P(None, "slab", "pencil", None),
        P("slab", "pencil", None),
        P(("slab", "pencil"), None, None),
        P(("slab", "pencil"), None),
        P(("slab", "pencil"), None),
        P(("slab", "pencil")),
    )
    out_specs = (P(None, "slab", "pencil", None), P(None, "slab", "pencil", None))
    return jax.shard_map(
        per_device, mesh=mesh, in_specs=in_specs, out_specs=out_specs, check_vma=False
    )
```

```python
import functools

import jax
import jax.numpy as jnp
from jax import lax
from jax.experimental import pallas as pl
from jax.experimental.pallas import tpu as pltpu
from jax.sharding import PartitionSpec as P

CB = 16
TIME_STEP = 0.1
LANES = 128
GROUP = 8
VMEM_LIMIT = 24 * 1024 * 1024

VMEM = pl.BlockSpec(memory_space=pltpu.VMEM)
ANY = pl.BlockSpec(memory_space=pl.ANY)
SMEM = pl.BlockSpec(memory_space=pltpu.SMEM)
FIRST_PARAMS = pltpu.CompilerParams(vmem_limit_bytes=60 * 1024 * 1024)
PARAMS = pltpu.CompilerParams(vmem_limit_bytes=VMEM_LIMIT)


def shaped(*shape):
    return jax.ShapeDtypeStruct(shape, jnp.float32)


def split(w):
    high = w.astype(jnp.bfloat16).astype(jnp.float32)
    return high, w - high


def tile_moments(cap, nz, packets, moments):
    n_slab = packets.shape[0] // cap
    ncl = nz // CB
    wide = cap * packets.shape[2]
    level = lax.broadcasted_iota(jnp.int32, (ncl, wide), 0)
    found = []
    for d in range(n_slab):
        block = jnp.concatenate([packets[d * cap + k] for k in range(cap)], axis=1)
        cell = block[3:4, :].astype(jnp.int32)
        spots = (level == cell % nz // CB).astype(jnp.float32).astype(jnp.bfloat16)
        high, low = split(block)
        left = jnp.concatenate([high, low], axis=0).astype(jnp.bfloat16)
        sums = lax.dot_general(left, spots, (((1,), (1,)), ((), ())), preferred_element_type=jnp.float32)
        found.append(sums[0:4] + sums[4:8])
    moments[...] = jnp.concatenate(found, axis=1)


class Copies:
    def __init__(self, sems):
        self.sems = sems
        self.made = []

    def start(self, source, target):
        self.made.append(pltpu.make_async_copy(source, target, self.sems.at[len(self.made)]))
        self.made[-1].start()

    def wait(self, first, last):
        for k in range(first, last):
            self.made[k].wait()


def send_kernel(
    cap,
    vort,
    velo,
    visc,
    weights_in,
    cells_in,
    dest_in,
    count_in,
    xlo,
    xhi,
    ylo,
    yhi,
    packets,
    moments,
    spin_rows,
    velo_rows,
    visc_rows,
    weights,
    cells,
    dest,
    count,
    filled,
    sems,
):
    cx, cy, nz = visc.shape
    copies = Copies(sems)
    copies.start(weights_in, weights)
    copies.start(cells_in, cells)
    copies.start(dest_in, dest)
    copies.start(count_in, count)
    for k, at in ((0, 0), (1, cy - 8)):
        copies.start(vort.at[:, :, pl.ds(at, 8), :], spin_rows.at[k])
        copies.start(velo.at[:, :, pl.ds(at, 8), :], velo_rows.at[k])
        copies.start(visc.at[:, pl.ds(at, 8), :], visc_rows.at[k])
    for face, at in ((xlo, 0), (xhi, cx - 1)):
        copies.start(vort.at[:, at], face.at[0:3])
        copies.start(velo.at[:, at], face.at[3:6])
        copies.start(visc.at[at], face.at[6])

    packets[...] = jnp.zeros_like(packets)
    n_slab = packets.shape[0] // cap
    for d in range(n_slab):
        filled[d] = 0
    copies.wait(0, 4)

    def place(r, carry):
        d = dest[0, r]
        slot = filled[d]
        at = d * cap + slot
        for c in range(3):
            packets[at, c : c + 1, :] = weights[c, pl.ds(r, 1), :]
        packets[at, 3:4, :] = cells[pl.ds(r, 1), :].astype(jnp.float32)
        filled[d] = slot + 1
        return carry

    lax.fori_loop(0, count[0], place, 0)
    for d in range(n_slab):
        held = (filled[d] * (cx * cy * nz)).astype(jnp.float32)
        packets[d * cap, 3:4, :] = packets[d * cap, 3:4, :] + held
    tile_moments(cap, nz, packets, moments)
    copies.wait(4, 10)
    for k, face, at in ((0, ylo, 0), (1, yhi, 7)):
        for x in range(cx):
            for c in range(3):
                face[c, x : x + 1, :] = spin_rows[k, c, x, at : at + 1, :]
                face[3 + c, x : x + 1, :] = velo_rows[k, c, x, at : at + 1, :]
            face[6, x : x + 1, :] = visc_rows[k, x, at : at + 1, :]
    copies.wait(10, 16)


def to_send(vort, velo, visc, weights, cells, dest, count, n_slab, cap):
    _, cx, cy, nz = vort.shape
    return pl.pallas_call(
        functools.partial(send_kernel, cap),
        out_shape=(
            shaped(7, cy, nz),
            shaped(7, cy, nz),
            shaped(7, cx, nz),
            shaped(7, cx, nz),
            shaped(n_slab * cap, 4, weights.shape[2]),
            shaped(4, n_slab * nz // CB),
        ),
        in_specs=[ANY] * 7,
        out_specs=(VMEM,) * 6,
        scratch_shapes=[
            pltpu.VMEM((2, 3, cx, 8, nz), jnp.float32),
            pltpu.VMEM((2, 3, cx, 8, nz), jnp.float32),
            pltpu.VMEM((2, cx, 8, nz), jnp.float32),
            pltpu.VMEM(weights.shape, jnp.float32),
            pltpu.VMEM(cells.shape, jnp.int32),
            pltpu.SMEM(dest.shape, jnp.int32),
            pltpu.SMEM(count.shape, jnp.int32),
            pltpu.SMEM((n_slab,), jnp.int32),
            pltpu.SemaphoreType.DMA((16,)),
        ],
        compiler_params=FIRST_PARAMS,
    )(vort, velo, visc, weights, cells, dest, count)


def ahead(a, axis):
    return pltpu.roll(a, a.shape[axis] - 1, axis)


def behind(a, axis):
    return pltpu.roll(a, 1, axis)


def interior_step(vort, velo, visc, out):
    cx, cy, nz = visc.shape
    row = lax.broadcasted_iota(jnp.int32, (cy, nz), 0)
    has_ahead = row < cy - 1
    has_behind = row > 0
    for x in range(cx):
        nu = visc[x]
        spin = [vort[c, x] for c in range(3)]
        mean_y = jnp.where(has_ahead, 0.5 * (nu + ahead(nu, 0)), 0.0)
        mean_z = 0.5 * (nu + ahead(nu, 1))
        if x < cx - 1:
            mean_next = 0.5 * (nu + visc[x + 1])
        if x > 0:
            mean_last = 0.5 * (nu + visc[x - 1])
        for c in range(3):
            w = spin[c]
            u = velo[c, x]
            flux_y = mean_y * (ahead(w, 0) - w)
            flux_z = mean_z * (ahead(w, 1) - w)
            change = (flux_y - behind(flux_y, 0)) + (flux_z - behind(flux_z, 1))
            slope_y = jnp.where(has_ahead, ahead(u, 0), 0.0) - jnp.where(has_behind, behind(u, 0), 0.0)
            slope_z = ahead(u, 1) - behind(u, 1)
            if x == 0:
                slope_x = velo[c, x + 1]
            elif x == cx - 1:
                slope_x = -velo[c, x - 1]
            else:
                slope_x = velo[c, x + 1] - velo[c, x - 1]
            stretch = 0.5 * (spin[0] * slope_x + spin[1] * slope_y + spin[2] * slope_z)
            if x < cx - 1:
                change = change + mean_next * (vort[c, x + 1] - w)
            if x > 0:
                change = change + mean_last * (vort[c, x - 1] - w)
            out[c, x] = w + TIME_STEP * (stretch + change)


def by_level(totals, width):
    nz = totals[0].shape[1]
    shape = (nz, width)
    level = lax.broadcasted_iota(jnp.int32, shape, 0) // CB
    lane = lax.broadcasted_iota(jnp.int32, shape, 1)
    pick = (lane == lax.axis_index("slab") * (nz // CB) + level).astype(jnp.float32)
    rows = jnp.concatenate(totals + [jnp.zeros_like(totals[0])], axis=0)
    return jnp.dot(rows, pick, precision=lax.Precision.HIGHEST, preferred_element_type=jnp.float32)


def inner_kernel(vort, velo, visc, tiles_in, out, moments, tiles, sem):
    copy = pltpu.make_async_copy(tiles_in, tiles, sem)
    copy.start()
    interior_step(vort, velo, visc, out)
    totals = [jnp.sum(out[c].reshape(-1, out.shape[3]), axis=0, keepdims=True) for c in range(3)]
    own = by_level(totals, moments.shape[1])
    copy.wait()
    moments[...] = tiles[...] + own


def inner(vort, velo, visc, tiles):
    return pl.pallas_call(
        inner_kernel,
        out_shape=(shaped(*vort.shape), shaped(*tiles.shape)),
        in_specs=[VMEM] * 3 + [ANY],
        out_specs=(VMEM,) * 2,
        scratch_shapes=[pltpu.VMEM(tiles.shape, jnp.float32), pltpu.SemaphoreType.DMA],
        compiler_params=PARAMS,
    )(vort, velo, visc, tiles)


def face_change(own, other, along, sign, c):
    stretch = (0.5 * sign) * own[along] * other[3 + c]
    diffuse = 0.5 * (own[6] + other[6]) * (other[c] - own[c])
    return TIME_STEP * (stretch + diffuse)


def edge_kernel(inside, moments, xlo, xhi, ylo, yhi, xlo_in, xhi_in, ylo_in, yhi_in, out, load):
    _, cx, cy, nz = out.shape
    out[...] = inside[...]
    totals = []
    for c in range(3):
        total = jnp.zeros((1, nz), jnp.float32)
        for own, other, at, sign in ((xlo, xlo_in, 0, -1.0), (xhi, xhi_in, cx - 1, 1.0)):
            change = face_change(own, other, 0, sign, c)
            out[c, at] = out[c, at] + change
            total = total + jnp.sum(change, axis=0, keepdims=True)
        for own, other, at, sign in ((ylo, ylo_in, 0, -1.0), (yhi, yhi_in, cy - 1, 1.0)):
            change = face_change(own, other, 1, sign, c)
            for x in range(cx):
                out[c, x, at : at + 1, :] = out[c, x, at : at + 1, :] + change[x : x + 1, :]
            total = total + jnp.sum(change, axis=0, keepdims=True)
        totals.append(total)
    moment = moments[...] + by_level(totals, moments.shape[1])
    for k in range(load.shape[1] // 4):
        part = moment[:, k * LANES : (k + 1) * LANES]
        for j in range(load.shape[0]):
            load[j, 4 * k : 4 * k + 4, :] = part


def edges(inside, moments, faces, halos, n_all):
    return pl.pallas_call(
        edge_kernel,
        out_shape=(shaped(*inside.shape), shaped(n_all, 4 * moments.shape[1] // LANES, LANES)),
        in_specs=[VMEM] * 10,
        out_specs=(VMEM,) * 2,
        compiler_params=PARAMS,
    )(inside, moments, *faces, *halos)


def far_kernel(cx, cy, ncl, n_pencil, load, out):
    n_all = load.shape[0]
    n_slab = n_all // n_pencil
    slab = lax.axis_index("slab")
    pencil = lax.axis_index("pencil")
    shape = (ncl, n_slab * ncl)
    target = lax.broadcasted_iota(jnp.int32, shape, 0)
    source = lax.broadcasted_iota(jnp.int32, shape, 1)
    sigma = jnp.float32(cx * n_slab // 4)
    rel_x = ((slab - source // ncl) * cx).astype(jnp.float32)
    rel_z = ((target - source % ncl) * CB).astype(jnp.float32)
    flat = rel_x * rel_x + rel_z * rel_z + sigma * sigma
    turned = [jnp.zeros(shape, jnp.float32) for _ in range(3)]
    for p in range(n_pencil):
        total = load[p]
        for s in range(1, n_slab):
            total = total + load[s * n_pencil + p]
        moment = jnp.concatenate([total[4 * k : 4 * k + 4] for k in range(load.shape[1] // 4)], axis=1)
        first, second, third = moment[0:1], moment[1:2], moment[2:3]
        rel_y = ((pencil - p) * cy).astype(jnp.float32)
        inverse = lax.rsqrt(flat + rel_y * rel_y)
        weight = inverse * inverse * inverse
        turned[0] = turned[0] + weight * (rel_z * second - rel_y * third)
        turned[1] = turned[1] + weight * (rel_x * third - rel_z * first)
        turned[2] = turned[2] + weight * (rel_y * first - rel_x * second)
    ones = jnp.ones((8, shape[1]), jnp.float32)
    for c in range(3):
        row = lax.dot_general(
            ones,
            turned[c],
            (((1,), (1,)), ((), ())),
            precision=lax.Precision.HIGHEST,
            preferred_element_type=jnp.float32,
        )
        out[c, 0] = row[0:1]


def far(load, cx, cy, ncl, n_pencil):
    return pl.pallas_call(
        functools.partial(far_kernel, cx, cy, ncl, n_pencil),
        out_shape=shaped(3, 1, 1, ncl),
        in_specs=[VMEM],
        out_specs=VMEM,
        compiler_params=PARAMS,
    )(load)


def deposit_kernel(cap, inside, load, out, acc, order):
    _, cx, cy, nz = out.shape
    rows = cx * cy // 2
    cells = 2 * rows * nz
    n_slab = load.shape[0] // cap
    wide = GROUP * load.shape[2]
    acc[...] = jnp.zeros_like(acc)
    listed = jnp.int32(0)
    for d in range(n_slab):
        first = d * cap
        held = jnp.max(load[first, 3:4, :]).astype(jnp.int32) // cells
        for k in range(cap):
            order[listed + k] = first + k
        listed = listed + held
    for k in range(GROUP):
        order[listed + k] = 0
    def numbers(length):
        shape = (length // 16, 16, wide)
        return (lax.broadcasted_iota(jnp.int32, shape, 0) * 16 + lax.broadcasted_iota(jnp.int32, shape, 1)).astype(
            jnp.float32
        ).astype(jnp.bfloat16)

    def spread(row):
        return jnp.broadcast_to(row, (16, wide)).astype(jnp.bfloat16)[None]

    row_numbers = numbers(rows)
    col_numbers = numbers(nz)
    place = lax.broadcasted_iota(jnp.int32, (1, wide), 1) // load.shape[2]
    zero = jnp.zeros((), jnp.bfloat16)
    one = jnp.ones((), jnp.bfloat16)

    def group(g, carry):
        tiles = [load[order[g * GROUP + k]] for k in range(GROUP)]
        block = jnp.concatenate(tiles, axis=1)
        live = place < listed - g * GROUP
        cell = block[3:4, :].astype(jnp.int32) % cells
        row = cell // nz
        half = row // rows
        at_row = row_numbers == spread(jnp.where(live, row % rows, -1).astype(jnp.float32))
        right = []
        for h in range(2):
            at_col = col_numbers == spread(jnp.where(half == h, cell % nz, -1).astype(jnp.float32))
            right.append(jnp.where(at_col, one, zero).reshape(nz, wide))
        left = []
        for piece in split(block):
            for c in range(3):
                left.append(jnp.where(at_row, spread(piece[c : c + 1, :]), zero).reshape(rows, wide))
        added = lax.dot_general(
            jnp.concatenate(left, axis=0),
            jnp.concatenate(right, axis=0),
            (((1,), (1,)), ((), ())),
            preferred_element_type=jnp.float32,
        )
        acc[...] += added[: 3 * rows] + added[3 * rows :]
        return carry

    lax.fori_loop(0, (listed + GROUP - 1) // GROUP, group, 0)
    for h in range(2):
        span = slice(h * (cx // 2), (h + 1) * (cx // 2))
        change = acc[:, h * nz : (h + 1) * nz].reshape(3, cx // 2, cy, nz)
        out[:, span] = inside[:, span] + change


def deposit(inside, load, cap):
    return pl.pallas_call(
        functools.partial(deposit_kernel, cap),
        out_shape=shaped(*inside.shape),
        in_specs=[VMEM] * 2,
        out_specs=VMEM,
        scratch_shapes=[
            pltpu.VMEM((3 * inside.shape[1] * inside.shape[2] // 2, 2 * inside.shape[3]), jnp.float32),
            pltpu.SMEM((load.shape[0] + max(cap, GROUP),), jnp.int32),
        ],
        compiler_params=PARAMS,
    )(inside, load)


def shift(array, axis, step):
    n = lax.axis_size(axis)
    pairs = [(i, i + step) for i in range(n) if 0 <= i + step < n]
    return lax.ppermute(array, axis, pairs)


def per_device(vorticity, velocity, viscosity, tile_weights, tile_cells, tile_dest, tile_count):
    _, cx, cy, nz = vorticity.shape
    ncl = nz // CB
    n_slab = lax.axis_size("slab")
    n_pencil = lax.axis_size("pencil")
    cap = 2 * tile_weights.shape[0] // n_slab
    weights = jnp.transpose(tile_weights, (1, 0, 2))
    xlo, xhi, ylo, yhi, packets, tiles = to_send(
        vorticity, velocity, viscosity, weights, tile_cells, tile_dest.T, tile_count, n_slab, cap
    )
    xhi_in = shift(xlo, "slab", -1)
    xlo_in = shift(xhi, "slab", 1)
    arrived = lax.all_to_all(packets, "slab", 0, 0, tiled=True)
    yhi_in = shift(ylo, "pencil", -1)
    ylo_in = shift(yhi, "pencil", 1)
    inside, moments = inner(vorticity, velocity, viscosity, tiles)
    advanced, load = edges(
        inside, moments, (xlo, xhi, ylo, yhi), (xlo_in, xhi_in, ylo_in, yhi_in), n_slab * n_pencil
    )
    load = lax.all_to_all(load, ("slab", "pencil"), 0, 0, tiled=True)
    vorticity_out = deposit(advanced, arrived, cap)
    return (vorticity_out, far(load, cx, cy, ncl, n_pencil))


def solution(mesh):
    in_specs = (
        P(None, "slab", "pencil", None),
        P(None, "slab", "pencil", None),
        P("slab", "pencil", None),
        P(("slab", "pencil"), None, None),
        P(("slab", "pencil"), None),
        P(("slab", "pencil"), None),
        P(("slab", "pencil")),
    )
    out_specs = (P(None, "slab", "pencil", None), P(None, "slab", "pencil", None))
    return jax.shard_map(
        per_device, mesh=mesh, in_specs=in_specs, out_specs=out_specs, check_vma=False
    )
```

```python
import functools

import jax
import jax.numpy as jnp
from jax import lax
from jax.experimental import pallas as pl
from jax.experimental.pallas import tpu as pltpu
from jax.sharding import PartitionSpec as P

CB = 16
TIME_STEP = 0.1
LANES = 128
GROUP = 8
VMEM_LIMIT = 24 * 1024 * 1024

VMEM = pl.BlockSpec(memory_space=pltpu.VMEM)
ANY = pl.BlockSpec(memory_space=pl.ANY)
SMEM = pl.BlockSpec(memory_space=pltpu.SMEM)
FIRST_PARAMS = pltpu.CompilerParams(vmem_limit_bytes=60 * 1024 * 1024)
PARAMS = pltpu.CompilerParams(vmem_limit_bytes=VMEM_LIMIT)


def shaped(*shape):
    return jax.ShapeDtypeStruct(shape, jnp.float32)


def split(w):
    high = w.astype(jnp.bfloat16).astype(jnp.float32)
    return high, w - high


def tile_moments(cap, nz, packets, moments):
    n_slab = packets.shape[0] // cap
    ncl = nz // CB
    wide = cap * packets.shape[2]
    level = lax.broadcasted_iota(jnp.int32, (ncl, wide), 0)
    found = []
    for d in range(n_slab):
        block = jnp.concatenate([packets[d * cap + k] for k in range(cap)], axis=1)
        cell = block[3:4, :].astype(jnp.int32)
        spots = (level == cell % nz // CB).astype(jnp.float32).astype(jnp.bfloat16)
        high, low = split(block)
        left = jnp.concatenate([high, low], axis=0).astype(jnp.bfloat16)
        sums = lax.dot_general(left, spots, (((1,), (1,)), ((), ())), preferred_element_type=jnp.float32)
        found.append(sums[0:4] + sums[4:8])
    moments[...] = jnp.concatenate(found, axis=1)


class Copies:
    def __init__(self, sems):
        self.sems = sems
        self.made = []

    def start(self, source, target):
        self.made.append(pltpu.make_async_copy(source, target, self.sems.at[len(self.made)]))
        self.made[-1].start()

    def wait(self, first, last):
        for k in range(first, last):
            self.made[k].wait()


def send_kernel(
    cap,
    vort,
    velo,
    visc,
    weights_in,
    cells_in,
    dest_in,
    count_in,
    xlo_out,
    xhi_out,
    swap_out,
    other_out,
    packets_out,
    moments_out,
    xlo,
    xhi,
    swap,
    other,
    packets,
    moments,
    lows,
    highs,
    weights,
    cells,
    dest,
    count,
    filled,
    sems,
):
    cx, cy, nz = visc.shape
    copies = Copies(sems)
    copies.start(weights_in, weights)
    copies.start(cells_in, cells)
    copies.start(dest_in, dest)
    copies.start(count_in, count)
    for face, at in ((xlo, 0), (xhi, cx - 1)):
        copies.start(vort.at[:, at], face.at[0:3])
        copies.start(velo.at[:, at], face.at[3:6])
        copies.start(visc.at[at], face.at[6])
    for rows, at in ((lows, 0), (highs, cy - 8)):
        copies.start(vort.at[:, :, pl.ds(at, 8), :], rows.at[0:3])
        copies.start(velo.at[:, :, pl.ds(at, 8), :], rows.at[3:6])
        copies.start(visc.at[:, pl.ds(at, 8), :], rows.at[6])

    packets[...] = jnp.zeros_like(packets)
    n_slab = packets.shape[0] // cap
    for d in range(n_slab):
        filled[d] = 0
    copies.wait(0, 4)

    def place(r, carry):
        d = dest[0, r]
        slot = filled[d]
        at = d * cap + slot
        for c in range(3):
            packets[at, c : c + 1, :] = weights[c, pl.ds(r, 1), :]
        packets[at, 3:4, :] = cells[pl.ds(r, 1), :].astype(jnp.float32)
        filled[d] = slot + 1
        return carry

    lax.fori_loop(0, count[0], place, 0)
    for d in range(n_slab):
        held = (filled[d] * (cx * cy * nz)).astype(jnp.float32)
        packets[d * cap, 3:4, :] = packets[d * cap, 3:4, :] + held
    copies.start(packets, packets_out)
    copies.wait(4, 10)
    copies.start(xlo, xlo_out)
    copies.start(xhi, xhi_out)
    copies.wait(10, 16)
    even = lax.axis_index("pencil") % 2 == 0
    for k in range(7):
        for x in range(cx):
            low = lows[k, x, 0:1, :]
            high = highs[k, x, 7:8, :]
            swap[k, x : x + 1, :] = jnp.where(even, high, low)
            other[k, x : x + 1, :] = jnp.where(even, low, high)
    copies.start(swap, swap_out)
    copies.start(other, other_out)
    tile_moments(cap, nz, packets, moments)
    copies.start(moments, moments_out)
    copies.wait(16, 22)


def to_send(vort, velo, visc, weights, cells, dest, count, n_slab, cap):
    _, cx, cy, nz = vort.shape
    made = (
        shaped(7, cy, nz),
        shaped(7, cy, nz),
        shaped(7, cx, nz),
        shaped(7, cx, nz),
        shaped(n_slab * cap, 4, weights.shape[2]),
        shaped(4, n_slab * nz // CB),
    )
    return pl.pallas_call(
        functools.partial(send_kernel, cap),
        out_shape=made,
        in_specs=[ANY] * 7,
        out_specs=(ANY,) * 6,
        scratch_shapes=[pltpu.VMEM(one.shape, jnp.float32) for one in made]
        + [
            pltpu.VMEM((7, cx, 8, nz), jnp.float32),
            pltpu.VMEM((7, cx, 8, nz), jnp.float32),
            pltpu.VMEM(weights.shape, jnp.float32),
            pltpu.VMEM(cells.shape, jnp.int32),
            pltpu.SMEM(dest.shape, jnp.int32),
            pltpu.SMEM(count.shape, jnp.int32),
            pltpu.SMEM((n_slab,), jnp.int32),
            pltpu.SemaphoreType.DMA((22,)),
        ],
        compiler_params=FIRST_PARAMS,
    )(vort, velo, visc, weights, cells, dest, count)


def ahead(a, axis):
    return pltpu.roll(a, a.shape[axis] - 1, axis)


def behind(a, axis):
    return pltpu.roll(a, 1, axis)


def interior_step(vort, velo, visc, out):
    cx, cy, nz = visc.shape
    has_ahead = lax.broadcasted_iota(jnp.int32, (cy, nz), 0) < cy - 1
    totals = [jnp.zeros((8, nz), jnp.float32) for _ in range(3)]
    flux_x = [None] * 3
    for x in range(cx):
        nu = visc[x]
        spin = [vort[c, x] for c in range(3)]
        mean_y = jnp.where(has_ahead, 0.5 * (nu + ahead(nu, 0)), 0.0)
        mean_z = 0.5 * (nu + ahead(nu, 1))
        half_y = 0.5 * spin[1]
        half_z = 0.5 * spin[2]
        next_y = jnp.where(has_ahead, ahead(half_y, 0), 0.0)
        next_z = ahead(half_z, 1)
        half_y = jnp.where(has_ahead, half_y, 0.0)
        half_x = 0.5 * spin[0]
        if x < cx - 1:
            mean_x = 0.5 * (nu + visc[x + 1])
        for c in range(3):
            w = spin[c]
            u = velo[c, x]
            flux_y = mean_y * (ahead(w, 0) - w)
            flux_z = mean_z * (ahead(w, 1) - w)
            change = flux_y + half_y * ahead(u, 0) - behind(flux_y + next_y * u, 0)
            change = change + (flux_z + half_z * ahead(u, 1) - behind(flux_z + next_z * u, 1))
            if x == 0:
                change = change + half_x * velo[c, x + 1]
            elif x == cx - 1:
                change = change - half_x * velo[c, x - 1]
            else:
                change = change + half_x * (velo[c, x + 1] - velo[c, x - 1])
            if x > 0:
                change = change - flux_x[c]
            if x < cx - 1:
                flux_x[c] = mean_x * (vort[c, x + 1] - w)
                change = change + flux_x[c]
            new = w + TIME_STEP * change
            out[c, x] = new
            totals[c] = totals[c] + jnp.sum(new.reshape(cy // 8, 8, nz), axis=0)
    return [jnp.sum(total, axis=0, keepdims=True) for total in totals]


def by_level(totals, width):
    nz = totals[0].shape[1]
    shape = (nz, width)
    level = lax.broadcasted_iota(jnp.int32, shape, 0) // CB
    lane = lax.broadcasted_iota(jnp.int32, shape, 1)
    pick = (lane == lax.axis_index("slab") * (nz // CB) + level).astype(jnp.float32)
    rows = jnp.concatenate(totals + [jnp.zeros_like(totals[0])], axis=0)
    return jnp.dot(rows, pick, precision=lax.Precision.HIGHEST, preferred_element_type=jnp.float32)


def inner_kernel(vort, velo, visc, tiles_in, out, moments, tiles, sem):
    copy = pltpu.make_async_copy(tiles_in, tiles, sem)
    copy.start()
    own = by_level(interior_step(vort, velo, visc, out), moments.shape[1])
    copy.wait()
    moments[...] = tiles[...] + own


def inner(vort, velo, visc, tiles):
    return pl.pallas_call(
        inner_kernel,
        out_shape=(shaped(*vort.shape), shaped(*tiles.shape)),
        in_specs=[VMEM] * 3 + [ANY],
        out_specs=(VMEM,) * 2,
        scratch_shapes=[pltpu.VMEM(tiles.shape, jnp.float32), pltpu.SemaphoreType.DMA],
        compiler_params=PARAMS,
    )(vort, velo, visc, tiles)


def face_change(own, other, along, sign, c):
    stretch = (0.5 * sign) * own[along] * other[3 + c]
    diffuse = 0.5 * (own[6] + other[6]) * (other[c] - own[c])
    return TIME_STEP * (stretch + diffuse)


def edge_kernel(
    inside, moments, xlo, xhi, swap, other, xlo_in, xhi_in, swap_in, other_in, out, load_out, load, side_change, sem
):
    _, cx, cy, nz = out.shape
    even = lax.axis_index("pencil") % 2 == 0
    low, low_in = jnp.where(even, other[...], swap[...]), jnp.where(even, other_in[...], swap_in[...])
    high, high_in = jnp.where(even, swap[...], other[...]), jnp.where(even, swap_in[...], other_in[...])
    totals = []
    for c in range(3):
        total = jnp.zeros((8, nz), jnp.float32)
        for own, came, at, sign in ((xlo, xlo_in, 0, -1.0), (xhi, xhi_in, cx - 1, 1.0)):
            change = face_change(own, came, 0, sign, c)
            out[c, at] = inside[c, at] + change
            total = total + jnp.sum(change.reshape(cy // 8, 8, nz), axis=0)
        for k, own, came, sign in ((0, low, low_in, -1.0), (1, high, high_in, 1.0)):
            change = face_change(own, came, 1, sign, c)
            side_change[k, c] = change
            total = total + change
        totals.append(jnp.sum(total, axis=0, keepdims=True))
    moment = moments[...] + by_level(totals, moments.shape[1])
    for k in range(load.shape[1] // 4):
        part = moment[:, k * LANES : (k + 1) * LANES]
        load[:, 4 * k : 4 * k + 4, :] = jnp.broadcast_to(part[None], (load.shape[0], 4, LANES))
    copy = pltpu.make_async_copy(load, load_out, sem)
    copy.start()
    for c in range(3):
        out[c, 1 : cx - 1] = inside[c, 1 : cx - 1]
        for k, at in ((0, 0), (1, cy - 1)):
            for x in range(cx):
                out[c, x, at : at + 1, :] = out[c, x, at : at + 1, :] + side_change[k, c, x : x + 1, :]
    copy.wait()


def edges(inside, moments, faces, halos, n_all):
    _, cx, _, nz = inside.shape
    load = shaped(n_all, 4 * moments.shape[1] // LANES, LANES)
    return pl.pallas_call(
        edge_kernel,
        out_shape=(shaped(*inside.shape), load),
        in_specs=[VMEM] * 10,
        out_specs=(VMEM, ANY),
        scratch_shapes=[
            pltpu.VMEM(load.shape, jnp.float32),
            pltpu.VMEM((2, 3, cx, nz), jnp.float32),
            pltpu.SemaphoreType.DMA,
        ],
        compiler_params=PARAMS,
    )(inside, moments, *faces, *halos)


def far_kernel(cx, cy, ncl, n_pencil, load, out):
    n_all = load.shape[0]
    n_slab = n_all // n_pencil
    slab = lax.axis_index("slab")
    pencil = lax.axis_index("pencil")
    shape = (ncl, n_slab * ncl)
    target = lax.broadcasted_iota(jnp.int32, shape, 0)
    source = lax.broadcasted_iota(jnp.int32, shape, 1)
    sigma = jnp.float32(cx * n_slab // 4)
    rel_x = ((slab - source // ncl) * cx).astype(jnp.float32)
    rel_z = ((target - source % ncl) * CB).astype(jnp.float32)
    flat = rel_x * rel_x + rel_z * rel_z + sigma * sigma
    turned = [jnp.zeros(shape, jnp.float32) for _ in range(3)]
    for p in range(n_pencil):
        total = load[p]
        for s in range(1, n_slab):
            total = total + load[s * n_pencil + p]
        moment = jnp.concatenate([total[4 * k : 4 * k + 4] for k in range(load.shape[1] // 4)], axis=1)
        first, second, third = moment[0:1], moment[1:2], moment[2:3]
        rel_y = ((pencil - p) * cy).astype(jnp.float32)
        inverse = lax.rsqrt(flat + rel_y * rel_y)
        weight = inverse * inverse * inverse
        turned[0] = turned[0] + weight * (rel_z * second - rel_y * third)
        turned[1] = turned[1] + weight * (rel_x * third - rel_z * first)
        turned[2] = turned[2] + weight * (rel_y * first - rel_x * second)
    ones = jnp.ones((8, shape[1]), jnp.float32)
    for c in range(3):
        row = lax.dot_general(
            ones,
            turned[c],
            (((1,), (1,)), ((), ())),
            precision=lax.Precision.HIGHEST,
            preferred_element_type=jnp.float32,
        )
        out[c, 0] = row[0:1]


def far(load, cx, cy, ncl, n_pencil):
    return pl.pallas_call(
        functools.partial(far_kernel, cx, cy, ncl, n_pencil),
        out_shape=shaped(3, 1, 1, ncl),
        in_specs=[VMEM],
        out_specs=VMEM,
        compiler_params=PARAMS,
    )(load)


def deposit_kernel(cap, inside, load, out, acc, order):
    _, cx, cy, nz = out.shape
    rows = cx * cy // 2
    cells = 2 * rows * nz
    n_slab = load.shape[0] // cap
    wide = GROUP * load.shape[2]
    acc[...] = jnp.zeros_like(acc)
    listed = jnp.int32(0)
    for d in range(n_slab):
        first = d * cap
        held = jnp.max(load[first, 3:4, :]).astype(jnp.int32) // cells
        for k in range(cap):
            order[listed + k] = first + k
        listed = listed + held
    for k in range(GROUP):
        order[listed + k] = 0
    def numbers(length):
        shape = (length // 16, 16, wide)
        return (lax.broadcasted_iota(jnp.int32, shape, 0) * 16 + lax.broadcasted_iota(jnp.int32, shape, 1)).astype(
            jnp.float32
        ).astype(jnp.bfloat16)

    def spread(row):
        return jnp.broadcast_to(row, (16, wide)).astype(jnp.bfloat16)[None]

    row_numbers = numbers(rows)
    col_numbers = numbers(nz)
    place = lax.broadcasted_iota(jnp.int32, (1, wide), 1) // load.shape[2]
    zero = jnp.zeros((), jnp.bfloat16)
    one = jnp.ones((), jnp.bfloat16)

    def group(g, carry):
        tiles = [load[order[g * GROUP + k]] for k in range(GROUP)]
        block = jnp.concatenate(tiles, axis=1)
        live = place < listed - g * GROUP
        cell = block[3:4, :].astype(jnp.int32) % cells
        row = cell // nz
        half = row // rows
        at_row = row_numbers == spread(jnp.where(live, row % rows, -1).astype(jnp.float32))
        right = []
        for h in range(2):
            at_col = col_numbers == spread(jnp.where(half == h, cell % nz, -1).astype(jnp.float32))
            right.append(jnp.where(at_col, one, zero).reshape(nz, wide))
        left = []
        for piece in split(block):
            for c in range(3):
                left.append(jnp.where(at_row, spread(piece[c : c + 1, :]), zero).reshape(rows, wide))
        added = lax.dot_general(
            jnp.concatenate(left, axis=0),
            jnp.concatenate(right, axis=0),
            (((1,), (1,)), ((), ())),
            preferred_element_type=jnp.float32,
        )
        acc[...] += added[: 3 * rows] + added[3 * rows :]
        return carry

    lax.fori_loop(0, (listed + GROUP - 1) // GROUP, group, 0)
    for h in range(2):
        span = slice(h * (cx // 2), (h + 1) * (cx // 2))
        change = acc[:, h * nz : (h + 1) * nz].reshape(3, cx // 2, cy, nz)
        out[:, span] = inside[:, span] + change


def deposit(inside, load, cap):
    return pl.pallas_call(
        functools.partial(deposit_kernel, cap),
        out_shape=shaped(*inside.shape),
        in_specs=[VMEM] * 2,
        out_specs=VMEM,
        scratch_shapes=[
            pltpu.VMEM((3 * inside.shape[1] * inside.shape[2] // 2, 2 * inside.shape[3]), jnp.float32),
            pltpu.SMEM((load.shape[0] + max(cap, GROUP),), jnp.int32),
        ],
        compiler_params=PARAMS,
    )(inside, load)


def shift(array, axis, step):
    n = lax.axis_size(axis)
    pairs = [(i, i + step) for i in range(n) if 0 <= i + step < n]
    return lax.ppermute(array, axis, pairs)


def swapped(array, axis, first):
    up = [(i, i + 1) for i in range(first, lax.axis_size(axis) - 1, 2)]
    return lax.ppermute(array, axis, up + [(j, i) for i, j in up])


def per_device(vorticity, velocity, viscosity, tile_weights, tile_cells, tile_dest, tile_count):
    _, cx, cy, nz = vorticity.shape
    ncl = nz // CB
    n_slab = lax.axis_size("slab")
    n_pencil = lax.axis_size("pencil")
    cap = 2 * tile_weights.shape[0] // n_slab
    weights = jnp.transpose(tile_weights, (1, 0, 2))
    count = tile_count
    *faces, packets, tiles = to_send(
        vorticity, velocity, viscosity, weights, tile_cells, tile_dest.T, count, n_slab, cap
    )
    xlo, xhi, swap, other = faces
    halos = (
        shift(xhi, "slab", 1),
        shift(xlo, "slab", -1),
        swapped(swap, "pencil", 0),
        swapped(other, "pencil", 1),
    )
    arrived = lax.all_to_all(packets, "slab", 0, 0, tiled=True)
    inside, moments = inner(vorticity, velocity, viscosity, tiles)
    advanced, load = edges(inside, moments, faces, halos, n_slab * n_pencil)
    load = lax.all_to_all(load, ("slab", "pencil"), 0, 0, tiled=True)
    vorticity_out = deposit(advanced, arrived, cap)
    return (vorticity_out, far(load, cx, cy, ncl, n_pencil))


def solution(mesh):
    in_specs = (
        P(None, "slab", "pencil", None),
        P(None, "slab", "pencil", None),
        P("slab", "pencil", None),
        P(("slab", "pencil"), None, None),
        P(("slab", "pencil"), None),
        P(("slab", "pencil"), None),
        P(("slab", "pencil")),
    )
    out_specs = (P(None, "slab", "pencil", None), P(None, "slab", "pencil", None))
    return jax.shard_map(
        per_device, mesh=mesh, in_specs=in_specs, out_specs=out_specs, check_vma=False
    )
```

```python
import functools

import jax
import jax.numpy as jnp
from jax import lax
from jax.experimental import pallas as pl
from jax.experimental.pallas import tpu as pltpu
from jax.sharding import PartitionSpec as P

CB = 16
TIME_STEP = 0.1
LANES = 128
SIDES = ("slab", "slab", "pencil", "pencil")
GROUP = 8
VMEM_LIMIT = 24 * 1024 * 1024

VMEM = pl.BlockSpec(memory_space=pltpu.VMEM)
ANY = pl.BlockSpec(memory_space=pl.ANY)
SMEM = pl.BlockSpec(memory_space=pltpu.SMEM)
FIRST_PARAMS = pltpu.CompilerParams(vmem_limit_bytes=60 * 1024 * 1024)
PARAMS = pltpu.CompilerParams(vmem_limit_bytes=VMEM_LIMIT)


def shaped(*shape):
    return jax.ShapeDtypeStruct(shape, jnp.float32)


def split(w):
    high = w.astype(jnp.bfloat16).astype(jnp.float32)
    return high, w - high


def tile_moments(cap, nz, packets, moments):
    n_slab = packets.shape[0] // cap
    ncl = nz // CB
    wide = cap * packets.shape[2]
    level = lax.broadcasted_iota(jnp.int32, (ncl, wide), 0)
    found = []
    for d in range(n_slab):
        block = jnp.concatenate([packets[d * cap + k] for k in range(cap)], axis=1)
        cell = block[3:4, :].astype(jnp.int32)
        spots = (level == cell % nz // CB).astype(jnp.float32).astype(jnp.bfloat16)
        high, low = split(block)
        left = jnp.concatenate([high, low], axis=0).astype(jnp.bfloat16)
        sums = lax.dot_general(left, spots, (((1,), (1,)), ((), ())), preferred_element_type=jnp.float32)
        found.append(sums[0:4] + sums[4:8])
    moments[...] = jnp.concatenate(found, axis=1)


class Copies:
    def __init__(self, sems):
        self.sems = sems
        self.made = []

    def start(self, source, target):
        self.made.append(pltpu.make_async_copy(source, target, self.sems.at[len(self.made)]))
        self.made[-1].start()

    def wait(self, first, last):
        for k in range(first, last):
            self.made[k].wait()


def send_kernel(
    cap,
    vort,
    velo,
    visc,
    weights_in,
    cells_in,
    dest_in,
    count_in,
    near_out,
    far_out,
    swap_out,
    other_out,
    packets_out,
    moments_out,
    near,
    far,
    swap,
    other,
    packets,
    moments,
    lows,
    highs,
    weights,
    cells,
    dest,
    count,
    filled,
    sems,
):
    cx, cy, nz = visc.shape
    copies = Copies(sems)
    copies.start(weights_in, weights)
    copies.start(cells_in, cells)
    copies.start(dest_in, dest)
    copies.start(count_in, count)
    even = lax.axis_index("slab") % 2 == 0
    for face, at in ((near, jnp.where(even, cx - 1, 0)), (far, jnp.where(even, 0, cx - 1))):
        copies.start(vort.at[:, at], face.at[0:3])
        copies.start(velo.at[:, at], face.at[3:6])
        copies.start(visc.at[at], face.at[6])
    for rows, at in ((lows, 0), (highs, cy - 8)):
        copies.start(vort.at[:, :, pl.ds(at, 8), :], rows.at[0:3])
        copies.start(velo.at[:, :, pl.ds(at, 8), :], rows.at[3:6])
        copies.start(visc.at[:, pl.ds(at, 8), :], rows.at[6])

    packets[...] = jnp.zeros_like(packets)
    n_slab = packets.shape[0] // cap
    for d in range(n_slab):
        filled[d] = 0
    copies.wait(0, 4)

    def place(r, carry):
        d = dest[0, r]
        slot = filled[d]
        at = d * cap + slot
        for c in range(3):
            packets[at, c : c + 1, :] = weights[c, pl.ds(r, 1), :]
        packets[at, 3:4, :] = cells[pl.ds(r, 1), :].astype(jnp.float32)
        filled[d] = slot + 1
        return carry

    lax.fori_loop(0, count[0], place, 0)
    for d in range(n_slab):
        held = (filled[d] * (cx * cy * nz)).astype(jnp.float32)
        packets[d * cap, 3:4, :] = packets[d * cap, 3:4, :] + held
    copies.start(packets, packets_out)
    copies.wait(4, 10)
    copies.start(near, near_out)
    copies.start(far, far_out)
    copies.wait(10, 16)
    even = lax.axis_index("pencil") % 2 == 0
    for k in range(7):
        for x in range(cx):
            low = lows[k, x, 0:1, :]
            high = highs[k, x, 7:8, :]
            swap[k, x : x + 1, :] = jnp.where(even, high, low)
            other[k, x : x + 1, :] = jnp.where(even, low, high)
    copies.start(swap, swap_out)
    copies.start(other, other_out)
    tile_moments(cap, nz, packets, moments)
    copies.start(moments, moments_out)
    copies.wait(16, 22)


def to_send(vort, velo, visc, weights, cells, dest, count, n_slab, cap):
    _, cx, cy, nz = vort.shape
    made = (
        shaped(7, cy, nz),
        shaped(7, cy, nz),
        shaped(7, cx, nz),
        shaped(7, cx, nz),
        shaped(n_slab * cap, 4, weights.shape[2]),
        shaped(4, n_slab * nz // CB),
    )
    return pl.pallas_call(
        functools.partial(send_kernel, cap),
        out_shape=made,
        in_specs=[ANY] * 7,
        out_specs=(ANY,) * 6,
        scratch_shapes=[pltpu.VMEM(one.shape, jnp.float32) for one in made]
        + [
            pltpu.VMEM((7, cx, 8, nz), jnp.float32),
            pltpu.VMEM((7, cx, 8, nz), jnp.float32),
            pltpu.VMEM(weights.shape, jnp.float32),
            pltpu.VMEM(cells.shape, jnp.int32),
            pltpu.SMEM(dest.shape, jnp.int32),
            pltpu.SMEM(count.shape, jnp.int32),
            pltpu.SMEM((n_slab,), jnp.int32),
            pltpu.SemaphoreType.DMA((22,)),
        ],
        compiler_params=FIRST_PARAMS,
    )(vort, velo, visc, weights, cells, dest, count)


def ahead(a, axis):
    return pltpu.roll(a, a.shape[axis] - 1, axis)


def behind(a, axis):
    return pltpu.roll(a, 1, axis)


def interior_step(vort, velo, visc, out):
    cx, cy, nz = visc.shape
    has_ahead = lax.broadcasted_iota(jnp.int32, (cy, nz), 0) < cy - 1
    totals = [jnp.zeros((8, nz), jnp.float32) for _ in range(3)]
    flux_x = [None] * 3
    for x in range(cx):
        nu = visc[x]
        spin = [vort[c, x] for c in range(3)]
        mean_y = jnp.where(has_ahead, 0.5 * (nu + ahead(nu, 0)), 0.0)
        mean_z = 0.5 * (nu + ahead(nu, 1))
        half_y = 0.5 * spin[1]
        half_z = 0.5 * spin[2]
        next_y = jnp.where(has_ahead, ahead(half_y, 0), 0.0)
        next_z = ahead(half_z, 1)
        half_y = jnp.where(has_ahead, half_y, 0.0)
        half_x = 0.5 * spin[0]
        if x < cx - 1:
            mean_x = 0.5 * (nu + visc[x + 1])
        for c in range(3):
            w = spin[c]
            u = velo[c, x]
            flux_y = mean_y * (ahead(w, 0) - w)
            flux_z = mean_z * (ahead(w, 1) - w)
            change = flux_y + half_y * ahead(u, 0) - behind(flux_y + next_y * u, 0)
            change = change + (flux_z + half_z * ahead(u, 1) - behind(flux_z + next_z * u, 1))
            if x == 0:
                change = change + half_x * velo[c, x + 1]
            elif x == cx - 1:
                change = change - half_x * velo[c, x - 1]
            else:
                change = change + half_x * (velo[c, x + 1] - velo[c, x - 1])
            if x > 0:
                change = change - flux_x[c]
            if x < cx - 1:
                flux_x[c] = mean_x * (vort[c, x + 1] - w)
                change = change + flux_x[c]
            new = w + TIME_STEP * change
            out[c, x] = new
            totals[c] = totals[c] + jnp.sum(new.reshape(cy // 8, 8, nz), axis=0)
    return [jnp.sum(total, axis=0, keepdims=True) for total in totals]


def by_level(totals, width):
    nz = totals[0].shape[1]
    shape = (nz, width)
    level = lax.broadcasted_iota(jnp.int32, shape, 0) // CB
    lane = lax.broadcasted_iota(jnp.int32, shape, 1)
    pick = (lane == lax.axis_index("slab") * (nz // CB) + level).astype(jnp.float32)
    rows = jnp.concatenate(totals + [jnp.zeros_like(totals[0])], axis=0)
    return jnp.dot(rows, pick, precision=lax.Precision.HIGHEST, preferred_element_type=jnp.float32)


def inner_kernel(vort, velo, visc, tiles_in, out, moments, tiles, sem):
    copy = pltpu.make_async_copy(tiles_in, tiles, sem)
    copy.start()
    own = by_level(interior_step(vort, velo, visc, out), moments.shape[1])
    copy.wait()
    moments[...] = tiles[...] + own


def inner(vort, velo, visc, tiles):
    return pl.pallas_call(
        inner_kernel,
        out_shape=(shaped(*vort.shape), shaped(*tiles.shape)),
        in_specs=[VMEM] * 3 + [ANY],
        out_specs=(VMEM,) * 2,
        scratch_shapes=[pltpu.VMEM(tiles.shape, jnp.float32), pltpu.SemaphoreType.DMA],
        compiler_params=PARAMS,
    )(vort, velo, visc, tiles)


def face_change(own, other, along, sign, c):
    stretch = (0.5 * sign) * own[along] * other[3 + c]
    diffuse = 0.5 * (own[6] + other[6]) * (other[c] - own[c])
    return TIME_STEP * (stretch + diffuse)


def edge_kernel(
    inside, moments, near, far, swap, other, near_in, far_in, swap_in, other_in, out, load_out, load, side_change, sem
):
    _, cx, cy, nz = out.shape
    even = lax.axis_index("pencil") % 2 == 0
    low, low_in = jnp.where(even, other[...], swap[...]), jnp.where(even, other_in[...], swap_in[...])
    high, high_in = jnp.where(even, swap[...], other[...]), jnp.where(even, swap_in[...], other_in[...])
    even = lax.axis_index("slab") % 2 == 0
    near_at, far_at = jnp.where(even, cx - 1, 0), jnp.where(even, 0, cx - 1)
    near_sign = jnp.where(even, 1.0, -1.0)
    totals = []
    for c in range(3):
        total = jnp.zeros((8, nz), jnp.float32)
        for own, came, at, sign in ((near, near_in, near_at, near_sign), (far, far_in, far_at, -near_sign)):
            change = face_change(own, came, 0, sign, c)
            out[c, at] = inside[c, at] + change
            total = total + jnp.sum(change.reshape(cy // 8, 8, nz), axis=0)
        for k, own, came, sign in ((0, low, low_in, -1.0), (1, high, high_in, 1.0)):
            change = face_change(own, came, 1, sign, c)
            side_change[k, c] = change
            total = total + change
        totals.append(jnp.sum(total, axis=0, keepdims=True))
    moment = moments[...] + by_level(totals, moments.shape[1])
    for k in range(load.shape[1] // 4):
        part = moment[:, k * LANES : (k + 1) * LANES]
        load[:, 4 * k : 4 * k + 4, :] = jnp.broadcast_to(part[None], (load.shape[0], 4, LANES))
    copy = pltpu.make_async_copy(load, load_out, sem)
    copy.start()
    for c in range(3):
        out[c, 1 : cx - 1] = inside[c, 1 : cx - 1]
        for k, at in ((0, 0), (1, cy - 1)):
            for x in range(cx):
                out[c, x, at : at + 1, :] = out[c, x, at : at + 1, :] + side_change[k, c, x : x + 1, :]
    copy.wait()


def edges(inside, moments, faces, halos, n_all):
    _, cx, _, nz = inside.shape
    load = shaped(n_all, 4 * moments.shape[1] // LANES, LANES)
    return pl.pallas_call(
        edge_kernel,
        out_shape=(shaped(*inside.shape), load),
        in_specs=[VMEM] * 10,
        out_specs=(VMEM, ANY),
        scratch_shapes=[
            pltpu.VMEM(load.shape, jnp.float32),
            pltpu.VMEM((2, 3, cx, nz), jnp.float32),
            pltpu.SemaphoreType.DMA,
        ],
        compiler_params=PARAMS,
    )(inside, moments, *faces, *halos)


def far_kernel(cx, cy, ncl, n_pencil, load, out):
    n_all = load.shape[0]
    n_slab = n_all // n_pencil
    slab = lax.axis_index("slab")
    pencil = lax.axis_index("pencil")
    shape = (ncl, n_slab * ncl)
    target = lax.broadcasted_iota(jnp.int32, shape, 0)
    source = lax.broadcasted_iota(jnp.int32, shape, 1)
    sigma = jnp.float32(cx * n_slab // 4)
    rel_x = ((slab - source // ncl) * cx).astype(jnp.float32)
    rel_z = ((target - source % ncl) * CB).astype(jnp.float32)
    flat = rel_x * rel_x + rel_z * rel_z + sigma * sigma
    turned = [jnp.zeros(shape, jnp.float32) for _ in range(3)]
    for p in range(n_pencil):
        total = load[p]
        for s in range(1, n_slab):
            total = total + load[s * n_pencil + p]
        moment = jnp.concatenate([total[4 * k : 4 * k + 4] for k in range(load.shape[1] // 4)], axis=1)
        first, second, third = moment[0:1], moment[1:2], moment[2:3]
        rel_y = ((pencil - p) * cy).astype(jnp.float32)
        inverse = lax.rsqrt(flat + rel_y * rel_y)
        weight = inverse * inverse * inverse
        turned[0] = turned[0] + weight * (rel_z * second - rel_y * third)
        turned[1] = turned[1] + weight * (rel_x * third - rel_z * first)
        turned[2] = turned[2] + weight * (rel_y * first - rel_x * second)
    ones = jnp.ones((8, shape[1]), jnp.float32)
    for c in range(3):
        row = lax.dot_general(
            ones,
            turned[c],
            (((1,), (1,)), ((), ())),
            precision=lax.Precision.HIGHEST,
            preferred_element_type=jnp.float32,
        )
        out[c, 0] = row[0:1]


def far(load, cx, cy, ncl, n_pencil):
    return pl.pallas_call(
        functools.partial(far_kernel, cx, cy, ncl, n_pencil),
        out_shape=shaped(3, 1, 1, ncl),
        in_specs=[VMEM],
        out_specs=VMEM,
        compiler_params=PARAMS,
    )(load)


def deposit_kernel(cap, inside, load, out, acc, order):
    _, cx, cy, nz = out.shape
    rows = cx * cy // 2
    cells = 2 * rows * nz
    n_slab = load.shape[0] // cap
    wide = GROUP * load.shape[2]
    acc[...] = jnp.zeros_like(acc)
    listed = jnp.int32(0)
    for d in range(n_slab):
        first = d * cap
        held = jnp.max(load[first, 3:4, :]).astype(jnp.int32) // cells
        for k in range(cap):
            order[listed + k] = first + k
        listed = listed + held
    for k in range(GROUP):
        order[listed + k] = 0
    def numbers(length):
        shape = (length // 16, 16, wide)
        return (lax.broadcasted_iota(jnp.int32, shape, 0) * 16 + lax.broadcasted_iota(jnp.int32, shape, 1)).astype(
            jnp.float32
        ).astype(jnp.bfloat16)

    def spread(row):
        return jnp.broadcast_to(row, (16, wide)).astype(jnp.bfloat16)[None]

    row_numbers = numbers(rows)
    col_numbers = numbers(nz)
    place = lax.broadcasted_iota(jnp.int32, (1, wide), 1) // load.shape[2]
    zero = jnp.zeros((), jnp.bfloat16)
    one = jnp.ones((), jnp.bfloat16)

    def group(g, carry):
        tiles = [load[order[g * GROUP + k]] for k in range(GROUP)]
        block = jnp.concatenate(tiles, axis=1)
        live = place < listed - g * GROUP
        cell = block[3:4, :].astype(jnp.int32) % cells
        row = cell // nz
        half = row // rows
        at_row = row_numbers == spread(jnp.where(live, row % rows, -1).astype(jnp.float32))
        right = []
        for h in range(2):
            at_col = col_numbers == spread(jnp.where(half == h, cell % nz, -1).astype(jnp.float32))
            right.append(jnp.where(at_col, one, zero).reshape(nz, wide))
        left = []
        for piece in split(block):
            for c in range(3):
                left.append(jnp.where(at_row, spread(piece[c : c + 1, :]), zero).reshape(rows, wide))
        added = lax.dot_general(
            jnp.concatenate(left, axis=0),
            jnp.concatenate(right, axis=0),
            (((1,), (1,)), ((), ())),
            preferred_element_type=jnp.float32,
        )
        acc[...] += added[: 3 * rows] + added[3 * rows :]
        return carry

    lax.fori_loop(0, (listed + GROUP - 1) // GROUP, group, 0)
    for h in range(2):
        span = slice(h * (cx // 2), (h + 1) * (cx // 2))
        change = acc[:, h * nz : (h + 1) * nz].reshape(3, cx // 2, cy, nz)
        out[:, span] = inside[:, span] + change


def deposit(inside, load, cap):
    return pl.pallas_call(
        functools.partial(deposit_kernel, cap),
        out_shape=shaped(*inside.shape),
        in_specs=[VMEM] * 2,
        out_specs=VMEM,
        scratch_shapes=[
            pltpu.VMEM((3 * inside.shape[1] * inside.shape[2] // 2, 2 * inside.shape[3]), jnp.float32),
            pltpu.SMEM((load.shape[0] + max(cap, GROUP),), jnp.int32),
        ],
        compiler_params=PARAMS,
    )(inside, load)


def swapped(array, axis, first):
    up = [(i, i + 1) for i in range(first, lax.axis_size(axis) - 1, 2)]
    return lax.ppermute(array, axis, up + [(j, i) for i, j in up])


def per_device(vorticity, velocity, viscosity, tile_weights, tile_cells, tile_dest, tile_count):
    _, cx, cy, nz = vorticity.shape
    ncl = nz // CB
    n_slab = lax.axis_size("slab")
    n_pencil = lax.axis_size("pencil")
    cap = 2 * tile_weights.shape[0] // n_slab
    weights = jnp.transpose(tile_weights, (1, 0, 2))
    count = tile_count
    *faces, packets, tiles = to_send(
        vorticity, velocity, viscosity, weights, tile_cells, tile_dest.T, count, n_slab, cap
    )
    halos = [swapped(face, axis, k % 2) for k, (face, axis) in enumerate(zip(faces, SIDES))]
    arrived = lax.all_to_all(packets, "slab", 0, 0, tiled=True)
    inside, moments = inner(vorticity, velocity, viscosity, tiles)
    advanced, load = edges(inside, moments, faces, halos, n_slab * n_pencil)
    load = lax.all_to_all(load, ("slab", "pencil"), 0, 0, tiled=True)
    vorticity_out = deposit(advanced, arrived, cap)
    return (vorticity_out, far(load, cx, cy, ncl, n_pencil))


def solution(mesh):
    in_specs = (
        P(None, "slab", "pencil", None),
        P(None, "slab", "pencil", None),
        P("slab", "pencil", None),
        P(("slab", "pencil"), None, None),
        P(("slab", "pencil"), None),
        P(("slab", "pencil"), None),
        P(("slab", "pencil")),
    )
    out_specs = (P(None, "slab", "pencil", None), P(None, "slab", "pencil", None))
    return jax.shard_map(
        per_device, mesh=mesh, in_specs=in_specs, out_specs=out_specs, check_vma=False
    )
```

```python
import functools

import jax
import jax.numpy as jnp
from jax import lax
from jax.experimental import pallas as pl
from jax.experimental.pallas import tpu as pltpu
from jax.sharding import PartitionSpec as P

CB = 16
TIME_STEP = 0.1
LANES = 128
SIDES = ("slab", "slab", "pencil", "pencil")
GROUP = 8
VMEM_LIMIT = 24 * 1024 * 1024

VMEM = pl.BlockSpec(memory_space=pltpu.VMEM)
ANY = pl.BlockSpec(memory_space=pl.ANY)
SMEM = pl.BlockSpec(memory_space=pltpu.SMEM)
FIRST_PARAMS = pltpu.CompilerParams(vmem_limit_bytes=60 * 1024 * 1024)
PARAMS = pltpu.CompilerParams(vmem_limit_bytes=VMEM_LIMIT)


def shaped(*shape):
    return jax.ShapeDtypeStruct(shape, jnp.float32)


def split(w):
    high = w.astype(jnp.bfloat16).astype(jnp.float32)
    return high, w - high


def pack_tiles(cap, cells_dev, weights, cells, dest, count, packets):
    slots = packets.shape[0]
    tiles = cells.shape[0]
    names = dest[...]
    live = (lax.broadcasted_iota(jnp.int32, (1, tiles), 1) < count[0]).astype(jnp.float32)
    same = (lax.broadcasted_iota(jnp.int32, (slots // cap, tiles), 0) == names).astype(jnp.float32)
    shape = (tiles, tiles)
    earlier = lax.broadcasted_iota(jnp.int32, shape, 0) < lax.broadcasted_iota(jnp.int32, shape, 1)
    before = jnp.dot(same, earlier.astype(jnp.float32), preferred_element_type=jnp.float32)
    rank = jnp.sum(same * before, axis=0, keepdims=True).astype(jnp.int32)
    slot = lax.broadcasted_iota(jnp.int32, (slots, tiles), 0)
    placed = (slot == names * cap + rank).astype(jnp.float32) * live
    held = jnp.sum((slot == names * cap).astype(jnp.float32) * live, axis=1, keepdims=True)
    rows = [weights[0], weights[1], weights[2], cells[...].astype(jnp.float32)]
    found = jnp.dot(
        placed,
        jnp.concatenate(rows, axis=1),
        precision=lax.Precision.HIGHEST,
        preferred_element_type=jnp.float32,
    )
    length = cells.shape[1]
    for c in range(3):
        packets[:, c, :] = found[:, c * length : (c + 1) * length]
    packets[:, 3, :] = found[:, 3 * length :] + held * cells_dev


def tile_moments(cap, nz, packets, moments):
    n_slab = packets.shape[0] // cap
    ncl = nz // CB
    wide = cap * packets.shape[2]
    level = lax.broadcasted_iota(jnp.int32, (ncl, wide), 0)
    found = []
    for d in range(n_slab):
        block = jnp.concatenate([packets[d * cap + k] for k in range(cap)], axis=1)
        cell = block[3:4, :].astype(jnp.int32)
        spots = (level == cell % nz // CB).astype(jnp.float32).astype(jnp.bfloat16)
        high, low = split(block)
        left = jnp.concatenate([high, low], axis=0).astype(jnp.bfloat16)
        sums = lax.dot_general(left, spots, (((1,), (1,)), ((), ())), preferred_element_type=jnp.float32)
        found.append(sums[0:4] + sums[4:8])
    moments[...] = jnp.concatenate(found, axis=1)


class Copies:
    def __init__(self, sems):
        self.sems = sems
        self.made = []

    def start(self, source, target):
        self.made.append(pltpu.make_async_copy(source, target, self.sems.at[len(self.made)]))
        self.made[-1].start()

    def wait(self, first, last):
        for k in range(first, last):
            self.made[k].wait()


def send_kernel(
    cap,
    vort,
    velo,
    visc,
    weights_in,
    cells_in,
    dest_in,
    count_in,
    near_out,
    far_out,
    swap_out,
    other_out,
    packets_out,
    moments_out,
    near,
    far,
    swap,
    other,
    packets,
    moments,
    lows,
    highs,
    weights,
    cells,
    dest,
    count,
    sems,
):
    cx, cy, nz = visc.shape
    copies = Copies(sems)
    copies.start(weights_in, weights)
    copies.start(cells_in, cells)
    copies.start(dest_in, dest)
    copies.start(count_in, count)
    even = lax.axis_index("slab") % 2 == 0
    for face, at in ((near, jnp.where(even, cx - 1, 0)), (far, jnp.where(even, 0, cx - 1))):
        copies.start(vort.at[:, at], face.at[0:3])
        copies.start(velo.at[:, at], face.at[3:6])
        copies.start(visc.at[at], face.at[6])
    for rows, at in ((lows, 0), (highs, cy - 8)):
        copies.start(vort.at[:, :, pl.ds(at, 8), :], rows.at[0:3])
        copies.start(velo.at[:, :, pl.ds(at, 8), :], rows.at[3:6])
        copies.start(visc.at[:, pl.ds(at, 8), :], rows.at[6])

    copies.wait(0, 4)
    pack_tiles(cap, cx * cy * nz, weights, cells, dest, count, packets)
    copies.start(packets, packets_out)
    copies.wait(4, 10)
    copies.start(near, near_out)
    copies.start(far, far_out)
    copies.wait(10, 16)
    even = lax.axis_index("pencil") % 2 == 0
    for k in range(7):
        for x in range(cx):
            low = lows[k, x, 0:1, :]
            high = highs[k, x, 7:8, :]
            swap[k, x : x + 1, :] = jnp.where(even, high, low)
            other[k, x : x + 1, :] = jnp.where(even, low, high)
    copies.start(swap, swap_out)
    copies.start(other, other_out)
    tile_moments(cap, nz, packets, moments)
    copies.start(moments, moments_out)
    copies.wait(16, 22)


def to_send(vort, velo, visc, weights, cells, dest, count, n_slab, cap):
    _, cx, cy, nz = vort.shape
    made = (
        shaped(7, cy, nz),
        shaped(7, cy, nz),
        shaped(7, cx, nz),
        shaped(7, cx, nz),
        shaped(n_slab * cap, 4, weights.shape[2]),
        shaped(4, n_slab * nz // CB),
    )
    return pl.pallas_call(
        functools.partial(send_kernel, cap),
        out_shape=made,
        in_specs=[ANY] * 7,
        out_specs=(ANY,) * 6,
        scratch_shapes=[pltpu.VMEM(one.shape, jnp.float32) for one in made]
        + [
            pltpu.VMEM((7, cx, 8, nz), jnp.float32),
            pltpu.VMEM((7, cx, 8, nz), jnp.float32),
            pltpu.VMEM(weights.shape, jnp.float32),
            pltpu.VMEM(cells.shape, jnp.int32),
            pltpu.VMEM(dest.shape, jnp.int32),
            pltpu.SMEM(count.shape, jnp.int32),
            pltpu.SemaphoreType.DMA((22,)),
        ],
        compiler_params=FIRST_PARAMS,
    )(vort, velo, visc, weights, cells, dest, count)


def ahead(a, axis):
    return pltpu.roll(a, a.shape[axis] - 1, axis)


def behind(a, axis):
    return pltpu.roll(a, 1, axis)


def interior_step(vort, velo, visc, out):
    cx, cy, nz = visc.shape
    has_ahead = lax.broadcasted_iota(jnp.int32, (cy, nz), 0) < cy - 1
    totals = [jnp.zeros((8, nz), jnp.float32) for _ in range(3)]
    flux_x = [None] * 3
    for x in range(cx):
        nu = visc[x]
        spin = [vort[c, x] for c in range(3)]
        mean_y = jnp.where(has_ahead, 0.5 * (nu + ahead(nu, 0)), 0.0)
        mean_z = 0.5 * (nu + ahead(nu, 1))
        half_y = 0.5 * spin[1]
        half_z = 0.5 * spin[2]
        next_y = jnp.where(has_ahead, ahead(half_y, 0), 0.0)
        next_z = ahead(half_z, 1)
        half_y = jnp.where(has_ahead, half_y, 0.0)
        half_x = 0.5 * spin[0]
        if x < cx - 1:
            mean_x = 0.5 * (nu + visc[x + 1])
        for c in range(3):
            w = spin[c]
            u = velo[c, x]
            flux_y = mean_y * (ahead(w, 0) - w)
            flux_z = mean_z * (ahead(w, 1) - w)
            change = flux_y + half_y * ahead(u, 0) - behind(flux_y + next_y * u, 0)
            change = change + (flux_z + half_z * ahead(u, 1) - behind(flux_z + next_z * u, 1))
            if x == 0:
                change = change + half_x * velo[c, x + 1]
            elif x == cx - 1:
                change = change - half_x * velo[c, x - 1]
            else:
                change = change + half_x * (velo[c, x + 1] - velo[c, x - 1])
            if x > 0:
                change = change - flux_x[c]
            if x < cx - 1:
                flux_x[c] = mean_x * (vort[c, x + 1] - w)
                change = change + flux_x[c]
            new = w + TIME_STEP * change
            out[c, x] = new
            totals[c] = totals[c] + jnp.sum(new.reshape(cy // 8, 8, nz), axis=0)
    return [jnp.sum(total, axis=0, keepdims=True) for total in totals]


def by_level(totals, width):
    nz = totals[0].shape[1]
    shape = (nz, width)
    level = lax.broadcasted_iota(jnp.int32, shape, 0) // CB
    lane = lax.broadcasted_iota(jnp.int32, shape, 1)
    pick = (lane == lax.axis_index("slab") * (nz // CB) + level).astype(jnp.float32)
    rows = jnp.concatenate(totals + [jnp.zeros_like(totals[0])], axis=0)
    return jnp.dot(rows, pick, precision=lax.Precision.HIGHEST, preferred_element_type=jnp.float32)


def inner_kernel(vort, velo, visc, tiles_in, out, moments, tiles, sem):
    copy = pltpu.make_async_copy(tiles_in, tiles, sem)
    copy.start()
    own = by_level(interior_step(vort, velo, visc, out), moments.shape[1])
    copy.wait()
    moments[...] = tiles[...] + own


def inner(vort, velo, visc, tiles):
    return pl.pallas_call(
        inner_kernel,
        out_shape=(shaped(*vort.shape), shaped(*tiles.shape)),
        in_specs=[VMEM] * 3 + [ANY],
        out_specs=(VMEM,) * 2,
        scratch_shapes=[pltpu.VMEM(tiles.shape, jnp.float32), pltpu.SemaphoreType.DMA],
        compiler_params=PARAMS,
    )(vort, velo, visc, tiles)


def face_change(own, other, along, sign, c):
    stretch = (0.5 * sign) * own[along] * other[3 + c]
    diffuse = 0.5 * (own[6] + other[6]) * (other[c] - own[c])
    return TIME_STEP * (stretch + diffuse)


def edge_kernel(
    inside, moments, near, far, swap, other, near_in, far_in, swap_in, other_in, out, load_out, load, side_change, sem
):
    _, cx, cy, nz = out.shape
    even = lax.axis_index("pencil") % 2 == 0
    low, low_in = jnp.where(even, other[...], swap[...]), jnp.where(even, other_in[...], swap_in[...])
    high, high_in = jnp.where(even, swap[...], other[...]), jnp.where(even, swap_in[...], other_in[...])
    even = lax.axis_index("slab") % 2 == 0
    near_at, far_at = jnp.where(even, cx - 1, 0), jnp.where(even, 0, cx - 1)
    near_sign = jnp.where(even, 1.0, -1.0)
    totals = []
    for c in range(3):
        total = jnp.zeros((8, nz), jnp.float32)
        for own, came, at, sign in ((near, near_in, near_at, near_sign), (far, far_in, far_at, -near_sign)):
            change = face_change(own, came, 0, sign, c)
            out[c, at] = inside[c, at] + change
            total = total + jnp.sum(change.reshape(cy // 8, 8, nz), axis=0)
        for k, own, came, sign in ((0, low, low_in, -1.0), (1, high, high_in, 1.0)):
            change = face_change(own, came, 1, sign, c)
            side_change[k, c] = change
            total = total + change
        totals.append(jnp.sum(total, axis=0, keepdims=True))
    moment = moments[...] + by_level(totals, moments.shape[1])
    for k in range(load.shape[1] // 4):
        part = moment[:, k * LANES : (k + 1) * LANES]
        load[:, 4 * k : 4 * k + 4, :] = jnp.broadcast_to(part[None], (load.shape[0], 4, LANES))
    copy = pltpu.make_async_copy(load, load_out, sem)
    copy.start()
    for c in range(3):
        out[c, 1 : cx - 1] = inside[c, 1 : cx - 1]
        for k, at in ((0, 0), (1, cy - 1)):
            for x in range(cx):
                out[c, x, at : at + 1, :] = out[c, x, at : at + 1, :] + side_change[k, c, x : x + 1, :]
    copy.wait()


def edges(inside, moments, faces, halos, n_all):
    _, cx, _, nz = inside.shape
    load = shaped(n_all, 4 * moments.shape[1] // LANES, LANES)
    return pl.pallas_call(
        edge_kernel,
        out_shape=(shaped(*inside.shape), load),
        in_specs=[VMEM] * 10,
        out_specs=(VMEM, ANY),
        scratch_shapes=[
            pltpu.VMEM(load.shape, jnp.float32),
            pltpu.VMEM((2, 3, cx, nz), jnp.float32),
            pltpu.SemaphoreType.DMA,
        ],
        compiler_params=PARAMS,
    )(inside, moments, *faces, *halos)


def far_kernel(cx, cy, ncl, n_pencil, load, out):
    n_all = load.shape[0]
    n_slab = n_all // n_pencil
    slab = lax.axis_index("slab")
    pencil = lax.axis_index("pencil")
    shape = (ncl, n_slab * ncl)
    target = lax.broadcasted_iota(jnp.int32, shape, 0)
    source = lax.broadcasted_iota(jnp.int32, shape, 1)
    sigma = jnp.float32(cx * n_slab // 4)
    rel_x = ((slab - source // ncl) * cx).astype(jnp.float32)
    rel_z = ((target - source % ncl) * CB).astype(jnp.float32)
    flat = rel_x * rel_x + rel_z * rel_z + sigma * sigma
    turned = [jnp.zeros(shape, jnp.float32) for _ in range(3)]
    for p in range(n_pencil):
        total = load[p]
        for s in range(1, n_slab):
            total = total + load[s * n_pencil + p]
        moment = jnp.concatenate([total[4 * k : 4 * k + 4] for k in range(load.shape[1] // 4)], axis=1)
        first, second, third = moment[0:1], moment[1:2], moment[2:3]
        rel_y = ((pencil - p) * cy).astype(jnp.float32)
        inverse = lax.rsqrt(flat + rel_y * rel_y)
        weight = inverse * inverse * inverse
        turned[0] = turned[0] + weight * (rel_z * second - rel_y * third)
        turned[1] = turned[1] + weight * (rel_x * third - rel_z * first)
        turned[2] = turned[2] + weight * (rel_y * first - rel_x * second)
    ones = jnp.ones((8, shape[1]), jnp.float32)
    for c in range(3):
        row = lax.dot_general(
            ones,
            turned[c],
            (((1,), (1,)), ((), ())),
            precision=lax.Precision.HIGHEST,
            preferred_element_type=jnp.float32,
        )
        out[c, 0] = row[0:1]


def far(load, cx, cy, ncl, n_pencil):
    return pl.pallas_call(
        functools.partial(far_kernel, cx, cy, ncl, n_pencil),
        out_shape=shaped(3, 1, 1, ncl),
        in_specs=[VMEM],
        out_specs=VMEM,
        compiler_params=PARAMS,
    )(load)


def deposit_kernel(cap, inside, load, out, acc, order):
    _, cx, cy, nz = out.shape
    rows = cx * cy // 2
    cells = 2 * rows * nz
    n_slab = load.shape[0] // cap
    wide = GROUP * load.shape[2]
    acc[...] = jnp.zeros_like(acc)
    listed = jnp.int32(0)
    for d in range(n_slab):
        first = d * cap
        held = jnp.max(load[first, 3:4, :]).astype(jnp.int32) // cells
        for k in range(cap):
            order[listed + k] = first + k
        listed = listed + held
    for k in range(GROUP):
        order[listed + k] = 0
    def numbers(length):
        shape = (length // 16, 16, wide)
        return (lax.broadcasted_iota(jnp.int32, shape, 0) * 16 + lax.broadcasted_iota(jnp.int32, shape, 1)).astype(
            jnp.float32
        ).astype(jnp.bfloat16)

    def spread(row):
        return jnp.broadcast_to(row, (16, wide)).astype(jnp.bfloat16)[None]

    row_numbers = numbers(rows)
    col_numbers = numbers(nz)
    place = lax.broadcasted_iota(jnp.int32, (1, wide), 1) // load.shape[2]
    zero = jnp.zeros((), jnp.bfloat16)
    one = jnp.ones((), jnp.bfloat16)

    def group(g, carry):
        tiles = [load[order[g * GROUP + k]] for k in range(GROUP)]
        block = jnp.concatenate(tiles, axis=1)
        live = place < listed - g * GROUP
        cell = block[3:4, :].astype(jnp.int32) % cells
        row = cell // nz
        half = row // rows
        at_row = row_numbers == spread(jnp.where(live, row % rows, -1).astype(jnp.float32))
        right = []
        for h in range(2):
            at_col = col_numbers == spread(jnp.where(half == h, cell % nz, -1).astype(jnp.float32))
            right.append(jnp.where(at_col, one, zero).reshape(nz, wide))
        left = []
        for piece in split(block):
            for c in range(3):
                left.append(jnp.where(at_row, spread(piece[c : c + 1, :]), zero).reshape(rows, wide))
        added = lax.dot_general(
            jnp.concatenate(left, axis=0),
            jnp.concatenate(right, axis=0),
            (((1,), (1,)), ((), ())),
            preferred_element_type=jnp.float32,
        )
        acc[...] += added[: 3 * rows] + added[3 * rows :]
        return carry

    lax.fori_loop(0, (listed + GROUP - 1) // GROUP, group, 0)
    for h in range(2):
        span = slice(h * (cx // 2), (h + 1) * (cx // 2))
        change = acc[:, h * nz : (h + 1) * nz].reshape(3, cx // 2, cy, nz)
        out[:, span] = inside[:, span] + change


def deposit(inside, load, cap):
    return pl.pallas_call(
        functools.partial(deposit_kernel, cap),
        out_shape=shaped(*inside.shape),
        in_specs=[VMEM] * 2,
        out_specs=VMEM,
        scratch_shapes=[
            pltpu.VMEM((3 * inside.shape[1] * inside.shape[2] // 2, 2 * inside.shape[3]), jnp.float32),
            pltpu.SMEM((load.shape[0] + max(cap, GROUP),), jnp.int32),
        ],
        compiler_params=PARAMS,
    )(inside, load)


def swapped(array, axis, first):
    up = [(i, i + 1) for i in range(first, lax.axis_size(axis) - 1, 2)]
    return lax.ppermute(array, axis, up + [(j, i) for i, j in up])


def per_device(vorticity, velocity, viscosity, tile_weights, tile_cells, tile_dest, tile_count):
    _, cx, cy, nz = vorticity.shape
    ncl = nz // CB
    n_slab = lax.axis_size("slab")
    n_pencil = lax.axis_size("pencil")
    cap = 2 * tile_weights.shape[0] // n_slab
    weights = jnp.transpose(tile_weights, (1, 0, 2))
    count = tile_count
    *faces, packets, tiles = to_send(
        vorticity, velocity, viscosity, weights, tile_cells, tile_dest.T, count, n_slab, cap
    )
    halos = [swapped(face, axis, k % 2) for k, (face, axis) in enumerate(zip(faces, SIDES))]
    arrived = lax.all_to_all(packets, "slab", 0, 0, tiled=True)
    inside, moments = inner(vorticity, velocity, viscosity, tiles)
    advanced, load = edges(inside, moments, faces, halos, n_slab * n_pencil)
    load = lax.all_to_all(load, ("slab", "pencil"), 0, 0, tiled=True)
    vorticity_out = deposit(advanced, arrived, cap)
    return (vorticity_out, far(load, cx, cy, ncl, n_pencil))


def solution(mesh):
    in_specs = (
        P(None, "slab", "pencil", None),
        P(None, "slab", "pencil", None),
        P("slab", "pencil", None),
        P(("slab", "pencil"), None, None),
        P(("slab", "pencil"), None),
        P(("slab", "pencil"), None),
        P(("slab", "pencil")),
    )
    out_specs = (P(None, "slab", "pencil", None), P(None, "slab", "pencil", None))
    return jax.shard_map(
        per_device, mesh=mesh, in_specs=in_specs, out_specs=out_specs, check_vma=False
    )
```

```python
import functools

import jax
import jax.numpy as jnp
from jax import lax
from jax.experimental import pallas as pl
from jax.experimental.pallas import tpu as pltpu
from jax.sharding import PartitionSpec as P

CB = 16
TIME_STEP = 0.1
LANES = 128
SIDES = ("slab", "slab", "pencil", "pencil")
GROUP = 8
VMEM_LIMIT = 24 * 1024 * 1024

VMEM = pl.BlockSpec(memory_space=pltpu.VMEM)
ANY = pl.BlockSpec(memory_space=pl.ANY)
SMEM = pl.BlockSpec(memory_space=pltpu.SMEM)
FIRST_PARAMS = pltpu.CompilerParams(vmem_limit_bytes=60 * 1024 * 1024)
PARAMS = pltpu.CompilerParams(vmem_limit_bytes=VMEM_LIMIT)


def shaped(*shape):
    return jax.ShapeDtypeStruct(shape, jnp.float32)


def split(w):
    high = w.astype(jnp.bfloat16).astype(jnp.float32)
    return high, w - high


def pack_tiles(cap, cells_dev, weights, cells, dest, count, packets):
    slots = packets.shape[0]
    tiles = cells.shape[0]
    names = dest[...]
    live = (lax.broadcasted_iota(jnp.int32, (1, tiles), 1) < count[0]).astype(jnp.float32)
    same = (lax.broadcasted_iota(jnp.int32, (slots // cap, tiles), 0) == names).astype(jnp.float32)
    shape = (tiles, tiles)
    earlier = lax.broadcasted_iota(jnp.int32, shape, 0) < lax.broadcasted_iota(jnp.int32, shape, 1)
    before = jnp.dot(same, earlier.astype(jnp.float32), preferred_element_type=jnp.float32)
    rank = jnp.sum(same * before, axis=0, keepdims=True).astype(jnp.int32)
    slot = lax.broadcasted_iota(jnp.int32, (slots, tiles), 0)
    placed = (slot == names * cap + rank).astype(jnp.float32) * live
    held = jnp.sum((slot == names * cap).astype(jnp.float32) * live, axis=1, keepdims=True)
    rows = [weights[0], weights[1], weights[2], cells[...].astype(jnp.float32)]
    found = jnp.dot(
        placed,
        jnp.concatenate(rows, axis=1),
        precision=lax.Precision.HIGHEST,
        preferred_element_type=jnp.float32,
    )
    length = cells.shape[1]
    for c in range(3):
        packets[:, c, :] = found[:, c * length : (c + 1) * length]
    packets[:, 3, :] = found[:, 3 * length :] + held * cells_dev


def tile_moments(cap, nz, packets, moments):
    n_slab = packets.shape[0] // cap
    ncl = nz // CB
    wide = cap * packets.shape[2]
    level = lax.broadcasted_iota(jnp.int32, (ncl, wide), 0)
    found = []
    for d in range(n_slab):
        block = jnp.concatenate([packets[d * cap + k] for k in range(cap)], axis=1)
        cell = block[3:4, :].astype(jnp.int32)
        spots = (level == cell % nz // CB).astype(jnp.float32).astype(jnp.bfloat16)
        high, low = split(block)
        left = jnp.concatenate([high, low], axis=0).astype(jnp.bfloat16)
        sums = lax.dot_general(left, spots, (((1,), (1,)), ((), ())), preferred_element_type=jnp.float32)
        found.append(sums[0:4] + sums[4:8])
    moments[...] = jnp.concatenate(found, axis=1)


class Copies:
    def __init__(self, sems):
        self.sems = sems
        self.made = []

    def start(self, source, target):
        self.made.append(pltpu.make_async_copy(source, target, self.sems.at[len(self.made)]))
        self.made[-1].start()

    def wait(self, first, last):
        for k in range(first, last):
            self.made[k].wait()


def send_kernel(
    cap,
    vort,
    velo,
    visc,
    weights_in,
    cells_in,
    dest_in,
    count_in,
    near_out,
    far_out,
    swap_out,
    other_out,
    packets_out,
    moments_out,
    near,
    far,
    swap,
    other,
    packets,
    moments,
    weights,
    cells,
    dest,
    count,
    sems,
):
    cx, cy, nz = visc.shape
    copies = Copies(sems)
    copies.start(weights_in, weights)
    copies.start(cells_in, cells)
    copies.start(dest_in, dest)
    copies.start(count_in, count)
    even = lax.axis_index("slab") % 2 == 0
    for face, at in ((near, jnp.where(even, cx - 1, 0)), (far, jnp.where(even, 0, cx - 1))):
        copies.start(vort.at[:, at], face.at[0:3])
        copies.start(velo.at[:, at], face.at[3:6])
        copies.start(visc.at[at], face.at[6])
    even = lax.axis_index("pencil") % 2 == 0
    for face, at in ((swap, jnp.where(even, cy - 1, 0)), (other, jnp.where(even, 0, cy - 1))):
        copies.start(vort.at[:, :, at], face.at[0:3])
        copies.start(velo.at[:, :, at], face.at[3:6])
        copies.start(visc.at[:, at], face.at[6])
    copies.wait(0, 4)
    pack_tiles(cap, cx * cy * nz, weights, cells, dest, count, packets)
    copies.start(packets, packets_out)
    copies.wait(4, 10)
    copies.start(near, near_out)
    copies.start(far, far_out)
    copies.wait(10, 16)
    copies.start(swap, swap_out)
    copies.start(other, other_out)
    tile_moments(cap, nz, packets, moments)
    copies.start(moments, moments_out)
    copies.wait(16, 22)


def to_send(vort, velo, visc, weights, cells, dest, count, n_slab, cap):
    _, cx, cy, nz = vort.shape
    made = (
        shaped(7, cy, nz),
        shaped(7, cy, nz),
        shaped(7, cx, nz),
        shaped(7, cx, nz),
        shaped(n_slab * cap, 4, weights.shape[2]),
        shaped(4, n_slab * nz // CB),
    )
    return pl.pallas_call(
        functools.partial(send_kernel, cap),
        out_shape=made,
        in_specs=[ANY] * 7,
        out_specs=(ANY,) * 6,
        scratch_shapes=[pltpu.VMEM(one.shape, jnp.float32) for one in made]
        + [
            pltpu.VMEM(weights.shape, jnp.float32),
            pltpu.VMEM(cells.shape, jnp.int32),
            pltpu.VMEM(dest.shape, jnp.int32),
            pltpu.SMEM(count.shape, jnp.int32),
            pltpu.SemaphoreType.DMA((22,)),
        ],
        compiler_params=FIRST_PARAMS,
    )(vort, velo, visc, weights, cells, dest, count)


def ahead(a, axis):
    return pltpu.roll(a, a.shape[axis] - 1, axis)


def behind(a, axis):
    return pltpu.roll(a, 1, axis)


def interior_step(vort, velo, visc, out):
    cx, cy, nz = visc.shape
    has_ahead = lax.broadcasted_iota(jnp.int32, (cy, nz), 0) < cy - 1
    totals = [jnp.zeros((8, nz), jnp.float32) for _ in range(3)]
    flux_x = [None] * 3
    for x in range(cx):
        nu = visc[x]
        spin = [vort[c, x] for c in range(3)]
        mean_y = jnp.where(has_ahead, 0.5 * (nu + ahead(nu, 0)), 0.0)
        mean_z = 0.5 * (nu + ahead(nu, 1))
        half_y = 0.5 * spin[1]
        half_z = 0.5 * spin[2]
        next_y = jnp.where(has_ahead, ahead(half_y, 0), 0.0)
        next_z = ahead(half_z, 1)
        half_y = jnp.where(has_ahead, half_y, 0.0)
        half_x = 0.5 * spin[0]
        if x < cx - 1:
            mean_x = 0.5 * (nu + visc[x + 1])
        for c in range(3):
            w = spin[c]
            u = velo[c, x]
            flux_y = mean_y * (ahead(w, 0) - w)
            flux_z = mean_z * (ahead(w, 1) - w)
            change = flux_y + half_y * ahead(u, 0) - behind(flux_y + next_y * u, 0)
            change = change + (flux_z + half_z * ahead(u, 1) - behind(flux_z + next_z * u, 1))
            if x == 0:
                change = change + half_x * velo[c, x + 1]
            elif x == cx - 1:
                change = change - half_x * velo[c, x - 1]
            else:
                change = change + half_x * (velo[c, x + 1] - velo[c, x - 1])
            if x > 0:
                change = change - flux_x[c]
            if x < cx - 1:
                flux_x[c] = mean_x * (vort[c, x + 1] - w)
                change = change + flux_x[c]
            new = w + TIME_STEP * change
            out[c, x] = new
            totals[c] = totals[c] + jnp.sum(new.reshape(cy // 8, 8, nz), axis=0)
    return [jnp.sum(total, axis=0, keepdims=True) for total in totals]


def by_level(totals, width):
    nz = totals[0].shape[1]
    shape = (nz, width)
    level = lax.broadcasted_iota(jnp.int32, shape, 0) // CB
    lane = lax.broadcasted_iota(jnp.int32, shape, 1)
    pick = (lane == lax.axis_index("slab") * (nz // CB) + level).astype(jnp.float32)
    rows = jnp.concatenate(totals + [jnp.zeros_like(totals[0])], axis=0)
    return jnp.dot(rows, pick, precision=lax.Precision.HIGHEST, preferred_element_type=jnp.float32)


def inner_kernel(vort, velo, visc, tiles_in, out, moments, tiles, sem):
    copy = pltpu.make_async_copy(tiles_in, tiles, sem)
    copy.start()
    own = by_level(interior_step(vort, velo, visc, out), moments.shape[1])
    copy.wait()
    moments[...] = tiles[...] + own


def inner(vort, velo, visc, tiles):
    return pl.pallas_call(
        inner_kernel,
        out_shape=(shaped(*vort.shape), shaped(*tiles.shape)),
        in_specs=[VMEM] * 3 + [ANY],
        out_specs=(VMEM,) * 2,
        scratch_shapes=[pltpu.VMEM(tiles.shape, jnp.float32), pltpu.SemaphoreType.DMA],
        compiler_params=PARAMS,
    )(vort, velo, visc, tiles)


def face_change(own, other, along, sign, c):
    stretch = (0.5 * sign) * own[along] * other[3 + c]
    diffuse = 0.5 * (own[6] + other[6]) * (other[c] - own[c])
    return TIME_STEP * (stretch + diffuse)


def edge_kernel(
    inside, moments, near, far, swap, other, near_in, far_in, swap_in, other_in, out, load_out, load, side_change, sem
):
    _, cx, cy, nz = out.shape
    even = lax.axis_index("pencil") % 2 == 0
    low, low_in = jnp.where(even, other[...], swap[...]), jnp.where(even, other_in[...], swap_in[...])
    high, high_in = jnp.where(even, swap[...], other[...]), jnp.where(even, swap_in[...], other_in[...])
    even = lax.axis_index("slab") % 2 == 0
    near_at, far_at = jnp.where(even, cx - 1, 0), jnp.where(even, 0, cx - 1)
    near_sign = jnp.where(even, 1.0, -1.0)
    totals = []
    for c in range(3):
        total = jnp.zeros((8, nz), jnp.float32)
        for own, came, at, sign in ((near, near_in, near_at, near_sign), (far, far_in, far_at, -near_sign)):
            change = face_change(own, came, 0, sign, c)
            out[c, at] = inside[c, at] + change
            total = total + jnp.sum(change.reshape(cy // 8, 8, nz), axis=0)
        for k, own, came, sign in ((0, low, low_in, -1.0), (1, high, high_in, 1.0)):
            change = face_change(own, came, 1, sign, c)
            side_change[k, c] = change
            total = total + change
        totals.append(jnp.sum(total, axis=0, keepdims=True))
    moment = moments[...] + by_level(totals, moments.shape[1])
    for k in range(load.shape[1] // 4):
        part = moment[:, k * LANES : (k + 1) * LANES]
        load[:, 4 * k : 4 * k + 4, :] = jnp.broadcast_to(part[None], (load.shape[0], 4, LANES))
    copy = pltpu.make_async_copy(load, load_out, sem)
    copy.start()
    for c in range(3):
        out[c, 1 : cx - 1] = inside[c, 1 : cx - 1]
        for k, at in ((0, 0), (1, cy - 1)):
            for x in range(cx):
                out[c, x, at : at + 1, :] = out[c, x, at : at + 1, :] + side_change[k, c, x : x + 1, :]
    copy.wait()


def edges(inside, moments, faces, halos, n_all):
    _, cx, _, nz = inside.shape
    load = shaped(n_all, 4 * moments.shape[1] // LANES, LANES)
    return pl.pallas_call(
        edge_kernel,
        out_shape=(shaped(*inside.shape), load),
        in_specs=[VMEM] * 10,
        out_specs=(VMEM, ANY),
        scratch_shapes=[
            pltpu.VMEM(load.shape, jnp.float32),
            pltpu.VMEM((2, 3, cx, nz), jnp.float32),
            pltpu.SemaphoreType.DMA,
        ],
        compiler_params=PARAMS,
    )(inside, moments, *faces, *halos)


def far_kernel(cx, cy, ncl, n_pencil, load, out):
    n_all = load.shape[0]
    n_slab = n_all // n_pencil
    slab = lax.axis_index("slab")
    pencil = lax.axis_index("pencil")
    shape = (ncl, n_slab * ncl)
    target = lax.broadcasted_iota(jnp.int32, shape, 0)
    source = lax.broadcasted_iota(jnp.int32, shape, 1)
    sigma = jnp.float32(cx * n_slab // 4)
    rel_x = ((slab - source // ncl) * cx).astype(jnp.float32)
    rel_z = ((target - source % ncl) * CB).astype(jnp.float32)
    flat = rel_x * rel_x + rel_z * rel_z + sigma * sigma
    turned = [jnp.zeros(shape, jnp.float32) for _ in range(3)]
    for p in range(n_pencil):
        total = load[p]
        for s in range(1, n_slab):
            total = total + load[s * n_pencil + p]
        moment = jnp.concatenate([total[4 * k : 4 * k + 4] for k in range(load.shape[1] // 4)], axis=1)
        first, second, third = moment[0:1], moment[1:2], moment[2:3]
        rel_y = ((pencil - p) * cy).astype(jnp.float32)
        inverse = lax.rsqrt(flat + rel_y * rel_y)
        weight = inverse * inverse * inverse
        turned[0] = turned[0] + weight * (rel_z * second - rel_y * third)
        turned[1] = turned[1] + weight * (rel_x * third - rel_z * first)
        turned[2] = turned[2] + weight * (rel_y * first - rel_x * second)
    ones = jnp.ones((8, shape[1]), jnp.float32)
    for c in range(3):
        row = lax.dot_general(
            ones,
            turned[c],
            (((1,), (1,)), ((), ())),
            precision=lax.Precision.HIGHEST,
            preferred_element_type=jnp.float32,
        )
        out[c, 0] = row[0:1]


def far(load, cx, cy, ncl, n_pencil):
    return pl.pallas_call(
        functools.partial(far_kernel, cx, cy, ncl, n_pencil),
        out_shape=shaped(3, 1, 1, ncl),
        in_specs=[VMEM],
        out_specs=VMEM,
        compiler_params=PARAMS,
    )(load)


def deposit_kernel(cap, inside, load, out, acc, order):
    _, cx, cy, nz = out.shape
    rows = cx * cy // 2
    cells = 2 * rows * nz
    n_slab = load.shape[0] // cap
    wide = GROUP * load.shape[2]
    acc[...] = jnp.zeros_like(acc)
    listed = jnp.int32(0)
    for d in range(n_slab):
        first = d * cap
        held = jnp.max(load[first, 3:4, :]).astype(jnp.int32) // cells
        for k in range(cap):
            order[listed + k] = first + k
        listed = listed + held
    for k in range(GROUP):
        order[listed + k] = 0
    def numbers(length):
        shape = (length // 16, 16, wide)
        return (lax.broadcasted_iota(jnp.int32, shape, 0) * 16 + lax.broadcasted_iota(jnp.int32, shape, 1)).astype(
            jnp.float32
        ).astype(jnp.bfloat16)

    def spread(row):
        return jnp.broadcast_to(row, (16, wide)).astype(jnp.bfloat16)[None]

    row_numbers = numbers(rows)
    col_numbers = numbers(nz)
    place = lax.broadcasted_iota(jnp.int32, (1, wide), 1) // load.shape[2]
    zero = jnp.zeros((), jnp.bfloat16)
    one = jnp.ones((), jnp.bfloat16)

    def group(g, carry):
        tiles = [load[order[g * GROUP + k]] for k in range(GROUP)]
        block = jnp.concatenate(tiles, axis=1)
        live = place < listed - g * GROUP
        cell = block[3:4, :].astype(jnp.int32) % cells
        row = cell // nz
        half = row // rows
        at_row = row_numbers == spread(jnp.where(live, row % rows, -1).astype(jnp.float32))
        right = []
        for h in range(2):
            at_col = col_numbers == spread(jnp.where(half == h, cell % nz, -1).astype(jnp.float32))
            right.append(jnp.where(at_col, one, zero).reshape(nz, wide))
        left = []
        for piece in split(block):
            for c in range(3):
                left.append(jnp.where(at_row, spread(piece[c : c + 1, :]), zero).reshape(rows, wide))
        added = lax.dot_general(
            jnp.concatenate(left, axis=0),
            jnp.concatenate(right, axis=0),
            (((1,), (1,)), ((), ())),
            preferred_element_type=jnp.float32,
        )
        acc[...] += added[: 3 * rows] + added[3 * rows :]
        return carry

    lax.fori_loop(0, (listed + GROUP - 1) // GROUP, group, 0)
    for h in range(2):
        span = slice(h * (cx // 2), (h + 1) * (cx // 2))
        change = acc[:, h * nz : (h + 1) * nz].reshape(3, cx // 2, cy, nz)
        out[:, span] = inside[:, span] + change


def deposit(inside, load, cap):
    return pl.pallas_call(
        functools.partial(deposit_kernel, cap),
        out_shape=shaped(*inside.shape),
        in_specs=[VMEM] * 2,
        out_specs=VMEM,
        scratch_shapes=[
            pltpu.VMEM((3 * inside.shape[1] * inside.shape[2] // 2, 2 * inside.shape[3]), jnp.float32),
            pltpu.SMEM((load.shape[0] + max(cap, GROUP),), jnp.int32),
        ],
        compiler_params=PARAMS,
    )(inside, load)


def swapped(array, axis, first):
    up = [(i, i + 1) for i in range(first, lax.axis_size(axis) - 1, 2)]
    return lax.ppermute(array, axis, up + [(j, i) for i, j in up])


def per_device(vorticity, velocity, viscosity, tile_weights, tile_cells, tile_dest, tile_count):
    _, cx, cy, nz = vorticity.shape
    ncl = nz // CB
    n_slab = lax.axis_size("slab")
    n_pencil = lax.axis_size("pencil")
    cap = 2 * tile_weights.shape[0] // n_slab
    weights = jnp.transpose(tile_weights, (1, 0, 2))
    count = tile_count
    *faces, packets, tiles = to_send(
        vorticity, velocity, viscosity, weights, tile_cells, tile_dest.T, count, n_slab, cap
    )
    halos = [swapped(face, axis, k % 2) for k, (face, axis) in enumerate(zip(faces, SIDES))]
    arrived = lax.all_to_all(packets, "slab", 0, 0, tiled=True)
    inside, moments = inner(vorticity, velocity, viscosity, tiles)
    advanced, load = edges(inside, moments, faces, halos, n_slab * n_pencil)
    load = lax.all_to_all(load, ("slab", "pencil"), 0, 0, tiled=True)
    vorticity_out = deposit(advanced, arrived, cap)
    return (vorticity_out, far(load, cx, cy, ncl, n_pencil))


def solution(mesh):
    in_specs = (
        P(None, "slab", "pencil", None),
        P(None, "slab", "pencil", None),
        P("slab", "pencil", None),
        P(("slab", "pencil"), None, None),
        P(("slab", "pencil"), None),
        P(("slab", "pencil"), None),
        P(("slab", "pencil")),
    )
    out_specs = (P(None, "slab", "pencil", None), P(None, "slab", "pencil", None))
    return jax.shard_map(
        per_device, mesh=mesh, in_specs=in_specs, out_specs=out_specs, check_vma=False
    )
```

```python
import functools

import jax
import jax.numpy as jnp
from jax import lax
from jax.experimental import pallas as pl
from jax.experimental.pallas import tpu as pltpu
from jax.sharding import PartitionSpec as P

CB = 16
TIME_STEP = 0.1
LANES = 128
SIDES = ("slab", "slab", "pencil", "pencil")
GROUP = 16
VMEM_LIMIT = 24 * 1024 * 1024

VMEM = pl.BlockSpec(memory_space=pltpu.VMEM)
ANY = pl.BlockSpec(memory_space=pl.ANY)
SMEM = pl.BlockSpec(memory_space=pltpu.SMEM)
FIRST_PARAMS = pltpu.CompilerParams(vmem_limit_bytes=60 * 1024 * 1024)
PARAMS = pltpu.CompilerParams(vmem_limit_bytes=VMEM_LIMIT)


def shaped(*shape):
    return jax.ShapeDtypeStruct(shape, jnp.float32)


def split(w):
    high = w.astype(jnp.bfloat16).astype(jnp.float32)
    return high, w - high


def pack_tiles(cap, cells_dev, weights, cells, dest, count, packets):
    slots = packets.shape[0]
    tiles = cells.shape[0]
    names = dest[...]
    live = (lax.broadcasted_iota(jnp.int32, (1, tiles), 1) < count[0]).astype(jnp.float32)
    same = (lax.broadcasted_iota(jnp.int32, (slots // cap, tiles), 0) == names).astype(jnp.float32)
    shape = (tiles, tiles)
    earlier = lax.broadcasted_iota(jnp.int32, shape, 0) < lax.broadcasted_iota(jnp.int32, shape, 1)
    before = jnp.dot(same, earlier.astype(jnp.float32), preferred_element_type=jnp.float32)
    rank = jnp.sum(same * before, axis=0, keepdims=True).astype(jnp.int32)
    slot = lax.broadcasted_iota(jnp.int32, (slots, tiles), 0)
    placed = (slot == names * cap + rank).astype(jnp.float32) * live
    held = jnp.sum((slot == names * cap).astype(jnp.float32) * live, axis=1, keepdims=True)
    rows = [weights[0], weights[1], weights[2], cells[...].astype(jnp.float32)]
    found = jnp.dot(
        placed,
        jnp.concatenate(rows, axis=1),
        precision=lax.Precision.HIGHEST,
        preferred_element_type=jnp.float32,
    )
    length = cells.shape[1]
    for c in range(3):
        packets[:, c, :] = found[:, c * length : (c + 1) * length]
    packets[:, 3, :] = found[:, 3 * length :] + held * cells_dev


def tile_moments(cap, nz, packets, moments):
    n_slab = packets.shape[0] // cap
    ncl = nz // CB
    wide = cap * packets.shape[2]
    level = lax.broadcasted_iota(jnp.int32, (ncl, wide), 0)
    found = []
    for d in range(n_slab):
        block = jnp.concatenate([packets[d * cap + k] for k in range(cap)], axis=1)
        cell = block[3:4, :].astype(jnp.int32)
        spots = (level == cell % nz // CB).astype(jnp.float32).astype(jnp.bfloat16)
        high, low = split(block)
        left = jnp.concatenate([high, low], axis=0).astype(jnp.bfloat16)
        sums = lax.dot_general(left, spots, (((1,), (1,)), ((), ())), preferred_element_type=jnp.float32)
        found.append(sums[0:4] + sums[4:8])
    moments[...] = jnp.concatenate(found, axis=1)


class Copies:
    def __init__(self, sems):
        self.sems = sems
        self.made = []

    def start(self, source, target):
        self.made.append(pltpu.make_async_copy(source, target, self.sems.at[len(self.made)]))
        self.made[-1].start()

    def wait(self, first, last):
        for k in range(first, last):
            self.made[k].wait()


def send_kernel(
    cap,
    vort,
    velo,
    visc,
    weights_in,
    cells_in,
    dest_in,
    count_in,
    far_out,
    near_out,
    other_out,
    swap_out,
    packets_out,
    moments_out,
    far,
    near,
    other,
    swap,
    packets,
    moments,
    weights,
    cells,
    dest,
    count,
    sems,
):
    cx, cy, nz = visc.shape
    copies = Copies(sems)
    even = lax.axis_index("slab") % 2 == 0
    for face, at in ((far, jnp.where(even, 0, cx - 1)), (near, jnp.where(even, cx - 1, 0))):
        copies.start(vort.at[:, at], face.at[0:3])
        copies.start(velo.at[:, at], face.at[3:6])
        copies.start(visc.at[at], face.at[6])
    copies.start(weights_in, weights)
    copies.start(cells_in, cells)
    copies.start(dest_in, dest)
    copies.start(count_in, count)
    even = lax.axis_index("pencil") % 2 == 0
    for face, at in ((other, jnp.where(even, 0, cy - 1)), (swap, jnp.where(even, cy - 1, 0))):
        copies.start(vort.at[:, :, at], face.at[0:3])
        copies.start(velo.at[:, :, at], face.at[3:6])
        copies.start(visc.at[:, at], face.at[6])
    copies.wait(0, 3)
    copies.start(far, far_out)
    copies.wait(3, 6)
    copies.start(near, near_out)
    copies.wait(6, 10)
    pack_tiles(cap, cx * cy * nz, weights, cells, dest, count, packets)
    copies.start(packets, packets_out)
    copies.wait(10, 16)
    copies.start(other, other_out)
    copies.start(swap, swap_out)
    tile_moments(cap, nz, packets, moments)
    copies.start(moments, moments_out)
    copies.wait(16, 22)


def to_send(vort, velo, visc, weights, cells, dest, count, n_slab, cap):
    _, cx, cy, nz = vort.shape
    made = (
        shaped(7, cy, nz),
        shaped(7, cy, nz),
        shaped(7, cx, nz),
        shaped(7, cx, nz),
        shaped(n_slab * cap, 4, weights.shape[2]),
        shaped(4, n_slab * nz // CB),
    )
    return pl.pallas_call(
        functools.partial(send_kernel, cap),
        out_shape=made,
        in_specs=[ANY] * 7,
        out_specs=(ANY,) * 6,
        scratch_shapes=[pltpu.VMEM(one.shape, jnp.float32) for one in made]
        + [
            pltpu.VMEM(weights.shape, jnp.float32),
            pltpu.VMEM(cells.shape, jnp.int32),
            pltpu.VMEM(dest.shape, jnp.int32),
            pltpu.SMEM(count.shape, jnp.int32),
            pltpu.SemaphoreType.DMA((22,)),
        ],
        compiler_params=FIRST_PARAMS,
    )(vort, velo, visc, weights, cells, dest, count)


def ahead(a, axis):
    return pltpu.roll(a, a.shape[axis] - 1, axis)


def behind(a, axis):
    return pltpu.roll(a, 1, axis)


def interior_step(vort, velo, visc, out):
    cx, cy, nz = visc.shape
    has_ahead = lax.broadcasted_iota(jnp.int32, (cy, nz), 0) < cy - 1
    totals = [jnp.zeros((8, nz), jnp.float32) for _ in range(3)]
    flux_x = [None] * 3
    for x in range(cx):
        nu = visc[x]
        spin = [vort[c, x] for c in range(3)]
        mean_y = jnp.where(has_ahead, 0.5 * (nu + ahead(nu, 0)), 0.0)
        mean_z = 0.5 * (nu + ahead(nu, 1))
        half_y = 0.5 * spin[1]
        half_z = 0.5 * spin[2]
        next_y = jnp.where(has_ahead, ahead(half_y, 0), 0.0)
        next_z = ahead(half_z, 1)
        half_y = jnp.where(has_ahead, half_y, 0.0)
        half_x = 0.5 * spin[0]
        if x < cx - 1:
            mean_x = 0.5 * (nu + visc[x + 1])
        for c in range(3):
            w = spin[c]
            u = velo[c, x]
            flux_y = mean_y * (ahead(w, 0) - w)
            flux_z = mean_z * (ahead(w, 1) - w)
            change = flux_y + half_y * ahead(u, 0) - behind(flux_y + next_y * u, 0)
            change = change + (flux_z + half_z * ahead(u, 1) - behind(flux_z + next_z * u, 1))
            if x == 0:
                change = change + half_x * velo[c, x + 1]
            elif x == cx - 1:
                change = change - half_x * velo[c, x - 1]
            else:
                change = change + half_x * (velo[c, x + 1] - velo[c, x - 1])
            if x > 0:
                change = change - flux_x[c]
            if x < cx - 1:
                flux_x[c] = mean_x * (vort[c, x + 1] - w)
                change = change + flux_x[c]
            new = w + TIME_STEP * change
            out[c, x] = new
            totals[c] = totals[c] + jnp.sum(new.reshape(cy // 8, 8, nz), axis=0)
    return [jnp.sum(total, axis=0, keepdims=True) for total in totals]


def by_level(totals, width):
    nz = totals[0].shape[1]
    shape = (nz, width)
    level = lax.broadcasted_iota(jnp.int32, shape, 0) // CB
    lane = lax.broadcasted_iota(jnp.int32, shape, 1)
    pick = (lane == lax.axis_index("slab") * (nz // CB) + level).astype(jnp.float32)
    rows = jnp.concatenate(totals + [jnp.zeros_like(totals[0])], axis=0)
    return jnp.dot(rows, pick, precision=lax.Precision.HIGHEST, preferred_element_type=jnp.float32)


def inner_kernel(vort, velo, visc, tiles_in, out, moments, tiles, sem):
    copy = pltpu.make_async_copy(tiles_in, tiles, sem)
    copy.start()
    own = by_level(interior_step(vort, velo, visc, out), moments.shape[1])
    copy.wait()
    moments[...] = tiles[...] + own


def inner(vort, velo, visc, tiles):
    return pl.pallas_call(
        inner_kernel,
        out_shape=(shaped(*vort.shape), shaped(*tiles.shape)),
        in_specs=[VMEM] * 3 + [ANY],
        out_specs=(VMEM,) * 2,
        scratch_shapes=[pltpu.VMEM(tiles.shape, jnp.float32), pltpu.SemaphoreType.DMA],
        compiler_params=PARAMS,
    )(vort, velo, visc, tiles)


def face_change(own, other, along, sign, c):
    stretch = (0.5 * sign) * own[along] * other[3 + c]
    diffuse = 0.5 * (own[6] + other[6]) * (other[c] - own[c])
    return TIME_STEP * (stretch + diffuse)


def edge_kernel(
    inside, moments, far, near, other, swap, far_in, near_in, other_in, swap_in, out, load_out, load, side_change, sem
):
    _, cx, cy, nz = out.shape
    even = lax.axis_index("pencil") % 2 == 0
    low, low_in = jnp.where(even, other[...], swap[...]), jnp.where(even, other_in[...], swap_in[...])
    high, high_in = jnp.where(even, swap[...], other[...]), jnp.where(even, swap_in[...], other_in[...])
    even = lax.axis_index("slab") % 2 == 0
    near_at, far_at = jnp.where(even, cx - 1, 0), jnp.where(even, 0, cx - 1)
    near_sign = jnp.where(even, 1.0, -1.0)
    totals = []
    for c in range(3):
        total = jnp.zeros((8, nz), jnp.float32)
        for own, came, at, sign in ((near, near_in, near_at, near_sign), (far, far_in, far_at, -near_sign)):
            change = face_change(own, came, 0, sign, c)
            out[c, at] = inside[c, at] + change
            total = total + jnp.sum(change.reshape(cy // 8, 8, nz), axis=0)
        for k, own, came, sign in ((0, low, low_in, -1.0), (1, high, high_in, 1.0)):
            change = face_change(own, came, 1, sign, c)
            side_change[k, c] = change
            total = total + change
        totals.append(jnp.sum(total, axis=0, keepdims=True))
    moment = moments[...] + by_level(totals, moments.shape[1])
    for k in range(load.shape[1] // 4):
        part = moment[:, k * LANES : (k + 1) * LANES]
        load[:, 4 * k : 4 * k + 4, :] = jnp.broadcast_to(part[None], (load.shape[0], 4, LANES))
    copy = pltpu.make_async_copy(load, load_out, sem)
    copy.start()
    for c in range(3):
        out[c, 1 : cx - 1] = inside[c, 1 : cx - 1]
        for k, at in ((0, 0), (1, cy - 1)):
            for x in range(cx):
                out[c, x, at : at + 1, :] = out[c, x, at : at + 1, :] + side_change[k, c, x : x + 1, :]
    copy.wait()


def edges(inside, moments, faces, halos, n_all):
    _, cx, _, nz = inside.shape
    load = shaped(n_all, 4 * moments.shape[1] // LANES, LANES)
    return pl.pallas_call(
        edge_kernel,
        out_shape=(shaped(*inside.shape), load),
        in_specs=[VMEM] * 10,
        out_specs=(VMEM, ANY),
        scratch_shapes=[
            pltpu.VMEM(load.shape, jnp.float32),
            pltpu.VMEM((2, 3, cx, nz), jnp.float32),
            pltpu.SemaphoreType.DMA,
        ],
        compiler_params=PARAMS,
    )(inside, moments, *faces, *halos)


def far_kernel(cx, cy, ncl, n_pencil, load, out):
    n_all = load.shape[0]
    n_slab = n_all // n_pencil
    slab = lax.axis_index("slab")
    pencil = lax.axis_index("pencil")
    shape = (ncl, n_slab * ncl)
    target = lax.broadcasted_iota(jnp.int32, shape, 0)
    source = lax.broadcasted_iota(jnp.int32, shape, 1)
    sigma = jnp.float32(cx * n_slab // 4)
    rel_x = ((slab - source // ncl) * cx).astype(jnp.float32)
    rel_z = ((target - source % ncl) * CB).astype(jnp.float32)
    flat = rel_x * rel_x + rel_z * rel_z + sigma * sigma
    turned = [jnp.zeros(shape, jnp.float32) for _ in range(3)]
    for p in range(n_pencil):
        total = load[p]
        for s in range(1, n_slab):
            total = total + load[s * n_pencil + p]
        moment = jnp.concatenate([total[4 * k : 4 * k + 4] for k in range(load.shape[1] // 4)], axis=1)
        first, second, third = moment[0:1], moment[1:2], moment[2:3]
        rel_y = ((pencil - p) * cy).astype(jnp.float32)
        inverse = lax.rsqrt(flat + rel_y * rel_y)
        weight = inverse * inverse * inverse
        turned[0] = turned[0] + weight * (rel_z * second - rel_y * third)
        turned[1] = turned[1] + weight * (rel_x * third - rel_z * first)
        turned[2] = turned[2] + weight * (rel_y * first - rel_x * second)
    ones = jnp.ones((8, shape[1]), jnp.float32)
    for c in range(3):
        row = lax.dot_general(
            ones,
            turned[c],
            (((1,), (1,)), ((), ())),
            precision=lax.Precision.HIGHEST,
            preferred_element_type=jnp.float32,
        )
        out[c, 0] = row[0:1]


def far(load, cx, cy, ncl, n_pencil):
    return pl.pallas_call(
        functools.partial(far_kernel, cx, cy, ncl, n_pencil),
        out_shape=shaped(3, 1, 1, ncl),
        in_specs=[VMEM],
        out_specs=VMEM,
        compiler_params=PARAMS,
    )(load)


def deposit_step(group, first, listed, load, order, acc, shape):
    cx, cy, nz = shape
    rows = cx * cy // 2
    wide = group * load.shape[2]

    def numbers(length):
        shape = (length // 16, 16, wide)
        return (lax.broadcasted_iota(jnp.int32, shape, 0) * 16 + lax.broadcasted_iota(jnp.int32, shape, 1)).astype(
            jnp.float32
        ).astype(jnp.bfloat16)

    def spread(row):
        return jnp.broadcast_to(row, (16, wide)).astype(jnp.bfloat16)[None]

    zero = jnp.zeros((), jnp.bfloat16)
    one = jnp.ones((), jnp.bfloat16)
    block = jnp.concatenate([load[order[first + k]] for k in range(group)], axis=1)
    live = lax.broadcasted_iota(jnp.int32, (1, wide), 1) // load.shape[2] < listed - first
    cell = block[3:4, :].astype(jnp.int32) % (cx * cy * nz)
    row = cell // nz
    half = row // rows
    at_row = numbers(rows) == spread(jnp.where(live, row % rows, -1).astype(jnp.float32))
    right = []
    for h in range(2):
        at_col = numbers(nz) == spread(jnp.where(half == h, cell % nz, -1).astype(jnp.float32))
        right.append(jnp.where(at_col, one, zero).reshape(nz, wide))
    left = []
    for piece in split(block):
        for c in range(3):
            left.append(jnp.where(at_row, spread(piece[c : c + 1, :]), zero).reshape(rows, wide))
    added = lax.dot_general(
        jnp.concatenate(left, axis=0),
        jnp.concatenate(right, axis=0),
        (((1,), (1,)), ((), ())),
        preferred_element_type=jnp.float32,
    )
    acc[...] += added[: 3 * rows] + added[3 * rows :]


def deposit_kernel(cap, inside, load, out, acc, order):
    _, cx, cy, nz = out.shape
    shape = (cx, cy, nz)
    acc[...] = jnp.zeros_like(acc)
    listed = jnp.int32(0)
    for d in range(load.shape[0] // cap):
        first = d * cap
        held = jnp.max(load[first, 3:4, :]).astype(jnp.int32) // (cx * cy * nz)
        for k in range(cap):
            order[listed + k] = first + k
        listed = listed + held
    for k in range(GROUP):
        order[listed + k] = 0
    rest = listed % GROUP
    whole = listed // GROUP + (rest > GROUP // 2).astype(jnp.int32)

    def step(g, carry):
        deposit_step(GROUP, g * GROUP, listed, load, order, acc, shape)
        return carry

    lax.fori_loop(0, whole, step, 0)

    @pl.when((rest > 0) & (rest <= GROUP // 2))
    def _():
        deposit_step(GROUP // 2, whole * GROUP, listed, load, order, acc, shape)

    for h in range(2):
        span = slice(h * (cx // 2), (h + 1) * (cx // 2))
        change = acc[:, h * nz : (h + 1) * nz].reshape(3, cx // 2, cy, nz)
        out[:, span] = inside[:, span] + change


def deposit(inside, load, cap):
    return pl.pallas_call(
        functools.partial(deposit_kernel, cap),
        out_shape=shaped(*inside.shape),
        in_specs=[VMEM] * 2,
        out_specs=VMEM,
        scratch_shapes=[
            pltpu.VMEM((3 * inside.shape[1] * inside.shape[2] // 2, 2 * inside.shape[3]), jnp.float32),
            pltpu.SMEM((load.shape[0] + max(cap, GROUP),), jnp.int32),
        ],
        compiler_params=PARAMS,
    )(inside, load)


def swapped(array, axis, first):
    up = [(i, i + 1) for i in range(first, lax.axis_size(axis) - 1, 2)]
    return lax.ppermute(array, axis, up + [(j, i) for i, j in up])


def per_device(vorticity, velocity, viscosity, tile_weights, tile_cells, tile_dest, tile_count):
    _, cx, cy, nz = vorticity.shape
    ncl = nz // CB
    n_slab = lax.axis_size("slab")
    n_pencil = lax.axis_size("pencil")
    cap = 2 * tile_weights.shape[0] // n_slab
    weights = jnp.transpose(tile_weights, (1, 0, 2))
    count = tile_count
    *faces, packets, tiles = to_send(
        vorticity, velocity, viscosity, weights, tile_cells, tile_dest.T, count, n_slab, cap
    )
    halos = [swapped(face, axis, 1 - k % 2) for k, (face, axis) in enumerate(zip(faces, SIDES))]
    arrived = lax.all_to_all(packets, "slab", 0, 0, tiled=True)
    inside, moments = inner(vorticity, velocity, viscosity, tiles)
    advanced, load = edges(inside, moments, faces, halos, n_slab * n_pencil)
    load = lax.all_to_all(load, ("slab", "pencil"), 0, 0, tiled=True)
    vorticity_out = deposit(advanced, arrived, cap)
    return (vorticity_out, far(load, cx, cy, ncl, n_pencil))


def solution(mesh):
    in_specs = (
        P(None, "slab", "pencil", None),
        P(None, "slab", "pencil", None),
        P("slab", "pencil", None),
        P(("slab", "pencil"), None, None),
        P(("slab", "pencil"), None),
        P(("slab", "pencil"), None),
        P(("slab", "pencil")),
    )
    out_specs = (P(None, "slab", "pencil", None), P(None, "slab", "pencil", None))
    return jax.shard_map(
        per_device, mesh=mesh, in_specs=in_specs, out_specs=out_specs, check_vma=False
    )
```

```python
import functools

import jax
import jax.numpy as jnp
from jax import lax
from jax.experimental import pallas as pl
from jax.experimental.pallas import tpu as pltpu
from jax.sharding import PartitionSpec as P

CB = 16
TIME_STEP = 0.1
LANES = 128
SIDES = ("slab", "slab", "pencil", "pencil")
GROUP = 16
VMEM_LIMIT = 24 * 1024 * 1024

VMEM = pl.BlockSpec(memory_space=pltpu.VMEM)
ANY = pl.BlockSpec(memory_space=pl.ANY)
SMEM = pl.BlockSpec(memory_space=pltpu.SMEM)
FIRST_PARAMS = pltpu.CompilerParams(vmem_limit_bytes=60 * 1024 * 1024)
PARAMS = pltpu.CompilerParams(vmem_limit_bytes=VMEM_LIMIT)


def shaped(*shape):
    return jax.ShapeDtypeStruct(shape, jnp.float32)


def split(w):
    high = w.astype(jnp.bfloat16).astype(jnp.float32)
    return high, w - high


def pack_tiles(cap, cells_dev, weights, cells, dest, count, packets):
    slots = packets.shape[0]
    tiles = cells.shape[0]
    names = dest[...]
    live = (lax.broadcasted_iota(jnp.int32, (1, tiles), 1) < count[0]).astype(jnp.float32)
    same = (lax.broadcasted_iota(jnp.int32, (slots // cap, tiles), 0) == names).astype(jnp.float32)
    shape = (tiles, tiles)
    earlier = lax.broadcasted_iota(jnp.int32, shape, 0) < lax.broadcasted_iota(jnp.int32, shape, 1)
    before = jnp.dot(same, earlier.astype(jnp.float32), preferred_element_type=jnp.float32)
    rank = jnp.sum(same * before, axis=0, keepdims=True).astype(jnp.int32)
    slot = lax.broadcasted_iota(jnp.int32, (slots, tiles), 0)
    placed = (slot == names * cap + rank).astype(jnp.float32) * live
    held = jnp.sum((slot == names * cap).astype(jnp.float32) * live, axis=1, keepdims=True)
    rows = [weights[0], weights[1], weights[2], cells[...].astype(jnp.float32)]
    found = jnp.dot(
        placed,
        jnp.concatenate(rows, axis=1),
        precision=lax.Precision.HIGHEST,
        preferred_element_type=jnp.float32,
    )
    length = cells.shape[1]
    for c in range(3):
        packets[:, c, :] = found[:, c * length : (c + 1) * length]
    packets[:, 3, :] = found[:, 3 * length :] + held * cells_dev


def tile_moments(cap, nz, packets, moments):
    n_slab = packets.shape[0] // cap
    ncl = nz // CB
    wide = cap * packets.shape[2]
    level = lax.broadcasted_iota(jnp.int32, (ncl, wide), 0)
    found = []
    for d in range(n_slab):
        block = jnp.concatenate([packets[d * cap + k] for k in range(cap)], axis=1)
        cell = block[3:4, :].astype(jnp.int32)
        spots = (level == cell % nz // CB).astype(jnp.float32).astype(jnp.bfloat16)
        high, low = split(block)
        left = jnp.concatenate([high, low], axis=0).astype(jnp.bfloat16)
        sums = lax.dot_general(left, spots, (((1,), (1,)), ((), ())), preferred_element_type=jnp.float32)
        found.append(sums[0:4] + sums[4:8])
    moments[...] = jnp.concatenate(found, axis=1)


class Copies:
    def __init__(self, sems):
        self.sems = sems
        self.made = []

    def start(self, source, target):
        self.made.append(pltpu.make_async_copy(source, target, self.sems.at[len(self.made)]))
        self.made[-1].start()

    def wait(self, first, last):
        for k in range(first, last):
            self.made[k].wait()


def slab_kernel(vort, velo, visc, near_out, far_out, near, far, sems):
    cx = visc.shape[0]
    copies = Copies(sems)
    even = lax.axis_index("slab") % 2 == 0
    for face, at in ((near, jnp.where(even, cx - 1, 0)), (far, jnp.where(even, 0, cx - 1))):
        copies.start(vort.at[:, at], face.at[0:3])
        copies.start(velo.at[:, at], face.at[3:6])
        copies.start(visc.at[at], face.at[6])
    copies.wait(0, 3)
    copies.start(near, near_out)
    copies.wait(3, 6)
    copies.start(far, far_out)
    copies.wait(6, 8)


def slab_faces(vort, velo, visc):
    _, _, cy, nz = vort.shape
    made = (shaped(7, cy, nz), shaped(7, cy, nz))
    return pl.pallas_call(
        slab_kernel,
        out_shape=made,
        in_specs=[ANY] * 3,
        out_specs=(ANY,) * 2,
        scratch_shapes=[pltpu.VMEM(one.shape, jnp.float32) for one in made] + [pltpu.SemaphoreType.DMA((8,))],
        compiler_params=FIRST_PARAMS,
    )(vort, velo, visc)


def send_kernel(
    cap,
    vort,
    velo,
    visc,
    weights_in,
    cells_in,
    dest_in,
    count_in,
    earlier,
    swap_out,
    other_out,
    packets_out,
    moments_out,
    swap,
    other,
    packets,
    moments,
    weights,
    cells,
    dest,
    count,
    sems,
):
    cx, cy, nz = visc.shape
    copies = Copies(sems)
    copies.start(weights_in, weights)
    copies.start(cells_in, cells)
    copies.start(dest_in, dest)
    copies.start(count_in, count)
    even = lax.axis_index("pencil") % 2 == 0
    for face, at in ((swap, jnp.where(even, cy - 1, 0)), (other, jnp.where(even, 0, cy - 1))):
        copies.start(vort.at[:, :, at], face.at[0:3])
        copies.start(velo.at[:, :, at], face.at[3:6])
        copies.start(visc.at[:, at], face.at[6])
    copies.wait(0, 4)
    pack_tiles(cap, cx * cy * nz, weights, cells, dest, count, packets)
    copies.start(packets, packets_out)
    tile_moments(cap, nz, packets, moments)
    copies.start(moments, moments_out)
    copies.wait(4, 10)
    copies.start(swap, swap_out)
    copies.start(other, other_out)
    copies.wait(10, 14)


def to_send(vort, velo, visc, weights, cells, dest, count, earlier, n_slab, cap):
    _, cx, cy, nz = vort.shape
    made = (
        shaped(7, cx, nz),
        shaped(7, cx, nz),
        shaped(n_slab * cap, 4, weights.shape[2]),
        shaped(4, n_slab * nz // CB),
    )
    return pl.pallas_call(
        functools.partial(send_kernel, cap),
        out_shape=made,
        in_specs=[ANY] * 8,
        out_specs=(ANY,) * 4,
        scratch_shapes=[pltpu.VMEM(one.shape, jnp.float32) for one in made]
        + [
            pltpu.VMEM(weights.shape, jnp.float32),
            pltpu.VMEM(cells.shape, jnp.int32),
            pltpu.VMEM(dest.shape, jnp.int32),
            pltpu.SMEM(count.shape, jnp.int32),
            pltpu.SemaphoreType.DMA((14,)),
        ],
        compiler_params=FIRST_PARAMS,
    )(vort, velo, visc, weights, cells, dest, count, earlier)


def ahead(a, axis):
    return pltpu.roll(a, a.shape[axis] - 1, axis)


def behind(a, axis):
    return pltpu.roll(a, 1, axis)


def interior_step(vort, velo, visc, out):
    cx, cy, nz = visc.shape
    has_ahead = lax.broadcasted_iota(jnp.int32, (cy, nz), 0) < cy - 1
    totals = [jnp.zeros((8, nz), jnp.float32) for _ in range(3)]
    flux_x = [None] * 3
    for x in range(cx):
        nu = visc[x]
        spin = [vort[c, x] for c in range(3)]
        mean_y = jnp.where(has_ahead, 0.5 * (nu + ahead(nu, 0)), 0.0)
        mean_z = 0.5 * (nu + ahead(nu, 1))
        half_y = 0.5 * spin[1]
        half_z = 0.5 * spin[2]
        next_y = jnp.where(has_ahead, ahead(half_y, 0), 0.0)
        next_z = ahead(half_z, 1)
        half_y = jnp.where(has_ahead, half_y, 0.0)
        half_x = 0.5 * spin[0]
        if x < cx - 1:
            mean_x = 0.5 * (nu + visc[x + 1])
        for c in range(3):
            w = spin[c]
            u = velo[c, x]
            flux_y = mean_y * (ahead(w, 0) - w)
            flux_z = mean_z * (ahead(w, 1) - w)
            change = flux_y + half_y * ahead(u, 0) - behind(flux_y + next_y * u, 0)
            change = change + (flux_z + half_z * ahead(u, 1) - behind(flux_z + next_z * u, 1))
            if x == 0:
                change = change + half_x * velo[c, x + 1]
            elif x == cx - 1:
                change = change - half_x * velo[c, x - 1]
            else:
                change = change + half_x * (velo[c, x + 1] - velo[c, x - 1])
            if x > 0:
                change = change - flux_x[c]
            if x < cx - 1:
                flux_x[c] = mean_x * (vort[c, x + 1] - w)
                change = change + flux_x[c]
            new = w + TIME_STEP * change
            out[c, x] = new
            totals[c] = totals[c] + jnp.sum(new.reshape(cy // 8, 8, nz), axis=0)
    return [jnp.sum(total, axis=0, keepdims=True) for total in totals]


def by_level(totals, width):
    nz = totals[0].shape[1]
    shape = (nz, width)
    level = lax.broadcasted_iota(jnp.int32, shape, 0) // CB
    lane = lax.broadcasted_iota(jnp.int32, shape, 1)
    pick = (lane == lax.axis_index("slab") * (nz // CB) + level).astype(jnp.float32)
    rows = jnp.concatenate(totals + [jnp.zeros_like(totals[0])], axis=0)
    return jnp.dot(rows, pick, precision=lax.Precision.HIGHEST, preferred_element_type=jnp.float32)


def inner_kernel(vort, velo, visc, tiles_in, out, moments, tiles, sem):
    copy = pltpu.make_async_copy(tiles_in, tiles, sem)
    copy.start()
    own = by_level(interior_step(vort, velo, visc, out), moments.shape[1])
    copy.wait()
    moments[...] = tiles[...] + own


def inner(vort, velo, visc, tiles):
    return pl.pallas_call(
        inner_kernel,
        out_shape=(shaped(*vort.shape), shaped(*tiles.shape)),
        in_specs=[VMEM] * 3 + [ANY],
        out_specs=(VMEM,) * 2,
        scratch_shapes=[pltpu.VMEM(tiles.shape, jnp.float32), pltpu.SemaphoreType.DMA],
        compiler_params=PARAMS,
    )(vort, velo, visc, tiles)


def face_change(own, other, along, sign, c):
    stretch = (0.5 * sign) * own[along] * other[3 + c]
    diffuse = 0.5 * (own[6] + other[6]) * (other[c] - own[c])
    return TIME_STEP * (stretch + diffuse)


def edge_kernel(
    inside, moments, near, far, swap, other, near_in, far_in, swap_in, other_in, out, load_out, load, side_change, sem
):
    _, cx, cy, nz = out.shape
    even = lax.axis_index("pencil") % 2 == 0
    low, low_in = jnp.where(even, other[...], swap[...]), jnp.where(even, other_in[...], swap_in[...])
    high, high_in = jnp.where(even, swap[...], other[...]), jnp.where(even, swap_in[...], other_in[...])
    even = lax.axis_index("slab") % 2 == 0
    near_at, far_at = jnp.where(even, cx - 1, 0), jnp.where(even, 0, cx - 1)
    near_sign = jnp.where(even, 1.0, -1.0)
    totals = []
    for c in range(3):
        total = jnp.zeros((8, nz), jnp.float32)
        for own, came, at, sign in ((near, near_in, near_at, near_sign), (far, far_in, far_at, -near_sign)):
            change = face_change(own, came, 0, sign, c)
            out[c, at] = inside[c, at] + change
            total = total + jnp.sum(change.reshape(cy // 8, 8, nz), axis=0)
        for k, own, came, sign in ((0, low, low_in, -1.0), (1, high, high_in, 1.0)):
            change = face_change(own, came, 1, sign, c)
            side_change[k, c] = change
            total = total + change
        totals.append(jnp.sum(total, axis=0, keepdims=True))
    moment = moments[...] + by_level(totals, moments.shape[1])
    for k in range(load.shape[1] // 4):
        part = moment[:, k * LANES : (k + 1) * LANES]
        load[:, 4 * k : 4 * k + 4, :] = jnp.broadcast_to(part[None], (load.shape[0], 4, LANES))
    copy = pltpu.make_async_copy(load, load_out, sem)
    copy.start()
    for c in range(3):
        out[c, 1 : cx - 1] = inside[c, 1 : cx - 1]
        for k, at in ((0, 0), (1, cy - 1)):
            for x in range(cx):
                out[c, x, at : at + 1, :] = out[c, x, at : at + 1, :] + side_change[k, c, x : x + 1, :]
    copy.wait()


def edges(inside, moments, faces, halos, n_all):
    _, cx, _, nz = inside.shape
    load = shaped(n_all, 4 * moments.shape[1] // LANES, LANES)
    return pl.pallas_call(
        edge_kernel,
        out_shape=(shaped(*inside.shape), load),
        in_specs=[VMEM] * 10,
        out_specs=(VMEM, ANY),
        scratch_shapes=[
            pltpu.VMEM(load.shape, jnp.float32),
            pltpu.VMEM((2, 3, cx, nz), jnp.float32),
            pltpu.SemaphoreType.DMA,
        ],
        compiler_params=PARAMS,
    )(inside, moments, *faces, *halos)


def far_kernel(cx, cy, ncl, n_pencil, load, out):
    n_all = load.shape[0]
    n_slab = n_all // n_pencil
    slab = lax.axis_index("slab")
    pencil = lax.axis_index("pencil")
    shape = (ncl, n_slab * ncl)
    target = lax.broadcasted_iota(jnp.int32, shape, 0)
    source = lax.broadcasted_iota(jnp.int32, shape, 1)
    sigma = jnp.float32(cx * n_slab // 4)
    rel_x = ((slab - source // ncl) * cx).astype(jnp.float32)
    rel_z = ((target - source % ncl) * CB).astype(jnp.float32)
    flat = rel_x * rel_x + rel_z * rel_z + sigma * sigma
    turned = [jnp.zeros(shape, jnp.float32) for _ in range(3)]
    for p in range(n_pencil):
        total = load[p]
        for s in range(1, n_slab):
            total = total + load[s * n_pencil + p]
        moment = jnp.concatenate([total[4 * k : 4 * k + 4] for k in range(load.shape[1] // 4)], axis=1)
        first, second, third = moment[0:1], moment[1:2], moment[2:3]
        rel_y = ((pencil - p) * cy).astype(jnp.float32)
        inverse = lax.rsqrt(flat + rel_y * rel_y)
        weight = inverse * inverse * inverse
        turned[0] = turned[0] + weight * (rel_z * second - rel_y * third)
        turned[1] = turned[1] + weight * (rel_x * third - rel_z * first)
        turned[2] = turned[2] + weight * (rel_y * first - rel_x * second)
    ones = jnp.ones((8, shape[1]), jnp.float32)
    for c in range(3):
        row = lax.dot_general(
            ones,
            turned[c],
            (((1,), (1,)), ((), ())),
            precision=lax.Precision.HIGHEST,
            preferred_element_type=jnp.float32,
        )
        out[c, 0] = row[0:1]


def far(load, cx, cy, ncl, n_pencil):
    return pl.pallas_call(
        functools.partial(far_kernel, cx, cy, ncl, n_pencil),
        out_shape=shaped(3, 1, 1, ncl),
        in_specs=[VMEM],
        out_specs=VMEM,
        compiler_params=PARAMS,
    )(load)


def deposit_step(group, first, listed, load, order, acc, shape):
    cx, cy, nz = shape
    rows = cx * cy // 2
    wide = group * load.shape[2]

    def numbers(length):
        shape = (length // 16, 16, wide)
        return (lax.broadcasted_iota(jnp.int32, shape, 0) * 16 + lax.broadcasted_iota(jnp.int32, shape, 1)).astype(
            jnp.float32
        ).astype(jnp.bfloat16)

    def spread(row):
        return jnp.broadcast_to(row, (16, wide)).astype(jnp.bfloat16)[None]

    zero = jnp.zeros((), jnp.bfloat16)
    one = jnp.ones((), jnp.bfloat16)
    block = jnp.concatenate([load[order[first + k]] for k in range(group)], axis=1)
    live = lax.broadcasted_iota(jnp.int32, (1, wide), 1) // load.shape[2] < listed - first
    cell = block[3:4, :].astype(jnp.int32) % (cx * cy * nz)
    row = cell // nz
    half = row // rows
    at_row = numbers(rows) == spread(jnp.where(live, row % rows, -1).astype(jnp.float32))
    right = []
    for h in range(2):
        at_col = numbers(nz) == spread(jnp.where(half == h, cell % nz, -1).astype(jnp.float32))
        right.append(jnp.where(at_col, one, zero).reshape(nz, wide))
    left = []
    for piece in split(block):
        for c in range(3):
            left.append(jnp.where(at_row, spread(piece[c : c + 1, :]), zero).reshape(rows, wide))
    added = lax.dot_general(
        jnp.concatenate(left, axis=0),
        jnp.concatenate(right, axis=0),
        (((1,), (1,)), ((), ())),
        preferred_element_type=jnp.float32,
    )
    acc[...] += added[: 3 * rows] + added[3 * rows :]


def deposit_kernel(cap, inside, load, out, acc, order):
    _, cx, cy, nz = out.shape
    shape = (cx, cy, nz)
    acc[...] = jnp.zeros_like(acc)
    listed = jnp.int32(0)
    for d in range(load.shape[0] // cap):
        first = d * cap
        held = jnp.max(load[first, 3:4, :]).astype(jnp.int32) // (cx * cy * nz)
        for k in range(cap):
            order[listed + k] = first + k
        listed = listed + held
    for k in range(GROUP):
        order[listed + k] = 0
    rest = listed % GROUP
    whole = listed // GROUP + (rest > GROUP // 2).astype(jnp.int32)

    def step(g, carry):
        deposit_step(GROUP, g * GROUP, listed, load, order, acc, shape)
        return carry

    lax.fori_loop(0, whole, step, 0)

    @pl.when((rest > 0) & (rest <= GROUP // 2))
    def _():
        deposit_step(GROUP // 2, whole * GROUP, listed, load, order, acc, shape)

    for h in range(2):
        span = slice(h * (cx // 2), (h + 1) * (cx // 2))
        change = acc[:, h * nz : (h + 1) * nz].reshape(3, cx // 2, cy, nz)
        out[:, span] = inside[:, span] + change


def deposit(inside, load, cap):
    return pl.pallas_call(
        functools.partial(deposit_kernel, cap),
        out_shape=shaped(*inside.shape),
        in_specs=[VMEM] * 2,
        out_specs=VMEM,
        scratch_shapes=[
            pltpu.VMEM((3 * inside.shape[1] * inside.shape[2] // 2, 2 * inside.shape[3]), jnp.float32),
            pltpu.SMEM((load.shape[0] + max(cap, GROUP),), jnp.int32),
        ],
        compiler_params=PARAMS,
    )(inside, load)


def swapped(array, axis, first):
    up = [(i, i + 1) for i in range(first, lax.axis_size(axis) - 1, 2)]
    return lax.ppermute(array, axis, up + [(j, i) for i, j in up])


def per_device(vorticity, velocity, viscosity, tile_weights, tile_cells, tile_dest, tile_count):
    _, cx, cy, nz = vorticity.shape
    ncl = nz // CB
    n_slab = lax.axis_size("slab")
    n_pencil = lax.axis_size("pencil")
    cap = 2 * tile_weights.shape[0] // n_slab
    weights = jnp.transpose(tile_weights, (1, 0, 2))
    near, far_face = slab_faces(vorticity, velocity, viscosity)
    swap, other, packets, tiles = to_send(
        vorticity, velocity, viscosity, weights, tile_cells, tile_dest.T, tile_count, far_face, n_slab, cap
    )
    faces = (near, far_face, swap, other)
    halos = [swapped(face, axis, k % 2) for k, (face, axis) in enumerate(zip(faces, SIDES))]
    arrived = lax.all_to_all(packets, "slab", 0, 0, tiled=True)
    inside, moments = inner(vorticity, velocity, viscosity, tiles)
    advanced, load = edges(inside, moments, faces, halos, n_slab * n_pencil)
    load = lax.all_to_all(load, ("slab", "pencil"), 0, 0, tiled=True)
    vorticity_out = deposit(advanced, arrived, cap)
    return (vorticity_out, far(load, cx, cy, ncl, n_pencil))


def solution(mesh):
    in_specs = (
        P(None, "slab", "pencil", None),
        P(None, "slab", "pencil", None),
        P("slab", "pencil", None),
        P(("slab", "pencil"), None, None),
        P(("slab", "pencil"), None),
        P(("slab", "pencil"), None),
        P(("slab", "pencil")),
    )
    out_specs = (P(None, "slab", "pencil", None), P(None, "slab", "pencil", None))
    return jax.shard_map(
        per_device, mesh=mesh, in_specs=in_specs, out_specs=out_specs, check_vma=False
    )
```

```python
import functools

import jax
import jax.numpy as jnp
from jax import lax
from jax.experimental import pallas as pl
from jax.experimental.pallas import tpu as pltpu
from jax.sharding import PartitionSpec as P

CB = 16
TIME_STEP = 0.1
LANES = 128
SIDES = ("slab", "slab", "pencil", "pencil")
GROUP = 16
VMEM_LIMIT = 24 * 1024 * 1024

VMEM = pl.BlockSpec(memory_space=pltpu.VMEM)
ANY = pl.BlockSpec(memory_space=pl.ANY)
SMEM = pl.BlockSpec(memory_space=pltpu.SMEM)
FIRST_PARAMS = pltpu.CompilerParams(vmem_limit_bytes=60 * 1024 * 1024)
PARAMS = pltpu.CompilerParams(vmem_limit_bytes=VMEM_LIMIT)


def shaped(*shape):
    return jax.ShapeDtypeStruct(shape, jnp.float32)


def split(w):
    high = w.astype(jnp.bfloat16).astype(jnp.float32)
    return high, w - high


def pack_tiles(cap, cells_dev, weights, cells, dest, count, packets):
    slots = packets.shape[0]
    tiles = cells.shape[0]
    names = dest[...]
    live = (lax.broadcasted_iota(jnp.int32, (1, tiles), 1) < count[0]).astype(jnp.float32)
    same = (lax.broadcasted_iota(jnp.int32, (slots // cap, tiles), 0) == names).astype(jnp.float32)
    shape = (tiles, tiles)
    earlier = lax.broadcasted_iota(jnp.int32, shape, 0) < lax.broadcasted_iota(jnp.int32, shape, 1)
    before = jnp.dot(same, earlier.astype(jnp.float32), preferred_element_type=jnp.float32)
    rank = jnp.sum(same * before, axis=0, keepdims=True).astype(jnp.int32)
    slot = lax.broadcasted_iota(jnp.int32, (slots, tiles), 0)
    placed = (slot == names * cap + rank).astype(jnp.float32) * live
    held = jnp.sum((slot == names * cap).astype(jnp.float32) * live, axis=1, keepdims=True)
    rows = [weights[0], weights[1], weights[2], cells[...].astype(jnp.float32)]
    found = jnp.dot(
        placed,
        jnp.concatenate(rows, axis=1),
        precision=lax.Precision.HIGHEST,
        preferred_element_type=jnp.float32,
    )
    length = cells.shape[1]
    for c in range(3):
        packets[:, c, :] = found[:, c * length : (c + 1) * length]
    packets[:, 3, :] = found[:, 3 * length :] + held * cells_dev


def tile_moments(cap, nz, packets, moments):
    n_slab = packets.shape[0] // cap
    ncl = nz // CB
    wide = cap * packets.shape[2]
    level = lax.broadcasted_iota(jnp.int32, (ncl, wide), 0)
    found = []
    for d in range(n_slab):
        block = jnp.concatenate([packets[d * cap + k] for k in range(cap)], axis=1)
        cell = block[3:4, :].astype(jnp.int32)
        spots = (level == cell % nz // CB).astype(jnp.float32).astype(jnp.bfloat16)
        high, low = split(block)
        left = jnp.concatenate([high, low], axis=0).astype(jnp.bfloat16)
        sums = lax.dot_general(left, spots, (((1,), (1,)), ((), ())), preferred_element_type=jnp.float32)
        found.append(sums[0:4] + sums[4:8])
    moments[...] = jnp.concatenate(found, axis=1)


class Copies:
    def __init__(self, sems):
        self.sems = sems
        self.made = []

    def start(self, source, target):
        self.made.append(pltpu.make_async_copy(source, target, self.sems.at[len(self.made)]))
        self.made[-1].start()

    def wait(self, first, last):
        for k in range(first, last):
            self.made[k].wait()


def slab_kernel(vort, velo, visc, near_out, far_out, near, far, sems):
    cx = visc.shape[0]
    copies = Copies(sems)
    even = lax.axis_index("slab") % 2 == 0
    for face, at in ((near, jnp.where(even, cx - 1, 0)), (far, jnp.where(even, 0, cx - 1))):
        copies.start(vort.at[:, at], face.at[0:3])
        copies.start(velo.at[:, at], face.at[3:6])
        copies.start(visc.at[at], face.at[6])
    copies.wait(0, 3)
    copies.start(near, near_out)
    copies.wait(3, 6)
    copies.start(far, far_out)
    copies.wait(6, 8)


def slab_faces(vort, velo, visc):
    _, _, cy, nz = vort.shape
    made = (shaped(7, cy, nz), shaped(7, cy, nz))
    return pl.pallas_call(
        slab_kernel,
        out_shape=made,
        in_specs=[ANY] * 3,
        out_specs=(ANY,) * 2,
        scratch_shapes=[pltpu.VMEM(one.shape, jnp.float32) for one in made] + [pltpu.SemaphoreType.DMA((8,))],
        compiler_params=FIRST_PARAMS,
    )(vort, velo, visc)


def send_kernel(cap, vort, velo, visc, weights, cells, dest, count, swap, other, packets, moments):
    cx, cy, nz = visc.shape
    even = lax.axis_index("pencil") % 2 == 0
    for face, at in ((swap, jnp.where(even, cy - 1, 0)), (other, jnp.where(even, 0, cy - 1))):
        for x in range(cx):
            for c in range(3):
                face[c, x : x + 1, :] = vort[c, x, pl.ds(at, 1), :]
                face[3 + c, x : x + 1, :] = velo[c, x, pl.ds(at, 1), :]
            face[6, x : x + 1, :] = visc[x, pl.ds(at, 1), :]
    pack_tiles(cap, cx * cy * nz, weights, cells, dest, count, packets)
    tile_moments(cap, nz, packets, moments)


def to_send(vort, velo, visc, weights, cells, dest, count, n_slab, cap):
    _, cx, cy, nz = vort.shape
    return pl.pallas_call(
        functools.partial(send_kernel, cap),
        out_shape=(
            shaped(7, cx, nz),
            shaped(7, cx, nz),
            shaped(n_slab * cap, 4, weights.shape[2]),
            shaped(4, n_slab * nz // CB),
        ),
        in_specs=[VMEM] * 6 + [SMEM],
        out_specs=(VMEM,) * 4,
        compiler_params=PARAMS,
    )(vort, velo, visc, weights, cells, dest, count)


def ahead(a, axis):
    return pltpu.roll(a, a.shape[axis] - 1, axis)


def behind(a, axis):
    return pltpu.roll(a, 1, axis)


def interior_step(vort, velo, visc, out):
    cx, cy, nz = visc.shape
    has_ahead = lax.broadcasted_iota(jnp.int32, (cy, nz), 0) < cy - 1
    totals = [jnp.zeros((8, nz), jnp.float32) for _ in range(3)]
    flux_x = [None] * 3
    for x in range(cx):
        nu = visc[x]
        spin = [vort[c, x] for c in range(3)]
        mean_y = jnp.where(has_ahead, 0.5 * (nu + ahead(nu, 0)), 0.0)
        mean_z = 0.5 * (nu + ahead(nu, 1))
        half_y = 0.5 * spin[1]
        half_z = 0.5 * spin[2]
        next_y = jnp.where(has_ahead, ahead(half_y, 0), 0.0)
        next_z = ahead(half_z, 1)
        half_y = jnp.where(has_ahead, half_y, 0.0)
        half_x = 0.5 * spin[0]
        if x < cx - 1:
            mean_x = 0.5 * (nu + visc[x + 1])
        for c in range(3):
            w = spin[c]
            u = velo[c, x]
            flux_y = mean_y * (ahead(w, 0) - w)
            flux_z = mean_z * (ahead(w, 1) - w)
            change = flux_y + half_y * ahead(u, 0) - behind(flux_y + next_y * u, 0)
            change = change + (flux_z + half_z * ahead(u, 1) - behind(flux_z + next_z * u, 1))
            if x == 0:
                change = change + half_x * velo[c, x + 1]
            elif x == cx - 1:
                change = change - half_x * velo[c, x - 1]
            else:
                change = change + half_x * (velo[c, x + 1] - velo[c, x - 1])
            if x > 0:
                change = change - flux_x[c]
            if x < cx - 1:
                flux_x[c] = mean_x * (vort[c, x + 1] - w)
                change = change + flux_x[c]
            new = w + TIME_STEP * change
            out[c, x] = new
            totals[c] = totals[c] + jnp.sum(new.reshape(cy // 8, 8, nz), axis=0)
    return [jnp.sum(total, axis=0, keepdims=True) for total in totals]


def by_level(totals, width):
    nz = totals[0].shape[1]
    shape = (nz, width)
    level = lax.broadcasted_iota(jnp.int32, shape, 0) // CB
    lane = lax.broadcasted_iota(jnp.int32, shape, 1)
    pick = (lane == lax.axis_index("slab") * (nz // CB) + level).astype(jnp.float32)
    rows = jnp.concatenate(totals + [jnp.zeros_like(totals[0])], axis=0)
    return jnp.dot(rows, pick, precision=lax.Precision.HIGHEST, preferred_element_type=jnp.float32)


def inner_kernel(vort, velo, visc, tiles_in, out, moments, tiles, sem):
    copy = pltpu.make_async_copy(tiles_in, tiles, sem)
    copy.start()
    own = by_level(interior_step(vort, velo, visc, out), moments.shape[1])
    copy.wait()
    moments[...] = tiles[...] + own


def inner(vort, velo, visc, tiles):
    return pl.pallas_call(
        inner_kernel,
        out_shape=(shaped(*vort.shape), shaped(*tiles.shape)),
        in_specs=[VMEM] * 3 + [ANY],
        out_specs=(VMEM,) * 2,
        scratch_shapes=[pltpu.VMEM(tiles.shape, jnp.float32), pltpu.SemaphoreType.DMA],
        compiler_params=PARAMS,
    )(vort, velo, visc, tiles)


def face_change(own, other, along, sign, c):
    stretch = (0.5 * sign) * own[along] * other[3 + c]
    diffuse = 0.5 * (own[6] + other[6]) * (other[c] - own[c])
    return TIME_STEP * (stretch + diffuse)


def edge_kernel(
    inside, moments, near, far, swap, other, near_in, far_in, swap_in, other_in, out, load_out, load, side_change, sem
):
    _, cx, cy, nz = out.shape
    even = lax.axis_index("pencil") % 2 == 0
    low, low_in = jnp.where(even, other[...], swap[...]), jnp.where(even, other_in[...], swap_in[...])
    high, high_in = jnp.where(even, swap[...], other[...]), jnp.where(even, swap_in[...], other_in[...])
    even = lax.axis_index("slab") % 2 == 0
    near_at, far_at = jnp.where(even, cx - 1, 0), jnp.where(even, 0, cx - 1)
    near_sign = jnp.where(even, 1.0, -1.0)
    totals = []
    for c in range(3):
        total = jnp.zeros((8, nz), jnp.float32)
        for own, came, at, sign in ((near, near_in, near_at, near_sign), (far, far_in, far_at, -near_sign)):
            change = face_change(own, came, 0, sign, c)
            out[c, at] = inside[c, at] + change
            total = total + jnp.sum(change.reshape(cy // 8, 8, nz), axis=0)
        for k, own, came, sign in ((0, low, low_in, -1.0), (1, high, high_in, 1.0)):
            change = face_change(own, came, 1, sign, c)
            side_change[k, c] = change
            total = total + change
        totals.append(jnp.sum(total, axis=0, keepdims=True))
    moment = moments[...] + by_level(totals, moments.shape[1])
    for k in range(load.shape[1] // 4):
        part = moment[:, k * LANES : (k + 1) * LANES]
        load[:, 4 * k : 4 * k + 4, :] = jnp.broadcast_to(part[None], (load.shape[0], 4, LANES))
    copy = pltpu.make_async_copy(load, load_out, sem)
    copy.start()
    for c in range(3):
        out[c, 1 : cx - 1] = inside[c, 1 : cx - 1]
        for k, at in ((0, 0), (1, cy - 1)):
            for x in range(cx):
                out[c, x, at : at + 1, :] = out[c, x, at : at + 1, :] + side_change[k, c, x : x + 1, :]
    copy.wait()


def edges(inside, moments, faces, halos, n_all):
    _, cx, _, nz = inside.shape
    load = shaped(n_all, 4 * moments.shape[1] // LANES, LANES)
    return pl.pallas_call(
        edge_kernel,
        out_shape=(shaped(*inside.shape), load),
        in_specs=[VMEM] * 10,
        out_specs=(VMEM, ANY),
        scratch_shapes=[
            pltpu.VMEM(load.shape, jnp.float32),
            pltpu.VMEM((2, 3, cx, nz), jnp.float32),
            pltpu.SemaphoreType.DMA,
        ],
        compiler_params=PARAMS,
    )(inside, moments, *faces, *halos)


def far_kernel(cx, cy, ncl, n_pencil, load, out):
    n_all = load.shape[0]
    n_slab = n_all // n_pencil
    slab = lax.axis_index("slab")
    pencil = lax.axis_index("pencil")
    shape = (ncl, n_slab * ncl)
    target = lax.broadcasted_iota(jnp.int32, shape, 0)
    source = lax.broadcasted_iota(jnp.int32, shape, 1)
    sigma = jnp.float32(cx * n_slab // 4)
    rel_x = ((slab - source // ncl) * cx).astype(jnp.float32)
    rel_z = ((target - source % ncl) * CB).astype(jnp.float32)
    flat = rel_x * rel_x + rel_z * rel_z + sigma * sigma
    turned = [jnp.zeros(shape, jnp.float32) for _ in range(3)]
    for p in range(n_pencil):
        total = load[p]
        for s in range(1, n_slab):
            total = total + load[s * n_pencil + p]
        moment = jnp.concatenate([total[4 * k : 4 * k + 4] for k in range(load.shape[1] // 4)], axis=1)
        first, second, third = moment[0:1], moment[1:2], moment[2:3]
        rel_y = ((pencil - p) * cy).astype(jnp.float32)
        inverse = lax.rsqrt(flat + rel_y * rel_y)
        weight = inverse * inverse * inverse
        turned[0] = turned[0] + weight * (rel_z * second - rel_y * third)
        turned[1] = turned[1] + weight * (rel_x * third - rel_z * first)
        turned[2] = turned[2] + weight * (rel_y * first - rel_x * second)
    ones = jnp.ones((8, shape[1]), jnp.float32)
    for c in range(3):
        row = lax.dot_general(
            ones,
            turned[c],
            (((1,), (1,)), ((), ())),
            precision=lax.Precision.HIGHEST,
            preferred_element_type=jnp.float32,
        )
        out[c, 0] = row[0:1]


def far(load, cx, cy, ncl, n_pencil):
    return pl.pallas_call(
        functools.partial(far_kernel, cx, cy, ncl, n_pencil),
        out_shape=shaped(3, 1, 1, ncl),
        in_specs=[VMEM],
        out_specs=VMEM,
        compiler_params=PARAMS,
    )(load)


def deposit_step(group, first, listed, load, order, acc, shape):
    cx, cy, nz = shape
    rows = cx * cy // 2
    wide = group * load.shape[2]

    def numbers(length):
        shape = (length // 16, 16, wide)
        return (lax.broadcasted_iota(jnp.int32, shape, 0) * 16 + lax.broadcasted_iota(jnp.int32, shape, 1)).astype(
            jnp.float32
        ).astype(jnp.bfloat16)

    def spread(row):
        return jnp.broadcast_to(row, (16, wide)).astype(jnp.bfloat16)[None]

    zero = jnp.zeros((), jnp.bfloat16)
    one = jnp.ones((), jnp.bfloat16)
    block = jnp.concatenate([load[order[first + k]] for k in range(group)], axis=1)
    live = lax.broadcasted_iota(jnp.int32, (1, wide), 1) // load.shape[2] < listed - first
    cell = block[3:4, :].astype(jnp.int32) % (cx * cy * nz)
    row = cell // nz
    half = row // rows
    at_row = numbers(rows) == spread(jnp.where(live, row % rows, -1).astype(jnp.float32))
    right = []
    for h in range(2):
        at_col = numbers(nz) == spread(jnp.where(half == h, cell % nz, -1).astype(jnp.float32))
        right.append(jnp.where(at_col, one, zero).reshape(nz, wide))
    left = []
    for piece in split(block):
        for c in range(3):
            left.append(jnp.where(at_row, spread(piece[c : c + 1, :]), zero).reshape(rows, wide))
    added = lax.dot_general(
        jnp.concatenate(left, axis=0),
        jnp.concatenate(right, axis=0),
        (((1,), (1,)), ((), ())),
        preferred_element_type=jnp.float32,
    )
    acc[...] += added[: 3 * rows] + added[3 * rows :]


def deposit_kernel(cap, inside, load, out, acc, order, made, sems):
    _, cx, cy, nz = out.shape
    shape = (cx, cy, nz)
    acc[...] = jnp.zeros_like(acc)
    listed = jnp.int32(0)
    for d in range(load.shape[0] // cap):
        first = d * cap
        held = jnp.max(load[first, 3:4, :]).astype(jnp.int32) // (cx * cy * nz)
        for k in range(cap):
            order[listed + k] = first + k
        listed = listed + held
    for k in range(GROUP):
        order[listed + k] = 0
    rest = listed % GROUP
    whole = listed // GROUP + (rest > GROUP // 2).astype(jnp.int32)

    def step(g, carry):
        deposit_step(GROUP, g * GROUP, listed, load, order, acc, shape)
        return carry

    lax.fori_loop(0, whole, step, 0)

    @pl.when((rest > 0) & (rest <= GROUP // 2))
    def _():
        deposit_step(GROUP // 2, whole * GROUP, listed, load, order, acc, shape)

    copies = Copies(sems)
    rows = cx * cy // 2
    for c in range(3):
        for h in range(2):
            span = slice(h * (cx // 2), (h + 1) * (cx // 2))
            change = acc[c * rows : (c + 1) * rows, h * nz : (h + 1) * nz].reshape(cx // 2, cy, nz)
            made[c, span] = inside[c, span] + change
            copies.start(made.at[c, span], out.at[c, span])
    copies.wait(0, 6)


def deposit(inside, load, cap):
    return pl.pallas_call(
        functools.partial(deposit_kernel, cap),
        out_shape=shaped(*inside.shape),
        in_specs=[VMEM] * 2,
        out_specs=ANY,
        scratch_shapes=[
            pltpu.VMEM((3 * inside.shape[1] * inside.shape[2] // 2, 2 * inside.shape[3]), jnp.float32),
            pltpu.SMEM((load.shape[0] + max(cap, GROUP),), jnp.int32),
            pltpu.VMEM(inside.shape, jnp.float32),
            pltpu.SemaphoreType.DMA((6,)),
        ],
        compiler_params=PARAMS,
    )(inside, load)


def swapped(array, axis, first):
    up = [(i, i + 1) for i in range(first, lax.axis_size(axis) - 1, 2)]
    return lax.ppermute(array, axis, up + [(j, i) for i, j in up])


def per_device(vorticity, velocity, viscosity, tile_weights, tile_cells, tile_dest, tile_count):
    _, cx, cy, nz = vorticity.shape
    ncl = nz // CB
    n_slab = lax.axis_size("slab")
    n_pencil = lax.axis_size("pencil")
    cap = 2 * tile_weights.shape[0] // n_slab
    weights = jnp.transpose(tile_weights, (1, 0, 2))
    near, far_face = slab_faces(vorticity, velocity, viscosity)
    swap, other, packets, tiles = to_send(
        vorticity, velocity, viscosity, weights, tile_cells, tile_dest.T, tile_count, n_slab, cap
    )
    faces = (near, far_face, swap, other)
    halos = [swapped(face, axis, k % 2) for k, (face, axis) in enumerate(zip(faces, SIDES))]
    arrived = lax.all_to_all(packets, "slab", 0, 0, tiled=True)
    inside, moments = inner(vorticity, velocity, viscosity, tiles)
    advanced, load = edges(inside, moments, faces, halos, n_slab * n_pencil)
    load = lax.all_to_all(load, ("slab", "pencil"), 0, 0, tiled=True)
    vorticity_out = deposit(advanced, arrived, cap)
    return (vorticity_out, far(load, cx, cy, ncl, n_pencil))


def solution(mesh):
    in_specs = (
        P(None, "slab", "pencil", None),
        P(None, "slab", "pencil", None),
        P("slab", "pencil", None),
        P(("slab", "pencil"), None, None),
        P(("slab", "pencil"), None),
        P(("slab", "pencil"), None),
        P(("slab", "pencil")),
    )
    out_specs = (P(None, "slab", "pencil", None), P(None, "slab", "pencil", None))
    return jax.shard_map(
        per_device, mesh=mesh, in_specs=in_specs, out_specs=out_specs, check_vma=False
    )
```

```python
import functools

import jax
import jax.numpy as jnp
from jax import lax
from jax.experimental import pallas as pl
from jax.experimental.pallas import tpu as pltpu
from jax.sharding import PartitionSpec as P

CB = 16
TIME_STEP = 0.1
LANES = 128
SIDES = ("slab", "slab", "pencil", "pencil")
GROUP = 16
VMEM_LIMIT = 24 * 1024 * 1024

VMEM = pl.BlockSpec(memory_space=pltpu.VMEM)
ANY = pl.BlockSpec(memory_space=pl.ANY)
SMEM = pl.BlockSpec(memory_space=pltpu.SMEM)
FIRST_PARAMS = pltpu.CompilerParams(vmem_limit_bytes=60 * 1024 * 1024)
PARAMS = pltpu.CompilerParams(vmem_limit_bytes=VMEM_LIMIT)


def shaped(*shape):
    return jax.ShapeDtypeStruct(shape, jnp.float32)


def split(w):
    high = w.astype(jnp.bfloat16).astype(jnp.float32)
    return high, w - high


def thirds(w):
    high, rest = split(w)
    middle, low = split(rest)
    return [piece.astype(jnp.bfloat16) for piece in (high, middle, low)]


def pack_tiles(cap, cells_dev, weights, cells, dest, count, packets):
    slots = packets.shape[0]
    tiles = cells.shape[0]
    names = dest[...]
    live = (lax.broadcasted_iota(jnp.int32, (1, tiles), 1) < count[0]).astype(jnp.float32)
    same = (lax.broadcasted_iota(jnp.int32, (slots // cap, tiles), 0) == names).astype(jnp.float32)
    shape = (tiles, tiles)
    earlier = lax.broadcasted_iota(jnp.int32, shape, 0) < lax.broadcasted_iota(jnp.int32, shape, 1)
    before = jnp.dot(same, earlier.astype(jnp.float32), preferred_element_type=jnp.float32)
    rank = jnp.sum(same * before, axis=0, keepdims=True).astype(jnp.int32)
    slot = lax.broadcasted_iota(jnp.int32, (slots, tiles), 0)
    placed = (slot == names * cap + rank).astype(jnp.float32) * live
    held = jnp.sum((slot == names * cap).astype(jnp.float32) * live, axis=1, keepdims=True)
    rows = [weights[0], weights[1], weights[2], cells[...].astype(jnp.float32)]
    found = jnp.dot(
        jnp.concatenate([placed] * 3, axis=1).astype(jnp.bfloat16),
        jnp.concatenate(thirds(jnp.concatenate(rows, axis=1)), axis=0),
        preferred_element_type=jnp.float32,
    )
    length = cells.shape[1]
    for c in range(3):
        packets[:, c, :] = found[:, c * length : (c + 1) * length]
    packets[:, 3, :] = found[:, 3 * length :] + held * cells_dev


def tile_moments(cap, nz, packets, moments):
    n_slab = packets.shape[0] // cap
    ncl = nz // CB
    wide = cap * packets.shape[2]
    level = lax.broadcasted_iota(jnp.int32, (ncl, wide), 0)
    found = []
    for d in range(n_slab):
        block = jnp.concatenate([packets[d * cap + k] for k in range(cap)], axis=1)
        cell = block[3:4, :].astype(jnp.int32)
        spots = (level == cell % nz // CB).astype(jnp.float32).astype(jnp.bfloat16)
        high, low = split(block)
        left = jnp.concatenate([high, low], axis=0).astype(jnp.bfloat16)
        sums = lax.dot_general(left, spots, (((1,), (1,)), ((), ())), preferred_element_type=jnp.float32)
        found.append(sums[0:4] + sums[4:8])
    moments[...] = jnp.concatenate(found, axis=1)


class Copies:
    def __init__(self, sems):
        self.sems = sems
        self.made = []

    def start(self, source, target):
        self.made.append(pltpu.make_async_copy(source, target, self.sems.at[len(self.made)]))
        self.made[-1].start()

    def wait(self, first, last):
        for k in range(first, last):
            self.made[k].wait()


def send_kernel(
    cap,
    vort,
    velo,
    visc,
    weights_in,
    cells_in,
    dest_in,
    count_in,
    near_out,
    far_out,
    swap_out,
    other_out,
    packets_out,
    moments_out,
    near,
    far,
    swap,
    other,
    packets,
    moments,
    weights,
    cells,
    dest,
    count,
    sems,
):
    cx, cy, nz = visc.shape
    copies = Copies(sems)
    copies.start(weights_in, weights)
    copies.start(cells_in, cells)
    copies.start(dest_in, dest)
    copies.start(count_in, count)
    even = lax.axis_index("slab") % 2 == 0
    for face, at in ((near, jnp.where(even, cx - 1, 0)), (far, jnp.where(even, 0, cx - 1))):
        copies.start(vort.at[:, at], face.at[0:3])
        copies.start(velo.at[:, at], face.at[3:6])
        copies.start(visc.at[at], face.at[6])
    even = lax.axis_index("pencil") % 2 == 0
    for face, at in ((swap, jnp.where(even, cy - 1, 0)), (other, jnp.where(even, 0, cy - 1))):
        copies.start(vort.at[:, :, at], face.at[0:3])
        copies.start(velo.at[:, :, at], face.at[3:6])
        copies.start(visc.at[:, at], face.at[6])
    copies.wait(0, 4)
    pack_tiles(cap, cx * cy * nz, weights, cells, dest, count, packets)
    copies.start(packets, packets_out)
    copies.wait(4, 10)
    copies.start(near, near_out)
    copies.start(far, far_out)
    tile_moments(cap, nz, packets, moments)
    copies.start(moments, moments_out)
    copies.wait(10, 16)
    copies.start(swap, swap_out)
    copies.start(other, other_out)
    copies.wait(16, 22)


def to_send(vort, velo, visc, weights, cells, dest, count, n_slab, cap):
    _, cx, cy, nz = vort.shape
    made = (
        shaped(7, cy, nz),
        shaped(7, cy, nz),
        shaped(7, cx, nz),
        shaped(7, cx, nz),
        shaped(n_slab * cap, 4, weights.shape[2]),
        shaped(4, n_slab * nz // CB),
    )
    return pl.pallas_call(
        functools.partial(send_kernel, cap),
        out_shape=made,
        in_specs=[ANY] * 7,
        out_specs=(ANY,) * 6,
        scratch_shapes=[pltpu.VMEM(one.shape, jnp.float32) for one in made]
        + [
            pltpu.VMEM(weights.shape, jnp.float32),
            pltpu.VMEM(cells.shape, jnp.int32),
            pltpu.VMEM(dest.shape, jnp.int32),
            pltpu.SMEM(count.shape, jnp.int32),
            pltpu.SemaphoreType.DMA((22,)),
        ],
        compiler_params=FIRST_PARAMS,
    )(vort, velo, visc, weights, cells, dest, count)


def ahead(a, axis):
    return pltpu.roll(a, a.shape[axis] - 1, axis)


def behind(a, axis):
    return pltpu.roll(a, 1, axis)


def interior_step(vort, velo, visc, out):
    cx, cy, nz = visc.shape
    has_ahead = lax.broadcasted_iota(jnp.int32, (cy, nz), 0) < cy - 1
    totals = [jnp.zeros((8, nz), jnp.float32) for _ in range(3)]
    flux_x = [None] * 3
    for x in range(cx):
        nu = visc[x]
        spin = [vort[c, x] for c in range(3)]
        mean_y = jnp.where(has_ahead, 0.5 * (nu + ahead(nu, 0)), 0.0)
        mean_z = 0.5 * (nu + ahead(nu, 1))
        half_y = 0.5 * spin[1]
        half_z = 0.5 * spin[2]
        next_y = jnp.where(has_ahead, ahead(half_y, 0), 0.0)
        next_z = ahead(half_z, 1)
        half_y = jnp.where(has_ahead, half_y, 0.0)
        half_x = 0.5 * spin[0]
        if x < cx - 1:
            mean_x = 0.5 * (nu + visc[x + 1])
        for c in range(3):
            w = spin[c]
            u = velo[c, x]
            flux_y = mean_y * (ahead(w, 0) - w)
            flux_z = mean_z * (ahead(w, 1) - w)
            change = flux_y + half_y * ahead(u, 0) - behind(flux_y + next_y * u, 0)
            change = change + (flux_z + half_z * ahead(u, 1) - behind(flux_z + next_z * u, 1))
            if x == 0:
                change = change + half_x * velo[c, x + 1]
            elif x == cx - 1:
                change = change - half_x * velo[c, x - 1]
            else:
                change = change + half_x * (velo[c, x + 1] - velo[c, x - 1])
            if x > 0:
                change = change - flux_x[c]
            if x < cx - 1:
                flux_x[c] = mean_x * (vort[c, x + 1] - w)
                change = change + flux_x[c]
            new = w + TIME_STEP * change
            out[c, x] = new
            totals[c] = totals[c] + jnp.sum(new.reshape(cy // 8, 8, nz), axis=0)
    return [jnp.sum(total, axis=0, keepdims=True) for total in totals]


def by_level(totals, width):
    nz = totals[0].shape[1]
    shape = (nz, width)
    level = lax.broadcasted_iota(jnp.int32, shape, 0) // CB
    lane = lax.broadcasted_iota(jnp.int32, shape, 1)
    pick = (lane == lax.axis_index("slab") * (nz // CB) + level).astype(jnp.float32).astype(jnp.bfloat16)
    rows = jnp.concatenate(totals + [jnp.zeros_like(totals[0])], axis=0)
    found = jnp.dot(jnp.concatenate(thirds(rows), axis=0), pick, preferred_element_type=jnp.float32)
    return found[0:4] + (found[4:8] + found[8:12])


def inner_kernel(vort, velo, visc, tiles_in, out, moments, tiles, sem):
    copy = pltpu.make_async_copy(tiles_in, tiles, sem)
    copy.start()
    own = by_level(interior_step(vort, velo, visc, out), moments.shape[1])
    copy.wait()
    moments[...] = tiles[...] + own


def inner(vort, velo, visc, tiles):
    return pl.pallas_call(
        inner_kernel,
        out_shape=(shaped(*vort.shape), shaped(*tiles.shape)),
        in_specs=[VMEM] * 3 + [ANY],
        out_specs=(VMEM,) * 2,
        scratch_shapes=[pltpu.VMEM(tiles.shape, jnp.float32), pltpu.SemaphoreType.DMA],
        compiler_params=PARAMS,
    )(vort, velo, visc, tiles)


def face_change(own, other, along, sign, c):
    stretch = (0.5 * sign) * own[along] * other[3 + c]
    diffuse = 0.5 * (own[6] + other[6]) * (other[c] - own[c])
    return TIME_STEP * (stretch + diffuse)


def edge_kernel(
    inside, moments, near, far, swap, other, near_in, far_in, swap_in, other_in, out, load_out, load, side_change, sem
):
    _, cx, cy, nz = out.shape
    even = lax.axis_index("pencil") % 2 == 0
    low, low_in = jnp.where(even, other[...], swap[...]), jnp.where(even, other_in[...], swap_in[...])
    high, high_in = jnp.where(even, swap[...], other[...]), jnp.where(even, swap_in[...], other_in[...])
    even = lax.axis_index("slab") % 2 == 0
    near_at, far_at = jnp.where(even, cx - 1, 0), jnp.where(even, 0, cx - 1)
    near_sign = jnp.where(even, 1.0, -1.0)
    totals = []
    for c in range(3):
        total = jnp.zeros((8, nz), jnp.float32)
        for own, came, at, sign in ((near, near_in, near_at, near_sign), (far, far_in, far_at, -near_sign)):
            change = face_change(own, came, 0, sign, c)
            out[c, at] = inside[c, at] + change
            total = total + jnp.sum(change.reshape(cy // 8, 8, nz), axis=0)
        for k, own, came, sign in ((0, low, low_in, -1.0), (1, high, high_in, 1.0)):
            change = face_change(own, came, 1, sign, c)
            side_change[k, c] = change
            total = total + change
        totals.append(jnp.sum(total, axis=0, keepdims=True))
    moment = moments[...] + by_level(totals, moments.shape[1])
    for k in range(load.shape[1] // 4):
        part = moment[:, k * LANES : (k + 1) * LANES]
        load[:, 4 * k : 4 * k + 4, :] = jnp.broadcast_to(part[None], (load.shape[0], 4, LANES))
    copy = pltpu.make_async_copy(load, load_out, sem)
    copy.start()
    for c in range(3):
        out[c, 1 : cx - 1] = inside[c, 1 : cx - 1]
        for k, at in ((0, 0), (1, cy - 1)):
            for x in range(cx):
                out[c, x, at : at + 1, :] = out[c, x, at : at + 1, :] + side_change[k, c, x : x + 1, :]
    copy.wait()


def edges(inside, moments, faces, halos, n_all):
    _, cx, _, nz = inside.shape
    load = shaped(n_all, 4 * moments.shape[1] // LANES, LANES)
    return pl.pallas_call(
        edge_kernel,
        out_shape=(shaped(*inside.shape), load),
        in_specs=[VMEM] * 10,
        out_specs=(VMEM, ANY),
        scratch_shapes=[
            pltpu.VMEM(load.shape, jnp.float32),
            pltpu.VMEM((2, 3, cx, nz), jnp.float32),
            pltpu.SemaphoreType.DMA,
        ],
        compiler_params=PARAMS,
    )(inside, moments, *faces, *halos)


def far_kernel(cx, cy, ncl, n_pencil, load, out):
    n_all = load.shape[0]
    n_slab = n_all // n_pencil
    slab = lax.axis_index("slab")
    pencil = lax.axis_index("pencil")
    shape = (ncl, n_slab * ncl)
    target = lax.broadcasted_iota(jnp.int32, shape, 0)
    source = lax.broadcasted_iota(jnp.int32, shape, 1)
    sigma = jnp.float32(cx * n_slab // 4)
    rel_x = ((slab - source // ncl) * cx).astype(jnp.float32)
    rel_z = ((target - source % ncl) * CB).astype(jnp.float32)
    flat = rel_x * rel_x + rel_z * rel_z + sigma * sigma
    turned = [jnp.zeros(shape, jnp.float32) for _ in range(3)]
    for p in range(n_pencil):
        total = load[p]
        for s in range(1, n_slab):
            total = total + load[s * n_pencil + p]
        moment = jnp.concatenate([total[4 * k : 4 * k + 4] for k in range(load.shape[1] // 4)], axis=1)
        first, second, third = moment[0:1], moment[1:2], moment[2:3]
        rel_y = ((pencil - p) * cy).astype(jnp.float32)
        inverse = lax.rsqrt(flat + rel_y * rel_y)
        weight = inverse * inverse * inverse
        turned[0] = turned[0] + weight * (rel_z * second - rel_y * third)
        turned[1] = turned[1] + weight * (rel_x * third - rel_z * first)
        turned[2] = turned[2] + weight * (rel_y * first - rel_x * second)
    pieces = jnp.concatenate(thirds(jnp.concatenate(turned, axis=0)), axis=1)
    ones = jnp.ones((16, pieces.shape[1]), jnp.bfloat16)
    rows = lax.dot_general(ones, pieces, (((1,), (1,)), ((), ())), preferred_element_type=jnp.float32)
    for c in range(3):
        out[c, 0] = rows[0:1, c * ncl : (c + 1) * ncl]


def far(load, cx, cy, ncl, n_pencil):
    return pl.pallas_call(
        functools.partial(far_kernel, cx, cy, ncl, n_pencil),
        out_shape=shaped(3, 1, 1, ncl),
        in_specs=[VMEM],
        out_specs=VMEM,
        compiler_params=PARAMS,
    )(load)


def deposit_step(group, first, listed, load, order, acc, shape):
    cx, cy, nz = shape
    rows = cx * cy // 2
    wide = group * load.shape[2]

    def numbers(length):
        shape = (length // 16, 16, wide)
        return (lax.broadcasted_iota(jnp.int32, shape, 0) * 16 + lax.broadcasted_iota(jnp.int32, shape, 1)).astype(
            jnp.float32
        ).astype(jnp.bfloat16)

    def spread(row):
        return jnp.broadcast_to(row, (16, wide)).astype(jnp.bfloat16)[None]

    zero = jnp.zeros((), jnp.bfloat16)
    one = jnp.ones((), jnp.bfloat16)
    block = jnp.concatenate([load[order[first + k]] for k in range(group)], axis=1)
    live = lax.broadcasted_iota(jnp.int32, (1, wide), 1) // load.shape[2] < listed - first
    cell = block[3:4, :].astype(jnp.int32) % (cx * cy * nz)
    row = cell // nz
    half = row // rows
    at_row = numbers(rows) == spread(jnp.where(live, row % rows, -1).astype(jnp.float32))
    right = []
    for h in range(2):
        at_col = numbers(nz) == spread(jnp.where(half == h, cell % nz, -1).astype(jnp.float32))
        right.append(jnp.where(at_col, one, zero).reshape(nz, wide))
    left = []
    for piece in split(block):
        for c in range(3):
            left.append(jnp.where(at_row, spread(piece[c : c + 1, :]), zero).reshape(rows, wide))
    added = lax.dot_general(
        jnp.concatenate(left, axis=0),
        jnp.concatenate(right, axis=0),
        (((1,), (1,)), ((), ())),
        preferred_element_type=jnp.float32,
    )
    acc[...] += added[: 3 * rows] + added[3 * rows :]


def deposit_kernel(cap, inside, load, out, acc, order, made, sems):
    _, cx, cy, nz = out.shape
    shape = (cx, cy, nz)
    acc[...] = jnp.zeros_like(acc)
    listed = jnp.int32(0)
    for d in range(load.shape[0] // cap):
        first = d * cap
        held = jnp.max(load[first, 3:4, :]).astype(jnp.int32) // (cx * cy * nz)
        for k in range(cap):
            order[listed + k] = first + k
        listed = listed + held
    for k in range(GROUP):
        order[listed + k] = 0
    rest = listed % GROUP
    whole = listed // GROUP + (rest > GROUP // 2).astype(jnp.int32)

    def step(g, carry):
        deposit_step(GROUP, g * GROUP, listed, load, order, acc, shape)
        return carry

    lax.fori_loop(0, whole, step, 0)

    @pl.when((rest > 0) & (rest <= GROUP // 2))
    def _():
        deposit_step(GROUP // 2, whole * GROUP, listed, load, order, acc, shape)

    copies = Copies(sems)
    rows = cx * cy // 2
    for c in range(3):
        for h in range(2):
            span = slice(h * (cx // 2), (h + 1) * (cx // 2))
            change = acc[c * rows : (c + 1) * rows, h * nz : (h + 1) * nz].reshape(cx // 2, cy, nz)
            made[c, span] = inside[c, span] + change
            copies.start(made.at[c, span], out.at[c, span])
    copies.wait(0, 6)


def deposit(inside, load, cap):
    return pl.pallas_call(
        functools.partial(deposit_kernel, cap),
        out_shape=shaped(*inside.shape),
        in_specs=[VMEM] * 2,
        out_specs=ANY,
        scratch_shapes=[
            pltpu.VMEM((3 * inside.shape[1] * inside.shape[2] // 2, 2 * inside.shape[3]), jnp.float32),
            pltpu.SMEM((load.shape[0] + max(cap, GROUP),), jnp.int32),
            pltpu.VMEM(inside.shape, jnp.float32),
            pltpu.SemaphoreType.DMA((6,)),
        ],
        compiler_params=PARAMS,
    )(inside, load)


def swapped(array, axis, first):
    up = [(i, i + 1) for i in range(first, lax.axis_size(axis) - 1, 2)]
    return lax.ppermute(array, axis, up + [(j, i) for i, j in up])


def per_device(vorticity, velocity, viscosity, tile_weights, tile_cells, tile_dest, tile_count):
    _, cx, cy, nz = vorticity.shape
    ncl = nz // CB
    n_slab = lax.axis_size("slab")
    n_pencil = lax.axis_size("pencil")
    cap = 2 * tile_weights.shape[0] // n_slab
    weights = jnp.transpose(tile_weights, (1, 0, 2))
    count = tile_count
    *faces, packets, tiles = to_send(
        vorticity, velocity, viscosity, weights, tile_cells, tile_dest.T, count, n_slab, cap
    )
    halos = [swapped(face, axis, k % 2) for k, (face, axis) in enumerate(zip(faces, SIDES))]
    arrived = lax.all_to_all(packets, "slab", 0, 0, tiled=True)
    inside, moments = inner(vorticity, velocity, viscosity, tiles)
    advanced, load = edges(inside, moments, faces, halos, n_slab * n_pencil)
    load = lax.all_to_all(load, ("slab", "pencil"), 0, 0, tiled=True)
    vorticity_out = deposit(advanced, arrived, cap)
    return (vorticity_out, far(load, cx, cy, ncl, n_pencil))


def solution(mesh):
    in_specs = (
        P(None, "slab", "pencil", None),
        P(None, "slab", "pencil", None),
        P("slab", "pencil", None),
        P(("slab", "pencil"), None, None),
        P(("slab", "pencil"), None),
        P(("slab", "pencil"), None),
        P(("slab", "pencil")),
    )
    out_specs = (P(None, "slab", "pencil", None), P(None, "slab", "pencil", None))
    return jax.shard_map(
        per_device, mesh=mesh, in_specs=in_specs, out_specs=out_specs, check_vma=False
    )
```

```python
import functools

import jax
import jax.numpy as jnp
from jax import lax
from jax.experimental import pallas as pl
from jax.experimental.pallas import tpu as pltpu
from jax.sharding import PartitionSpec as P

CB = 16
TIME_STEP = 0.1
LANES = 128
SIDES = ("slab", "slab", "pencil", "pencil")
GROUP = 16
VMEM_LIMIT = 24 * 1024 * 1024

VMEM = pl.BlockSpec(memory_space=pltpu.VMEM)
ANY = pl.BlockSpec(memory_space=pl.ANY)
SMEM = pl.BlockSpec(memory_space=pltpu.SMEM)
FIRST_PARAMS = pltpu.CompilerParams(vmem_limit_bytes=60 * 1024 * 1024)
PARAMS = pltpu.CompilerParams(vmem_limit_bytes=VMEM_LIMIT)


def shaped(*shape):
    return jax.ShapeDtypeStruct(shape, jnp.float32)


def split(w):
    high = w.astype(jnp.bfloat16).astype(jnp.float32)
    return high, w - high


def thirds(w):
    high, rest = split(w)
    middle, low = split(rest)
    return [piece.astype(jnp.bfloat16) for piece in (high, middle, low)]


def outward(count):
    half = count // 2
    return [half + k // 2 if k % 2 else half - 1 - k // 2 for k in range(count)]


def pack_tiles(cap, cells_dev, weights, cells, dest, count, packets):
    slots = packets.shape[0]
    tiles = cells.shape[0]
    half = slots // cap // 2
    names = dest[...]
    names = jnp.where(names < half, 2 * (half - 1 - names), 2 * (names - half) + 1)
    live = (lax.broadcasted_iota(jnp.int32, (1, tiles), 1) < count[0]).astype(jnp.float32)
    same = (lax.broadcasted_iota(jnp.int32, (slots // cap, tiles), 0) == names).astype(jnp.float32)
    shape = (tiles, tiles)
    earlier = lax.broadcasted_iota(jnp.int32, shape, 0) < lax.broadcasted_iota(jnp.int32, shape, 1)
    before = jnp.dot(same, earlier.astype(jnp.float32), preferred_element_type=jnp.float32)
    rank = jnp.sum(same * before, axis=0, keepdims=True).astype(jnp.int32)
    slot = lax.broadcasted_iota(jnp.int32, (slots, tiles), 0)
    placed = (slot == names * cap + rank).astype(jnp.float32) * live
    held = jnp.sum((slot == names * cap).astype(jnp.float32) * live, axis=1, keepdims=True)
    rows = [weights[0], weights[1], weights[2], cells[...].astype(jnp.float32)]
    found = jnp.dot(
        jnp.concatenate([placed] * 3, axis=1).astype(jnp.bfloat16),
        jnp.concatenate(thirds(jnp.concatenate(rows, axis=1)), axis=0),
        preferred_element_type=jnp.float32,
    )
    length = cells.shape[1]
    for c in range(3):
        packets[:, c, :] = found[:, c * length : (c + 1) * length]
    packets[:, 3, :] = found[:, 3 * length :] + held * cells_dev


def tile_moments(cap, nz, packets, moments):
    n_slab = packets.shape[0] // cap
    ncl = nz // CB
    wide = cap * packets.shape[2]
    level = lax.broadcasted_iota(jnp.int32, (ncl, wide), 0)
    found = []
    order = outward(n_slab)
    for d in range(n_slab):
        block = jnp.concatenate([packets[order.index(d) * cap + k] for k in range(cap)], axis=1)
        cell = block[3:4, :].astype(jnp.int32)
        spots = (level == cell % nz // CB).astype(jnp.float32).astype(jnp.bfloat16)
        high, low = split(block)
        left = jnp.concatenate([high, low], axis=0).astype(jnp.bfloat16)
        sums = lax.dot_general(left, spots, (((1,), (1,)), ((), ())), preferred_element_type=jnp.float32)
        found.append(sums[0:4] + sums[4:8])
    moments[...] = jnp.concatenate(found, axis=1)


class Copies:
    def __init__(self, sems):
        self.sems = sems
        self.made = []

    def start(self, source, target):
        self.made.append(pltpu.make_async_copy(source, target, self.sems.at[len(self.made)]))
        self.made[-1].start()

    def wait(self, first, last):
        for k in range(first, last):
            self.made[k].wait()


def send_kernel(
    cap,
    vort,
    velo,
    visc,
    weights_in,
    cells_in,
    dest_in,
    count_in,
    near_out,
    far_out,
    swap_out,
    other_out,
    packets_out,
    moments_out,
    near,
    far,
    swap,
    other,
    packets,
    moments,
    weights,
    cells,
    dest,
    count,
    sems,
):
    cx, cy, nz = visc.shape
    copies = Copies(sems)
    copies.start(weights_in, weights)
    copies.start(cells_in, cells)
    copies.start(dest_in, dest)
    copies.start(count_in, count)
    even = lax.axis_index("slab") % 2 == 0
    for face, at in ((near, jnp.where(even, cx - 1, 0)), (far, jnp.where(even, 0, cx - 1))):
        copies.start(vort.at[:, at], face.at[0:3])
        copies.start(velo.at[:, at], face.at[3:6])
        copies.start(visc.at[at], face.at[6])
    even = lax.axis_index("pencil") % 2 == 0
    for face, at in ((swap, jnp.where(even, cy - 1, 0)), (other, jnp.where(even, 0, cy - 1))):
        copies.start(vort.at[:, :, at], face.at[0:3])
        copies.start(velo.at[:, :, at], face.at[3:6])
        copies.start(visc.at[:, at], face.at[6])
    copies.wait(0, 4)
    pack_tiles(cap, cx * cy * nz, weights, cells, dest, count, packets)
    copies.start(packets, packets_out)
    copies.wait(4, 10)
    copies.start(near, near_out)
    copies.start(far, far_out)
    tile_moments(cap, nz, packets, moments)
    copies.start(moments, moments_out)
    copies.wait(10, 16)
    copies.start(swap, swap_out)
    copies.start(other, other_out)
    copies.wait(16, 22)


def to_send(vort, velo, visc, weights, cells, dest, count, n_slab, cap):
    _, cx, cy, nz = vort.shape
    made = (
        shaped(7, cy, nz),
        shaped(7, cy, nz),
        shaped(7, cx, nz),
        shaped(7, cx, nz),
        shaped(n_slab * cap, 4, weights.shape[2]),
        shaped(4, n_slab * nz // CB),
    )
    return pl.pallas_call(
        functools.partial(send_kernel, cap),
        out_shape=made,
        in_specs=[ANY] * 7,
        out_specs=(ANY,) * 6,
        scratch_shapes=[pltpu.VMEM(one.shape, jnp.float32) for one in made]
        + [
            pltpu.VMEM(weights.shape, jnp.float32),
            pltpu.VMEM(cells.shape, jnp.int32),
            pltpu.VMEM(dest.shape, jnp.int32),
            pltpu.SMEM(count.shape, jnp.int32),
            pltpu.SemaphoreType.DMA((22,)),
        ],
        compiler_params=FIRST_PARAMS,
    )(vort, velo, visc, weights, cells, dest, count)


def ahead(a, axis):
    return pltpu.roll(a, a.shape[axis] - 1, axis)


def behind(a, axis):
    return pltpu.roll(a, 1, axis)


def interior_step(vort, velo, visc, out):
    cx, cy, nz = visc.shape
    has_ahead = lax.broadcasted_iota(jnp.int32, (cy, nz), 0) < cy - 1
    totals = [jnp.zeros((8, nz), jnp.float32) for _ in range(3)]
    flux_x = [None] * 3
    for x in range(cx):
        nu = visc[x]
        spin = [vort[c, x] for c in range(3)]
        mean_y = jnp.where(has_ahead, 0.5 * (nu + ahead(nu, 0)), 0.0)
        mean_z = 0.5 * (nu + ahead(nu, 1))
        half_y = 0.5 * spin[1]
        half_z = 0.5 * spin[2]
        next_y = jnp.where(has_ahead, ahead(half_y, 0), 0.0)
        next_z = ahead(half_z, 1)
        half_y = jnp.where(has_ahead, half_y, 0.0)
        half_x = 0.5 * spin[0]
        if x < cx - 1:
            mean_x = 0.5 * (nu + visc[x + 1])
        for c in range(3):
            w = spin[c]
            u = velo[c, x]
            flux_y = mean_y * (ahead(w, 0) - w)
            flux_z = mean_z * (ahead(w, 1) - w)
            change = flux_y + half_y * ahead(u, 0) - behind(flux_y + next_y * u, 0)
            change = change + (flux_z + half_z * ahead(u, 1) - behind(flux_z + next_z * u, 1))
            if x == 0:
                change = change + half_x * velo[c, x + 1]
            elif x == cx - 1:
                change = change - half_x * velo[c, x - 1]
            else:
                change = change + half_x * (velo[c, x + 1] - velo[c, x - 1])
            if x > 0:
                change = change - flux_x[c]
            if x < cx - 1:
                flux_x[c] = mean_x * (vort[c, x + 1] - w)
                change = change + flux_x[c]
            new = w + TIME_STEP * change
            out[c, x] = new
            totals[c] = totals[c] + jnp.sum(new.reshape(cy // 8, 8, nz), axis=0)
    return [jnp.sum(total, axis=0, keepdims=True) for total in totals]


def by_level(totals, width):
    nz = totals[0].shape[1]
    shape = (nz, width)
    level = lax.broadcasted_iota(jnp.int32, shape, 0) // CB
    lane = lax.broadcasted_iota(jnp.int32, shape, 1)
    pick = (lane == lax.axis_index("slab") * (nz // CB) + level).astype(jnp.float32).astype(jnp.bfloat16)
    rows = jnp.concatenate(totals + [jnp.zeros_like(totals[0])], axis=0)
    found = jnp.dot(jnp.concatenate(thirds(rows), axis=0), pick, preferred_element_type=jnp.float32)
    return found[0:4] + (found[4:8] + found[8:12])


def inner_kernel(vort, velo, visc, tiles_in, out, moments, tiles, sem):
    copy = pltpu.make_async_copy(tiles_in, tiles, sem)
    copy.start()
    own = by_level(interior_step(vort, velo, visc, out), moments.shape[1])
    copy.wait()
    moments[...] = tiles[...] + own


def inner(vort, velo, visc, tiles):
    return pl.pallas_call(
        inner_kernel,
        out_shape=(shaped(*vort.shape), shaped(*tiles.shape)),
        in_specs=[VMEM] * 3 + [ANY],
        out_specs=(VMEM,) * 2,
        scratch_shapes=[pltpu.VMEM(tiles.shape, jnp.float32), pltpu.SemaphoreType.DMA],
        compiler_params=PARAMS,
    )(vort, velo, visc, tiles)


def face_change(own, other, along, sign, c):
    stretch = (0.5 * sign) * own[along] * other[3 + c]
    diffuse = 0.5 * (own[6] + other[6]) * (other[c] - own[c])
    return TIME_STEP * (stretch + diffuse)


def edge_kernel(
    inside, moments, near, far, swap, other, near_in, far_in, swap_in, other_in, out, load_out, load, side_change, sem
):
    _, cx, cy, nz = out.shape
    even = lax.axis_index("pencil") % 2 == 0
    low, low_in = jnp.where(even, other[...], swap[...]), jnp.where(even, other_in[...], swap_in[...])
    high, high_in = jnp.where(even, swap[...], other[...]), jnp.where(even, swap_in[...], other_in[...])
    even = lax.axis_index("slab") % 2 == 0
    near_at, far_at = jnp.where(even, cx - 1, 0), jnp.where(even, 0, cx - 1)
    near_sign = jnp.where(even, 1.0, -1.0)
    totals = []
    for c in range(3):
        total = jnp.zeros((8, nz), jnp.float32)
        for own, came, at, sign in ((near, near_in, near_at, near_sign), (far, far_in, far_at, -near_sign)):
            change = face_change(own, came, 0, sign, c)
            out[c, at] = inside[c, at] + change
            total = total + jnp.sum(change.reshape(cy // 8, 8, nz), axis=0)
        for k, own, came, sign in ((0, low, low_in, -1.0), (1, high, high_in, 1.0)):
            change = face_change(own, came, 1, sign, c)
            side_change[k, c] = change
            total = total + change
        totals.append(jnp.sum(total, axis=0, keepdims=True))
    moment = moments[...] + by_level(totals, moments.shape[1])
    for k in range(load.shape[1] // 4):
        part = moment[:, k * LANES : (k + 1) * LANES]
        load[:, 4 * k : 4 * k + 4, :] = jnp.broadcast_to(part[None], (load.shape[0], 4, LANES))
    copy = pltpu.make_async_copy(load, load_out, sem)
    copy.start()
    for c in range(3):
        out[c, 1 : cx - 1] = inside[c, 1 : cx - 1]
        for k, at in ((0, 0), (1, cy - 1)):
            for x in range(cx):
                out[c, x, at : at + 1, :] = out[c, x, at : at + 1, :] + side_change[k, c, x : x + 1, :]
    copy.wait()


def edges(inside, moments, faces, halos, n_all):
    _, cx, _, nz = inside.shape
    load = shaped(n_all, 4 * moments.shape[1] // LANES, LANES)
    return pl.pallas_call(
        edge_kernel,
        out_shape=(shaped(*inside.shape), load),
        in_specs=[VMEM] * 10,
        out_specs=(VMEM, ANY),
        scratch_shapes=[
            pltpu.VMEM(load.shape, jnp.float32),
            pltpu.VMEM((2, 3, cx, nz), jnp.float32),
            pltpu.SemaphoreType.DMA,
        ],
        compiler_params=PARAMS,
    )(inside, moments, *faces, *halos)


def far_kernel(cx, cy, ncl, n_pencil, load, out):
    n_all = load.shape[0]
    n_slab = n_all // n_pencil
    slab = lax.axis_index("slab")
    pencil = lax.axis_index("pencil")
    shape = (ncl, n_slab * ncl)
    target = lax.broadcasted_iota(jnp.int32, shape, 0)
    source = lax.broadcasted_iota(jnp.int32, shape, 1)
    sigma = jnp.float32(cx * n_slab // 4)
    rel_x = ((slab - source // ncl) * cx).astype(jnp.float32)
    rel_z = ((target - source % ncl) * CB).astype(jnp.float32)
    flat = rel_x * rel_x + rel_z * rel_z + sigma * sigma
    turned = [jnp.zeros(shape, jnp.float32) for _ in range(3)]
    for p in range(n_pencil):
        total = load[p]
        for s in range(1, n_slab):
            total = total + load[s * n_pencil + p]
        moment = jnp.concatenate([total[4 * k : 4 * k + 4] for k in range(load.shape[1] // 4)], axis=1)
        first, second, third = moment[0:1], moment[1:2], moment[2:3]
        rel_y = ((pencil - p) * cy).astype(jnp.float32)
        inverse = lax.rsqrt(flat + rel_y * rel_y)
        weight = inverse * inverse * inverse
        turned[0] = turned[0] + weight * (rel_z * second - rel_y * third)
        turned[1] = turned[1] + weight * (rel_x * third - rel_z * first)
        turned[2] = turned[2] + weight * (rel_y * first - rel_x * second)
    pieces = jnp.concatenate(thirds(jnp.concatenate(turned, axis=0)), axis=1)
    ones = jnp.ones((16, pieces.shape[1]), jnp.bfloat16)
    rows = lax.dot_general(ones, pieces, (((1,), (1,)), ((), ())), preferred_element_type=jnp.float32)
    for c in range(3):
        out[c, 0] = rows[0:1, c * ncl : (c + 1) * ncl]


def far(load, cx, cy, ncl, n_pencil):
    return pl.pallas_call(
        functools.partial(far_kernel, cx, cy, ncl, n_pencil),
        out_shape=shaped(3, 1, 1, ncl),
        in_specs=[VMEM],
        out_specs=VMEM,
        compiler_params=PARAMS,
    )(load)


def deposit_step(group, first, listed, load, order, acc, shape):
    cx, cy, nz = shape
    rows = cx * cy // 2
    wide = group * load.shape[2]

    def numbers(length):
        shape = (length // 16, 16, wide)
        return (lax.broadcasted_iota(jnp.int32, shape, 0) * 16 + lax.broadcasted_iota(jnp.int32, shape, 1)).astype(
            jnp.float32
        ).astype(jnp.bfloat16)

    def spread(row):
        return jnp.broadcast_to(row, (16, wide)).astype(jnp.bfloat16)[None]

    zero = jnp.zeros((), jnp.bfloat16)
    one = jnp.ones((), jnp.bfloat16)
    block = jnp.concatenate([load[order[first + k]] for k in range(group)], axis=1)
    live = lax.broadcasted_iota(jnp.int32, (1, wide), 1) // load.shape[2] < listed - first
    cell = block[3:4, :].astype(jnp.int32) % (cx * cy * nz)
    row = cell // nz
    half = row // rows
    at_row = numbers(rows) == spread(jnp.where(live, row % rows, -1).astype(jnp.float32))
    right = []
    for h in range(2):
        at_col = numbers(nz) == spread(jnp.where(half == h, cell % nz, -1).astype(jnp.float32))
        right.append(jnp.where(at_col, one, zero).reshape(nz, wide))
    left = []
    for piece in split(block):
        for c in range(3):
            left.append(jnp.where(at_row, spread(piece[c : c + 1, :]), zero).reshape(rows, wide))
    added = lax.dot_general(
        jnp.concatenate(left, axis=0),
        jnp.concatenate(right, axis=0),
        (((1,), (1,)), ((), ())),
        preferred_element_type=jnp.float32,
    )
    acc[...] += added[: 3 * rows] + added[3 * rows :]


def deposit_kernel(cap, inside, load, out, acc, order, made, sems):
    _, cx, cy, nz = out.shape
    shape = (cx, cy, nz)
    acc[...] = jnp.zeros_like(acc)
    listed = jnp.int32(0)
    for d in range(load.shape[0] // cap):
        first = d * cap
        held = jnp.max(load[first, 3:4, :]).astype(jnp.int32) // (cx * cy * nz)
        for k in range(cap):
            order[listed + k] = first + k
        listed = listed + held
    for k in range(GROUP):
        order[listed + k] = 0
    rest = listed % GROUP
    whole = listed // GROUP + (rest > GROUP // 2).astype(jnp.int32)

    def step(g, carry):
        deposit_step(GROUP, g * GROUP, listed, load, order, acc, shape)
        return carry

    lax.fori_loop(0, whole, step, 0)

    @pl.when((rest > 0) & (rest <= GROUP // 2))
    def _():
        deposit_step(GROUP // 2, whole * GROUP, listed, load, order, acc, shape)

    copies = Copies(sems)
    rows = cx * cy // 2
    for c in range(3):
        for h in range(2):
            span = slice(h * (cx // 2), (h + 1) * (cx // 2))
            change = acc[c * rows : (c + 1) * rows, h * nz : (h + 1) * nz].reshape(cx // 2, cy, nz)
            made[c, span] = inside[c, span] + change
            copies.start(made.at[c, span], out.at[c, span])
    copies.wait(0, 6)


def deposit(inside, load, cap):
    return pl.pallas_call(
        functools.partial(deposit_kernel, cap),
        out_shape=shaped(*inside.shape),
        in_specs=[VMEM] * 2,
        out_specs=ANY,
        scratch_shapes=[
            pltpu.VMEM((3 * inside.shape[1] * inside.shape[2] // 2, 2 * inside.shape[3]), jnp.float32),
            pltpu.SMEM((load.shape[0] + max(cap, GROUP),), jnp.int32),
            pltpu.VMEM(inside.shape, jnp.float32),
            pltpu.SemaphoreType.DMA((6,)),
        ],
        compiler_params=PARAMS,
    )(inside, load)


def swapped(array, axis, first):
    up = [(i, i + 1) for i in range(first, lax.axis_size(axis) - 1, 2)]
    return lax.ppermute(array, axis, up + [(j, i) for i, j in up])


def per_device(vorticity, velocity, viscosity, tile_weights, tile_cells, tile_dest, tile_count):
    _, cx, cy, nz = vorticity.shape
    ncl = nz // CB
    n_slab = lax.axis_size("slab")
    n_pencil = lax.axis_size("pencil")
    cap = 2 * tile_weights.shape[0] // n_slab
    weights = jnp.transpose(tile_weights, (1, 0, 2))
    count = tile_count
    *faces, packets, tiles = to_send(
        vorticity, velocity, viscosity, weights, tile_cells, tile_dest.T, count, n_slab, cap
    )
    halos = [swapped(face, axis, k % 2) for k, (face, axis) in enumerate(zip(faces, SIDES))]
    order = outward(n_slab)
    arrived = lax.all_to_all(packets, "slab", 0, 0, axis_index_groups=[order], tiled=True)
    inside, moments = inner(vorticity, velocity, viscosity, tiles)
    advanced, load = edges(inside, moments, faces, halos, n_slab * n_pencil)
    everyone = [s * n_pencil + p for s in order for p in range(n_pencil)]
    load = lax.all_to_all(load, ("slab", "pencil"), 0, 0, axis_index_groups=[everyone], tiled=True)
    vorticity_out = deposit(advanced, arrived, cap)
    return (vorticity_out, far(load, cx, cy, ncl, n_pencil))


def solution(mesh):
    in_specs = (
        P(None, "slab", "pencil", None),
        P(None, "slab", "pencil", None),
        P("slab", "pencil", None),
        P(("slab", "pencil"), None, None),
        P(("slab", "pencil"), None),
        P(("slab", "pencil"), None),
        P(("slab", "pencil")),
    )
    out_specs = (P(None, "slab", "pencil", None), P(None, "slab", "pencil", None))
    return jax.shard_map(
        per_device, mesh=mesh, in_specs=in_specs, out_specs=out_specs, check_vma=False
    )
```

```python
import functools

import jax
import jax.numpy as jnp
from jax import lax
from jax.experimental import pallas as pl
from jax.experimental.pallas import tpu as pltpu
from jax.sharding import PartitionSpec as P

CB = 16
TIME_STEP = 0.1
LANES = 128
SIDES = ("slab", "slab", "pencil", "pencil")
GROUP = 16
VMEM_LIMIT = 24 * 1024 * 1024

VMEM = pl.BlockSpec(memory_space=pltpu.VMEM)
ANY = pl.BlockSpec(memory_space=pl.ANY)
SMEM = pl.BlockSpec(memory_space=pltpu.SMEM)
FIRST_PARAMS = pltpu.CompilerParams(vmem_limit_bytes=60 * 1024 * 1024)
PARAMS = pltpu.CompilerParams(vmem_limit_bytes=VMEM_LIMIT)


def shaped(*shape):
    return jax.ShapeDtypeStruct(shape, jnp.float32)


def split(w):
    high = w.astype(jnp.bfloat16).astype(jnp.float32)
    return high, w - high


def thirds(w):
    high, rest = split(w)
    middle, low = split(rest)
    return [piece.astype(jnp.bfloat16) for piece in (high, middle, low)]


def outward(count):
    half = count // 2
    return [half - 1 - k // 2 if k % 2 else half + k // 2 for k in range(count)]


def pack_tiles(cap, cells_dev, weights, cells, dest, count, packets):
    slots = packets.shape[0]
    tiles = cells.shape[0]
    half = slots // cap // 2
    names = dest[...]
    names = jnp.where(names < half, 2 * (half - 1 - names) + 1, 2 * (names - half))
    live = (lax.broadcasted_iota(jnp.int32, (1, tiles), 1) < count[0]).astype(jnp.float32)
    same = (lax.broadcasted_iota(jnp.int32, (slots // cap, tiles), 0) == names).astype(jnp.float32)
    shape = (tiles, tiles)
    earlier = lax.broadcasted_iota(jnp.int32, shape, 0) < lax.broadcasted_iota(jnp.int32, shape, 1)
    before = jnp.dot(same, earlier.astype(jnp.float32), preferred_element_type=jnp.float32)
    rank = jnp.sum(same * before, axis=0, keepdims=True).astype(jnp.int32)
    slot = lax.broadcasted_iota(jnp.int32, (slots, tiles), 0)
    placed = (slot == names * cap + rank).astype(jnp.float32) * live
    held = jnp.sum((slot == names * cap).astype(jnp.float32) * live, axis=1, keepdims=True)
    rows = [weights[0], weights[1], weights[2], cells[...].astype(jnp.float32)]
    found = jnp.dot(
        jnp.concatenate([placed] * 3, axis=1).astype(jnp.bfloat16),
        jnp.concatenate(thirds(jnp.concatenate(rows, axis=1)), axis=0),
        preferred_element_type=jnp.float32,
    )
    length = cells.shape[1]
    for c in range(3):
        packets[:, c, :] = found[:, c * length : (c + 1) * length]
    packets[:, 3, :] = found[:, 3 * length :] + held * cells_dev


def tile_moments(cap, nz, packets, moments):
    n_slab = packets.shape[0] // cap
    ncl = nz // CB
    wide = cap * packets.shape[2]
    level = lax.broadcasted_iota(jnp.int32, (ncl, wide), 0)
    found = []
    order = outward(n_slab)
    for d in range(n_slab):
        block = jnp.concatenate([packets[order.index(d) * cap + k] for k in range(cap)], axis=1)
        cell = block[3:4, :].astype(jnp.int32)
        spots = (level == cell % nz // CB).astype(jnp.float32).astype(jnp.bfloat16)
        high, low = split(block)
        left = jnp.concatenate([high, low], axis=0).astype(jnp.bfloat16)
        sums = lax.dot_general(left, spots, (((1,), (1,)), ((), ())), preferred_element_type=jnp.float32)
        found.append(sums[0:4] + sums[4:8])
    moments[...] = jnp.concatenate(found, axis=1)


class Copies:
    def __init__(self, sems):
        self.sems = sems
        self.made = []

    def start(self, source, target):
        self.made.append(pltpu.make_async_copy(source, target, self.sems.at[len(self.made)]))
        self.made[-1].start()

    def wait(self, first, last):
        for k in range(first, last):
            self.made[k].wait()


def send_kernel(
    cap,
    vort,
    velo,
    visc,
    weights_in,
    cells_in,
    dest_in,
    count_in,
    near_out,
    far_out,
    swap_out,
    other_out,
    packets_out,
    moments_out,
    near,
    far,
    swap,
    other,
    packets,
    moments,
    weights,
    cells,
    dest,
    count,
    sems,
):
    cx, cy, nz = visc.shape
    copies = Copies(sems)
    copies.start(weights_in, weights)
    copies.start(cells_in, cells)
    copies.start(dest_in, dest)
    copies.start(count_in, count)
    even = lax.axis_index("slab") % 2 == 0
    for face, at in ((near, jnp.where(even, cx - 1, 0)), (far, jnp.where(even, 0, cx - 1))):
        copies.start(vort.at[:, at], face.at[0:3])
        copies.start(velo.at[:, at], face.at[3:6])
        copies.start(visc.at[at], face.at[6])
    even = lax.axis_index("pencil") % 2 == 0
    for face, at in ((swap, jnp.where(even, cy - 1, 0)), (other, jnp.where(even, 0, cy - 1))):
        copies.start(vort.at[:, :, at], face.at[0:3])
        copies.start(velo.at[:, :, at], face.at[3:6])
        copies.start(visc.at[:, at], face.at[6])
    copies.wait(0, 4)
    pack_tiles(cap, cx * cy * nz, weights, cells, dest, count, packets)
    copies.start(packets, packets_out)
    copies.wait(4, 10)
    copies.start(near, near_out)
    copies.start(far, far_out)
    tile_moments(cap, nz, packets, moments)
    copies.start(moments, moments_out)
    copies.wait(10, 16)
    copies.start(swap, swap_out)
    copies.start(other, other_out)
    copies.wait(16, 22)


def to_send(vort, velo, visc, weights, cells, dest, count, n_slab, cap):
    _, cx, cy, nz = vort.shape
    made = (
        shaped(7, cy, nz),
        shaped(7, cy, nz),
        shaped(7, cx, nz),
        shaped(7, cx, nz),
        shaped(n_slab * cap, 4, weights.shape[2]),
        shaped(4, n_slab * nz // CB),
    )
    return pl.pallas_call(
        functools.partial(send_kernel, cap),
        out_shape=made,
        in_specs=[ANY] * 7,
        out_specs=(ANY,) * 6,
        scratch_shapes=[pltpu.VMEM(one.shape, jnp.float32) for one in made]
        + [
            pltpu.VMEM(weights.shape, jnp.float32),
            pltpu.VMEM(cells.shape, jnp.int32),
            pltpu.VMEM(dest.shape, jnp.int32),
            pltpu.SMEM(count.shape, jnp.int32),
            pltpu.SemaphoreType.DMA((22,)),
        ],
        compiler_params=FIRST_PARAMS,
    )(vort, velo, visc, weights, cells, dest, count)


def ahead(a, axis):
    return pltpu.roll(a, a.shape[axis] - 1, axis)


def behind(a, axis):
    return pltpu.roll(a, 1, axis)


def interior_step(vort, velo, visc, out):
    cx, cy, nz = visc.shape
    has_ahead = lax.broadcasted_iota(jnp.int32, (cy, nz), 0) < cy - 1
    totals = [jnp.zeros((8, nz), jnp.float32) for _ in range(3)]
    flux_x = [None] * 3
    for x in range(cx):
        nu = visc[x]
        spin = [vort[c, x] for c in range(3)]
        mean_y = jnp.where(has_ahead, 0.5 * (nu + ahead(nu, 0)), 0.0)
        mean_z = 0.5 * (nu + ahead(nu, 1))
        half_y = 0.5 * spin[1]
        half_z = 0.5 * spin[2]
        next_y = jnp.where(has_ahead, ahead(half_y, 0), 0.0)
        next_z = ahead(half_z, 1)
        half_y = jnp.where(has_ahead, half_y, 0.0)
        half_x = 0.5 * spin[0]
        if x < cx - 1:
            mean_x = 0.5 * (nu + visc[x + 1])
        for c in range(3):
            w = spin[c]
            u = velo[c, x]
            flux_y = mean_y * (ahead(w, 0) - w)
            flux_z = mean_z * (ahead(w, 1) - w)
            change = flux_y + half_y * ahead(u, 0) - behind(flux_y + next_y * u, 0)
            change = change + (flux_z + half_z * ahead(u, 1) - behind(flux_z + next_z * u, 1))
            if x == 0:
                change = change + half_x * velo[c, x + 1]
            elif x == cx - 1:
                change = change - half_x * velo[c, x - 1]
            else:
                change = change + half_x * (velo[c, x + 1] - velo[c, x - 1])
            if x > 0:
                change = change - flux_x[c]
            if x < cx - 1:
                flux_x[c] = mean_x * (vort[c, x + 1] - w)
                change = change + flux_x[c]
            new = w + TIME_STEP * change
            out[c, x] = new
            totals[c] = totals[c] + jnp.sum(new.reshape(cy // 8, 8, nz), axis=0)
    return [jnp.sum(total, axis=0, keepdims=True) for total in totals]


def by_level(totals, width):
    nz = totals[0].shape[1]
    shape = (nz, width)
    level = lax.broadcasted_iota(jnp.int32, shape, 0) // CB
    lane = lax.broadcasted_iota(jnp.int32, shape, 1)
    pick = (lane == lax.axis_index("slab") * (nz // CB) + level).astype(jnp.float32).astype(jnp.bfloat16)
    rows = jnp.concatenate(totals + [jnp.zeros_like(totals[0])], axis=0)
    found = jnp.dot(jnp.concatenate(thirds(rows), axis=0), pick, preferred_element_type=jnp.float32)
    return found[0:4] + (found[4:8] + found[8:12])


def inner_kernel(vort, velo, visc, tiles_in, out, moments, tiles, sem):
    copy = pltpu.make_async_copy(tiles_in, tiles, sem)
    copy.start()
    own = by_level(interior_step(vort, velo, visc, out), moments.shape[1])
    copy.wait()
    moments[...] = tiles[...] + own


def inner(vort, velo, visc, tiles):
    return pl.pallas_call(
        inner_kernel,
        out_shape=(shaped(*vort.shape), shaped(*tiles.shape)),
        in_specs=[VMEM] * 3 + [ANY],
        out_specs=(VMEM,) * 2,
        scratch_shapes=[pltpu.VMEM(tiles.shape, jnp.float32), pltpu.SemaphoreType.DMA],
        compiler_params=PARAMS,
    )(vort, velo, visc, tiles)


def face_change(own, other, along, sign, c):
    stretch = (0.5 * sign) * own[along] * other[3 + c]
    diffuse = 0.5 * (own[6] + other[6]) * (other[c] - own[c])
    return TIME_STEP * (stretch + diffuse)


def edge_kernel(
    inside, moments, near, far, swap, other, near_in, far_in, swap_in, other_in, out, load_out, load, side_change, sem
):
    _, cx, cy, nz = out.shape
    even = lax.axis_index("pencil") % 2 == 0
    low, low_in = jnp.where(even, other[...], swap[...]), jnp.where(even, other_in[...], swap_in[...])
    high, high_in = jnp.where(even, swap[...], other[...]), jnp.where(even, swap_in[...], other_in[...])
    even = lax.axis_index("slab") % 2 == 0
    near_at, far_at = jnp.where(even, cx - 1, 0), jnp.where(even, 0, cx - 1)
    near_sign = jnp.where(even, 1.0, -1.0)
    totals = []
    for c in range(3):
        total = jnp.zeros((8, nz), jnp.float32)
        for own, came, at, sign in ((near, near_in, near_at, near_sign), (far, far_in, far_at, -near_sign)):
            change = face_change(own, came, 0, sign, c)
            out[c, at] = inside[c, at] + change
            total = total + jnp.sum(change.reshape(cy // 8, 8, nz), axis=0)
        for k, own, came, sign in ((0, low, low_in, -1.0), (1, high, high_in, 1.0)):
            change = face_change(own, came, 1, sign, c)
            side_change[k, c] = change
            total = total + change
        totals.append(jnp.sum(total, axis=0, keepdims=True))
    moment = moments[...] + by_level(totals, moments.shape[1])
    for k in range(load.shape[1] // 4):
        part = moment[:, k * LANES : (k + 1) * LANES]
        load[:, 4 * k : 4 * k + 4, :] = jnp.broadcast_to(part[None], (load.shape[0], 4, LANES))
    copy = pltpu.make_async_copy(load, load_out, sem)
    copy.start()
    for c in range(3):
        out[c, 1 : cx - 1] = inside[c, 1 : cx - 1]
        for k, at in ((0, 0), (1, cy - 1)):
            for x in range(cx):
                out[c, x, at : at + 1, :] = out[c, x, at : at + 1, :] + side_change[k, c, x : x + 1, :]
    copy.wait()


def edges(inside, moments, faces, halos, n_all):
    _, cx, _, nz = inside.shape
    load = shaped(n_all, 4 * moments.shape[1] // LANES, LANES)
    return pl.pallas_call(
        edge_kernel,
        out_shape=(shaped(*inside.shape), load),
        in_specs=[VMEM] * 10,
        out_specs=(VMEM, ANY),
        scratch_shapes=[
            pltpu.VMEM(load.shape, jnp.float32),
            pltpu.VMEM((2, 3, cx, nz), jnp.float32),
            pltpu.SemaphoreType.DMA,
        ],
        compiler_params=PARAMS,
    )(inside, moments, *faces, *halos)


def far_kernel(cx, cy, ncl, n_pencil, load, out):
    n_all = load.shape[0]
    n_slab = n_all // n_pencil
    slab = lax.axis_index("slab")
    pencil = lax.axis_index("pencil")
    shape = (ncl, n_slab * ncl)
    target = lax.broadcasted_iota(jnp.int32, shape, 0)
    source = lax.broadcasted_iota(jnp.int32, shape, 1)
    sigma = jnp.float32(cx * n_slab // 4)
    rel_x = ((slab - source // ncl) * cx).astype(jnp.float32)
    rel_z = ((target - source % ncl) * CB).astype(jnp.float32)
    flat = rel_x * rel_x + rel_z * rel_z + sigma * sigma
    turned = [jnp.zeros(shape, jnp.float32) for _ in range(3)]
    for p in range(n_pencil):
        total = load[p]
        for s in range(1, n_slab):
            total = total + load[s * n_pencil + p]
        moment = jnp.concatenate([total[4 * k : 4 * k + 4] for k in range(load.shape[1] // 4)], axis=1)
        first, second, third = moment[0:1], moment[1:2], moment[2:3]
        rel_y = ((pencil - p) * cy).astype(jnp.float32)
        inverse = lax.rsqrt(flat + rel_y * rel_y)
        weight = inverse * inverse * inverse
        turned[0] = turned[0] + weight * (rel_z * second - rel_y * third)
        turned[1] = turned[1] + weight * (rel_x * third - rel_z * first)
        turned[2] = turned[2] + weight * (rel_y * first - rel_x * second)
    pieces = jnp.concatenate(thirds(jnp.concatenate(turned, axis=0)), axis=1)
    ones = jnp.ones((16, pieces.shape[1]), jnp.bfloat16)
    rows = lax.dot_general(ones, pieces, (((1,), (1,)), ((), ())), preferred_element_type=jnp.float32)
    for c in range(3):
        out[c, 0] = rows[0:1, c * ncl : (c + 1) * ncl]


def far(load, cx, cy, ncl, n_pencil):
    return pl.pallas_call(
        functools.partial(far_kernel, cx, cy, ncl, n_pencil),
        out_shape=shaped(3, 1, 1, ncl),
        in_specs=[VMEM],
        out_specs=VMEM,
        compiler_params=PARAMS,
    )(load)


def deposit_step(group, first, listed, load, order, acc, shape):
    cx, cy, nz = shape
    rows = cx * cy // 2
    wide = group * load.shape[2]

    def numbers(length):
        shape = (length // 16, 16, wide)
        return (lax.broadcasted_iota(jnp.int32, shape, 0) * 16 + lax.broadcasted_iota(jnp.int32, shape, 1)).astype(
            jnp.float32
        ).astype(jnp.bfloat16)

    def spread(row):
        return jnp.broadcast_to(row, (16, wide)).astype(jnp.bfloat16)[None]

    zero = jnp.zeros((), jnp.bfloat16)
    one = jnp.ones((), jnp.bfloat16)
    block = jnp.concatenate([load[order[first + k]] for k in range(group)], axis=1)
    live = lax.broadcasted_iota(jnp.int32, (1, wide), 1) // load.shape[2] < listed - first
    cell = block[3:4, :].astype(jnp.int32) % (cx * cy * nz)
    row = cell // nz
    half = row // rows
    at_row = numbers(rows) == spread(jnp.where(live, row % rows, -1).astype(jnp.float32))
    right = []
    for h in range(2):
        at_col = numbers(nz) == spread(jnp.where(half == h, cell % nz, -1).astype(jnp.float32))
        right.append(jnp.where(at_col, one, zero).reshape(nz, wide))
    left = []
    for piece in split(block):
        for c in range(3):
            left.append(jnp.where(at_row, spread(piece[c : c + 1, :]), zero).reshape(rows, wide))
    added = lax.dot_general(
        jnp.concatenate(left, axis=0),
        jnp.concatenate(right, axis=0),
        (((1,), (1,)), ((), ())),
        preferred_element_type=jnp.float32,
    )
    acc[...] += added[: 3 * rows] + added[3 * rows :]


def deposit_kernel(cap, inside, load, out, acc, order, made, sems):
    _, cx, cy, nz = out.shape
    shape = (cx, cy, nz)
    acc[...] = jnp.zeros_like(acc)
    listed = jnp.int32(0)
    for d in range(load.shape[0] // cap):
        first = d * cap
        held = jnp.max(load[first, 3:4, :]).astype(jnp.int32) // (cx * cy * nz)
        for k in range(cap):
            order[listed + k] = first + k
        listed = listed + held
    for k in range(GROUP):
        order[listed + k] = 0
    rest = listed % GROUP
    whole = listed // GROUP + (rest > GROUP // 2).astype(jnp.int32)

    def step(g, carry):
        deposit_step(GROUP, g * GROUP, listed, load, order, acc, shape)
        return carry

    lax.fori_loop(0, whole, step, 0)

    @pl.when((rest > 0) & (rest <= GROUP // 2))
    def _():
        deposit_step(GROUP // 2, whole * GROUP, listed, load, order, acc, shape)

    copies = Copies(sems)
    rows = cx * cy // 2
    for c in range(3):
        for h in range(2):
            span = slice(h * (cx // 2), (h + 1) * (cx // 2))
            change = acc[c * rows : (c + 1) * rows, h * nz : (h + 1) * nz].reshape(cx // 2, cy, nz)
            made[c, span] = inside[c, span] + change
            copies.start(made.at[c, span], out.at[c, span])
    copies.wait(0, 6)


def deposit(inside, load, cap):
    return pl.pallas_call(
        functools.partial(deposit_kernel, cap),
        out_shape=shaped(*inside.shape),
        in_specs=[VMEM] * 2,
        out_specs=ANY,
        scratch_shapes=[
            pltpu.VMEM((3 * inside.shape[1] * inside.shape[2] // 2, 2 * inside.shape[3]), jnp.float32),
            pltpu.SMEM((load.shape[0] + max(cap, GROUP),), jnp.int32),
            pltpu.VMEM(inside.shape, jnp.float32),
            pltpu.SemaphoreType.DMA((6,)),
        ],
        compiler_params=PARAMS,
    )(inside, load)


def swapped(array, axis, first):
    up = [(i, i + 1) for i in range(first, lax.axis_size(axis) - 1, 2)]
    return lax.ppermute(array, axis, up + [(j, i) for i, j in up])


def per_device(vorticity, velocity, viscosity, tile_weights, tile_cells, tile_dest, tile_count):
    _, cx, cy, nz = vorticity.shape
    ncl = nz // CB
    n_slab = lax.axis_size("slab")
    n_pencil = lax.axis_size("pencil")
    cap = 2 * tile_weights.shape[0] // n_slab
    weights = jnp.transpose(tile_weights, (1, 0, 2))
    count = tile_count
    *faces, packets, tiles = to_send(
        vorticity, velocity, viscosity, weights, tile_cells, tile_dest.T, count, n_slab, cap
    )
    halos = [swapped(face, axis, k % 2) for k, (face, axis) in enumerate(zip(faces, SIDES))]
    order = outward(n_slab)
    arrived = lax.all_to_all(packets, "slab", 0, 0, axis_index_groups=[order], tiled=True)
    inside, moments = inner(vorticity, velocity, viscosity, tiles)
    advanced, load = edges(inside, moments, faces, halos, n_slab * n_pencil)
    everyone = [s * n_pencil + p for s in order for p in range(n_pencil)]
    load = lax.all_to_all(load, ("slab", "pencil"), 0, 0, axis_index_groups=[everyone], tiled=True)
    vorticity_out = deposit(advanced, arrived, cap)
    return (vorticity_out, far(load, cx, cy, ncl, n_pencil))


def solution(mesh):
    in_specs = (
        P(None, "slab", "pencil", None),
        P(None, "slab", "pencil", None),
        P("slab", "pencil", None),
        P(("slab", "pencil"), None, None),
        P(("slab", "pencil"), None),
        P(("slab", "pencil"), None),
        P(("slab", "pencil")),
    )
    out_specs = (P(None, "slab", "pencil", None), P(None, "slab", "pencil", None))
    return jax.shard_map(
        per_device, mesh=mesh, in_specs=in_specs, out_specs=out_specs, check_vma=False
    )
```

```python
import functools

import jax
import jax.numpy as jnp
from jax import lax
from jax.experimental import pallas as pl
from jax.experimental.pallas import tpu as pltpu
from jax.sharding import PartitionSpec as P

CB = 16
TIME_STEP = 0.1
LANES = 128
SIDES = ("slab", "slab", "pencil", "pencil")
GROUP = 16
VMEM_LIMIT = 24 * 1024 * 1024

VMEM = pl.BlockSpec(memory_space=pltpu.VMEM)
ANY = pl.BlockSpec(memory_space=pl.ANY)
SMEM = pl.BlockSpec(memory_space=pltpu.SMEM)
FIRST_PARAMS = pltpu.CompilerParams(vmem_limit_bytes=60 * 1024 * 1024)
PARAMS = pltpu.CompilerParams(vmem_limit_bytes=VMEM_LIMIT)


def shaped(*shape):
    return jax.ShapeDtypeStruct(shape, jnp.float32)


def split(w):
    high = w.astype(jnp.bfloat16).astype(jnp.float32)
    return high, w - high


def thirds(w):
    high, rest = split(w)
    middle, low = split(rest)
    return [piece.astype(jnp.bfloat16) for piece in (high, middle, low)]


def outward(count):
    half = count // 2
    return [half - 1 - k // 2 if k % 2 else half + k // 2 for k in range(count)]


def pack_tiles(cap, cells_dev, weights, cells, dest, count, packets):
    slots = packets.shape[0]
    tiles = cells.shape[0]
    half = slots // cap // 2
    names = dest[...]
    names = jnp.where(names < half, 2 * (half - 1 - names) + 1, 2 * (names - half))
    live = (lax.broadcasted_iota(jnp.int32, (1, tiles), 1) < count[0]).astype(jnp.float32)
    same = (lax.broadcasted_iota(jnp.int32, (slots // cap, tiles), 0) == names).astype(jnp.float32)
    shape = (tiles, tiles)
    earlier = lax.broadcasted_iota(jnp.int32, shape, 0) < lax.broadcasted_iota(jnp.int32, shape, 1)
    before = jnp.dot(same, earlier.astype(jnp.float32), preferred_element_type=jnp.float32)
    rank = jnp.sum(same * before, axis=0, keepdims=True).astype(jnp.int32)
    slot = lax.broadcasted_iota(jnp.int32, (slots, tiles), 0)
    placed = (slot == names * cap + rank).astype(jnp.float32) * live
    held = jnp.sum((slot == names * cap).astype(jnp.float32) * live, axis=1, keepdims=True)
    rows = [weights[0], weights[1], weights[2], cells[...].astype(jnp.float32)]
    found = jnp.dot(
        jnp.concatenate([placed] * 3, axis=1).astype(jnp.bfloat16),
        jnp.concatenate(thirds(jnp.concatenate(rows, axis=1)), axis=0),
        preferred_element_type=jnp.float32,
    )
    length = cells.shape[1]
    for c in range(3):
        packets[:, c, :] = found[:, c * length : (c + 1) * length]
    packets[:, 3, :] = found[:, 3 * length :] + held * cells_dev


def tile_moments(cap, nz, packets, moments):
    n_slab = packets.shape[0] // cap
    ncl = nz // CB
    wide = cap * packets.shape[2]
    level = lax.broadcasted_iota(jnp.int32, (ncl, wide), 0)
    found = []
    order = outward(n_slab)
    for d in range(n_slab):
        block = jnp.concatenate([packets[order.index(d) * cap + k] for k in range(cap)], axis=1)
        cell = block[3:4, :].astype(jnp.int32)
        spots = (level == cell % nz // CB).astype(jnp.float32).astype(jnp.bfloat16)
        high, low = split(block)
        left = jnp.concatenate([high, low], axis=0).astype(jnp.bfloat16)
        sums = lax.dot_general(left, spots, (((1,), (1,)), ((), ())), preferred_element_type=jnp.float32)
        found.append(sums[0:4] + sums[4:8])
    moments[...] = jnp.concatenate(found, axis=1)


class Copies:
    def __init__(self, sems):
        self.sems = sems
        self.made = []

    def start(self, source, target):
        self.made.append(pltpu.make_async_copy(source, target, self.sems.at[len(self.made)]))
        self.made[-1].start()

    def wait(self, first, last):
        for k in range(first, last):
            self.made[k].wait()


def send_kernel(
    cap,
    vort,
    velo,
    visc,
    weights_in,
    cells_in,
    dest_in,
    count_in,
    near_out,
    far_out,
    swap_out,
    other_out,
    packets_out,
    moments_out,
    near,
    far,
    swap,
    other,
    packets,
    moments,
    weights,
    cells,
    dest,
    count,
    sems,
):
    cx, cy, nz = visc.shape
    copies = Copies(sems)
    copies.start(weights_in, weights)
    copies.start(cells_in, cells)
    copies.start(dest_in, dest)
    copies.start(count_in, count)
    even = lax.axis_index("slab") % 2 == 0
    for face, at in ((near, jnp.where(even, cx - 1, 0)), (far, jnp.where(even, 0, cx - 1))):
        copies.start(vort.at[:, at], face.at[0:3])
        copies.start(velo.at[:, at], face.at[3:6])
        copies.start(visc.at[at], face.at[6])
    even = lax.axis_index("pencil") % 2 == 0
    for face, at in ((swap, jnp.where(even, cy - 1, 0)), (other, jnp.where(even, 0, cy - 1))):
        copies.start(vort.at[:, :, at], face.at[0:3])
        copies.start(velo.at[:, :, at], face.at[3:6])
        copies.start(visc.at[:, at], face.at[6])
    copies.wait(0, 4)
    pack_tiles(cap, cx * cy * nz, weights, cells, dest, count, packets)
    copies.start(packets, packets_out)
    copies.wait(4, 10)
    copies.start(near, near_out)
    copies.start(far, far_out)
    tile_moments(cap, nz, packets, moments)
    copies.start(moments, moments_out)
    copies.wait(10, 16)
    copies.start(swap, swap_out)
    copies.start(other, other_out)
    copies.wait(16, 22)


def to_send(vort, velo, visc, weights, cells, dest, count, n_slab, cap):
    _, cx, cy, nz = vort.shape
    made = (
        shaped(7, cy, nz),
        shaped(7, cy, nz),
        shaped(7, cx, nz),
        shaped(7, cx, nz),
        shaped(n_slab * cap, 4, weights.shape[2]),
        shaped(4, n_slab * nz // CB),
    )
    return pl.pallas_call(
        functools.partial(send_kernel, cap),
        out_shape=made,
        in_specs=[ANY] * 7,
        out_specs=(ANY,) * 6,
        scratch_shapes=[pltpu.VMEM(one.shape, jnp.float32) for one in made]
        + [
            pltpu.VMEM(weights.shape, jnp.float32),
            pltpu.VMEM(cells.shape, jnp.int32),
            pltpu.VMEM(dest.shape, jnp.int32),
            pltpu.SMEM(count.shape, jnp.int32),
            pltpu.SemaphoreType.DMA((22,)),
        ],
        compiler_params=FIRST_PARAMS,
    )(vort, velo, visc, weights, cells, dest, count)


def ahead(a, axis):
    return pltpu.roll(a, a.shape[axis] - 1, axis)


def behind(a, axis):
    return pltpu.roll(a, 1, axis)


def interior_step(vort, velo, visc, out):
    cx, cy, nz = visc.shape
    has_ahead = lax.broadcasted_iota(jnp.int32, (cy, nz), 0) < cy - 1
    totals = [jnp.zeros((8, nz), jnp.float32) for _ in range(3)]
    for x in range(cx):
        nu = visc[x]
        half = 0.5 * vort[1, x]
        mean = jnp.where(has_ahead, 0.5 * (nu + ahead(nu, 0)), 0.0)
        shifted = jnp.where(has_ahead, ahead(half, 0), 0.0)
        half = jnp.where(has_ahead, half, 0.0)
        for c in range(3):
            w, u = vort[c, x], velo[c, x]
            flux = mean * (ahead(w, 0) - w)
            out[c, x] = flux + half * ahead(u, 0) - behind(flux + shifted * u, 0)
        half = 0.5 * vort[2, x]
        mean = 0.5 * (nu + ahead(nu, 1))
        shifted = ahead(half, 1)
        for c in range(3):
            w, u = vort[c, x], velo[c, x]
            flux = mean * (ahead(w, 1) - w)
            out[c, x] = out[c, x] + (flux + half * ahead(u, 1) - behind(flux + shifted * u, 1))
        half = 0.5 * vort[0, x]
        for c in range(3):
            w = vort[c, x]
            change = out[c, x]
            if x < cx - 1:
                mean = 0.5 * (nu + visc[x + 1])
                change = change + half * velo[c, x + 1] + mean * (vort[c, x + 1] - w)
            if x > 0:
                mean = 0.5 * (nu + visc[x - 1])
                change = change - half * velo[c, x - 1] + mean * (vort[c, x - 1] - w)
            new = w + TIME_STEP * change
            out[c, x] = new
            totals[c] = totals[c] + jnp.sum(new.reshape(cy // 8, 8, nz), axis=0)
    return [jnp.sum(total, axis=0, keepdims=True) for total in totals]


def by_level(totals, width):
    nz = totals[0].shape[1]
    shape = (nz, width)
    level = lax.broadcasted_iota(jnp.int32, shape, 0) // CB
    lane = lax.broadcasted_iota(jnp.int32, shape, 1)
    pick = (lane == lax.axis_index("slab") * (nz // CB) + level).astype(jnp.float32).astype(jnp.bfloat16)
    rows = jnp.concatenate(totals + [jnp.zeros_like(totals[0])], axis=0)
    found = jnp.dot(jnp.concatenate(thirds(rows), axis=0), pick, preferred_element_type=jnp.float32)
    return found[0:4] + (found[4:8] + found[8:12])


def inner_kernel(vort, velo, visc, tiles_in, out, moments, tiles, sem):
    copy = pltpu.make_async_copy(tiles_in, tiles, sem)
    copy.start()
    own = by_level(interior_step(vort, velo, visc, out), moments.shape[1])
    copy.wait()
    moments[...] = tiles[...] + own


def inner(vort, velo, visc, tiles):
    return pl.pallas_call(
        inner_kernel,
        out_shape=(shaped(*vort.shape), shaped(*tiles.shape)),
        in_specs=[VMEM] * 3 + [ANY],
        out_specs=(VMEM,) * 2,
        scratch_shapes=[pltpu.VMEM(tiles.shape, jnp.float32), pltpu.SemaphoreType.DMA],
        compiler_params=PARAMS,
    )(vort, velo, visc, tiles)


def face_change(own, other, along, sign, c):
    stretch = (0.5 * sign) * own[along] * other[3 + c]
    diffuse = 0.5 * (own[6] + other[6]) * (other[c] - own[c])
    return TIME_STEP * (stretch + diffuse)


def edge_kernel(
    inside, moments, near, far, swap, other, near_in, far_in, swap_in, other_in, out, load_out, load, side_change, sem
):
    _, cx, cy, nz = out.shape
    even = lax.axis_index("pencil") % 2 == 0
    low, low_in = jnp.where(even, other[...], swap[...]), jnp.where(even, other_in[...], swap_in[...])
    high, high_in = jnp.where(even, swap[...], other[...]), jnp.where(even, swap_in[...], other_in[...])
    even = lax.axis_index("slab") % 2 == 0
    near_at, far_at = jnp.where(even, cx - 1, 0), jnp.where(even, 0, cx - 1)
    near_sign = jnp.where(even, 1.0, -1.0)
    totals = []
    for c in range(3):
        total = jnp.zeros((8, nz), jnp.float32)
        for own, came, at, sign in ((near, near_in, near_at, near_sign), (far, far_in, far_at, -near_sign)):
            change = face_change(own, came, 0, sign, c)
            out[c, at] = inside[c, at] + change
            total = total + jnp.sum(change.reshape(cy // 8, 8, nz), axis=0)
        for k, own, came, sign in ((0, low, low_in, -1.0), (1, high, high_in, 1.0)):
            change = face_change(own, came, 1, sign, c)
            side_change[k, c] = change
            total = total + change
        totals.append(jnp.sum(total, axis=0, keepdims=True))
    moment = moments[...] + by_level(totals, moments.shape[1])
    for k in range(load.shape[1] // 4):
        part = moment[:, k * LANES : (k + 1) * LANES]
        load[:, 4 * k : 4 * k + 4, :] = jnp.broadcast_to(part[None], (load.shape[0], 4, LANES))
    copy = pltpu.make_async_copy(load, load_out, sem)
    copy.start()
    for c in range(3):
        out[c, 1 : cx - 1] = inside[c, 1 : cx - 1]
        for k, at in ((0, 0), (1, cy - 1)):
            for x in range(cx):
                out[c, x, at : at + 1, :] = out[c, x, at : at + 1, :] + side_change[k, c, x : x + 1, :]
    copy.wait()


def edges(inside, moments, faces, halos, n_all):
    _, cx, _, nz = inside.shape
    load = shaped(n_all, 4 * moments.shape[1] // LANES, LANES)
    return pl.pallas_call(
        edge_kernel,
        out_shape=(shaped(*inside.shape), load),
        in_specs=[VMEM] * 10,
        out_specs=(VMEM, ANY),
        scratch_shapes=[
            pltpu.VMEM(load.shape, jnp.float32),
            pltpu.VMEM((2, 3, cx, nz), jnp.float32),
            pltpu.SemaphoreType.DMA,
        ],
        compiler_params=PARAMS,
    )(inside, moments, *faces, *halos)


def far_kernel(cx, cy, ncl, n_pencil, load, out):
    n_all = load.shape[0]
    n_slab = n_all // n_pencil
    slab = lax.axis_index("slab")
    pencil = lax.axis_index("pencil")
    shape = (ncl, n_slab * ncl)
    target = lax.broadcasted_iota(jnp.int32, shape, 0)
    source = lax.broadcasted_iota(jnp.int32, shape, 1)
    sigma = jnp.float32(cx * n_slab // 4)
    rel_x = ((slab - source // ncl) * cx).astype(jnp.float32)
    rel_z = ((target - source % ncl) * CB).astype(jnp.float32)
    flat = rel_x * rel_x + rel_z * rel_z + sigma * sigma
    turned = [jnp.zeros(shape, jnp.float32) for _ in range(3)]
    for p in range(n_pencil):
        total = load[p]
        for s in range(1, n_slab):
            total = total + load[s * n_pencil + p]
        moment = jnp.concatenate([total[4 * k : 4 * k + 4] for k in range(load.shape[1] // 4)], axis=1)
        first, second, third = moment[0:1], moment[1:2], moment[2:3]
        rel_y = ((pencil - p) * cy).astype(jnp.float32)
        inverse = lax.rsqrt(flat + rel_y * rel_y)
        weight = inverse * inverse * inverse
        turned[0] = turned[0] + weight * (rel_z * second - rel_y * third)
        turned[1] = turned[1] + weight * (rel_x * third - rel_z * first)
        turned[2] = turned[2] + weight * (rel_y * first - rel_x * second)
    pieces = jnp.concatenate(thirds(jnp.concatenate(turned, axis=0)), axis=1)
    ones = jnp.ones((16, pieces.shape[1]), jnp.bfloat16)
    rows = lax.dot_general(ones, pieces, (((1,), (1,)), ((), ())), preferred_element_type=jnp.float32)
    for c in range(3):
        out[c, 0] = rows[0:1, c * ncl : (c + 1) * ncl]


def far(load, cx, cy, ncl, n_pencil):
    return pl.pallas_call(
        functools.partial(far_kernel, cx, cy, ncl, n_pencil),
        out_shape=shaped(3, 1, 1, ncl),
        in_specs=[VMEM],
        out_specs=VMEM,
        compiler_params=PARAMS,
    )(load)


def deposit_step(group, first, listed, load, order, acc, shape):
    cx, cy, nz = shape
    rows = cx * cy // 2
    wide = group * load.shape[2]

    def numbers(length):
        shape = (length // 16, 16, wide)
        return (lax.broadcasted_iota(jnp.int32, shape, 0) * 16 + lax.broadcasted_iota(jnp.int32, shape, 1)).astype(
            jnp.float32
        ).astype(jnp.bfloat16)

    def spread(row):
        return jnp.broadcast_to(row, (16, wide)).astype(jnp.bfloat16)[None]

    zero = jnp.zeros((), jnp.bfloat16)
    one = jnp.ones((), jnp.bfloat16)
    block = jnp.concatenate([load[order[first + k]] for k in range(group)], axis=1)
    live = lax.broadcasted_iota(jnp.int32, (1, wide), 1) // load.shape[2] < listed - first
    cell = block[3:4, :].astype(jnp.int32) % (cx * cy * nz)
    row = cell // nz
    half = row // rows
    at_row = numbers(rows) == spread(jnp.where(live, row % rows, -1).astype(jnp.float32))
    right = []
    for h in range(2):
        at_col = numbers(nz) == spread(jnp.where(half == h, cell % nz, -1).astype(jnp.float32))
        right.append(jnp.where(at_col, one, zero).reshape(nz, wide))
    left = []
    for piece in split(block):
        for c in range(3):
            left.append(jnp.where(at_row, spread(piece[c : c + 1, :]), zero).reshape(rows, wide))
    added = lax.dot_general(
        jnp.concatenate(left, axis=0),
        jnp.concatenate(right, axis=0),
        (((1,), (1,)), ((), ())),
        preferred_element_type=jnp.float32,
    )
    acc[...] += added[: 3 * rows] + added[3 * rows :]


def deposit_kernel(cap, inside, load, out, acc, order, made, sems):
    _, cx, cy, nz = out.shape
    shape = (cx, cy, nz)
    acc[...] = jnp.zeros_like(acc)
    listed = jnp.int32(0)
    for d in range(load.shape[0] // cap):
        first = d * cap
        held = jnp.max(load[first, 3:4, :]).astype(jnp.int32) // (cx * cy * nz)
        for k in range(cap):
            order[listed + k] = first + k
        listed = listed + held
    for k in range(GROUP):
        order[listed + k] = 0
    rest = listed % GROUP
    whole = listed // GROUP + (rest > GROUP // 2).astype(jnp.int32)

    def step(g, carry):
        deposit_step(GROUP, g * GROUP, listed, load, order, acc, shape)
        return carry

    lax.fori_loop(0, whole, step, 0)

    @pl.when((rest > 0) & (rest <= GROUP // 2))
    def _():
        deposit_step(GROUP // 2, whole * GROUP, listed, load, order, acc, shape)

    copies = Copies(sems)
    rows = cx * cy // 2
    for c in range(3):
        for h in range(2):
            span = slice(h * (cx // 2), (h + 1) * (cx // 2))
            change = acc[c * rows : (c + 1) * rows, h * nz : (h + 1) * nz].reshape(cx // 2, cy, nz)
            made[c, span] = inside[c, span] + change
            copies.start(made.at[c, span], out.at[c, span])
    copies.wait(0, 6)


def deposit(inside, load, cap):
    return pl.pallas_call(
        functools.partial(deposit_kernel, cap),
        out_shape=shaped(*inside.shape),
        in_specs=[VMEM] * 2,
        out_specs=ANY,
        scratch_shapes=[
            pltpu.VMEM((3 * inside.shape[1] * inside.shape[2] // 2, 2 * inside.shape[3]), jnp.float32),
            pltpu.SMEM((load.shape[0] + max(cap, GROUP),), jnp.int32),
            pltpu.VMEM(inside.shape, jnp.float32),
            pltpu.SemaphoreType.DMA((6,)),
        ],
        compiler_params=PARAMS,
    )(inside, load)


def swapped(array, axis, first):
    up = [(i, i + 1) for i in range(first, lax.axis_size(axis) - 1, 2)]
    return lax.ppermute(array, axis, up + [(j, i) for i, j in up])


def per_device(vorticity, velocity, viscosity, tile_weights, tile_cells, tile_dest, tile_count):
    _, cx, cy, nz = vorticity.shape
    ncl = nz // CB
    n_slab = lax.axis_size("slab")
    n_pencil = lax.axis_size("pencil")
    cap = 2 * tile_weights.shape[0] // n_slab
    weights = jnp.transpose(tile_weights, (1, 0, 2))
    count = tile_count
    *faces, packets, tiles = to_send(
        vorticity, velocity, viscosity, weights, tile_cells, tile_dest.T, count, n_slab, cap
    )
    halos = [swapped(face, axis, k % 2) for k, (face, axis) in enumerate(zip(faces, SIDES))]
    order = outward(n_slab)
    arrived = lax.all_to_all(packets, "slab", 0, 0, axis_index_groups=[order], tiled=True)
    inside, moments = inner(vorticity, velocity, viscosity, tiles)
    advanced, load = edges(inside, moments, faces, halos, n_slab * n_pencil)
    everyone = [s * n_pencil + p for s in order for p in range(n_pencil)]
    load = lax.all_to_all(load, ("slab", "pencil"), 0, 0, axis_index_groups=[everyone], tiled=True)
    vorticity_out = deposit(advanced, arrived, cap)
    return (vorticity_out, far(load, cx, cy, ncl, n_pencil))


def solution(mesh):
    in_specs = (
        P(None, "slab", "pencil", None),
        P(None, "slab", "pencil", None),
        P("slab", "pencil", None),
        P(("slab", "pencil"), None, None),
        P(("slab", "pencil"), None),
        P(("slab", "pencil"), None),
        P(("slab", "pencil")),
    )
    out_specs = (P(None, "slab", "pencil", None), P(None, "slab", "pencil", None))
    return jax.shard_map(
        per_device, mesh=mesh, in_specs=in_specs, out_specs=out_specs, check_vma=False
    )
```

```python
import functools

import jax
import jax.numpy as jnp
from jax import lax
from jax.experimental import pallas as pl
from jax.experimental.pallas import tpu as pltpu
from jax.sharding import PartitionSpec as P

CB = 16
TIME_STEP = 0.1
LANES = 128
SIDES = ("slab", "slab", "pencil", "pencil")
GROUP = 16
VMEM_LIMIT = 24 * 1024 * 1024

VMEM = pl.BlockSpec(memory_space=pltpu.VMEM)
ANY = pl.BlockSpec(memory_space=pl.ANY)
SMEM = pl.BlockSpec(memory_space=pltpu.SMEM)
FIRST_PARAMS = pltpu.CompilerParams(vmem_limit_bytes=60 * 1024 * 1024)
PARAMS = pltpu.CompilerParams(vmem_limit_bytes=VMEM_LIMIT)


def shaped(*shape):
    return jax.ShapeDtypeStruct(shape, jnp.float32)


def split(w):
    high = w.astype(jnp.bfloat16).astype(jnp.float32)
    return high, w - high


def thirds(w):
    high, rest = split(w)
    middle, low = split(rest)
    return [piece.astype(jnp.bfloat16) for piece in (high, middle, low)]


def outward(count):
    half = count // 2
    return [half - 1 - k // 2 if k % 2 else half + k // 2 for k in range(count)]


def pack_tiles(cap, cells_dev, weights, cells, dest, count, packets):
    slots = packets.shape[0]
    tiles = cells.shape[0]
    half = slots // cap // 2
    names = dest[...]
    names = jnp.where(names < half, 2 * (half - 1 - names) + 1, 2 * (names - half))
    live = (lax.broadcasted_iota(jnp.int32, (1, tiles), 1) < count[0]).astype(jnp.float32)
    same = (lax.broadcasted_iota(jnp.int32, (slots // cap, tiles), 0) == names).astype(jnp.float32)
    shape = (tiles, tiles)
    earlier = lax.broadcasted_iota(jnp.int32, shape, 0) < lax.broadcasted_iota(jnp.int32, shape, 1)
    before = jnp.dot(same, earlier.astype(jnp.float32), preferred_element_type=jnp.float32)
    rank = jnp.sum(same * before, axis=0, keepdims=True).astype(jnp.int32)
    slot = lax.broadcasted_iota(jnp.int32, (slots, tiles), 0)
    placed = (slot == names * cap + rank).astype(jnp.float32) * live
    held = jnp.sum((slot == names * cap).astype(jnp.float32) * live, axis=1, keepdims=True)
    rows = [weights[0], weights[1], weights[2], cells[...].astype(jnp.float32)]
    found = jnp.dot(
        jnp.concatenate([placed] * 3, axis=1).astype(jnp.bfloat16),
        jnp.concatenate(thirds(jnp.concatenate(rows, axis=1)), axis=0),
        preferred_element_type=jnp.float32,
    )
    length = cells.shape[1]
    for c in range(3):
        packets[:, c, :] = found[:, c * length : (c + 1) * length]
    packets[:, 3, :] = found[:, 3 * length :] + held * cells_dev


def tile_moments(cap, nz, packets, moments):
    n_slab = packets.shape[0] // cap
    ncl = nz // CB
    wide = cap * packets.shape[2]
    level = lax.broadcasted_iota(jnp.int32, (ncl, wide), 0)
    found = []
    order = outward(n_slab)
    for d in range(n_slab):
        block = jnp.concatenate([packets[order.index(d) * cap + k] for k in range(cap)], axis=1)
        cell = block[3:4, :].astype(jnp.int32)
        spots = (level == cell % nz // CB).astype(jnp.float32).astype(jnp.bfloat16)
        high, low = split(block)
        left = jnp.concatenate([high, low], axis=0).astype(jnp.bfloat16)
        sums = lax.dot_general(left, spots, (((1,), (1,)), ((), ())), preferred_element_type=jnp.float32)
        found.append(sums[0:4] + sums[4:8])
    moments[...] = jnp.concatenate(found, axis=1)


class Copies:
    def __init__(self, sems):
        self.sems = sems
        self.made = []

    def start(self, source, target):
        self.made.append(pltpu.make_async_copy(source, target, self.sems.at[len(self.made)]))
        self.made[-1].start()

    def wait(self, first, last):
        for k in range(first, last):
            self.made[k].wait()


def send_kernel(
    cap,
    vort,
    velo,
    visc,
    weights_in,
    cells_in,
    dest_in,
    count_in,
    near_out,
    far_out,
    swap_out,
    other_out,
    packets_out,
    moments_out,
    near,
    far,
    swap,
    other,
    packets,
    moments,
    weights,
    cells,
    dest,
    count,
    sems,
):
    cx, cy, nz = visc.shape
    copies = Copies(sems)
    copies.start(weights_in, weights)
    copies.start(cells_in, cells)
    copies.start(dest_in, dest)
    copies.start(count_in, count)
    even = lax.axis_index("slab") % 2 == 0
    for face, at in ((near, jnp.where(even, cx - 1, 0)), (far, jnp.where(even, 0, cx - 1))):
        copies.start(vort.at[:, at], face.at[0:3])
        copies.start(velo.at[:, at], face.at[3:6])
        copies.start(visc.at[at], face.at[6])
    even = lax.axis_index("pencil") % 2 == 0
    for face, at in ((swap, jnp.where(even, cy - 1, 0)), (other, jnp.where(even, 0, cy - 1))):
        copies.start(vort.at[:, :, at], face.at[0:3])
        copies.start(velo.at[:, :, at], face.at[3:6])
        copies.start(visc.at[:, at], face.at[6])
    copies.wait(0, 4)
    pack_tiles(cap, cx * cy * nz, weights, cells, dest, count, packets)
    copies.start(packets, packets_out)
    copies.wait(4, 10)
    copies.start(near, near_out)
    copies.start(far, far_out)
    tile_moments(cap, nz, packets, moments)
    copies.start(moments, moments_out)
    copies.wait(10, 16)
    copies.start(swap, swap_out)
    copies.start(other, other_out)
    copies.wait(16, 22)


def to_send(vort, velo, visc, weights, cells, dest, count, n_slab, cap):
    _, cx, cy, nz = vort.shape
    made = (
        shaped(7, cy, nz),
        shaped(7, cy, nz),
        shaped(7, cx, nz),
        shaped(7, cx, nz),
        shaped(n_slab * cap, 4, weights.shape[2]),
        shaped(4, n_slab * nz // CB),
    )
    return pl.pallas_call(
        functools.partial(send_kernel, cap),
        out_shape=made,
        in_specs=[ANY] * 7,
        out_specs=(ANY,) * 6,
        scratch_shapes=[pltpu.VMEM(one.shape, jnp.float32) for one in made]
        + [
            pltpu.VMEM(weights.shape, jnp.float32),
            pltpu.VMEM(cells.shape, jnp.int32),
            pltpu.VMEM(dest.shape, jnp.int32),
            pltpu.SMEM(count.shape, jnp.int32),
            pltpu.SemaphoreType.DMA((22,)),
        ],
        compiler_params=FIRST_PARAMS,
    )(vort, velo, visc, weights, cells, dest, count)


def ahead(a, axis):
    return pltpu.roll(a, a.shape[axis] - 1, axis)


def behind(a, axis):
    return pltpu.roll(a, 1, axis)


def interior_step(vort, velo, visc, out):
    cx, cy, nz = visc.shape
    has_ahead = lax.broadcasted_iota(jnp.int32, (cy, nz), 0) < cy - 1
    totals = [jnp.zeros((8, nz), jnp.float32) for _ in range(3)]
    flux_x = [None] * 3
    for x in range(cx):
        nu = visc[x]
        spin = [vort[c, x] for c in range(3)]
        mean_y = jnp.where(has_ahead, 0.5 * (nu + ahead(nu, 0)), 0.0)
        mean_z = 0.5 * (nu + ahead(nu, 1))
        half_y = 0.5 * spin[1]
        half_z = 0.5 * spin[2]
        next_y = jnp.where(has_ahead, ahead(half_y, 0), 0.0)
        next_z = ahead(half_z, 1)
        half_y = jnp.where(has_ahead, half_y, 0.0)
        half_x = 0.5 * spin[0]
        if x < cx - 1:
            mean_x = 0.5 * (nu + visc[x + 1])
        for c in range(3):
            w = spin[c]
            u = velo[c, x]
            flux_y = mean_y * (ahead(w, 0) - w)
            flux_z = mean_z * (ahead(w, 1) - w)
            change = flux_y + half_y * ahead(u, 0) - behind(flux_y + next_y * u, 0)
            change = change + (flux_z + half_z * ahead(u, 1) - behind(flux_z + next_z * u, 1))
            if x == 0:
                change = change + half_x * velo[c, x + 1]
            elif x == cx - 1:
                change = change - half_x * velo[c, x - 1]
            else:
                change = change + half_x * (velo[c, x + 1] - velo[c, x - 1])
            if x > 0:
                change = change - flux_x[c]
            if x < cx - 1:
                flux_x[c] = mean_x * (vort[c, x + 1] - w)
                change = change + flux_x[c]
            new = w + TIME_STEP * change
            out[c, x] = new
            totals[c] = totals[c] + jnp.sum(new.reshape(cy // 8, 8, nz), axis=0)
    return [jnp.sum(total, axis=0, keepdims=True) for total in totals]


def by_level(totals, width):
    nz = totals[0].shape[1]
    shape = (nz, width)
    level = lax.broadcasted_iota(jnp.int32, shape, 0) // CB
    lane = lax.broadcasted_iota(jnp.int32, shape, 1)
    pick = (lane == lax.axis_index("slab") * (nz // CB) + level).astype(jnp.float32).astype(jnp.bfloat16)
    rows = jnp.concatenate(totals + [jnp.zeros_like(totals[0])], axis=0)
    found = jnp.dot(jnp.concatenate(thirds(rows), axis=0), pick, preferred_element_type=jnp.float32)
    return found[0:4] + (found[4:8] + found[8:12])


def inner_kernel(vort, velo, visc, tiles_in, out, moments, tiles, sem):
    copy = pltpu.make_async_copy(tiles_in, tiles, sem)
    copy.start()
    own = by_level(interior_step(vort, velo, visc, out), moments.shape[1])
    copy.wait()
    moments[...] = tiles[...] + own


def inner(vort, velo, visc, tiles):
    return pl.pallas_call(
        inner_kernel,
        out_shape=(shaped(*vort.shape), shaped(*tiles.shape)),
        in_specs=[VMEM] * 3 + [ANY],
        out_specs=(VMEM,) * 2,
        scratch_shapes=[pltpu.VMEM(tiles.shape, jnp.float32), pltpu.SemaphoreType.DMA],
        compiler_params=PARAMS,
    )(vort, velo, visc, tiles)


def face_change(own, other, along, sign, c):
    stretch = (0.5 * sign) * own[along] * other[3 + c]
    diffuse = 0.5 * (own[6] + other[6]) * (other[c] - own[c])
    return TIME_STEP * (stretch + diffuse)


def edge_kernel(
    inside, moments, near, far, swap, other, near_in, far_in, swap_in, other_in, out, load_out, load, side_change, sem
):
    _, cx, cy, nz = out.shape
    even = lax.axis_index("pencil") % 2 == 0
    low, low_in = jnp.where(even, other[...], swap[...]), jnp.where(even, other_in[...], swap_in[...])
    high, high_in = jnp.where(even, swap[...], other[...]), jnp.where(even, swap_in[...], other_in[...])
    even = lax.axis_index("slab") % 2 == 0
    near_at, far_at = jnp.where(even, cx - 1, 0), jnp.where(even, 0, cx - 1)
    near_sign = jnp.where(even, 1.0, -1.0)
    totals = []
    for c in range(3):
        total = jnp.zeros((8, nz), jnp.float32)
        for own, came, at, sign in ((near, near_in, near_at, near_sign), (far, far_in, far_at, -near_sign)):
            change = face_change(own, came, 0, sign, c)
            out[c, at] = inside[c, at] + change
            total = total + jnp.sum(change.reshape(cy // 8, 8, nz), axis=0)
        for k, own, came, sign in ((0, low, low_in, -1.0), (1, high, high_in, 1.0)):
            change = face_change(own, came, 1, sign, c)
            side_change[k, c] = change
            total = total + change
        totals.append(jnp.sum(total, axis=0, keepdims=True))
    moment = moments[...] + by_level(totals, moments.shape[1])
    for k in range(load.shape[1] // 4):
        part = moment[:, k * LANES : (k + 1) * LANES]
        load[:, 4 * k : 4 * k + 4, :] = jnp.broadcast_to(part[None], (load.shape[0], 4, LANES))
    copy = pltpu.make_async_copy(load, load_out, sem)
    copy.start()
    for c in range(3):
        out[c, 1 : cx - 1] = inside[c, 1 : cx - 1]
        for k, at in ((0, 0), (1, cy - 1)):
            for x in range(cx):
                out[c, x, at : at + 1, :] = out[c, x, at : at + 1, :] + side_change[k, c, x : x + 1, :]
    copy.wait()


def edges(inside, moments, faces, halos, n_all):
    _, cx, _, nz = inside.shape
    load = shaped(n_all, 4 * moments.shape[1] // LANES, LANES)
    return pl.pallas_call(
        edge_kernel,
        out_shape=(shaped(*inside.shape), load),
        in_specs=[VMEM] * 10,
        out_specs=(VMEM, ANY),
        scratch_shapes=[
            pltpu.VMEM(load.shape, jnp.float32),
            pltpu.VMEM((2, 3, cx, nz), jnp.float32),
            pltpu.SemaphoreType.DMA,
        ],
        compiler_params=PARAMS,
    )(inside, moments, *faces, *halos)


def far_kernel(cx, cy, ncl, n_pencil, load, out):
    n_all = load.shape[0]
    n_slab = n_all // n_pencil
    slab = lax.axis_index("slab")
    pencil = lax.axis_index("pencil")
    shape = (ncl, n_slab * ncl)
    target = lax.broadcasted_iota(jnp.int32, shape, 0)
    source = lax.broadcasted_iota(jnp.int32, shape, 1)
    sigma = jnp.float32(cx * n_slab // 4)
    rel_x = ((slab - source // ncl) * cx).astype(jnp.float32)
    rel_z = ((target - source % ncl) * CB).astype(jnp.float32)
    flat = rel_x * rel_x + rel_z * rel_z + sigma * sigma
    turned = [jnp.zeros(shape, jnp.float32) for _ in range(3)]
    for p in range(n_pencil):
        total = load[p]
        for s in range(1, n_slab):
            total = total + load[s * n_pencil + p]
        moment = jnp.concatenate([total[4 * k : 4 * k + 4] for k in range(load.shape[1] // 4)], axis=1)
        first, second, third = moment[0:1], moment[1:2], moment[2:3]
        rel_y = ((pencil - p) * cy).astype(jnp.float32)
        inverse = lax.rsqrt(flat + rel_y * rel_y)
        weight = inverse * inverse * inverse
        turned[0] = turned[0] + weight * (rel_z * second - rel_y * third)
        turned[1] = turned[1] + weight * (rel_x * third - rel_z * first)
        turned[2] = turned[2] + weight * (rel_y * first - rel_x * second)
    ones = jnp.ones((8, shape[1]), jnp.float32)
    for c in range(3):
        row = lax.dot_general(
            ones,
            turned[c],
            (((1,), (1,)), ((), ())),
            precision=lax.Precision.HIGHEST,
            preferred_element_type=jnp.float32,
        )
        out[c, 0] = row[0:1]


def far(load, cx, cy, ncl, n_pencil):
    return pl.pallas_call(
        functools.partial(far_kernel, cx, cy, ncl, n_pencil),
        out_shape=shaped(3, 1, 1, ncl),
        in_specs=[VMEM],
        out_specs=VMEM,
        compiler_params=PARAMS,
    )(load)


def deposit_step(group, first, listed, load, order, acc, shape):
    cx, cy, nz = shape
    rows = cx * cy // 2
    wide = group * load.shape[2]

    def numbers(length):
        shape = (length // 16, 16, wide)
        return (lax.broadcasted_iota(jnp.int32, shape, 0) * 16 + lax.broadcasted_iota(jnp.int32, shape, 1)).astype(
            jnp.float32
        ).astype(jnp.bfloat16)

    def spread(row):
        return jnp.broadcast_to(row, (16, wide)).astype(jnp.bfloat16)[None]

    zero = jnp.zeros((), jnp.bfloat16)
    one = jnp.ones((), jnp.bfloat16)
    block = jnp.concatenate([load[order[first + k]] for k in range(group)], axis=1)
    live = lax.broadcasted_iota(jnp.int32, (1, wide), 1) // load.shape[2] < listed - first
    cell = block[3:4, :].astype(jnp.int32) % (cx * cy * nz)
    row = cell // nz
    half = row // rows
    at_row = numbers(rows) == spread(jnp.where(live, row % rows, -1).astype(jnp.float32))
    right = []
    for h in range(2):
        at_col = numbers(nz) == spread(jnp.where(half == h, cell % nz, -1).astype(jnp.float32))
        right.append(jnp.where(at_col, one, zero).reshape(nz, wide))
    left = []
    for piece in split(block):
        for c in range(3):
            left.append(jnp.where(at_row, spread(piece[c : c + 1, :]), zero).reshape(rows, wide))
    added = lax.dot_general(
        jnp.concatenate(left, axis=0),
        jnp.concatenate(right, axis=0),
        (((1,), (1,)), ((), ())),
        preferred_element_type=jnp.float32,
    )
    acc[...] += (added[: 3 * rows] + added[3 * rows :]).reshape(acc.shape)


def deposit_kernel(cap, inside, load, out, acc, order, sems):
    _, cx, cy, nz = out.shape
    shape = (cx, cy, nz)
    for h in range(2):
        acc[:, :, :, h * nz : (h + 1) * nz] = inside[:, h * (cx // 2) : (h + 1) * (cx // 2)]
    listed = jnp.int32(0)
    for d in range(load.shape[0] // cap):
        first = d * cap
        held = jnp.max(load[first, 3:4, :]).astype(jnp.int32) // (cx * cy * nz)
        for k in range(cap):
            order[listed + k] = first + k
        listed = listed + held
    for k in range(GROUP):
        order[listed + k] = 0
    rest = listed % GROUP
    whole = listed // GROUP + (rest > GROUP // 2).astype(jnp.int32)

    def step(g, carry):
        deposit_step(GROUP, g * GROUP, listed, load, order, acc, shape)
        return carry

    lax.fori_loop(0, whole, step, 0)

    @pl.when((rest > 0) & (rest <= GROUP // 2))
    def _():
        deposit_step(GROUP // 2, whole * GROUP, listed, load, order, acc, shape)

    copies = Copies(sems)
    for c in range(3):
        for h in range(2):
            part = acc.at[c, :, :, h * nz : (h + 1) * nz]
            copies.start(part, out.at[c, h * (cx // 2) : (h + 1) * (cx // 2)])
    copies.wait(0, 6)


def deposit(inside, load, cap):
    return pl.pallas_call(
        functools.partial(deposit_kernel, cap),
        out_shape=shaped(*inside.shape),
        in_specs=[VMEM] * 2,
        out_specs=ANY,
        scratch_shapes=[
            pltpu.VMEM((3, inside.shape[1] // 2, inside.shape[2], 2 * inside.shape[3]), jnp.float32),
            pltpu.SMEM((load.shape[0] + max(cap, GROUP),), jnp.int32),
            pltpu.SemaphoreType.DMA((6,)),
        ],
        compiler_params=PARAMS,
    )(inside, load)


def swapped(array, axis, first):
    up = [(i, i + 1) for i in range(first, lax.axis_size(axis) - 1, 2)]
    return lax.ppermute(array, axis, up + [(j, i) for i, j in up])


def per_device(vorticity, velocity, viscosity, tile_weights, tile_cells, tile_dest, tile_count):
    _, cx, cy, nz = vorticity.shape
    ncl = nz // CB
    n_slab = lax.axis_size("slab")
    n_pencil = lax.axis_size("pencil")
    cap = 2 * tile_weights.shape[0] // n_slab
    weights = jnp.transpose(tile_weights, (1, 0, 2))
    count = tile_count
    *faces, packets, tiles = to_send(
        vorticity, velocity, viscosity, weights, tile_cells, tile_dest.T, count, n_slab, cap
    )
    halos = [swapped(face, axis, k % 2) for k, (face, axis) in enumerate(zip(faces, SIDES))]
    order = outward(n_slab)
    arrived = lax.all_to_all(packets, "slab", 0, 0, axis_index_groups=[order], tiled=True)
    inside, moments = inner(vorticity, velocity, viscosity, tiles)
    advanced, load = edges(inside, moments, faces, halos, n_slab * n_pencil)
    everyone = [s * n_pencil + p for s in order for p in range(n_pencil)]
    load = lax.all_to_all(load, ("slab", "pencil"), 0, 0, axis_index_groups=[everyone], tiled=True)
    vorticity_out = deposit(advanced, arrived, cap)
    return (vorticity_out, far(load, cx, cy, ncl, n_pencil))


def solution(mesh):
    in_specs = (
        P(None, "slab", "pencil", None),
        P(None, "slab", "pencil", None),
        P("slab", "pencil", None),
        P(("slab", "pencil"), None, None),
        P(("slab", "pencil"), None),
        P(("slab", "pencil"), None),
        P(("slab", "pencil")),
    )
    out_specs = (P(None, "slab", "pencil", None), P(None, "slab", "pencil", None))
    return jax.shard_map(
        per_device, mesh=mesh, in_specs=in_specs, out_specs=out_specs, check_vma=False
    )
```

```python
import functools

import jax
import jax.numpy as jnp
from jax import lax
from jax.experimental import pallas as pl
from jax.experimental.pallas import tpu as pltpu
from jax.sharding import PartitionSpec as P

CB = 16
TIME_STEP = 0.1
LANES = 128
SIDES = ("slab", "slab", "pencil", "pencil")
GROUP = 16
VMEM_LIMIT = 24 * 1024 * 1024

VMEM = pl.BlockSpec(memory_space=pltpu.VMEM)
ANY = pl.BlockSpec(memory_space=pl.ANY)
SMEM = pl.BlockSpec(memory_space=pltpu.SMEM)
FIRST_PARAMS = pltpu.CompilerParams(vmem_limit_bytes=60 * 1024 * 1024)
PARAMS = pltpu.CompilerParams(vmem_limit_bytes=VMEM_LIMIT)


def shaped(*shape):
    return jax.ShapeDtypeStruct(shape, jnp.float32)


def split(w):
    high = w.astype(jnp.bfloat16).astype(jnp.float32)
    return high, w - high


def thirds(w):
    high, rest = split(w)
    middle, low = split(rest)
    return [piece.astype(jnp.bfloat16) for piece in (high, middle, low)]


def outward(count):
    half = count // 2
    return [(half + (k + 1) // 2) % count if k % 2 else half - k // 2 for k in range(count)]


def pack_tiles(cap, cells_dev, weights, cells, dest, count, packets):
    slots = packets.shape[0]
    tiles = cells.shape[0]
    half = slots // cap // 2
    names = dest[...]
    names = jnp.where(names > half, 2 * (names - half) - 1, 2 * (half - names))
    names = jnp.minimum(names, 2 * half - 1)
    live = (lax.broadcasted_iota(jnp.int32, (1, tiles), 1) < count[0]).astype(jnp.float32)
    same = (lax.broadcasted_iota(jnp.int32, (slots // cap, tiles), 0) == names).astype(jnp.float32)
    shape = (tiles, tiles)
    earlier = lax.broadcasted_iota(jnp.int32, shape, 0) < lax.broadcasted_iota(jnp.int32, shape, 1)
    before = jnp.dot(same, earlier.astype(jnp.float32), preferred_element_type=jnp.float32)
    rank = jnp.sum(same * before, axis=0, keepdims=True).astype(jnp.int32)
    slot = lax.broadcasted_iota(jnp.int32, (slots, tiles), 0)
    placed = (slot == names * cap + rank).astype(jnp.float32) * live
    held = jnp.sum((slot == names * cap).astype(jnp.float32) * live, axis=1, keepdims=True)
    rows = [weights[0], weights[1], weights[2], cells[...].astype(jnp.float32)]
    found = jnp.dot(
        jnp.concatenate([placed] * 3, axis=1).astype(jnp.bfloat16),
        jnp.concatenate(thirds(jnp.concatenate(rows, axis=1)), axis=0),
        preferred_element_type=jnp.float32,
    )
    length = cells.shape[1]
    for c in range(3):
        packets[:, c, :] = found[:, c * length : (c + 1) * length]
    packets[:, 3, :] = found[:, 3 * length :] + held * cells_dev


def tile_moments(cap, nz, packets, moments):
    n_slab = packets.shape[0] // cap
    ncl = nz // CB
    wide = cap * packets.shape[2]
    level = lax.broadcasted_iota(jnp.int32, (ncl, wide), 0)
    found = []
    order = outward(n_slab)
    for d in range(n_slab):
        block = jnp.concatenate([packets[order.index(d) * cap + k] for k in range(cap)], axis=1)
        cell = block[3:4, :].astype(jnp.int32)
        spots = (level == cell % nz // CB).astype(jnp.float32).astype(jnp.bfloat16)
        high, low = split(block)
        left = jnp.concatenate([high, low], axis=0).astype(jnp.bfloat16)
        sums = lax.dot_general(left, spots, (((1,), (1,)), ((), ())), preferred_element_type=jnp.float32)
        found.append(sums[0:4] + sums[4:8])
    moments[...] = jnp.concatenate(found, axis=1)


class Copies:
    def __init__(self, sems):
        self.sems = sems
        self.made = []

    def start(self, source, target):
        self.made.append(pltpu.make_async_copy(source, target, self.sems.at[len(self.made)]))
        self.made[-1].start()

    def wait(self, first, last):
        for k in range(first, last):
            self.made[k].wait()


def send_kernel(
    cap,
    vort,
    velo,
    visc,
    weights_in,
    cells_in,
    dest_in,
    count_in,
    near_out,
    far_out,
    swap_out,
    other_out,
    packets_out,
    moments_out,
    near,
    far,
    swap,
    other,
    packets,
    moments,
    weights,
    cells,
    dest,
    count,
    sems,
):
    cx, cy, nz = visc.shape
    copies = Copies(sems)
    copies.start(weights_in, weights)
    copies.start(cells_in, cells)
    copies.start(dest_in, dest)
    copies.start(count_in, count)
    even = lax.axis_index("slab") % 2 == 0
    for face, at in ((near, jnp.where(even, cx - 1, 0)), (far, jnp.where(even, 0, cx - 1))):
        copies.start(vort.at[:, at], face.at[0:3])
        copies.start(velo.at[:, at], face.at[3:6])
        copies.start(visc.at[at], face.at[6])
    even = lax.axis_index("pencil") % 2 == 0
    for face, at in ((swap, jnp.where(even, cy - 1, 0)), (other, jnp.where(even, 0, cy - 1))):
        copies.start(vort.at[:, :, at], face.at[0:3])
        copies.start(velo.at[:, :, at], face.at[3:6])
        copies.start(visc.at[:, at], face.at[6])
    copies.wait(0, 4)
    pack_tiles(cap, cx * cy * nz, weights, cells, dest, count, packets)
    copies.start(packets, packets_out)
    copies.wait(4, 10)
    copies.start(near, near_out)
    copies.start(far, far_out)
    tile_moments(cap, nz, packets, moments)
    copies.start(moments, moments_out)
    copies.wait(10, 16)
    copies.start(swap, swap_out)
    copies.start(other, other_out)
    copies.wait(16, 22)


def to_send(vort, velo, visc, weights, cells, dest, count, n_slab, cap):
    _, cx, cy, nz = vort.shape
    made = (
        shaped(7, cy, nz),
        shaped(7, cy, nz),
        shaped(7, cx, nz),
        shaped(7, cx, nz),
        shaped(n_slab * cap, 4, weights.shape[2]),
        shaped(4, n_slab * nz // CB),
    )
    return pl.pallas_call(
        functools.partial(send_kernel, cap),
        out_shape=made,
        in_specs=[ANY] * 7,
        out_specs=(ANY,) * 6,
        scratch_shapes=[pltpu.VMEM(one.shape, jnp.float32) for one in made]
        + [
            pltpu.VMEM(weights.shape, jnp.float32),
            pltpu.VMEM(cells.shape, jnp.int32),
            pltpu.VMEM(dest.shape, jnp.int32),
            pltpu.SMEM(count.shape, jnp.int32),
            pltpu.SemaphoreType.DMA((22,)),
        ],
        compiler_params=FIRST_PARAMS,
    )(vort, velo, visc, weights, cells, dest, count)


def ahead(a, axis):
    return pltpu.roll(a, a.shape[axis] - 1, axis)


def behind(a, axis):
    return pltpu.roll(a, 1, axis)


def interior_step(vort, velo, visc, out):
    cx, cy, nz = visc.shape
    has_ahead = lax.broadcasted_iota(jnp.int32, (cy, nz), 0) < cy - 1
    totals = [jnp.zeros((8, nz), jnp.float32) for _ in range(3)]
    flux_x = [None] * 3
    for x in range(cx):
        nu = visc[x]
        spin = [vort[c, x] for c in range(3)]
        mean_y = jnp.where(has_ahead, 0.5 * (nu + ahead(nu, 0)), 0.0)
        mean_z = 0.5 * (nu + ahead(nu, 1))
        half_y = 0.5 * spin[1]
        half_z = 0.5 * spin[2]
        next_y = jnp.where(has_ahead, ahead(half_y, 0), 0.0)
        next_z = ahead(half_z, 1)
        half_y = jnp.where(has_ahead, half_y, 0.0)
        half_x = 0.5 * spin[0]
        if x < cx - 1:
            mean_x = 0.5 * (nu + visc[x + 1])
        for c in range(3):
            w = spin[c]
            u = velo[c, x]
            flux_y = mean_y * (ahead(w, 0) - w)
            flux_z = mean_z * (ahead(w, 1) - w)
            change = flux_y + half_y * ahead(u, 0) - behind(flux_y + next_y * u, 0)
            change = change + (flux_z + half_z * ahead(u, 1) - behind(flux_z + next_z * u, 1))
            if x == 0:
                change = change + half_x * velo[c, x + 1]
            elif x == cx - 1:
                change = change - half_x * velo[c, x - 1]
            else:
                change = change + half_x * (velo[c, x + 1] - velo[c, x - 1])
            if x > 0:
                change = change - flux_x[c]
            if x < cx - 1:
                flux_x[c] = mean_x * (vort[c, x + 1] - w)
                change = change + flux_x[c]
            new = w + TIME_STEP * change
            out[c, x] = new
            totals[c] = totals[c] + jnp.sum(new.reshape(cy // 8, 8, nz), axis=0)
    return [jnp.sum(total, axis=0, keepdims=True) for total in totals]


def by_level(totals, width):
    nz = totals[0].shape[1]
    shape = (nz, width)
    level = lax.broadcasted_iota(jnp.int32, shape, 0) // CB
    lane = lax.broadcasted_iota(jnp.int32, shape, 1)
    pick = (lane == lax.axis_index("slab") * (nz // CB) + level).astype(jnp.float32).astype(jnp.bfloat16)
    rows = jnp.concatenate(totals + [jnp.zeros_like(totals[0])], axis=0)
    found = jnp.dot(jnp.concatenate(thirds(rows), axis=0), pick, preferred_element_type=jnp.float32)
    return found[0:4] + (found[4:8] + found[8:12])


def inner_kernel(vort, velo, visc, tiles_in, out, moments, tiles, sem):
    copy = pltpu.make_async_copy(tiles_in, tiles, sem)
    copy.start()
    own = by_level(interior_step(vort, velo, visc, out), moments.shape[1])
    copy.wait()
    moments[...] = tiles[...] + own


def inner(vort, velo, visc, tiles):
    return pl.pallas_call(
        inner_kernel,
        out_shape=(shaped(*vort.shape), shaped(*tiles.shape)),
        in_specs=[VMEM] * 3 + [ANY],
        out_specs=(VMEM,) * 2,
        scratch_shapes=[pltpu.VMEM(tiles.shape, jnp.float32), pltpu.SemaphoreType.DMA],
        compiler_params=PARAMS,
    )(vort, velo, visc, tiles)


def face_change(own, other, along, sign, c):
    stretch = (0.5 * sign) * own[along] * other[3 + c]
    diffuse = 0.5 * (own[6] + other[6]) * (other[c] - own[c])
    return TIME_STEP * (stretch + diffuse)


def edge_kernel(
    inside, moments, near, far, swap, other, near_in, far_in, swap_in, other_in, out, load_out, load, side_change, sem
):
    _, cx, cy, nz = out.shape
    even = lax.axis_index("pencil") % 2 == 0
    low, low_in = jnp.where(even, other[...], swap[...]), jnp.where(even, other_in[...], swap_in[...])
    high, high_in = jnp.where(even, swap[...], other[...]), jnp.where(even, swap_in[...], other_in[...])
    even = lax.axis_index("slab") % 2 == 0
    near_at, far_at = jnp.where(even, cx - 1, 0), jnp.where(even, 0, cx - 1)
    near_sign = jnp.where(even, 1.0, -1.0)
    totals = []
    for c in range(3):
        total = jnp.zeros((8, nz), jnp.float32)
        for own, came, at, sign in ((near, near_in, near_at, near_sign), (far, far_in, far_at, -near_sign)):
            change = face_change(own, came, 0, sign, c)
            out[c, at] = inside[c, at] + change
            total = total + jnp.sum(change.reshape(cy // 8, 8, nz), axis=0)
        for k, own, came, sign in ((0, low, low_in, -1.0), (1, high, high_in, 1.0)):
            change = face_change(own, came, 1, sign, c)
            side_change[k, c] = change
            total = total + change
        totals.append(jnp.sum(total, axis=0, keepdims=True))
    moment = moments[...] + by_level(totals, moments.shape[1])
    for k in range(load.shape[1] // 4):
        part = moment[:, k * LANES : (k + 1) * LANES]
        load[:, 4 * k : 4 * k + 4, :] = jnp.broadcast_to(part[None], (load.shape[0], 4, LANES))
    copy = pltpu.make_async_copy(load, load_out, sem)
    copy.start()
    for c in range(3):
        out[c, 1 : cx - 1] = inside[c, 1 : cx - 1]
        for k, at in ((0, 0), (1, cy - 1)):
            for x in range(cx):
                out[c, x, at : at + 1, :] = out[c, x, at : at + 1, :] + side_change[k, c, x : x + 1, :]
    copy.wait()


def edges(inside, moments, faces, halos, n_all):
    _, cx, _, nz = inside.shape
    load = shaped(n_all, 4 * moments.shape[1] // LANES, LANES)
    return pl.pallas_call(
        edge_kernel,
        out_shape=(shaped(*inside.shape), load),
        in_specs=[VMEM] * 10,
        out_specs=(VMEM, ANY),
        scratch_shapes=[
            pltpu.VMEM(load.shape, jnp.float32),
            pltpu.VMEM((2, 3, cx, nz), jnp.float32),
            pltpu.SemaphoreType.DMA,
        ],
        compiler_params=PARAMS,
    )(inside, moments, *faces, *halos)


def far_kernel(cx, cy, ncl, n_pencil, load, out):
    n_all = load.shape[0]
    n_slab = n_all // n_pencil
    slab = lax.axis_index("slab")
    pencil = lax.axis_index("pencil")
    shape = (ncl, n_slab * ncl)
    target = lax.broadcasted_iota(jnp.int32, shape, 0)
    source = lax.broadcasted_iota(jnp.int32, shape, 1)
    sigma = jnp.float32(cx * n_slab // 4)
    rel_x = ((slab - source // ncl) * cx).astype(jnp.float32)
    rel_z = ((target - source % ncl) * CB).astype(jnp.float32)
    flat = rel_x * rel_x + rel_z * rel_z + sigma * sigma
    turned = [jnp.zeros(shape, jnp.float32) for _ in range(3)]
    for p in range(n_pencil):
        total = load[p]
        for s in range(1, n_slab):
            total = total + load[s * n_pencil + p]
        moment = jnp.concatenate([total[4 * k : 4 * k + 4] for k in range(load.shape[1] // 4)], axis=1)
        first, second, third = moment[0:1], moment[1:2], moment[2:3]
        rel_y = ((pencil - p) * cy).astype(jnp.float32)
        inverse = lax.rsqrt(flat + rel_y * rel_y)
        weight = inverse * inverse * inverse
        turned[0] = turned[0] + weight * (rel_z * second - rel_y * third)
        turned[1] = turned[1] + weight * (rel_x * third - rel_z * first)
        turned[2] = turned[2] + weight * (rel_y * first - rel_x * second)
    ones = jnp.ones((8, shape[1]), jnp.float32)
    for c in range(3):
        row = lax.dot_general(
            ones,
            turned[c],
            (((1,), (1,)), ((), ())),
            precision=lax.Precision.HIGHEST,
            preferred_element_type=jnp.float32,
        )
        out[c, 0] = row[0:1]


def far(load, cx, cy, ncl, n_pencil):
    return pl.pallas_call(
        functools.partial(far_kernel, cx, cy, ncl, n_pencil),
        out_shape=shaped(3, 1, 1, ncl),
        in_specs=[VMEM],
        out_specs=VMEM,
        compiler_params=PARAMS,
    )(load)


def deposit_step(group, first, listed, load, order, acc, shape):
    cx, cy, nz = shape
    rows = cx * cy // 2
    wide = group * load.shape[2]

    def numbers(length):
        shape = (length // 16, 16, wide)
        return (lax.broadcasted_iota(jnp.int32, shape, 0) * 16 + lax.broadcasted_iota(jnp.int32, shape, 1)).astype(
            jnp.float32
        ).astype(jnp.bfloat16)

    def spread(row):
        return jnp.broadcast_to(row, (16, wide)).astype(jnp.bfloat16)[None]

    zero = jnp.zeros((), jnp.bfloat16)
    one = jnp.ones((), jnp.bfloat16)
    block = jnp.concatenate([load[order[first + k]] for k in range(group)], axis=1)
    live = lax.broadcasted_iota(jnp.int32, (1, wide), 1) // load.shape[2] < listed - first
    cell = block[3:4, :].astype(jnp.int32) % (cx * cy * nz)
    row = cell // nz
    half = row // rows
    at_row = numbers(rows) == spread(jnp.where(live, row % rows, -1).astype(jnp.float32))
    right = []
    for h in range(2):
        at_col = numbers(nz) == spread(jnp.where(half == h, cell % nz, -1).astype(jnp.float32))
        right.append(jnp.where(at_col, one, zero).reshape(nz, wide))
    left = []
    for piece in split(block):
        for c in range(3):
            left.append(jnp.where(at_row, spread(piece[c : c + 1, :]), zero).reshape(rows, wide))
    added = lax.dot_general(
        jnp.concatenate(left, axis=0),
        jnp.concatenate(right, axis=0),
        (((1,), (1,)), ((), ())),
        preferred_element_type=jnp.float32,
    )
    acc[...] += (added[: 3 * rows] + added[3 * rows :]).reshape(acc.shape)


def deposit_kernel(cap, inside, load, out, acc, order, sems):
    _, cx, cy, nz = out.shape
    shape = (cx, cy, nz)
    for h in range(2):
        acc[:, :, :, h * nz : (h + 1) * nz] = inside[:, h * (cx // 2) : (h + 1) * (cx // 2)]
    listed = jnp.int32(0)
    for d in range(load.shape[0] // cap):
        first = d * cap
        held = jnp.max(load[first, 3:4, :]).astype(jnp.int32) // (cx * cy * nz)
        for k in range(cap):
            order[listed + k] = first + k
        listed = listed + held
    for k in range(GROUP):
        order[listed + k] = 0
    rest = listed % GROUP
    whole = listed // GROUP + (rest > GROUP // 2).astype(jnp.int32)

    def step(g, carry):
        deposit_step(GROUP, g * GROUP, listed, load, order, acc, shape)
        return carry

    lax.fori_loop(0, whole, step, 0)

    @pl.when((rest > 0) & (rest <= GROUP // 2))
    def _():
        deposit_step(GROUP // 2, whole * GROUP, listed, load, order, acc, shape)

    copies = Copies(sems)
    for c in range(3):
        for h in range(2):
            part = acc.at[c, :, :, h * nz : (h + 1) * nz]
            copies.start(part, out.at[c, h * (cx // 2) : (h + 1) * (cx // 2)])
    copies.wait(0, 6)


def deposit(inside, load, cap):
    return pl.pallas_call(
        functools.partial(deposit_kernel, cap),
        out_shape=shaped(*inside.shape),
        in_specs=[VMEM] * 2,
        out_specs=ANY,
        scratch_shapes=[
            pltpu.VMEM((3, inside.shape[1] // 2, inside.shape[2], 2 * inside.shape[3]), jnp.float32),
            pltpu.SMEM((load.shape[0] + max(cap, GROUP),), jnp.int32),
            pltpu.SemaphoreType.DMA((6,)),
        ],
        compiler_params=PARAMS,
    )(inside, load)


def swapped(array, axis, first):
    up = [(i, i + 1) for i in range(first, lax.axis_size(axis) - 1, 2)]
    return lax.ppermute(array, axis, up + [(j, i) for i, j in up])


def per_device(vorticity, velocity, viscosity, tile_weights, tile_cells, tile_dest, tile_count):
    _, cx, cy, nz = vorticity.shape
    ncl = nz // CB
    n_slab = lax.axis_size("slab")
    n_pencil = lax.axis_size("pencil")
    cap = 2 * tile_weights.shape[0] // n_slab
    weights = jnp.transpose(tile_weights, (1, 0, 2))
    count = tile_count
    *faces, packets, tiles = to_send(
        vorticity, velocity, viscosity, weights, tile_cells, tile_dest.T, count, n_slab, cap
    )
    halos = [swapped(face, axis, k % 2) for k, (face, axis) in enumerate(zip(faces, SIDES))]
    order = outward(n_slab)
    arrived = lax.all_to_all(packets, "slab", 0, 0, axis_index_groups=[order], tiled=True)
    inside, moments = inner(vorticity, velocity, viscosity, tiles)
    advanced, load = edges(inside, moments, faces, halos, n_slab * n_pencil)
    everyone = [s * n_pencil + p for s in order for p in range(n_pencil)]
    load = lax.all_to_all(load, ("slab", "pencil"), 0, 0, axis_index_groups=[everyone], tiled=True)
    vorticity_out = deposit(advanced, arrived, cap)
    return (vorticity_out, far(load, cx, cy, ncl, n_pencil))


def solution(mesh):
    in_specs = (
        P(None, "slab", "pencil", None),
        P(None, "slab", "pencil", None),
        P("slab", "pencil", None),
        P(("slab", "pencil"), None, None),
        P(("slab", "pencil"), None),
        P(("slab", "pencil"), None),
        P(("slab", "pencil")),
    )
    out_specs = (P(None, "slab", "pencil", None), P(None, "slab", "pencil", None))
    return jax.shard_map(
        per_device, mesh=mesh, in_specs=in_specs, out_specs=out_specs, check_vma=False
    )
```

```python
import functools

import jax
import jax.numpy as jnp
from jax import lax
from jax.experimental import pallas as pl
from jax.experimental.pallas import tpu as pltpu
from jax.sharding import PartitionSpec as P

CB = 16
TIME_STEP = 0.1
LANES = 128
SIDES = ("slab", "slab", "pencil", "pencil")
GROUP = 16
VMEM_LIMIT = 24 * 1024 * 1024

VMEM = pl.BlockSpec(memory_space=pltpu.VMEM)
ANY = pl.BlockSpec(memory_space=pl.ANY)
SMEM = pl.BlockSpec(memory_space=pltpu.SMEM)
FIRST_PARAMS = pltpu.CompilerParams(vmem_limit_bytes=60 * 1024 * 1024)
PARAMS = pltpu.CompilerParams(vmem_limit_bytes=VMEM_LIMIT)


def shaped(*shape):
    return jax.ShapeDtypeStruct(shape, jnp.float32)


def split(w):
    high = w.astype(jnp.bfloat16).astype(jnp.float32)
    return high, w - high


def thirds(w):
    high, rest = split(w)
    middle, low = split(rest)
    return [piece.astype(jnp.bfloat16) for piece in (high, middle, low)]


def outward(count):
    half = count // 2
    return [(half + (k + 1) // 2) % count if k % 2 else half - k // 2 for k in range(count)]


def pack_tiles(cap, cells_dev, weights, cells, dest, count, packets):
    slots = packets.shape[0]
    tiles = cells.shape[0]
    half = slots // cap // 2
    names = dest[...]
    names = jnp.where(names > half, 2 * (names - half) - 1, 2 * (half - names))
    names = jnp.minimum(names, 2 * half - 1)
    live = (lax.broadcasted_iota(jnp.int32, (1, tiles), 1) < count[0]).astype(jnp.float32)
    same = (lax.broadcasted_iota(jnp.int32, (slots // cap, tiles), 0) == names).astype(jnp.float32)
    shape = (tiles, tiles)
    earlier = lax.broadcasted_iota(jnp.int32, shape, 0) < lax.broadcasted_iota(jnp.int32, shape, 1)
    before = jnp.dot(same, earlier.astype(jnp.float32), preferred_element_type=jnp.float32)
    rank = jnp.sum(same * before, axis=0, keepdims=True).astype(jnp.int32)
    slot = lax.broadcasted_iota(jnp.int32, (slots, tiles), 0)
    placed = (slot == names * cap + rank).astype(jnp.float32) * live
    held = jnp.sum((slot == names * cap).astype(jnp.float32) * live, axis=1, keepdims=True)
    rows = [weights[0], weights[1], weights[2], cells[...].astype(jnp.float32)]
    found = jnp.dot(
        jnp.concatenate([placed] * 3, axis=1).astype(jnp.bfloat16),
        jnp.concatenate(thirds(jnp.concatenate(rows, axis=1)), axis=0),
        preferred_element_type=jnp.float32,
    )
    length = cells.shape[1]
    for c in range(3):
        packets[:, c, :] = found[:, c * length : (c + 1) * length]
    packets[:, 3, :] = found[:, 3 * length :] + held * cells_dev


def tile_moments(cap, nz, packets, moments):
    n_slab = packets.shape[0] // cap
    ncl = nz // CB
    wide = cap * packets.shape[2]
    level = lax.broadcasted_iota(jnp.int32, (ncl, wide), 0)
    found = []
    order = outward(n_slab)
    for d in range(n_slab):
        block = jnp.concatenate([packets[order.index(d) * cap + k] for k in range(cap)], axis=1)
        cell = block[3:4, :].astype(jnp.int32)
        spots = (level == cell % nz // CB).astype(jnp.float32).astype(jnp.bfloat16)
        high, low = split(block)
        left = jnp.concatenate([high, low], axis=0).astype(jnp.bfloat16)
        sums = lax.dot_general(left, spots, (((1,), (1,)), ((), ())), preferred_element_type=jnp.float32)
        found.append(sums[0:4] + sums[4:8])
    moments[...] = jnp.concatenate(found, axis=1)


class Copies:
    def __init__(self, sems):
        self.sems = sems
        self.made = []

    def start(self, source, target):
        self.made.append(pltpu.make_async_copy(source, target, self.sems.at[len(self.made)]))
        self.made[-1].start()

    def wait(self, first, last):
        for k in range(first, last):
            self.made[k].wait()


def send_kernel(
    cap,
    vort,
    velo,
    visc,
    weights_in,
    cells_in,
    dest_in,
    count_in,
    near_out,
    far_out,
    swap_out,
    other_out,
    packets_out,
    moments_out,
    near,
    far,
    swap,
    other,
    packets,
    moments,
    weights,
    cells,
    dest,
    count,
    sems,
):
    cx, cy, nz = visc.shape
    copies = Copies(sems)
    even = lax.axis_index("slab") % 2 == 0
    for face, at in ((near, jnp.where(even, cx - 1, 0)), (far, jnp.where(even, 0, cx - 1))):
        copies.start(vort.at[:, at], face.at[0:3])
        copies.start(velo.at[:, at], face.at[3:6])
        copies.start(visc.at[at], face.at[6])
    copies.start(weights_in, weights)
    copies.start(cells_in, cells)
    copies.start(dest_in, dest)
    copies.start(count_in, count)
    even = lax.axis_index("pencil") % 2 == 0
    for face, at in ((swap, jnp.where(even, cy - 1, 0)), (other, jnp.where(even, 0, cy - 1))):
        copies.start(vort.at[:, :, at], face.at[0:3])
        copies.start(velo.at[:, :, at], face.at[3:6])
        copies.start(visc.at[:, at], face.at[6])
    copies.wait(6, 10)
    pack_tiles(cap, cx * cy * nz, weights, cells, dest, count, packets)
    copies.start(packets, packets_out)
    copies.wait(0, 6)
    copies.start(near, near_out)
    copies.start(far, far_out)
    tile_moments(cap, nz, packets, moments)
    copies.start(moments, moments_out)
    copies.wait(10, 16)
    copies.start(swap, swap_out)
    copies.start(other, other_out)
    copies.wait(16, 22)


def to_send(vort, velo, visc, weights, cells, dest, count, n_slab, cap):
    _, cx, cy, nz = vort.shape
    made = (
        shaped(7, cy, nz),
        shaped(7, cy, nz),
        shaped(7, cx, nz),
        shaped(7, cx, nz),
        shaped(n_slab * cap, 4, weights.shape[2]),
        shaped(4, n_slab * nz // CB),
    )
    return pl.pallas_call(
        functools.partial(send_kernel, cap),
        out_shape=made,
        in_specs=[ANY] * 7,
        out_specs=(ANY,) * 6,
        scratch_shapes=[pltpu.VMEM(one.shape, jnp.float32) for one in made]
        + [
            pltpu.VMEM(weights.shape, jnp.float32),
            pltpu.VMEM(cells.shape, jnp.int32),
            pltpu.VMEM(dest.shape, jnp.int32),
            pltpu.SMEM(count.shape, jnp.int32),
            pltpu.SemaphoreType.DMA((22,)),
        ],
        compiler_params=FIRST_PARAMS,
    )(vort, velo, visc, weights, cells, dest, count)


def ahead(a, axis):
    return pltpu.roll(a, a.shape[axis] - 1, axis)


def behind(a, axis):
    return pltpu.roll(a, 1, axis)


def interior_step(vort, velo, visc, out):
    cx, cy, nz = visc.shape
    has_ahead = lax.broadcasted_iota(jnp.int32, (cy, nz), 0) < cy - 1
    totals = [jnp.zeros((8, nz), jnp.float32) for _ in range(3)]
    flux_x = [None] * 3
    for x in range(cx):
        nu = visc[x]
        spin = [vort[c, x] for c in range(3)]
        mean_y = jnp.where(has_ahead, 0.5 * (nu + ahead(nu, 0)), 0.0)
        mean_z = 0.5 * (nu + ahead(nu, 1))
        half_y = 0.5 * spin[1]
        half_z = 0.5 * spin[2]
        next_y = jnp.where(has_ahead, ahead(half_y, 0), 0.0)
        next_z = ahead(half_z, 1)
        half_y = jnp.where(has_ahead, half_y, 0.0)
        half_x = 0.5 * spin[0]
        if x < cx - 1:
            mean_x = 0.5 * (nu + visc[x + 1])
        for c in range(3):
            w = spin[c]
            u = velo[c, x]
            flux_y = mean_y * (ahead(w, 0) - w)
            flux_z = mean_z * (ahead(w, 1) - w)
            change = flux_y + half_y * ahead(u, 0) - behind(flux_y + next_y * u, 0)
            change = change + (flux_z + half_z * ahead(u, 1) - behind(flux_z + next_z * u, 1))
            if x == 0:
                change = change + half_x * velo[c, x + 1]
            elif x == cx - 1:
                change = change - half_x * velo[c, x - 1]
            else:
                change = change + half_x * (velo[c, x + 1] - velo[c, x - 1])
            if x > 0:
                change = change - flux_x[c]
            if x < cx - 1:
                flux_x[c] = mean_x * (vort[c, x + 1] - w)
                change = change + flux_x[c]
            new = w + TIME_STEP * change
            out[c, x] = new
            totals[c] = totals[c] + jnp.sum(new.reshape(cy // 8, 8, nz), axis=0)
    return [jnp.sum(total, axis=0, keepdims=True) for total in totals]


def by_level(totals, width):
    nz = totals[0].shape[1]
    shape = (nz, width)
    level = lax.broadcasted_iota(jnp.int32, shape, 0) // CB
    lane = lax.broadcasted_iota(jnp.int32, shape, 1)
    pick = (lane == lax.axis_index("slab") * (nz // CB) + level).astype(jnp.float32).astype(jnp.bfloat16)
    rows = jnp.concatenate(totals + [jnp.zeros_like(totals[0])], axis=0)
    found = jnp.dot(jnp.concatenate(thirds(rows), axis=0), pick, preferred_element_type=jnp.float32)
    return found[0:4] + (found[4:8] + found[8:12])


def inner_kernel(vort, velo, visc, tiles_in, out, moments, tiles, sem):
    copy = pltpu.make_async_copy(tiles_in, tiles, sem)
    copy.start()
    own = by_level(interior_step(vort, velo, visc, out), moments.shape[1])
    copy.wait()
    moments[...] = tiles[...] + own


def inner(vort, velo, visc, tiles):
    return pl.pallas_call(
        inner_kernel,
        out_shape=(shaped(*vort.shape), shaped(*tiles.shape)),
        in_specs=[VMEM] * 3 + [ANY],
        out_specs=(VMEM,) * 2,
        scratch_shapes=[pltpu.VMEM(tiles.shape, jnp.float32), pltpu.SemaphoreType.DMA],
        compiler_params=PARAMS,
    )(vort, velo, visc, tiles)


def face_change(own, other, along, sign, c):
    stretch = (0.5 * sign) * own[along] * other[3 + c]
    diffuse = 0.5 * (own[6] + other[6]) * (other[c] - own[c])
    return TIME_STEP * (stretch + diffuse)


def edge_kernel(
    inside, moments, near, far, swap, other, near_in, far_in, swap_in, other_in, out, load_out, load, side_change, sem
):
    _, cx, cy, nz = out.shape
    even = lax.axis_index("pencil") % 2 == 0
    low, low_in = jnp.where(even, other[...], swap[...]), jnp.where(even, other_in[...], swap_in[...])
    high, high_in = jnp.where(even, swap[...], other[...]), jnp.where(even, swap_in[...], other_in[...])
    even = lax.axis_index("slab") % 2 == 0
    near_at, far_at = jnp.where(even, cx - 1, 0), jnp.where(even, 0, cx - 1)
    near_sign = jnp.where(even, 1.0, -1.0)
    totals = []
    for c in range(3):
        total = jnp.zeros((8, nz), jnp.float32)
        for own, came, at, sign in ((near, near_in, near_at, near_sign), (far, far_in, far_at, -near_sign)):
            change = face_change(own, came, 0, sign, c)
            out[c, at] = inside[c, at] + change
            total = total + jnp.sum(change.reshape(cy // 8, 8, nz), axis=0)
        for k, own, came, sign in ((0, low, low_in, -1.0), (1, high, high_in, 1.0)):
            change = face_change(own, came, 1, sign, c)
            side_change[k, c] = change
            total = total + change
        totals.append(jnp.sum(total, axis=0, keepdims=True))
    moment = moments[...] + by_level(totals, moments.shape[1])
    for k in range(load.shape[1] // 4):
        part = moment[:, k * LANES : (k + 1) * LANES]
        load[:, 4 * k : 4 * k + 4, :] = jnp.broadcast_to(part[None], (load.shape[0], 4, LANES))
    copy = pltpu.make_async_copy(load, load_out, sem)
    copy.start()
    for c in range(3):
        out[c, 1 : cx - 1] = inside[c, 1 : cx - 1]
        for k, at in ((0, 0), (1, cy - 1)):
            for x in range(cx):
                out[c, x, at : at + 1, :] = out[c, x, at : at + 1, :] + side_change[k, c, x : x + 1, :]
    copy.wait()


def edges(inside, moments, faces, halos, n_all):
    _, cx, _, nz = inside.shape
    load = shaped(n_all, 4 * moments.shape[1] // LANES, LANES)
    return pl.pallas_call(
        edge_kernel,
        out_shape=(shaped(*inside.shape), load),
        in_specs=[VMEM] * 10,
        out_specs=(VMEM, ANY),
        scratch_shapes=[
            pltpu.VMEM(load.shape, jnp.float32),
            pltpu.VMEM((2, 3, cx, nz), jnp.float32),
            pltpu.SemaphoreType.DMA,
        ],
        compiler_params=PARAMS,
    )(inside, moments, *faces, *halos)


def far_kernel(cx, cy, ncl, n_pencil, load, out):
    n_all = load.shape[0]
    n_slab = n_all // n_pencil
    slab = lax.axis_index("slab")
    pencil = lax.axis_index("pencil")
    shape = (ncl, n_slab * ncl)
    target = lax.broadcasted_iota(jnp.int32, shape, 0)
    source = lax.broadcasted_iota(jnp.int32, shape, 1)
    sigma = jnp.float32(cx * n_slab // 4)
    rel_x = ((slab - source // ncl) * cx).astype(jnp.float32)
    rel_z = ((target - source % ncl) * CB).astype(jnp.float32)
    flat = rel_x * rel_x + rel_z * rel_z + sigma * sigma
    turned = [jnp.zeros(shape, jnp.float32) for _ in range(3)]
    for p in range(n_pencil):
        total = load[p]
        for s in range(1, n_slab):
            total = total + load[s * n_pencil + p]
        moment = jnp.concatenate([total[4 * k : 4 * k + 4] for k in range(load.shape[1] // 4)], axis=1)
        first, second, third = moment[0:1], moment[1:2], moment[2:3]
        rel_y = ((pencil - p) * cy).astype(jnp.float32)
        inverse = lax.rsqrt(flat + rel_y * rel_y)
        weight = inverse * inverse * inverse
        turned[0] = turned[0] + weight * (rel_z * second - rel_y * third)
        turned[1] = turned[1] + weight * (rel_x * third - rel_z * first)
        turned[2] = turned[2] + weight * (rel_y * first - rel_x * second)
    ones = jnp.ones((8, shape[1]), jnp.float32)
    for c in range(3):
        row = lax.dot_general(
            ones,
            turned[c],
            (((1,), (1,)), ((), ())),
            precision=lax.Precision.HIGHEST,
            preferred_element_type=jnp.float32,
        )
        out[c, 0] = row[0:1]


def far(load, cx, cy, ncl, n_pencil):
    return pl.pallas_call(
        functools.partial(far_kernel, cx, cy, ncl, n_pencil),
        out_shape=shaped(3, 1, 1, ncl),
        in_specs=[VMEM],
        out_specs=VMEM,
        compiler_params=PARAMS,
    )(load)


def deposit_step(group, first, listed, load, order, acc, shape):
    cx, cy, nz = shape
    rows = cx * cy // 2
    wide = group * load.shape[2]

    def numbers(length):
        shape = (length // 16, 16, wide)
        return (lax.broadcasted_iota(jnp.int32, shape, 0) * 16 + lax.broadcasted_iota(jnp.int32, shape, 1)).astype(
            jnp.float32
        ).astype(jnp.bfloat16)

    def spread(row):
        return jnp.broadcast_to(row, (16, wide)).astype(jnp.bfloat16)[None]

    zero = jnp.zeros((), jnp.bfloat16)
    one = jnp.ones((), jnp.bfloat16)
    block = jnp.concatenate([load[order[first + k]] for k in range(group)], axis=1)
    live = lax.broadcasted_iota(jnp.int32, (1, wide), 1) // load.shape[2] < listed - first
    cell = block[3:4, :].astype(jnp.int32) % (cx * cy * nz)
    row = cell // nz
    half = row // rows
    at_row = numbers(rows) == spread(jnp.where(live, row % rows, -1).astype(jnp.float32))
    right = []
    for h in range(2):
        at_col = numbers(nz) == spread(jnp.where(half == h, cell % nz, -1).astype(jnp.float32))
        right.append(jnp.where(at_col, one, zero).reshape(nz, wide))
    left = []
    for piece in split(block):
        for c in range(3):
            left.append(jnp.where(at_row, spread(piece[c : c + 1, :]), zero).reshape(rows, wide))
    added = lax.dot_general(
        jnp.concatenate(left, axis=0),
        jnp.concatenate(right, axis=0),
        (((1,), (1,)), ((), ())),
        preferred_element_type=jnp.float32,
    )
    acc[...] += (added[: 3 * rows] + added[3 * rows :]).reshape(acc.shape)


def deposit_kernel(cap, inside, load, out, acc, order, sems):
    _, cx, cy, nz = out.shape
    shape = (cx, cy, nz)
    for h in range(2):
        acc[:, :, :, h * nz : (h + 1) * nz] = inside[:, h * (cx // 2) : (h + 1) * (cx // 2)]
    listed = jnp.int32(0)
    for d in range(0, load.shape[0] // cap, 4):
        rows = jnp.concatenate([load[(d + k) * cap, 3:4, :] for k in range(4)], axis=0)
        held = rows.astype(jnp.int32) // (cx * cy * nz)
        place = lax.broadcasted_iota(jnp.int32, held.shape, 0)
        scale = jnp.where(place < 2, jnp.where(place == 0, 1, 16), jnp.where(place == 2, 256, 4096))
        packed = jnp.max(jnp.sum((held * scale).astype(jnp.float32), axis=0, keepdims=True)).astype(jnp.int32)
        for k in range(4):
            first = (d + k) * cap
            for j in range(cap):
                order[listed + j] = first + j
            listed = listed + packed % 16
            packed = packed // 16
    for k in range(GROUP):
        order[listed + k] = 0
    rest = listed % GROUP
    whole = listed // GROUP + (rest > GROUP // 2).astype(jnp.int32)

    def step(g, carry):
        deposit_step(GROUP, g * GROUP, listed, load, order, acc, shape)
        return carry

    lax.fori_loop(0, whole, step, 0)

    @pl.when((rest > 0) & (rest <= GROUP // 2))
    def _():
        deposit_step(GROUP // 2, whole * GROUP, listed, load, order, acc, shape)

    copies = Copies(sems)
    for c in range(3):
        for h in range(2):
            part = acc.at[c, :, :, h * nz : (h + 1) * nz]
            copies.start(part, out.at[c, h * (cx // 2) : (h + 1) * (cx // 2)])
    copies.wait(0, 6)


def deposit(inside, load, cap):
    return pl.pallas_call(
        functools.partial(deposit_kernel, cap),
        out_shape=shaped(*inside.shape),
        in_specs=[VMEM] * 2,
        out_specs=ANY,
        scratch_shapes=[
            pltpu.VMEM((3, inside.shape[1] // 2, inside.shape[2], 2 * inside.shape[3]), jnp.float32),
            pltpu.SMEM((load.shape[0] + max(cap, GROUP),), jnp.int32),
            pltpu.SemaphoreType.DMA((6,)),
        ],
        compiler_params=PARAMS,
    )(inside, load)


def swapped(array, axis, first):
    up = [(i, i + 1) for i in range(first, lax.axis_size(axis) - 1, 2)]
    return lax.ppermute(array, axis, up + [(j, i) for i, j in up])


def per_device(vorticity, velocity, viscosity, tile_weights, tile_cells, tile_dest, tile_count):
    _, cx, cy, nz = vorticity.shape
    ncl = nz // CB
    n_slab = lax.axis_size("slab")
    n_pencil = lax.axis_size("pencil")
    cap = 2 * tile_weights.shape[0] // n_slab
    weights = jnp.transpose(tile_weights, (1, 0, 2))
    count = tile_count
    *faces, packets, tiles = to_send(
        vorticity, velocity, viscosity, weights, tile_cells, tile_dest.T, count, n_slab, cap
    )
    halos = [swapped(face, axis, k % 2) for k, (face, axis) in enumerate(zip(faces, SIDES))]
    order = outward(n_slab)
    arrived = lax.all_to_all(packets, "slab", 0, 0, axis_index_groups=[order], tiled=True)
    inside, moments = inner(vorticity, velocity, viscosity, tiles)
    advanced, load = edges(inside, moments, faces, halos, n_slab * n_pencil)
    everyone = [s * n_pencil + p for s in order for p in range(n_pencil)]
    load = lax.all_to_all(load, ("slab", "pencil"), 0, 0, axis_index_groups=[everyone], tiled=True)
    vorticity_out = deposit(advanced, arrived, cap)
    return (vorticity_out, far(load, cx, cy, ncl, n_pencil))


def solution(mesh):
    in_specs = (
        P(None, "slab", "pencil", None),
        P(None, "slab", "pencil", None),
        P("slab", "pencil", None),
        P(("slab", "pencil"), None, None),
        P(("slab", "pencil"), None),
        P(("slab", "pencil"), None),
        P(("slab", "pencil")),
    )
    out_specs = (P(None, "slab", "pencil", None), P(None, "slab", "pencil", None))
    return jax.shard_map(
        per_device, mesh=mesh, in_specs=in_specs, out_specs=out_specs, check_vma=False
    )
```

```python
import functools

import jax
import jax.numpy as jnp
from jax import lax
from jax.experimental import pallas as pl
from jax.experimental.pallas import tpu as pltpu
from jax.sharding import PartitionSpec as P

CB = 16
TIME_STEP = 0.1
LANES = 128
SIDES = ("slab", "slab", "pencil", "pencil")
GROUP = 16
VMEM_LIMIT = 24 * 1024 * 1024

VMEM = pl.BlockSpec(memory_space=pltpu.VMEM)
ANY = pl.BlockSpec(memory_space=pl.ANY)
SMEM = pl.BlockSpec(memory_space=pltpu.SMEM)
FIRST_PARAMS = pltpu.CompilerParams(vmem_limit_bytes=60 * 1024 * 1024)
PARAMS = pltpu.CompilerParams(vmem_limit_bytes=VMEM_LIMIT)


def shaped(*shape):
    return jax.ShapeDtypeStruct(shape, jnp.float32)


def split(w):
    high = w.astype(jnp.bfloat16).astype(jnp.float32)
    return high, w - high


def thirds(w):
    high, rest = split(w)
    middle, low = split(rest)
    return [piece.astype(jnp.bfloat16) for piece in (high, middle, low)]


def outward(count):
    half = count // 2
    return [(half + (k + 1) // 2) % count if k % 2 else half - k // 2 for k in range(count)]


def pack_tiles(cap, cells_dev, weights, cells, dest, count, packets):
    slots = packets.shape[0]
    tiles = cells.shape[0]
    half = slots // cap // 2
    names = dest[...]
    names = jnp.where(names > half, 2 * (names - half) - 1, 2 * (half - names))
    names = jnp.minimum(names, 2 * half - 1)
    live = (lax.broadcasted_iota(jnp.int32, (1, tiles), 1) < count[0]).astype(jnp.float32)
    same = (lax.broadcasted_iota(jnp.int32, (slots // cap, tiles), 0) == names).astype(jnp.float32)
    shape = (tiles, tiles)
    earlier = lax.broadcasted_iota(jnp.int32, shape, 0) < lax.broadcasted_iota(jnp.int32, shape, 1)
    before = jnp.dot(same, earlier.astype(jnp.float32), preferred_element_type=jnp.float32)
    rank = jnp.sum(same * before, axis=0, keepdims=True).astype(jnp.int32)
    slot = lax.broadcasted_iota(jnp.int32, (slots, tiles), 0)
    placed = (slot == names * cap + rank).astype(jnp.float32) * live
    held = jnp.sum((slot == names * cap).astype(jnp.float32) * live, axis=1, keepdims=True)
    rows = [weights[0], weights[1], weights[2], cells[...].astype(jnp.float32)]
    found = jnp.dot(
        jnp.concatenate([placed] * 3, axis=1).astype(jnp.bfloat16),
        jnp.concatenate(thirds(jnp.concatenate(rows, axis=1)), axis=0),
        preferred_element_type=jnp.float32,
    )
    length = cells.shape[1]
    for c in range(3):
        packets[:, c, :] = found[:, c * length : (c + 1) * length]
    packets[:, 3, :] = found[:, 3 * length :] + held * cells_dev


def tile_moments(cap, nz, packets, moments):
    n_slab = packets.shape[0] // cap
    ncl = nz // CB
    wide = cap * packets.shape[2]
    level = lax.broadcasted_iota(jnp.int32, (ncl, wide), 0)
    found = []
    order = outward(n_slab)
    for d in range(n_slab):
        block = jnp.concatenate([packets[order.index(d) * cap + k] for k in range(cap)], axis=1)
        cell = block[3:4, :].astype(jnp.int32)
        spots = (level == cell % nz // CB).astype(jnp.float32).astype(jnp.bfloat16)
        high, low = split(block)
        left = jnp.concatenate([high, low], axis=0).astype(jnp.bfloat16)
        sums = lax.dot_general(left, spots, (((1,), (1,)), ((), ())), preferred_element_type=jnp.float32)
        found.append(sums[0:4] + sums[4:8])
    moments[...] = jnp.concatenate(found, axis=1)


class Copies:
    def __init__(self, sems):
        self.sems = sems
        self.made = []

    def start(self, source, target):
        self.made.append(pltpu.make_async_copy(source, target, self.sems.at[len(self.made)]))
        self.made[-1].start()

    def wait(self, first, last):
        for k in range(first, last):
            self.made[k].wait()


def send_kernel(
    cap,
    vort,
    velo,
    visc,
    weights_in,
    cells_in,
    dest_in,
    count_in,
    near_out,
    far_out,
    swap_out,
    other_out,
    packets_out,
    moments_out,
    near,
    far,
    swap,
    other,
    packets,
    moments,
    weights,
    cells,
    dest,
    count,
    sems,
):
    cx, cy, nz = visc.shape
    copies = Copies(sems)
    copies.start(weights_in, weights)
    copies.start(cells_in, cells)
    copies.start(dest_in, dest)
    copies.start(count_in, count)
    even = lax.axis_index("slab") % 2 == 0
    for face, at in ((near, jnp.where(even, cx - 1, 0)), (far, jnp.where(even, 0, cx - 1))):
        copies.start(vort.at[:, at], face.at[0:3])
        copies.start(velo.at[:, at], face.at[3:6])
        copies.start(visc.at[at], face.at[6])
    even = lax.axis_index("pencil") % 2 == 0
    for face, at in ((swap, jnp.where(even, cy - 1, 0)), (other, jnp.where(even, 0, cy - 1))):
        copies.start(vort.at[:, :, at], face.at[0:3])
        copies.start(velo.at[:, :, at], face.at[3:6])
        copies.start(visc.at[:, at], face.at[6])
    copies.wait(0, 4)
    pack_tiles(cap, cx * cy * nz, weights, cells, dest, count, packets)
    copies.start(packets, packets_out)
    tile_moments(cap, nz, packets, moments)
    copies.start(moments, moments_out)
    copies.wait(4, 10)
    copies.start(near, near_out)
    copies.start(far, far_out)
    copies.wait(10, 16)
    copies.start(swap, swap_out)
    copies.start(other, other_out)
    copies.wait(16, 22)


def to_send(vort, velo, visc, weights, cells, dest, count, n_slab, cap):
    _, cx, cy, nz = vort.shape
    made = (
        shaped(7, cy, nz),
        shaped(7, cy, nz),
        shaped(7, cx, nz),
        shaped(7, cx, nz),
        shaped(n_slab * cap, 4, weights.shape[2]),
        shaped(4, n_slab * nz // CB),
    )
    return pl.pallas_call(
        functools.partial(send_kernel, cap),
        out_shape=made,
        in_specs=[ANY] * 7,
        out_specs=(ANY,) * 6,
        scratch_shapes=[pltpu.VMEM(one.shape, jnp.float32) for one in made]
        + [
            pltpu.VMEM(weights.shape, jnp.float32),
            pltpu.VMEM(cells.shape, jnp.int32),
            pltpu.VMEM(dest.shape, jnp.int32),
            pltpu.SMEM(count.shape, jnp.int32),
            pltpu.SemaphoreType.DMA((22,)),
        ],
        compiler_params=FIRST_PARAMS,
    )(vort, velo, visc, weights, cells, dest, count)


def ahead(a, axis):
    return pltpu.roll(a, a.shape[axis] - 1, axis)


def behind(a, axis):
    return pltpu.roll(a, 1, axis)


def interior_step(vort, velo, visc, out):
    cx, cy, nz = visc.shape
    has_ahead = lax.broadcasted_iota(jnp.int32, (cy, nz), 0) < cy - 1
    totals = [jnp.zeros((8, nz), jnp.float32) for _ in range(3)]
    flux_x = [None] * 3
    for x in range(cx):
        nu = visc[x]
        spin = [vort[c, x] for c in range(3)]
        mean_y = jnp.where(has_ahead, 0.5 * (nu + ahead(nu, 0)), 0.0)
        mean_z = 0.5 * (nu + ahead(nu, 1))
        half_y = 0.5 * spin[1]
        half_z = 0.5 * spin[2]
        next_y = jnp.where(has_ahead, ahead(half_y, 0), 0.0)
        next_z = ahead(half_z, 1)
        half_y = jnp.where(has_ahead, half_y, 0.0)
        half_x = 0.5 * spin[0]
        if x < cx - 1:
            mean_x = 0.5 * (nu + visc[x + 1])
        for c in range(3):
            w = spin[c]
            u = velo[c, x]
            flux_y = mean_y * (ahead(w, 0) - w)
            flux_z = mean_z * (ahead(w, 1) - w)
            change = flux_y + half_y * ahead(u, 0) - behind(flux_y + next_y * u, 0)
            change = change + (flux_z + half_z * ahead(u, 1) - behind(flux_z + next_z * u, 1))
            if x == 0:
                change = change + half_x * velo[c, x + 1]
            elif x == cx - 1:
                change = change - half_x * velo[c, x - 1]
            else:
                change = change + half_x * (velo[c, x + 1] - velo[c, x - 1])
            if x > 0:
                change = change - flux_x[c]
            if x < cx - 1:
                flux_x[c] = mean_x * (vort[c, x + 1] - w)
                change = change + flux_x[c]
            new = w + TIME_STEP * change
            out[c, x] = new
            totals[c] = totals[c] + jnp.sum(new.reshape(cy // 8, 8, nz), axis=0)
    return [jnp.sum(total, axis=0, keepdims=True) for total in totals]


def by_level(totals, width):
    nz = totals[0].shape[1]
    shape = (nz, width)
    level = lax.broadcasted_iota(jnp.int32, shape, 0) // CB
    lane = lax.broadcasted_iota(jnp.int32, shape, 1)
    pick = (lane == lax.axis_index("slab") * (nz // CB) + level).astype(jnp.float32).astype(jnp.bfloat16)
    rows = jnp.concatenate(totals + [jnp.zeros_like(totals[0])], axis=0)
    found = jnp.dot(jnp.concatenate(thirds(rows), axis=0), pick, preferred_element_type=jnp.float32)
    return found[0:4] + (found[4:8] + found[8:12])


def inner_kernel(vort, velo, visc, tiles_in, out, moments, tiles, sem):
    copy = pltpu.make_async_copy(tiles_in, tiles, sem)
    copy.start()
    own = by_level(interior_step(vort, velo, visc, out), moments.shape[1])
    copy.wait()
    moments[...] = tiles[...] + own


def inner(vort, velo, visc, tiles):
    return pl.pallas_call(
        inner_kernel,
        out_shape=(shaped(*vort.shape), shaped(*tiles.shape)),
        in_specs=[VMEM] * 3 + [ANY],
        out_specs=(VMEM,) * 2,
        scratch_shapes=[pltpu.VMEM(tiles.shape, jnp.float32), pltpu.SemaphoreType.DMA],
        compiler_params=PARAMS,
    )(vort, velo, visc, tiles)


def face_change(own, other, along, sign, c):
    stretch = (0.5 * sign) * own[along] * other[3 + c]
    diffuse = 0.5 * (own[6] + other[6]) * (other[c] - own[c])
    return TIME_STEP * (stretch + diffuse)


def edge_kernel(
    inside, moments, near, far, swap, other, near_in, far_in, swap_in, other_in, out, load_out, load, side_change, sem
):
    _, cx, cy, nz = out.shape
    even = lax.axis_index("pencil") % 2 == 0
    low, low_in = jnp.where(even, other[...], swap[...]), jnp.where(even, other_in[...], swap_in[...])
    high, high_in = jnp.where(even, swap[...], other[...]), jnp.where(even, swap_in[...], other_in[...])
    even = lax.axis_index("slab") % 2 == 0
    near_at, far_at = jnp.where(even, cx - 1, 0), jnp.where(even, 0, cx - 1)
    near_sign = jnp.where(even, 1.0, -1.0)
    totals = []
    for c in range(3):
        total = jnp.zeros((8, nz), jnp.float32)
        for own, came, at, sign in ((near, near_in, near_at, near_sign), (far, far_in, far_at, -near_sign)):
            change = face_change(own, came, 0, sign, c)
            out[c, at] = inside[c, at] + change
            total = total + jnp.sum(change.reshape(cy // 8, 8, nz), axis=0)
        for k, own, came, sign in ((0, low, low_in, -1.0), (1, high, high_in, 1.0)):
            change = face_change(own, came, 1, sign, c)
            side_change[k, c] = change
            total = total + change
        totals.append(jnp.sum(total, axis=0, keepdims=True))
    moment = moments[...] + by_level(totals, moments.shape[1])
    for k in range(load.shape[1] // 4):
        part = moment[:, k * LANES : (k + 1) * LANES]
        load[:, 4 * k : 4 * k + 4, :] = jnp.broadcast_to(part[None], (load.shape[0], 4, LANES))
    copy = pltpu.make_async_copy(load, load_out, sem)
    copy.start()
    for c in range(3):
        out[c, 1 : cx - 1] = inside[c, 1 : cx - 1]
        for k, at in ((0, 0), (1, cy - 1)):
            for x in range(cx):
                out[c, x, at : at + 1, :] = out[c, x, at : at + 1, :] + side_change[k, c, x : x + 1, :]
    copy.wait()


def edges(inside, moments, faces, halos, n_all):
    _, cx, _, nz = inside.shape
    load = shaped(n_all, 4 * moments.shape[1] // LANES, LANES)
    return pl.pallas_call(
        edge_kernel,
        out_shape=(shaped(*inside.shape), load),
        in_specs=[VMEM] * 10,
        out_specs=(VMEM, ANY),
        scratch_shapes=[
            pltpu.VMEM(load.shape, jnp.float32),
            pltpu.VMEM((2, 3, cx, nz), jnp.float32),
            pltpu.SemaphoreType.DMA,
        ],
        compiler_params=PARAMS,
    )(inside, moments, *faces, *halos)


def far_kernel(cx, cy, ncl, n_pencil, load, out):
    n_all = load.shape[0]
    n_slab = n_all // n_pencil
    slab = lax.axis_index("slab")
    pencil = lax.axis_index("pencil")
    shape = (ncl, n_slab * ncl)
    target = lax.broadcasted_iota(jnp.int32, shape, 0)
    source = lax.broadcasted_iota(jnp.int32, shape, 1)
    sigma = jnp.float32(cx * n_slab // 4)
    rel_x = ((slab - source // ncl) * cx).astype(jnp.float32)
    rel_z = ((target - source % ncl) * CB).astype(jnp.float32)
    flat = rel_x * rel_x + rel_z * rel_z + sigma * sigma
    turned = [jnp.zeros(shape, jnp.float32) for _ in range(3)]
    for p in range(n_pencil):
        total = load[p]
        for s in range(1, n_slab):
            total = total + load[s * n_pencil + p]
        moment = jnp.concatenate([total[4 * k : 4 * k + 4] for k in range(load.shape[1] // 4)], axis=1)
        first, second, third = moment[0:1], moment[1:2], moment[2:3]
        rel_y = ((pencil - p) * cy).astype(jnp.float32)
        inverse = lax.rsqrt(flat + rel_y * rel_y)
        weight = inverse * inverse * inverse
        turned[0] = turned[0] + weight * (rel_z * second - rel_y * third)
        turned[1] = turned[1] + weight * (rel_x * third - rel_z * first)
        turned[2] = turned[2] + weight * (rel_y * first - rel_x * second)
    ones = jnp.ones((8, shape[1]), jnp.float32)
    for c in range(3):
        row = lax.dot_general(
            ones,
            turned[c],
            (((1,), (1,)), ((), ())),
            precision=lax.Precision.HIGHEST,
            preferred_element_type=jnp.float32,
        )
        out[c, 0] = row[0:1]


def far(load, cx, cy, ncl, n_pencil):
    return pl.pallas_call(
        functools.partial(far_kernel, cx, cy, ncl, n_pencil),
        out_shape=shaped(3, 1, 1, ncl),
        in_specs=[VMEM],
        out_specs=VMEM,
        compiler_params=PARAMS,
    )(load)


def deposit_step(group, first, listed, load, order, acc, shape):
    cx, cy, nz = shape
    rows = cx * cy // 2
    wide = group * load.shape[2]

    def numbers(length):
        shape = (length // 16, 16, wide)
        return (lax.broadcasted_iota(jnp.int32, shape, 0) * 16 + lax.broadcasted_iota(jnp.int32, shape, 1)).astype(
            jnp.float32
        ).astype(jnp.bfloat16)

    def spread(row):
        return jnp.broadcast_to(row, (16, wide)).astype(jnp.bfloat16)[None]

    zero = jnp.zeros((), jnp.bfloat16)
    one = jnp.ones((), jnp.bfloat16)
    block = jnp.concatenate([load[order[first + k]] for k in range(group)], axis=1)
    live = lax.broadcasted_iota(jnp.int32, (1, wide), 1) // load.shape[2] < listed - first
    cell = block[3:4, :].astype(jnp.int32) % (cx * cy * nz)
    row = cell // nz
    half = row // rows
    at_row = numbers(rows) == spread(jnp.where(live, row % rows, -1).astype(jnp.float32))
    right = []
    for h in range(2):
        at_col = numbers(nz) == spread(jnp.where(half == h, cell % nz, -1).astype(jnp.float32))
        right.append(jnp.where(at_col, one, zero).reshape(nz, wide))
    left = []
    for piece in split(block):
        for c in range(3):
            left.append(jnp.where(at_row, spread(piece[c : c + 1, :]), zero).reshape(rows, wide))
    added = lax.dot_general(
        jnp.concatenate(left, axis=0),
        jnp.concatenate(right, axis=0),
        (((1,), (1,)), ((), ())),
        preferred_element_type=jnp.float32,
    )
    acc[...] += (added[: 3 * rows] + added[3 * rows :]).reshape(acc.shape)


def deposit_kernel(cap, inside, load, out, acc, order, sems):
    _, cx, cy, nz = out.shape
    shape = (cx, cy, nz)
    for h in range(2):
        acc[:, :, :, h * nz : (h + 1) * nz] = inside[:, h * (cx // 2) : (h + 1) * (cx // 2)]
    listed = jnp.int32(0)
    for d in range(load.shape[0] // cap):
        first = d * cap
        held = jnp.max(load[first, 3:4, :]).astype(jnp.int32) // (cx * cy * nz)
        for k in range(cap):
            order[listed + k] = first + k
        listed = listed + held
    for k in range(GROUP):
        order[listed + k] = 0
    rest = listed % GROUP
    whole = listed // GROUP + (rest > GROUP // 2).astype(jnp.int32)

    def step(g, carry):
        deposit_step(GROUP, g * GROUP, listed, load, order, acc, shape)
        return carry

    lax.fori_loop(0, whole, step, 0)

    @pl.when((rest > 0) & (rest <= GROUP // 2))
    def _():
        deposit_step(GROUP // 2, whole * GROUP, listed, load, order, acc, shape)

    copies = Copies(sems)
    for c in range(3):
        for h in range(2):
            part = acc.at[c, :, :, h * nz : (h + 1) * nz]
            copies.start(part, out.at[c, h * (cx // 2) : (h + 1) * (cx // 2)])
    copies.wait(0, 6)


def deposit(inside, load, cap):
    return pl.pallas_call(
        functools.partial(deposit_kernel, cap),
        out_shape=shaped(*inside.shape),
        in_specs=[VMEM] * 2,
        out_specs=ANY,
        scratch_shapes=[
            pltpu.VMEM((3, inside.shape[1] // 2, inside.shape[2], 2 * inside.shape[3]), jnp.float32),
            pltpu.SMEM((load.shape[0] + max(cap, GROUP),), jnp.int32),
            pltpu.SemaphoreType.DMA((6,)),
        ],
        compiler_params=PARAMS,
    )(inside, load)


def swapped(array, axis, first):
    up = [(i, i + 1) for i in range(first, lax.axis_size(axis) - 1, 2)]
    return lax.ppermute(array, axis, up + [(j, i) for i, j in up])


def per_device(vorticity, velocity, viscosity, tile_weights, tile_cells, tile_dest, tile_count):
    _, cx, cy, nz = vorticity.shape
    ncl = nz // CB
    n_slab = lax.axis_size("slab")
    n_pencil = lax.axis_size("pencil")
    cap = 2 * tile_weights.shape[0] // n_slab
    weights = jnp.transpose(tile_weights, (1, 0, 2))
    count = tile_count
    *faces, packets, tiles = to_send(
        vorticity, velocity, viscosity, weights, tile_cells, tile_dest.T, count, n_slab, cap
    )
    halos = [swapped(face, axis, k % 2) for k, (face, axis) in enumerate(zip(faces, SIDES))]
    order = outward(n_slab)
    arrived = lax.all_to_all(packets, "slab", 0, 0, axis_index_groups=[order], tiled=True)
    inside, moments = inner(vorticity, velocity, viscosity, tiles)
    advanced, load = edges(inside, moments, faces, halos, n_slab * n_pencil)
    everyone = [s * n_pencil + p for s in order for p in range(n_pencil)]
    load = lax.all_to_all(load, ("slab", "pencil"), 0, 0, axis_index_groups=[everyone], tiled=True)
    vorticity_out = deposit(advanced, arrived, cap)
    return (vorticity_out, far(load, cx, cy, ncl, n_pencil))


def solution(mesh):
    in_specs = (
        P(None, "slab", "pencil", None),
        P(None, "slab", "pencil", None),
        P("slab", "pencil", None),
        P(("slab", "pencil"), None, None),
        P(("slab", "pencil"), None),
        P(("slab", "pencil"), None),
        P(("slab", "pencil")),
    )
    out_specs = (P(None, "slab", "pencil", None), P(None, "slab", "pencil", None))
    return jax.shard_map(
        per_device, mesh=mesh, in_specs=in_specs, out_specs=out_specs, check_vma=False
    )
```

```python
import functools

import jax
import jax.numpy as jnp
from jax import lax
from jax.experimental import pallas as pl
from jax.experimental.pallas import tpu as pltpu
from jax.sharding import PartitionSpec as P

CB = 16
TIME_STEP = 0.1
LANES = 128
SIDES = ("slab", "slab", "pencil", "pencil")
GROUP = 16
VMEM_LIMIT = 24 * 1024 * 1024

VMEM = pl.BlockSpec(memory_space=pltpu.VMEM)
ANY = pl.BlockSpec(memory_space=pl.ANY)
SMEM = pl.BlockSpec(memory_space=pltpu.SMEM)
FIRST_PARAMS = pltpu.CompilerParams(vmem_limit_bytes=60 * 1024 * 1024)
PARAMS = pltpu.CompilerParams(vmem_limit_bytes=VMEM_LIMIT)


def shaped(*shape):
    return jax.ShapeDtypeStruct(shape, jnp.float32)


def split(w):
    high = w.astype(jnp.bfloat16).astype(jnp.float32)
    return high, w - high


def thirds(w):
    high, rest = split(w)
    middle, low = split(rest)
    return [piece.astype(jnp.bfloat16) for piece in (high, middle, low)]


def outward(count):
    half = count // 2
    return [(half + (k + 1) // 2) % count if k % 2 else half - k // 2 for k in range(count)]


def pack_tiles(cap, cells_dev, weights, cells, dest, count, packets):
    slots = packets.shape[0]
    tiles = cells.shape[0]
    half = slots // cap // 2
    names = dest[...]
    names = jnp.where(names > half, 2 * (names - half) - 1, 2 * (half - names))
    names = jnp.minimum(names, 2 * half - 1)
    live = (lax.broadcasted_iota(jnp.int32, (1, tiles), 1) < count[0]).astype(jnp.float32)
    same = (lax.broadcasted_iota(jnp.int32, (slots // cap, tiles), 0) == names).astype(jnp.float32)
    shape = (tiles, tiles)
    earlier = lax.broadcasted_iota(jnp.int32, shape, 0) < lax.broadcasted_iota(jnp.int32, shape, 1)
    before = jnp.dot(same, earlier.astype(jnp.float32), preferred_element_type=jnp.float32)
    rank = jnp.sum(same * before, axis=0, keepdims=True).astype(jnp.int32)
    slot = lax.broadcasted_iota(jnp.int32, (slots, tiles), 0)
    placed = (slot == names * cap + rank).astype(jnp.float32) * live
    held = jnp.sum((slot == names * cap).astype(jnp.float32) * live, axis=1, keepdims=True)
    rows = [weights[0], weights[1], weights[2], cells[...].astype(jnp.float32)]
    found = jnp.dot(
        jnp.concatenate([placed] * 3, axis=1).astype(jnp.bfloat16),
        jnp.concatenate(thirds(jnp.concatenate(rows, axis=1)), axis=0),
        preferred_element_type=jnp.float32,
    )
    length = cells.shape[1]
    for c in range(3):
        packets[:, c, :] = found[:, c * length : (c + 1) * length]
    packets[:, 3, :] = found[:, 3 * length :] + held * cells_dev


def tile_moments(cap, nz, packets, moments):
    n_slab = packets.shape[0] // cap
    ncl = nz // CB
    wide = cap * packets.shape[2]
    level = lax.broadcasted_iota(jnp.int32, (ncl, wide), 0)
    found = []
    order = outward(n_slab)
    for d in range(n_slab):
        block = jnp.concatenate([packets[order.index(d) * cap + k] for k in range(cap)], axis=1)
        cell = block[3:4, :].astype(jnp.int32)
        spots = (level == cell % nz // CB).astype(jnp.float32).astype(jnp.bfloat16)
        high, low = split(block)
        left = jnp.concatenate([high, low], axis=0).astype(jnp.bfloat16)
        sums = lax.dot_general(left, spots, (((1,), (1,)), ((), ())), preferred_element_type=jnp.float32)
        found.append(sums[0:4] + sums[4:8])
    moments[...] = jnp.concatenate(found, axis=1)


class Copies:
    def __init__(self, sems):
        self.sems = sems
        self.made = []

    def start(self, source, target, priority=0):
        self.made.append(pltpu.make_async_copy(source, target, self.sems.at[len(self.made)]))
        self.made[-1].start(priority)

    def wait(self, first, last):
        for k in range(first, last):
            self.made[k].wait()


def send_kernel(
    cap,
    vort,
    velo,
    visc,
    weights_in,
    cells_in,
    dest_in,
    count_in,
    near_out,
    far_out,
    swap_out,
    other_out,
    packets_out,
    moments_out,
    near,
    far,
    swap,
    other,
    packets,
    moments,
    weights,
    cells,
    dest,
    count,
    sems,
):
    cx, cy, nz = visc.shape
    copies = Copies(sems)
    copies.start(weights_in, weights)
    copies.start(cells_in, cells)
    copies.start(dest_in, dest)
    copies.start(count_in, count)
    even = lax.axis_index("slab") % 2 == 0
    for face, at in ((near, jnp.where(even, cx - 1, 0)), (far, jnp.where(even, 0, cx - 1))):
        copies.start(vort.at[:, at], face.at[0:3], 1)
        copies.start(velo.at[:, at], face.at[3:6], 1)
        copies.start(visc.at[at], face.at[6], 1)
    even = lax.axis_index("pencil") % 2 == 0
    for face, at in ((swap, jnp.where(even, cy - 1, 0)), (other, jnp.where(even, 0, cy - 1))):
        copies.start(vort.at[:, :, at], face.at[0:3])
        copies.start(velo.at[:, :, at], face.at[3:6])
        copies.start(visc.at[:, at], face.at[6])
    copies.wait(0, 4)
    pack_tiles(cap, cx * cy * nz, weights, cells, dest, count, packets)
    copies.start(packets, packets_out)
    copies.wait(4, 10)
    copies.start(near, near_out, 1)
    copies.start(far, far_out, 1)
    tile_moments(cap, nz, packets, moments)
    copies.start(moments, moments_out)
    copies.wait(10, 16)
    copies.start(swap, swap_out)
    copies.start(other, other_out)
    copies.wait(16, 22)


def to_send(vort, velo, visc, weights, cells, dest, count, n_slab, cap):
    _, cx, cy, nz = vort.shape
    made = (
        shaped(7, cy, nz),
        shaped(7, cy, nz),
        shaped(7, cx, nz),
        shaped(7, cx, nz),
        shaped(n_slab * cap, 4, weights.shape[2]),
        shaped(4, n_slab * nz // CB),
    )
    return pl.pallas_call(
        functools.partial(send_kernel, cap),
        out_shape=made,
        in_specs=[ANY] * 7,
        out_specs=(ANY,) * 6,
        scratch_shapes=[pltpu.VMEM(one.shape, jnp.float32) for one in made]
        + [
            pltpu.VMEM(weights.shape, jnp.float32),
            pltpu.VMEM(cells.shape, jnp.int32),
            pltpu.VMEM(dest.shape, jnp.int32),
            pltpu.SMEM(count.shape, jnp.int32),
            pltpu.SemaphoreType.DMA((22,)),
        ],
        compiler_params=FIRST_PARAMS,
    )(vort, velo, visc, weights, cells, dest, count)


def ahead(a, axis):
    return pltpu.roll(a, a.shape[axis] - 1, axis)


def behind(a, axis):
    return pltpu.roll(a, 1, axis)


def interior_step(vort, velo, visc, out):
    cx, cy, nz = visc.shape
    has_ahead = lax.broadcasted_iota(jnp.int32, (cy, nz), 0) < cy - 1
    totals = [jnp.zeros((8, nz), jnp.float32) for _ in range(3)]
    flux_x = [None] * 3
    for x in range(cx):
        nu = visc[x]
        spin = [vort[c, x] for c in range(3)]
        mean_y = jnp.where(has_ahead, 0.5 * (nu + ahead(nu, 0)), 0.0)
        mean_z = 0.5 * (nu + ahead(nu, 1))
        half_y = 0.5 * spin[1]
        half_z = 0.5 * spin[2]
        next_y = jnp.where(has_ahead, ahead(half_y, 0), 0.0)
        next_z = ahead(half_z, 1)
        half_y = jnp.where(has_ahead, half_y, 0.0)
        half_x = 0.5 * spin[0]
        if x < cx - 1:
            mean_x = 0.5 * (nu + visc[x + 1])
        for c in range(3):
            w = spin[c]
            u = velo[c, x]
            flux_y = mean_y * (ahead(w, 0) - w)
            flux_z = mean_z * (ahead(w, 1) - w)
            change = flux_y + half_y * ahead(u, 0) - behind(flux_y + next_y * u, 0)
            change = change + (flux_z + half_z * ahead(u, 1) - behind(flux_z + next_z * u, 1))
            if x == 0:
                change = change + half_x * velo[c, x + 1]
            elif x == cx - 1:
                change = change - half_x * velo[c, x - 1]
            else:
                change = change + half_x * (velo[c, x + 1] - velo[c, x - 1])
            if x > 0:
                change = change - flux_x[c]
            if x < cx - 1:
                flux_x[c] = mean_x * (vort[c, x + 1] - w)
                change = change + flux_x[c]
            new = w + TIME_STEP * change
            out[c, x] = new
            totals[c] = totals[c] + jnp.sum(new.reshape(cy // 8, 8, nz), axis=0)
    return [jnp.sum(total, axis=0, keepdims=True) for total in totals]


def by_level(totals, width):
    nz = totals[0].shape[1]
    shape = (nz, width)
    level = lax.broadcasted_iota(jnp.int32, shape, 0) // CB
    lane = lax.broadcasted_iota(jnp.int32, shape, 1)
    pick = (lane == lax.axis_index("slab") * (nz // CB) + level).astype(jnp.float32).astype(jnp.bfloat16)
    rows = jnp.concatenate(totals + [jnp.zeros_like(totals[0])], axis=0)
    found = jnp.dot(jnp.concatenate(thirds(rows), axis=0), pick, preferred_element_type=jnp.float32)
    return found[0:4] + (found[4:8] + found[8:12])


def inner_kernel(vort, velo, visc, tiles_in, out, moments, tiles, sem):
    copy = pltpu.make_async_copy(tiles_in, tiles, sem)
    copy.start()
    own = by_level(interior_step(vort, velo, visc, out), moments.shape[1])
    copy.wait()
    moments[...] = tiles[...] + own


def inner(vort, velo, visc, tiles):
    return pl.pallas_call(
        inner_kernel,
        out_shape=(shaped(*vort.shape), shaped(*tiles.shape)),
        in_specs=[VMEM] * 3 + [ANY],
        out_specs=(VMEM,) * 2,
        scratch_shapes=[pltpu.VMEM(tiles.shape, jnp.float32), pltpu.SemaphoreType.DMA],
        compiler_params=PARAMS,
    )(vort, velo, visc, tiles)


def face_change(own, other, along, sign, c):
    stretch = (0.5 * sign) * own[along] * other[3 + c]
    diffuse = 0.5 * (own[6] + other[6]) * (other[c] - own[c])
    return TIME_STEP * (stretch + diffuse)


def edge_kernel(
    inside, moments, near, far, swap, other, near_in, far_in, swap_in, other_in, out, load_out, load, side_change, sem
):
    _, cx, cy, nz = out.shape
    even = lax.axis_index("pencil") % 2 == 0
    low, low_in = jnp.where(even, other[...], swap[...]), jnp.where(even, other_in[...], swap_in[...])
    high, high_in = jnp.where(even, swap[...], other[...]), jnp.where(even, swap_in[...], other_in[...])
    even = lax.axis_index("slab") % 2 == 0
    near_at, far_at = jnp.where(even, cx - 1, 0), jnp.where(even, 0, cx - 1)
    near_sign = jnp.where(even, 1.0, -1.0)
    totals = []
    for c in range(3):
        total = jnp.zeros((8, nz), jnp.float32)
        for own, came, at, sign in ((near, near_in, near_at, near_sign), (far, far_in, far_at, -near_sign)):
            change = face_change(own, came, 0, sign, c)
            out[c, at] = inside[c, at] + change
            total = total + jnp.sum(change.reshape(cy // 8, 8, nz), axis=0)
        for k, own, came, sign in ((0, low, low_in, -1.0), (1, high, high_in, 1.0)):
            change = face_change(own, came, 1, sign, c)
            side_change[k, c] = change
            total = total + change
        totals.append(jnp.sum(total, axis=0, keepdims=True))
    moment = moments[...] + by_level(totals, moments.shape[1])
    for k in range(load.shape[1] // 4):
        part = moment[:, k * LANES : (k + 1) * LANES]
        load[:, 4 * k : 4 * k + 4, :] = jnp.broadcast_to(part[None], (load.shape[0], 4, LANES))
    copy = pltpu.make_async_copy(load, load_out, sem)
    copy.start()
    for c in range(3):
        out[c, 1 : cx - 1] = inside[c, 1 : cx - 1]
        for k, at in ((0, 0), (1, cy - 1)):
            for x in range(cx):
                out[c, x, at : at + 1, :] = out[c, x, at : at + 1, :] + side_change[k, c, x : x + 1, :]
    copy.wait()


def edges(inside, moments, faces, halos, n_all):
    _, cx, _, nz = inside.shape
    load = shaped(n_all, 4 * moments.shape[1] // LANES, LANES)
    return pl.pallas_call(
        edge_kernel,
        out_shape=(shaped(*inside.shape), load),
        in_specs=[VMEM] * 10,
        out_specs=(VMEM, ANY),
        scratch_shapes=[
            pltpu.VMEM(load.shape, jnp.float32),
            pltpu.VMEM((2, 3, cx, nz), jnp.float32),
            pltpu.SemaphoreType.DMA,
        ],
        compiler_params=PARAMS,
    )(inside, moments, *faces, *halos)


def far_kernel(cx, cy, ncl, n_pencil, load, out):
    n_all = load.shape[0]
    n_slab = n_all // n_pencil
    slab = lax.axis_index("slab")
    pencil = lax.axis_index("pencil")
    shape = (ncl, n_slab * ncl)
    target = lax.broadcasted_iota(jnp.int32, shape, 0)
    source = lax.broadcasted_iota(jnp.int32, shape, 1)
    sigma = jnp.float32(cx * n_slab // 4)
    rel_x = ((slab - source // ncl) * cx).astype(jnp.float32)
    rel_z = ((target - source % ncl) * CB).astype(jnp.float32)
    flat = rel_x * rel_x + rel_z * rel_z + sigma * sigma
    turned = [jnp.zeros(shape, jnp.float32) for _ in range(3)]
    for p in range(n_pencil):
        total = load[p]
        for s in range(1, n_slab):
            total = total + load[s * n_pencil + p]
        moment = jnp.concatenate([total[4 * k : 4 * k + 4] for k in range(load.shape[1] // 4)], axis=1)
        first, second, third = moment[0:1], moment[1:2], moment[2:3]
        rel_y = ((pencil - p) * cy).astype(jnp.float32)
        inverse = lax.rsqrt(flat + rel_y * rel_y)
        weight = inverse * inverse * inverse
        turned[0] = turned[0] + weight * (rel_z * second - rel_y * third)
        turned[1] = turned[1] + weight * (rel_x * third - rel_z * first)
        turned[2] = turned[2] + weight * (rel_y * first - rel_x * second)
    ones = jnp.ones((8, shape[1]), jnp.float32)
    for c in range(3):
        row = lax.dot_general(
            ones,
            turned[c],
            (((1,), (1,)), ((), ())),
            precision=lax.Precision.HIGHEST,
            preferred_element_type=jnp.float32,
        )
        out[c, 0] = row[0:1]


def far(load, cx, cy, ncl, n_pencil):
    return pl.pallas_call(
        functools.partial(far_kernel, cx, cy, ncl, n_pencil),
        out_shape=shaped(3, 1, 1, ncl),
        in_specs=[VMEM],
        out_specs=VMEM,
        compiler_params=PARAMS,
    )(load)


def deposit_step(group, first, listed, load, order, acc, shape):
    cx, cy, nz = shape
    rows = cx * cy // 2
    wide = group * load.shape[2]

    def numbers(length):
        shape = (length // 16, 16, wide)
        return (lax.broadcasted_iota(jnp.int32, shape, 0) * 16 + lax.broadcasted_iota(jnp.int32, shape, 1)).astype(
            jnp.float32
        ).astype(jnp.bfloat16)

    def spread(row):
        return jnp.broadcast_to(row, (16, wide)).astype(jnp.bfloat16)[None]

    zero = jnp.zeros((), jnp.bfloat16)
    one = jnp.ones((), jnp.bfloat16)
    block = jnp.concatenate([load[order[first + k]] for k in range(group)], axis=1)
    live = lax.broadcasted_iota(jnp.int32, (1, wide), 1) // load.shape[2] < listed - first
    cell = block[3:4, :].astype(jnp.int32) % (cx * cy * nz)
    row = cell // nz
    half = row // rows
    at_row = numbers(rows) == spread(jnp.where(live, row % rows, -1).astype(jnp.float32))
    right = []
    for h in range(2):
        at_col = numbers(nz) == spread(jnp.where(half == h, cell % nz, -1).astype(jnp.float32))
        right.append(jnp.where(at_col, one, zero).reshape(nz, wide))
    left = []
    for piece in split(block):
        for c in range(3):
            left.append(jnp.where(at_row, spread(piece[c : c + 1, :]), zero).reshape(rows, wide))
    added = lax.dot_general(
        jnp.concatenate(left, axis=0),
        jnp.concatenate(right, axis=0),
        (((1,), (1,)), ((), ())),
        preferred_element_type=jnp.float32,
    )
    acc[...] += (added[: 3 * rows] + added[3 * rows :]).reshape(acc.shape)


def deposit_kernel(cap, inside, load, out, acc, order, sems):
    _, cx, cy, nz = out.shape
    shape = (cx, cy, nz)
    for h in range(2):
        acc[:, :, :, h * nz : (h + 1) * nz] = inside[:, h * (cx // 2) : (h + 1) * (cx // 2)]
    listed = jnp.int32(0)
    for d in range(load.shape[0] // cap):
        first = d * cap
        held = jnp.max(load[first, 3:4, :]).astype(jnp.int32) // (cx * cy * nz)
        for k in range(cap):
            order[listed + k] = first + k
        listed = listed + held
    for k in range(GROUP):
        order[listed + k] = 0
    rest = listed % GROUP
    whole = listed // GROUP + (rest > GROUP // 2).astype(jnp.int32)

    def step(g, carry):
        deposit_step(GROUP, g * GROUP, listed, load, order, acc, shape)
        return carry

    lax.fori_loop(0, whole, step, 0)

    @pl.when((rest > 0) & (rest <= GROUP // 2))
    def _():
        deposit_step(GROUP // 2, whole * GROUP, listed, load, order, acc, shape)

    copies = Copies(sems)
    for c in range(3):
        for h in range(2):
            part = acc.at[c, :, :, h * nz : (h + 1) * nz]
            copies.start(part, out.at[c, h * (cx // 2) : (h + 1) * (cx // 2)])
    copies.wait(0, 6)


def deposit(inside, load, cap):
    return pl.pallas_call(
        functools.partial(deposit_kernel, cap),
        out_shape=shaped(*inside.shape),
        in_specs=[VMEM] * 2,
        out_specs=ANY,
        scratch_shapes=[
            pltpu.VMEM((3, inside.shape[1] // 2, inside.shape[2], 2 * inside.shape[3]), jnp.float32),
            pltpu.SMEM((load.shape[0] + max(cap, GROUP),), jnp.int32),
            pltpu.SemaphoreType.DMA((6,)),
        ],
        compiler_params=PARAMS,
    )(inside, load)


def swapped(array, axis, first):
    up = [(i, i + 1) for i in range(first, lax.axis_size(axis) - 1, 2)]
    return lax.ppermute(array, axis, up + [(j, i) for i, j in up])


def per_device(vorticity, velocity, viscosity, tile_weights, tile_cells, tile_dest, tile_count):
    _, cx, cy, nz = vorticity.shape
    ncl = nz // CB
    n_slab = lax.axis_size("slab")
    n_pencil = lax.axis_size("pencil")
    cap = 2 * tile_weights.shape[0] // n_slab
    weights = jnp.transpose(tile_weights, (1, 0, 2))
    count = tile_count
    *faces, packets, tiles = to_send(
        vorticity, velocity, viscosity, weights, tile_cells, tile_dest.T, count, n_slab, cap
    )
    halos = [swapped(face, axis, k % 2) for k, (face, axis) in enumerate(zip(faces, SIDES))]
    order = outward(n_slab)
    arrived = lax.all_to_all(packets, "slab", 0, 0, axis_index_groups=[order], tiled=True)
    inside, moments = inner(vorticity, velocity, viscosity, tiles)
    advanced, load = edges(inside, moments, faces, halos, n_slab * n_pencil)
    everyone = [s * n_pencil + p for s in order for p in range(n_pencil)]
    load = lax.all_to_all(load, ("slab", "pencil"), 0, 0, axis_index_groups=[everyone], tiled=True)
    vorticity_out = deposit(advanced, arrived, cap)
    return (vorticity_out, far(load, cx, cy, ncl, n_pencil))


def solution(mesh):
    in_specs = (
        P(None, "slab", "pencil", None),
        P(None, "slab", "pencil", None),
        P("slab", "pencil", None),
        P(("slab", "pencil"), None, None),
        P(("slab", "pencil"), None),
        P(("slab", "pencil"), None),
        P(("slab", "pencil")),
    )
    out_specs = (P(None, "slab", "pencil", None), P(None, "slab", "pencil", None))
    return jax.shard_map(
        per_device, mesh=mesh, in_specs=in_specs, out_specs=out_specs, check_vma=False
    )
```

```python
import functools

import jax
import jax.numpy as jnp
from jax import lax
from jax.experimental import pallas as pl
from jax.experimental.pallas import tpu as pltpu
from jax.sharding import PartitionSpec as P

CB = 16
TIME_STEP = 0.1
LANES = 128
SIDES = ("slab", "slab", "pencil", "pencil")
GROUP = 16
VMEM_LIMIT = 24 * 1024 * 1024

VMEM = pl.BlockSpec(memory_space=pltpu.VMEM)
ANY = pl.BlockSpec(memory_space=pl.ANY)
SMEM = pl.BlockSpec(memory_space=pltpu.SMEM)
FIRST_PARAMS = pltpu.CompilerParams(vmem_limit_bytes=60 * 1024 * 1024)
PARAMS = pltpu.CompilerParams(vmem_limit_bytes=VMEM_LIMIT)


def shaped(*shape):
    return jax.ShapeDtypeStruct(shape, jnp.float32)


def split(w):
    high = w.astype(jnp.bfloat16).astype(jnp.float32)
    return high, w - high


def thirds(w):
    high, rest = split(w)
    middle, low = split(rest)
    return [piece.astype(jnp.bfloat16) for piece in (high, middle, low)]


def outward(count):
    half = count // 2
    return [(half + (k + 1) // 2) % count if k % 2 else half - k // 2 for k in range(count)]


def pack_tiles(cap, cells_dev, weights, cells, dest, count, packets):
    slots = packets.shape[0]
    tiles = cells.shape[0]
    half = slots // cap // 2
    names = dest[...]
    names = jnp.where(names > half, 2 * (names - half) - 1, 2 * (half - names))
    names = jnp.minimum(names, 2 * half - 1)
    live = (lax.broadcasted_iota(jnp.int32, (1, tiles), 1) < count[0]).astype(jnp.float32)
    same = (lax.broadcasted_iota(jnp.int32, (slots // cap, tiles), 0) == names).astype(jnp.float32)
    shape = (tiles, tiles)
    earlier = lax.broadcasted_iota(jnp.int32, shape, 0) < lax.broadcasted_iota(jnp.int32, shape, 1)
    before = jnp.dot(same, earlier.astype(jnp.float32), preferred_element_type=jnp.float32)
    rank = jnp.sum(same * before, axis=0, keepdims=True).astype(jnp.int32)
    slot = lax.broadcasted_iota(jnp.int32, (slots, tiles), 0)
    placed = (slot == names * cap + rank).astype(jnp.float32) * live
    held = jnp.sum((slot == names * cap).astype(jnp.float32) * live, axis=1, keepdims=True)
    rows = [weights[0], weights[1], weights[2], cells[...].astype(jnp.float32)]
    found = jnp.dot(
        jnp.concatenate([placed] * 3, axis=1).astype(jnp.bfloat16),
        jnp.concatenate(thirds(jnp.concatenate(rows, axis=1)), axis=0),
        preferred_element_type=jnp.float32,
    )
    length = cells.shape[1]
    for c in range(3):
        packets[:, c, :] = found[:, c * length : (c + 1) * length]
    packets[:, 3, :] = found[:, 3 * length :] + held * cells_dev


def tile_moments(cap, nz, packets, moments):
    n_slab = packets.shape[0] // cap
    ncl = nz // CB
    wide = cap * packets.shape[2]
    level = lax.broadcasted_iota(jnp.int32, (ncl, wide), 0)
    found = []
    order = outward(n_slab)
    for d in range(n_slab):
        block = jnp.concatenate([packets[order.index(d) * cap + k] for k in range(cap)], axis=1)
        cell = block[3:4, :].astype(jnp.int32)
        spots = (level == cell % nz // CB).astype(jnp.float32).astype(jnp.bfloat16)
        high, low = split(block)
        left = jnp.concatenate([high, low], axis=0).astype(jnp.bfloat16)
        sums = lax.dot_general(left, spots, (((1,), (1,)), ((), ())), preferred_element_type=jnp.float32)
        found.append(sums[0:4] + sums[4:8])
    moments[...] = jnp.concatenate(found, axis=1)


class Copies:
    def __init__(self, sems):
        self.sems = sems
        self.made = []

    def start(self, source, target):
        self.made.append(pltpu.make_async_copy(source, target, self.sems.at[len(self.made)]))
        self.made[-1].start()

    def wait(self, first, last):
        for k in range(first, last):
            self.made[k].wait()


def send_kernel(
    cap,
    vort,
    velo,
    visc,
    weights_in,
    cells_in,
    dest_in,
    count_in,
    near_out,
    far_out,
    swap_out,
    other_out,
    packets_out,
    moments_out,
    near,
    far,
    swap,
    other,
    packets,
    moments,
    weights,
    cells,
    dest,
    count,
    sems,
):
    cx, cy, nz = visc.shape
    copies = Copies(sems)
    copies.start(weights_in, weights)
    copies.start(cells_in, cells)
    copies.start(dest_in, dest)
    copies.start(count_in, count)
    even = lax.axis_index("pencil") % 2 == 0
    for face, at in ((swap, jnp.where(even, cy - 1, 0)), (other, jnp.where(even, 0, cy - 1))):
        copies.start(vort.at[:, :, at], face.at[0:3])
        copies.start(velo.at[:, :, at], face.at[3:6])
        copies.start(visc.at[:, at], face.at[6])
    even = lax.axis_index("slab") % 2 == 0
    for face, at in ((near, jnp.where(even, cx - 1, 0)), (far, jnp.where(even, 0, cx - 1))):
        copies.start(vort.at[:, at], face.at[0:3])
        copies.start(velo.at[:, at], face.at[3:6])
        copies.start(visc.at[at], face.at[6])
    copies.wait(0, 4)
    pack_tiles(cap, cx * cy * nz, weights, cells, dest, count, packets)
    copies.start(packets, packets_out)
    copies.wait(10, 16)
    copies.start(near, near_out)
    copies.start(far, far_out)
    tile_moments(cap, nz, packets, moments)
    copies.start(moments, moments_out)
    copies.wait(4, 10)
    copies.start(swap, swap_out)
    copies.start(other, other_out)
    copies.wait(16, 22)


def to_send(vort, velo, visc, weights, cells, dest, count, n_slab, cap):
    _, cx, cy, nz = vort.shape
    made = (
        shaped(7, cy, nz),
        shaped(7, cy, nz),
        shaped(7, cx, nz),
        shaped(7, cx, nz),
        shaped(n_slab * cap, 4, weights.shape[2]),
        shaped(4, n_slab * nz // CB),
    )
    return pl.pallas_call(
        functools.partial(send_kernel, cap),
        out_shape=made,
        in_specs=[ANY] * 7,
        out_specs=(ANY,) * 6,
        scratch_shapes=[pltpu.VMEM(one.shape, jnp.float32) for one in made]
        + [
            pltpu.VMEM(weights.shape, jnp.float32),
            pltpu.VMEM(cells.shape, jnp.int32),
            pltpu.VMEM(dest.shape, jnp.int32),
            pltpu.SMEM(count.shape, jnp.int32),
            pltpu.SemaphoreType.DMA((22,)),
        ],
        compiler_params=FIRST_PARAMS,
    )(vort, velo, visc, weights, cells, dest, count)


def ahead(a, axis):
    return pltpu.roll(a, a.shape[axis] - 1, axis)


def behind(a, axis):
    return pltpu.roll(a, 1, axis)


def interior_step(vort, velo, visc, out):
    cx, cy, nz = visc.shape
    has_ahead = lax.broadcasted_iota(jnp.int32, (cy, nz), 0) < cy - 1
    totals = [jnp.zeros((8, nz), jnp.float32) for _ in range(3)]
    flux_x = [None] * 3
    for x in range(cx):
        nu = visc[x]
        spin = [vort[c, x] for c in range(3)]
        mean_y = jnp.where(has_ahead, 0.5 * (nu + ahead(nu, 0)), 0.0)
        mean_z = 0.5 * (nu + ahead(nu, 1))
        half_y = 0.5 * spin[1]
        half_z = 0.5 * spin[2]
        next_y = jnp.where(has_ahead, ahead(half_y, 0), 0.0)
        next_z = ahead(half_z, 1)
        half_y = jnp.where(has_ahead, half_y, 0.0)
        half_x = 0.5 * spin[0]
        if x < cx - 1:
            mean_x = 0.5 * (nu + visc[x + 1])
        for c in range(3):
            w = spin[c]
            u = velo[c, x]
            flux_y = mean_y * (ahead(w, 0) - w)
            flux_z = mean_z * (ahead(w, 1) - w)
            change = flux_y + half_y * ahead(u, 0) - behind(flux_y + next_y * u, 0)
            change = change + (flux_z + half_z * ahead(u, 1) - behind(flux_z + next_z * u, 1))
            if x == 0:
                change = change + half_x * velo[c, x + 1]
            elif x == cx - 1:
                change = change - half_x * velo[c, x - 1]
            else:
                change = change + half_x * (velo[c, x + 1] - velo[c, x - 1])
            if x > 0:
                change = change - flux_x[c]
            if x < cx - 1:
                flux_x[c] = mean_x * (vort[c, x + 1] - w)
                change = change + flux_x[c]
            new = w + TIME_STEP * change
            out[c, x] = new
            totals[c] = totals[c] + jnp.sum(new.reshape(cy // 8, 8, nz), axis=0)
    return [jnp.sum(total, axis=0, keepdims=True) for total in totals]


def by_level(totals, width):
    nz = totals[0].shape[1]
    shape = (nz, width)
    level = lax.broadcasted_iota(jnp.int32, shape, 0) // CB
    lane = lax.broadcasted_iota(jnp.int32, shape, 1)
    pick = (lane == lax.axis_index("slab") * (nz // CB) + level).astype(jnp.float32).astype(jnp.bfloat16)
    rows = jnp.concatenate(totals + [jnp.zeros_like(totals[0])], axis=0)
    found = jnp.dot(jnp.concatenate(thirds(rows), axis=0), pick, preferred_element_type=jnp.float32)
    return found[0:4] + (found[4:8] + found[8:12])


def inner_kernel(vort, velo, visc, tiles_in, out, moments, tiles, sem):
    copy = pltpu.make_async_copy(tiles_in, tiles, sem)
    copy.start()
    own = by_level(interior_step(vort, velo, visc, out), moments.shape[1])
    copy.wait()
    moments[...] = tiles[...] + own


def inner(vort, velo, visc, tiles):
    return pl.pallas_call(
        inner_kernel,
        out_shape=(shaped(*vort.shape), shaped(*tiles.shape)),
        in_specs=[VMEM] * 3 + [ANY],
        out_specs=(VMEM,) * 2,
        scratch_shapes=[pltpu.VMEM(tiles.shape, jnp.float32), pltpu.SemaphoreType.DMA],
        compiler_params=PARAMS,
    )(vort, velo, visc, tiles)


def face_change(own, other, along, sign, c):
    stretch = (0.5 * sign) * own[along] * other[3 + c]
    diffuse = 0.5 * (own[6] + other[6]) * (other[c] - own[c])
    return TIME_STEP * (stretch + diffuse)


def edge_kernel(
    inside, moments, near, far, swap, other, near_in, far_in, swap_in, other_in, out, load_out, load, side_change, sem
):
    _, cx, cy, nz = out.shape
    even = lax.axis_index("pencil") % 2 == 0
    low, low_in = jnp.where(even, other[...], swap[...]), jnp.where(even, other_in[...], swap_in[...])
    high, high_in = jnp.where(even, swap[...], other[...]), jnp.where(even, swap_in[...], other_in[...])
    even = lax.axis_index("slab") % 2 == 0
    near_at, far_at = jnp.where(even, cx - 1, 0), jnp.where(even, 0, cx - 1)
    near_sign = jnp.where(even, 1.0, -1.0)
    totals = []
    for c in range(3):
        total = jnp.zeros((8, nz), jnp.float32)
        for own, came, at, sign in ((near, near_in, near_at, near_sign), (far, far_in, far_at, -near_sign)):
            change = face_change(own, came, 0, sign, c)
            out[c, at] = inside[c, at] + change
            total = total + jnp.sum(change.reshape(cy // 8, 8, nz), axis=0)
        for k, own, came, sign in ((0, low, low_in, -1.0), (1, high, high_in, 1.0)):
            change = face_change(own, came, 1, sign, c)
            side_change[k, c] = change
            total = total + change
        totals.append(jnp.sum(total, axis=0, keepdims=True))
    moment = moments[...] + by_level(totals, moments.shape[1])
    for k in range(load.shape[1] // 4):
        part = moment[:, k * LANES : (k + 1) * LANES]
        load[:, 4 * k : 4 * k + 4, :] = jnp.broadcast_to(part[None], (load.shape[0], 4, LANES))
    copy = pltpu.make_async_copy(load, load_out, sem)
    copy.start()
    for c in range(3):
        out[c, 1 : cx - 1] = inside[c, 1 : cx - 1]
        for k, at in ((0, 0), (1, cy - 1)):
            for x in range(cx):
                out[c, x, at : at + 1, :] = out[c, x, at : at + 1, :] + side_change[k, c, x : x + 1, :]
    copy.wait()


def edges(inside, moments, faces, halos, n_all):
    _, cx, _, nz = inside.shape
    load = shaped(n_all, 4 * moments.shape[1] // LANES, LANES)
    return pl.pallas_call(
        edge_kernel,
        out_shape=(shaped(*inside.shape), load),
        in_specs=[VMEM] * 10,
        out_specs=(VMEM, ANY),
        scratch_shapes=[
            pltpu.VMEM(load.shape, jnp.float32),
            pltpu.VMEM((2, 3, cx, nz), jnp.float32),
            pltpu.SemaphoreType.DMA,
        ],
        compiler_params=PARAMS,
    )(inside, moments, *faces, *halos)


def far_kernel(cx, cy, ncl, n_pencil, load, out):
    n_all = load.shape[0]
    n_slab = n_all // n_pencil
    slab = lax.axis_index("slab")
    pencil = lax.axis_index("pencil")
    shape = (ncl, n_slab * ncl)
    target = lax.broadcasted_iota(jnp.int32, shape, 0)
    source = lax.broadcasted_iota(jnp.int32, shape, 1)
    sigma = jnp.float32(cx * n_slab // 4)
    rel_x = ((slab - source // ncl) * cx).astype(jnp.float32)
    rel_z = ((target - source % ncl) * CB).astype(jnp.float32)
    flat = rel_x * rel_x + rel_z * rel_z + sigma * sigma
    turned = [jnp.zeros(shape, jnp.float32) for _ in range(3)]
    for p in range(n_pencil):
        total = load[p]
        for s in range(1, n_slab):
            total = total + load[s * n_pencil + p]
        moment = jnp.concatenate([total[4 * k : 4 * k + 4] for k in range(load.shape[1] // 4)], axis=1)
        first, second, third = moment[0:1], moment[1:2], moment[2:3]
        rel_y = ((pencil - p) * cy).astype(jnp.float32)
        inverse = lax.rsqrt(flat + rel_y * rel_y)
        weight = inverse * inverse * inverse
        turned[0] = turned[0] + weight * (rel_z * second - rel_y * third)
        turned[1] = turned[1] + weight * (rel_x * third - rel_z * first)
        turned[2] = turned[2] + weight * (rel_y * first - rel_x * second)
    ones = jnp.ones((8, shape[1]), jnp.float32)
    for c in range(3):
        row = lax.dot_general(
            ones,
            turned[c],
            (((1,), (1,)), ((), ())),
            precision=lax.Precision.HIGHEST,
            preferred_element_type=jnp.float32,
        )
        out[c, 0] = row[0:1]


def far(load, cx, cy, ncl, n_pencil):
    return pl.pallas_call(
        functools.partial(far_kernel, cx, cy, ncl, n_pencil),
        out_shape=shaped(3, 1, 1, ncl),
        in_specs=[VMEM],
        out_specs=VMEM,
        compiler_params=PARAMS,
    )(load)


def deposit_step(group, first, listed, load, order, acc, shape):
    cx, cy, nz = shape
    rows = cx * cy // 2
    wide = group * load.shape[2]

    def numbers(length):
        shape = (length // 16, 16, wide)
        return (lax.broadcasted_iota(jnp.int32, shape, 0) * 16 + lax.broadcasted_iota(jnp.int32, shape, 1)).astype(
            jnp.float32
        ).astype(jnp.bfloat16)

    def spread(row):
        return jnp.broadcast_to(row, (16, wide)).astype(jnp.bfloat16)[None]

    zero = jnp.zeros((), jnp.bfloat16)
    one = jnp.ones((), jnp.bfloat16)
    block = jnp.concatenate([load[order[first + k]] for k in range(group)], axis=1)
    live = lax.broadcasted_iota(jnp.int32, (1, wide), 1) // load.shape[2] < listed - first
    cell = block[3:4, :].astype(jnp.int32) % (cx * cy * nz)
    row = cell // nz
    half = row // rows
    at_row = numbers(rows) == spread(jnp.where(live, row % rows, -1).astype(jnp.float32))
    right = []
    for h in range(2):
        at_col = numbers(nz) == spread(jnp.where(half == h, cell % nz, -1).astype(jnp.float32))
        right.append(jnp.where(at_col, one, zero).reshape(nz, wide))
    left = []
    for piece in split(block):
        for c in range(3):
            left.append(jnp.where(at_row, spread(piece[c : c + 1, :]), zero).reshape(rows, wide))
    added = lax.dot_general(
        jnp.concatenate(left, axis=0),
        jnp.concatenate(right, axis=0),
        (((1,), (1,)), ((), ())),
        preferred_element_type=jnp.float32,
    )
    acc[...] += (added[: 3 * rows] + added[3 * rows :]).reshape(acc.shape)


def deposit_kernel(cap, inside, load, out, acc, order, sems):
    _, cx, cy, nz = out.shape
    shape = (cx, cy, nz)
    for h in range(2):
        acc[:, :, :, h * nz : (h + 1) * nz] = inside[:, h * (cx // 2) : (h + 1) * (cx // 2)]
    listed = jnp.int32(0)
    for d in range(load.shape[0] // cap):
        first = d * cap
        held = jnp.max(load[first, 3:4, :]).astype(jnp.int32) // (cx * cy * nz)
        for k in range(cap):
            order[listed + k] = first + k
        listed = listed + held
    for k in range(GROUP):
        order[listed + k] = 0
    rest = listed % GROUP
    whole = listed // GROUP + (rest > GROUP // 2).astype(jnp.int32)

    def step(g, carry):
        deposit_step(GROUP, g * GROUP, listed, load, order, acc, shape)
        return carry

    lax.fori_loop(0, whole, step, 0)

    @pl.when((rest > 0) & (rest <= GROUP // 2))
    def _():
        deposit_step(GROUP // 2, whole * GROUP, listed, load, order, acc, shape)

    copies = Copies(sems)
    for c in range(3):
        for h in range(2):
            part = acc.at[c, :, :, h * nz : (h + 1) * nz]
            copies.start(part, out.at[c, h * (cx // 2) : (h + 1) * (cx // 2)])
    copies.wait(0, 6)


def deposit(inside, load, cap):
    return pl.pallas_call(
        functools.partial(deposit_kernel, cap),
        out_shape=shaped(*inside.shape),
        in_specs=[VMEM] * 2,
        out_specs=ANY,
        scratch_shapes=[
            pltpu.VMEM((3, inside.shape[1] // 2, inside.shape[2], 2 * inside.shape[3]), jnp.float32),
            pltpu.SMEM((load.shape[0] + max(cap, GROUP),), jnp.int32),
            pltpu.SemaphoreType.DMA((6,)),
        ],
        compiler_params=PARAMS,
    )(inside, load)


def swapped(array, axis, first):
    up = [(i, i + 1) for i in range(first, lax.axis_size(axis) - 1, 2)]
    return lax.ppermute(array, axis, up + [(j, i) for i, j in up])


def per_device(vorticity, velocity, viscosity, tile_weights, tile_cells, tile_dest, tile_count):
    _, cx, cy, nz = vorticity.shape
    ncl = nz // CB
    n_slab = lax.axis_size("slab")
    n_pencil = lax.axis_size("pencil")
    cap = 2 * tile_weights.shape[0] // n_slab
    weights = jnp.transpose(tile_weights, (1, 0, 2))
    count = tile_count
    *faces, packets, tiles = to_send(
        vorticity, velocity, viscosity, weights, tile_cells, tile_dest.T, count, n_slab, cap
    )
    halos = [swapped(face, axis, k % 2) for k, (face, axis) in enumerate(zip(faces, SIDES))]
    order = outward(n_slab)
    arrived = lax.all_to_all(packets, "slab", 0, 0, axis_index_groups=[order], tiled=True)
    inside, moments = inner(vorticity, velocity, viscosity, tiles)
    advanced, load = edges(inside, moments, faces, halos, n_slab * n_pencil)
    everyone = [s * n_pencil + p for s in order for p in range(n_pencil)]
    load = lax.all_to_all(load, ("slab", "pencil"), 0, 0, axis_index_groups=[everyone], tiled=True)
    vorticity_out = deposit(advanced, arrived, cap)
    return (vorticity_out, far(load, cx, cy, ncl, n_pencil))


def solution(mesh):
    in_specs = (
        P(None, "slab", "pencil", None),
        P(None, "slab", "pencil", None),
        P("slab", "pencil", None),
        P(("slab", "pencil"), None, None),
        P(("slab", "pencil"), None),
        P(("slab", "pencil"), None),
        P(("slab", "pencil")),
    )
    out_specs = (P(None, "slab", "pencil", None), P(None, "slab", "pencil", None))
    return jax.shard_map(
        per_device, mesh=mesh, in_specs=in_specs, out_specs=out_specs, check_vma=False
    )
```

```python
import functools

import jax
import jax.numpy as jnp
from jax import lax
from jax.experimental import pallas as pl
from jax.experimental.pallas import tpu as pltpu
from jax.sharding import PartitionSpec as P

CB = 16
TIME_STEP = 0.1
LANES = 128
SIDES = ("slab", "slab", "pencil", "pencil")
GROUP = 16
VMEM_LIMIT = 24 * 1024 * 1024

VMEM = pl.BlockSpec(memory_space=pltpu.VMEM)
ANY = pl.BlockSpec(memory_space=pl.ANY)
SMEM = pl.BlockSpec(memory_space=pltpu.SMEM)
FIRST_PARAMS = pltpu.CompilerParams(vmem_limit_bytes=60 * 1024 * 1024)
PARAMS = pltpu.CompilerParams(vmem_limit_bytes=VMEM_LIMIT)


def shaped(*shape):
    return jax.ShapeDtypeStruct(shape, jnp.float32)


def split(w):
    high = w.astype(jnp.bfloat16).astype(jnp.float32)
    return high, w - high


def thirds(w):
    high, rest = split(w)
    middle, low = split(rest)
    return [high, middle, low]


def outward(count):
    half = count // 2
    return [(half + (k + 1) // 2) % count if k % 2 else half - k // 2 for k in range(count)]


def pack_tiles(cap, cells_dev, weights, cells, dest, count, packets):
    slots = packets.shape[0]
    tiles = cells.shape[0]
    half = slots // cap // 2
    names = dest[...]
    names = jnp.where(names > half, 2 * (names - half) - 1, 2 * (half - names))
    names = jnp.minimum(names, 2 * half - 1)
    live = (lax.broadcasted_iota(jnp.int32, (1, tiles), 1) < count[0]).astype(jnp.float32)
    same = (lax.broadcasted_iota(jnp.int32, (slots // cap, tiles), 0) == names).astype(jnp.float32)
    shape = (tiles, tiles)
    earlier = lax.broadcasted_iota(jnp.int32, shape, 0) < lax.broadcasted_iota(jnp.int32, shape, 1)
    before = jnp.dot(same, earlier.astype(jnp.float32), preferred_element_type=jnp.float32)
    rank = jnp.sum(same * before, axis=0, keepdims=True).astype(jnp.int32)
    slot = lax.broadcasted_iota(jnp.int32, (slots, tiles), 0)
    placed = (slot == names * cap + rank).astype(jnp.float32) * live
    held = jnp.sum((slot == names * cap).astype(jnp.float32) * live, axis=1, keepdims=True)
    rows = [weights[0], weights[1], weights[2], cells[...].astype(jnp.float32)]
    found = jnp.dot(
        jnp.concatenate([placed] * 3, axis=1).astype(jnp.bfloat16),
        jnp.concatenate(thirds(jnp.concatenate(rows, axis=1)), axis=0).astype(jnp.bfloat16),
        preferred_element_type=jnp.float32,
    )
    length = cells.shape[1]
    for c in range(3):
        packets[:, c, :] = found[:, c * length : (c + 1) * length]
    packets[:, 3, :] = found[:, 3 * length :] + held * cells_dev


def tile_moments(cap, nz, packets, moments):
    n_slab = packets.shape[0] // cap
    ncl = nz // CB
    wide = cap * packets.shape[2]
    level = lax.broadcasted_iota(jnp.int32, (ncl, wide), 0)
    found = []
    order = outward(n_slab)
    for d in range(n_slab):
        block = jnp.concatenate([packets[order.index(d) * cap + k] for k in range(cap)], axis=1)
        cell = block[3:4, :].astype(jnp.int32)
        spots = (level == cell % nz // CB).astype(jnp.float32).astype(jnp.bfloat16)
        high, low = split(block)
        left = jnp.concatenate([high, low], axis=0).astype(jnp.bfloat16)
        sums = lax.dot_general(left, spots, (((1,), (1,)), ((), ())), preferred_element_type=jnp.float32)
        found.append(sums[0:4] + sums[4:8])
    moments[...] = jnp.concatenate(found, axis=1)


class Copies:
    def __init__(self, sems):
        self.sems = sems
        self.made = []

    def start(self, source, target):
        self.made.append(pltpu.make_async_copy(source, target, self.sems.at[len(self.made)]))
        self.made[-1].start()

    def wait(self, first, last):
        for k in range(first, last):
            self.made[k].wait()


def send_kernel(
    cap,
    vort,
    velo,
    visc,
    weights_in,
    cells_in,
    dest_in,
    count_in,
    near_out,
    far_out,
    swap_out,
    other_out,
    packets_out,
    moments_out,
    near,
    far,
    swap,
    other,
    packets,
    moments,
    weights,
    cells,
    dest,
    count,
    sems,
):
    cx, cy, nz = visc.shape
    copies = Copies(sems)
    copies.start(weights_in, weights)
    copies.start(cells_in, cells)
    copies.start(dest_in, dest)
    copies.start(count_in, count)
    even = lax.axis_index("slab") % 2 == 0
    for face, at in ((near, jnp.where(even, cx - 1, 0)), (far, jnp.where(even, 0, cx - 1))):
        copies.start(vort.at[:, at], face.at[0:3])
        copies.start(velo.at[:, at], face.at[3:6])
        copies.start(visc.at[at], face.at[6])
    even = lax.axis_index("pencil") % 2 == 0
    for face, at in ((swap, jnp.where(even, cy - 1, 0)), (other, jnp.where(even, 0, cy - 1))):
        copies.start(vort.at[:, :, at], face.at[0:3])
        copies.start(velo.at[:, :, at], face.at[3:6])
        copies.start(visc.at[:, at], face.at[6])
    copies.wait(0, 4)
    pack_tiles(cap, cx * cy * nz, weights, cells, dest, count, packets)
    copies.start(packets, packets_out)
    tile_moments(cap, nz, packets, moments)
    copies.start(moments, moments_out)
    copies.wait(4, 10)
    copies.start(near, near_out)
    copies.start(far, far_out)
    copies.wait(10, 16)
    copies.start(swap, swap_out)
    copies.start(other, other_out)
    copies.wait(16, 22)


def to_send(vort, velo, visc, weights, cells, dest, count, n_slab, cap):
    _, cx, cy, nz = vort.shape
    made = (
        shaped(7, cy, nz),
        shaped(7, cy, nz),
        shaped(7, cx, nz),
        shaped(7, cx, nz),
        shaped(n_slab * cap, 4, weights.shape[2]),
        shaped(4, n_slab * nz // CB),
    )
    return pl.pallas_call(
        functools.partial(send_kernel, cap),
        out_shape=made,
        in_specs=[ANY] * 7,
        out_specs=(ANY,) * 6,
        scratch_shapes=[pltpu.VMEM(one.shape, jnp.float32) for one in made]
        + [
            pltpu.VMEM(weights.shape, jnp.float32),
            pltpu.VMEM(cells.shape, jnp.int32),
            pltpu.VMEM(dest.shape, jnp.int32),
            pltpu.SMEM(count.shape, jnp.int32),
            pltpu.SemaphoreType.DMA((22,)),
        ],
        compiler_params=FIRST_PARAMS,
    )(vort, velo, visc, weights, cells, dest, count)


def ahead(a, axis):
    return pltpu.roll(a, a.shape[axis] - 1, axis)


def behind(a, axis):
    return pltpu.roll(a, 1, axis)


def interior_step(vort, velo, visc, out):
    cx, cy, nz = visc.shape
    has_ahead = lax.broadcasted_iota(jnp.int32, (cy, nz), 0) < cy - 1
    totals = [jnp.zeros((8, nz), jnp.float32) for _ in range(3)]
    flux_x = [None] * 3
    for x in range(cx):
        nu = visc[x]
        spin = [vort[c, x] for c in range(3)]
        mean_y = jnp.where(has_ahead, 0.5 * (nu + ahead(nu, 0)), 0.0)
        mean_z = 0.5 * (nu + ahead(nu, 1))
        half_y = 0.5 * spin[1]
        half_z = 0.5 * spin[2]
        next_y = jnp.where(has_ahead, ahead(half_y, 0), 0.0)
        next_z = ahead(half_z, 1)
        half_y = jnp.where(has_ahead, half_y, 0.0)
        half_x = 0.5 * spin[0]
        if x < cx - 1:
            mean_x = 0.5 * (nu + visc[x + 1])
        for c in range(3):
            w = spin[c]
            u = velo[c, x]
            flux_y = mean_y * (ahead(w, 0) - w)
            flux_z = mean_z * (ahead(w, 1) - w)
            change = flux_y + half_y * ahead(u, 0) - behind(flux_y + next_y * u, 0)
            change = change + (flux_z + half_z * ahead(u, 1) - behind(flux_z + next_z * u, 1))
            if x == 0:
                change = change + half_x * velo[c, x + 1]
            elif x == cx - 1:
                change = change - half_x * velo[c, x - 1]
            else:
                change = change + half_x * (velo[c, x + 1] - velo[c, x - 1])
            if x > 0:
                change = change - flux_x[c]
            if x < cx - 1:
                flux_x[c] = mean_x * (vort[c, x + 1] - w)
                change = change + flux_x[c]
            new = w + TIME_STEP * change
            out[c, x] = new
            totals[c] = totals[c] + jnp.sum(new.reshape(cy // 8, 8, nz), axis=0)
    return [jnp.sum(total, axis=0, keepdims=True) for total in totals]


def by_level(totals, width):
    nz = totals[0].shape[1]
    shape = (nz, width)
    level = lax.broadcasted_iota(jnp.int32, shape, 0) // CB
    lane = lax.broadcasted_iota(jnp.int32, shape, 1)
    pick = (lane == lax.axis_index("slab") * (nz // CB) + level).astype(jnp.float32).astype(jnp.bfloat16)
    rows = jnp.concatenate(totals + [jnp.zeros_like(totals[0])], axis=0)
    pieces = jnp.concatenate(thirds(rows), axis=0).astype(jnp.bfloat16)
    found = jnp.dot(pieces, pick, preferred_element_type=jnp.float32)
    return found[0:4] + (found[4:8] + found[8:12])


def inner_kernel(vort, velo, visc, tiles_in, out, moments, tiles, sem):
    copy = pltpu.make_async_copy(tiles_in, tiles, sem)
    copy.start()
    own = by_level(interior_step(vort, velo, visc, out), moments.shape[1])
    copy.wait()
    moments[...] = tiles[...] + own


def inner(vort, velo, visc, tiles):
    return pl.pallas_call(
        inner_kernel,
        out_shape=(shaped(*vort.shape), shaped(*tiles.shape)),
        in_specs=[VMEM] * 3 + [ANY],
        out_specs=(VMEM,) * 2,
        scratch_shapes=[pltpu.VMEM(tiles.shape, jnp.float32), pltpu.SemaphoreType.DMA],
        compiler_params=PARAMS,
    )(vort, velo, visc, tiles)


def face_change(own, other, along, sign, c):
    stretch = (0.5 * sign) * own[along] * other[3 + c]
    diffuse = 0.5 * (own[6] + other[6]) * (other[c] - own[c])
    return TIME_STEP * (stretch + diffuse)


def edge_kernel(
    inside, moments, near, far, swap, other, near_in, far_in, swap_in, other_in, out, load_out, load, side_change, sem
):
    _, cx, cy, nz = out.shape
    even = lax.axis_index("pencil") % 2 == 0
    low, low_in = jnp.where(even, other[...], swap[...]), jnp.where(even, other_in[...], swap_in[...])
    high, high_in = jnp.where(even, swap[...], other[...]), jnp.where(even, swap_in[...], other_in[...])
    even = lax.axis_index("slab") % 2 == 0
    near_at, far_at = jnp.where(even, cx - 1, 0), jnp.where(even, 0, cx - 1)
    near_sign = jnp.where(even, 1.0, -1.0)
    totals = []
    for c in range(3):
        total = jnp.zeros((8, nz), jnp.float32)
        for own, came, at, sign in ((near, near_in, near_at, near_sign), (far, far_in, far_at, -near_sign)):
            change = face_change(own, came, 0, sign, c)
            out[c, at] = inside[c, at] + change
            total = total + jnp.sum(change.reshape(cy // 8, 8, nz), axis=0)
        for k, own, came, sign in ((0, low, low_in, -1.0), (1, high, high_in, 1.0)):
            change = face_change(own, came, 1, sign, c)
            side_change[k, c] = change
            total = total + change
        totals.append(jnp.sum(total, axis=0, keepdims=True))
    moment = moments[...] + by_level(totals, moments.shape[1])
    for k in range(load.shape[1] // 4):
        part = moment[:, k * LANES : (k + 1) * LANES]
        load[:, 4 * k : 4 * k + 4, :] = jnp.broadcast_to(part[None], (load.shape[0], 4, LANES))
    copy = pltpu.make_async_copy(load, load_out, sem)
    copy.start()
    for c in range(3):
        out[c, 1 : cx - 1] = inside[c, 1 : cx - 1]
        for k, at in ((0, 0), (1, cy - 1)):
            for x in range(cx):
                out[c, x, at : at + 1, :] = out[c, x, at : at + 1, :] + side_change[k, c, x : x + 1, :]
    copy.wait()


def edges(inside, moments, faces, halos, n_all):
    _, cx, _, nz = inside.shape
    load = shaped(n_all, 4 * moments.shape[1] // LANES, LANES)
    return pl.pallas_call(
        edge_kernel,
        out_shape=(shaped(*inside.shape), load),
        in_specs=[VMEM] * 10,
        out_specs=(VMEM, ANY),
        scratch_shapes=[
            pltpu.VMEM(load.shape, jnp.float32),
            pltpu.VMEM((2, 3, cx, nz), jnp.float32),
            pltpu.SemaphoreType.DMA,
        ],
        compiler_params=PARAMS,
    )(inside, moments, *faces, *halos)


def far_kernel(cx, cy, ncl, n_pencil, load, out):
    n_all = load.shape[0]
    n_slab = n_all // n_pencil
    slab = lax.axis_index("slab")
    pencil = lax.axis_index("pencil")
    shape = (ncl, n_slab * ncl)
    target = lax.broadcasted_iota(jnp.int32, shape, 0)
    source = lax.broadcasted_iota(jnp.int32, shape, 1)
    sigma = jnp.float32(cx * n_slab // 4)
    rel_x = ((slab - source // ncl) * cx).astype(jnp.float32)
    rel_z = ((target - source % ncl) * CB).astype(jnp.float32)
    flat = rel_x * rel_x + rel_z * rel_z + sigma * sigma
    turned = [jnp.zeros(shape, jnp.float32) for _ in range(3)]
    for p in range(n_pencil):
        total = load[p]
        for s in range(1, n_slab):
            total = total + load[s * n_pencil + p]
        moment = jnp.concatenate([total[4 * k : 4 * k + 4] for k in range(load.shape[1] // 4)], axis=1)
        first, second, third = moment[0:1], moment[1:2], moment[2:3]
        rel_y = ((pencil - p) * cy).astype(jnp.float32)
        inverse = lax.rsqrt(flat + rel_y * rel_y)
        weight = inverse * inverse * inverse
        turned[0] = turned[0] + weight * (rel_z * second - rel_y * third)
        turned[1] = turned[1] + weight * (rel_x * third - rel_z * first)
        turned[2] = turned[2] + weight * (rel_y * first - rel_x * second)
    ones = jnp.ones((8, shape[1]), jnp.float32)
    for c in range(3):
        row = lax.dot_general(
            ones,
            turned[c],
            (((1,), (1,)), ((), ())),
            precision=lax.Precision.HIGHEST,
            preferred_element_type=jnp.float32,
        )
        out[c, 0] = row[0:1]


def far(load, cx, cy, ncl, n_pencil):
    return pl.pallas_call(
        functools.partial(far_kernel, cx, cy, ncl, n_pencil),
        out_shape=shaped(3, 1, 1, ncl),
        in_specs=[VMEM],
        out_specs=VMEM,
        compiler_params=PARAMS,
    )(load)


def deposit_step(group, first, listed, load, order, acc, shape):
    cx, cy, nz = shape
    rows = cx * cy // 2
    wide = group * load.shape[2]

    def numbers(length):
        shape = (length // 16, 16, wide)
        return (lax.broadcasted_iota(jnp.int32, shape, 0) * 16 + lax.broadcasted_iota(jnp.int32, shape, 1)).astype(
            jnp.float32
        ).astype(jnp.bfloat16)

    def spread(row):
        return jnp.broadcast_to(row, (16, wide)).astype(jnp.bfloat16)[None]

    zero = jnp.zeros((), jnp.bfloat16)
    one = jnp.ones((), jnp.bfloat16)
    block = jnp.concatenate([load[order[first + k]] for k in range(group)], axis=1)
    live = lax.broadcasted_iota(jnp.int32, (1, wide), 1) // load.shape[2] < listed - first
    cell = block[3:4, :].astype(jnp.int32) % (cx * cy * nz)
    row = cell // nz
    half = row // rows
    at_row = numbers(rows) == spread(jnp.where(live, row % rows, -1).astype(jnp.float32))
    right = []
    for h in range(2):
        at_col = numbers(nz) == spread(jnp.where(half == h, cell % nz, -1).astype(jnp.float32))
        right.append(jnp.where(at_col, one, zero).reshape(nz, wide))
    left = []
    for piece in split(block):
        for c in range(3):
            left.append(jnp.where(at_row, spread(piece[c : c + 1, :]), zero).reshape(rows, wide))
    added = lax.dot_general(
        jnp.concatenate(left, axis=0),
        jnp.concatenate(right, axis=0),
        (((1,), (1,)), ((), ())),
        preferred_element_type=jnp.float32,
    )
    acc[...] += (added[: 3 * rows] + added[3 * rows :]).reshape(acc.shape)


def deposit_kernel(cap, inside, load, out, acc, order, sems):
    _, cx, cy, nz = out.shape
    shape = (cx, cy, nz)
    for h in range(2):
        acc[:, :, :, h * nz : (h + 1) * nz] = inside[:, h * (cx // 2) : (h + 1) * (cx // 2)]
    listed = jnp.int32(0)
    for d in range(load.shape[0] // cap):
        first = d * cap
        held = jnp.max(load[first, 3:4, :]).astype(jnp.int32) // (cx * cy * nz)
        for k in range(cap):
            order[listed + k] = first + k
        listed = listed + held
    for k in range(GROUP):
        order[listed + k] = 0
    rest = listed % GROUP
    whole = listed // GROUP + (rest > GROUP // 2).astype(jnp.int32)

    def step(g, carry):
        deposit_step(GROUP, g * GROUP, listed, load, order, acc, shape)
        return carry

    lax.fori_loop(0, whole, step, 0)

    @pl.when((rest > 0) & (rest <= GROUP // 2))
    def _():
        deposit_step(GROUP // 2, whole * GROUP, listed, load, order, acc, shape)

    copies = Copies(sems)
    for c in range(3):
        for h in range(2):
            part = acc.at[c, :, :, h * nz : (h + 1) * nz]
            copies.start(part, out.at[c, h * (cx // 2) : (h + 1) * (cx // 2)])
    copies.wait(0, 6)


def deposit(inside, load, cap):
    return pl.pallas_call(
        functools.partial(deposit_kernel, cap),
        out_shape=shaped(*inside.shape),
        in_specs=[VMEM] * 2,
        out_specs=ANY,
        scratch_shapes=[
            pltpu.VMEM((3, inside.shape[1] // 2, inside.shape[2], 2 * inside.shape[3]), jnp.float32),
            pltpu.SMEM((load.shape[0] + max(cap, GROUP),), jnp.int32),
            pltpu.SemaphoreType.DMA((6,)),
        ],
        compiler_params=PARAMS,
    )(inside, load)


def swapped(array, axis, first):
    up = [(i, i + 1) for i in range(first, lax.axis_size(axis) - 1, 2)]
    return lax.ppermute(array, axis, up + [(j, i) for i, j in up])


def per_device(vorticity, velocity, viscosity, tile_weights, tile_cells, tile_dest, tile_count):
    _, cx, cy, nz = vorticity.shape
    ncl = nz // CB
    n_slab = lax.axis_size("slab")
    n_pencil = lax.axis_size("pencil")
    cap = 2 * tile_weights.shape[0] // n_slab
    weights = jnp.transpose(tile_weights, (1, 0, 2))
    count = tile_count
    *faces, packets, tiles = to_send(
        vorticity, velocity, viscosity, weights, tile_cells, tile_dest.T, count, n_slab, cap
    )
    halos = [swapped(face, axis, k % 2) for k, (face, axis) in enumerate(zip(faces, SIDES))]
    order = outward(n_slab)
    arrived = lax.all_to_all(packets, "slab", 0, 0, axis_index_groups=[order], tiled=True)
    inside, moments = inner(vorticity, velocity, viscosity, tiles)
    advanced, load = edges(inside, moments, faces, halos, n_slab * n_pencil)
    everyone = [s * n_pencil + p for s in order for p in range(n_pencil)]
    load = lax.all_to_all(load, ("slab", "pencil"), 0, 0, axis_index_groups=[everyone], tiled=True)
    vorticity_out = deposit(advanced, arrived, cap)
    return (vorticity_out, far(load, cx, cy, ncl, n_pencil))


def solution(mesh):
    in_specs = (
        P(None, "slab", "pencil", None),
        P(None, "slab", "pencil", None),
        P("slab", "pencil", None),
        P(("slab", "pencil"), None, None),
        P(("slab", "pencil"), None),
        P(("slab", "pencil"), None),
        P(("slab", "pencil")),
    )
    out_specs = (P(None, "slab", "pencil", None), P(None, "slab", "pencil", None))
    return jax.shard_map(
        per_device, mesh=mesh, in_specs=in_specs, out_specs=out_specs, check_vma=False
    )
```

```python
import functools

import jax
import jax.numpy as jnp
from jax import lax
from jax.experimental import pallas as pl
from jax.experimental.pallas import tpu as pltpu
from jax.sharding import PartitionSpec as P

CB = 16
TIME_STEP = 0.1
LANES = 128
SIDES = ("slab", "slab", "pencil", "pencil")
GROUP = 16
VMEM_LIMIT = 24 * 1024 * 1024

VMEM = pl.BlockSpec(memory_space=pltpu.VMEM)
ANY = pl.BlockSpec(memory_space=pl.ANY)
SMEM = pl.BlockSpec(memory_space=pltpu.SMEM)
FIRST_PARAMS = pltpu.CompilerParams(vmem_limit_bytes=60 * 1024 * 1024)
PARAMS = pltpu.CompilerParams(vmem_limit_bytes=VMEM_LIMIT)


def shaped(*shape):
    return jax.ShapeDtypeStruct(shape, jnp.float32)


def split(w):
    high = w.astype(jnp.bfloat16).astype(jnp.float32)
    return high, w - high


def thirds(w):
    high, rest = split(w)
    middle, low = split(rest)
    return [high, middle, low]


def outward(count):
    half = count // 2
    return [(half + (k + 1) // 2) % count if k % 2 else half - k // 2 for k in range(count)]


def pack_tiles(cap, cells_dev, weights, cells, dest, count, packets):
    slots = packets.shape[0]
    tiles = cells.shape[0]
    half = slots // cap // 2
    names = dest[...]
    names = jnp.where(names > half, 2 * (names - half) - 1, 2 * (half - names))
    names = jnp.minimum(names, 2 * half - 1)
    live = (lax.broadcasted_iota(jnp.int32, (1, tiles), 1) < count[0]).astype(jnp.float32)
    same = (lax.broadcasted_iota(jnp.int32, (slots // cap, tiles), 0) == names).astype(jnp.float32)
    shape = (tiles, tiles)
    earlier = lax.broadcasted_iota(jnp.int32, shape, 0) < lax.broadcasted_iota(jnp.int32, shape, 1)
    before = jnp.dot(same, earlier.astype(jnp.float32), preferred_element_type=jnp.float32)
    rank = jnp.sum(same * before, axis=0, keepdims=True).astype(jnp.int32)
    slot = lax.broadcasted_iota(jnp.int32, (slots, tiles), 0)
    placed = (slot == names * cap + rank).astype(jnp.float32) * live
    held = jnp.sum((slot == names * cap).astype(jnp.float32) * live, axis=1, keepdims=True)
    rows = [weights[0], weights[1], weights[2], cells[...].astype(jnp.float32)]
    found = jnp.dot(
        jnp.concatenate([placed] * 3, axis=1).astype(jnp.bfloat16),
        jnp.concatenate(thirds(jnp.concatenate(rows, axis=1)), axis=0).astype(jnp.bfloat16),
        preferred_element_type=jnp.float32,
    )
    length = cells.shape[1]
    for c in range(3):
        packets[:, c, :] = found[:, c * length : (c + 1) * length]
    packets[:, 3, :] = found[:, 3 * length :] + held * cells_dev


def tile_moments(cap, nz, packets, moments):
    n_slab = packets.shape[0] // cap
    ncl = nz // CB
    wide = cap * packets.shape[2]
    level = lax.broadcasted_iota(jnp.int32, (ncl, wide), 0)
    found = []
    order = outward(n_slab)
    for d in range(n_slab):
        block = jnp.concatenate([packets[order.index(d) * cap + k] for k in range(cap)], axis=1)
        cell = block[3:4, :].astype(jnp.int32)
        spots = (level == cell % nz // CB).astype(jnp.float32).astype(jnp.bfloat16)
        high, low = split(block)
        left = jnp.concatenate([high, low], axis=0).astype(jnp.bfloat16)
        sums = lax.dot_general(left, spots, (((1,), (1,)), ((), ())), preferred_element_type=jnp.float32)
        found.append(sums[0:4] + sums[4:8])
    moments[...] = jnp.concatenate(found, axis=1)


class Copies:
    def __init__(self, sems):
        self.sems = sems
        self.made = []

    def start(self, source, target):
        self.made.append(pltpu.make_async_copy(source, target, self.sems.at[len(self.made)]))
        self.made[-1].start()

    def wait(self, first, last):
        for k in range(first, last):
            self.made[k].wait()


def send_kernel(
    cap,
    vort,
    velo,
    visc,
    weights_in,
    cells_in,
    dest_in,
    count_in,
    near_out,
    far_out,
    swap_out,
    other_out,
    packets_out,
    moments_out,
    near,
    far,
    swap,
    other,
    packets,
    moments,
    weights,
    cells,
    dest,
    count,
    sems,
):
    cx, cy, nz = visc.shape
    copies = Copies(sems)
    copies.start(weights_in, weights)
    copies.start(cells_in, cells)
    copies.start(dest_in, dest)
    copies.start(count_in, count)
    even = lax.axis_index("slab") % 2 == 0
    for face, at in ((near, jnp.where(even, cx - 1, 0)), (far, jnp.where(even, 0, cx - 1))):
        copies.start(vort.at[:, at], face.at[0:3])
        copies.start(velo.at[:, at], face.at[3:6])
        copies.start(visc.at[at], face.at[6])
    even = lax.axis_index("pencil") % 2 == 0
    for face, at in ((swap, jnp.where(even, cy - 1, 0)), (other, jnp.where(even, 0, cy - 1))):
        copies.start(vort.at[:, :, at], face.at[0:3])
        copies.start(velo.at[:, :, at], face.at[3:6])
        copies.start(visc.at[:, at], face.at[6])
    copies.wait(0, 4)
    pack_tiles(cap, cx * cy * nz, weights, cells, dest, count, packets)
    copies.start(packets, packets_out)
    copies.wait(4, 10)
    copies.start(near, near_out)
    copies.start(far, far_out)
    tile_moments(cap, nz, packets, moments)
    copies.start(moments, moments_out)
    copies.wait(10, 16)
    copies.start(swap, swap_out)
    copies.start(other, other_out)
    copies.wait(16, 22)


def to_send(vort, velo, visc, weights, cells, dest, count, n_slab, cap):
    _, cx, cy, nz = vort.shape
    made = (
        shaped(7, cy, nz),
        shaped(7, cy, nz),
        shaped(7, cx, nz),
        shaped(7, cx, nz),
        shaped(n_slab * cap, 4, weights.shape[2]),
        shaped(4, n_slab * nz // CB),
    )
    return pl.pallas_call(
        functools.partial(send_kernel, cap),
        out_shape=made,
        in_specs=[ANY] * 7,
        out_specs=(ANY,) * 6,
        scratch_shapes=[pltpu.VMEM(one.shape, jnp.float32) for one in made]
        + [
            pltpu.VMEM(weights.shape, jnp.float32),
            pltpu.VMEM(cells.shape, jnp.int32),
            pltpu.VMEM(dest.shape, jnp.int32),
            pltpu.SMEM(count.shape, jnp.int32),
            pltpu.SemaphoreType.DMA((22,)),
        ],
        compiler_params=FIRST_PARAMS,
    )(vort, velo, visc, weights, cells, dest, count)


def ahead(a, axis):
    return pltpu.roll(a, a.shape[axis] - 1, axis)


def behind(a, axis):
    return pltpu.roll(a, 1, axis)


def interior_step(vort, velo, visc, out):
    cx, cy, nz = visc.shape
    has_ahead = lax.broadcasted_iota(jnp.int32, (cy, nz), 0) < cy - 1
    totals = [jnp.zeros((8, nz), jnp.float32) for _ in range(3)]
    flux_x = [None] * 3
    for x in range(cx):
        nu = visc[x]
        spin = [vort[c, x] for c in range(3)]
        mean_y = jnp.where(has_ahead, 0.5 * (nu + ahead(nu, 0)), 0.0)
        mean_z = 0.5 * (nu + ahead(nu, 1))
        half_y = 0.5 * spin[1]
        half_z = 0.5 * spin[2]
        next_y = jnp.where(has_ahead, ahead(half_y, 0), 0.0)
        next_z = ahead(half_z, 1)
        half_y = jnp.where(has_ahead, half_y, 0.0)
        half_x = 0.5 * spin[0]
        if x < cx - 1:
            mean_x = 0.5 * (nu + visc[x + 1])
        for c in range(3):
            w = spin[c]
            u = velo[c, x]
            flux_y = mean_y * (ahead(w, 0) - w)
            flux_z = mean_z * (ahead(w, 1) - w)
            change = flux_y + half_y * ahead(u, 0) - behind(flux_y + next_y * u, 0)
            change = change + (flux_z + half_z * ahead(u, 1) - behind(flux_z + next_z * u, 1))
            if x == 0:
                change = change + half_x * velo[c, x + 1]
            elif x == cx - 1:
                change = change - half_x * velo[c, x - 1]
            else:
                change = change + half_x * (velo[c, x + 1] - velo[c, x - 1])
            if x > 0:
                change = change - flux_x[c]
            if x < cx - 1:
                flux_x[c] = mean_x * (vort[c, x + 1] - w)
                change = change + flux_x[c]
            new = w + TIME_STEP * change
            out[c, x] = new
            totals[c] = totals[c] + jnp.sum(new.reshape(cy // 8, 8, nz), axis=0)
    return [jnp.sum(total, axis=0, keepdims=True) for total in totals]


def by_level(totals, width):
    nz = totals[0].shape[1]
    shape = (nz, width)
    level = lax.broadcasted_iota(jnp.int32, shape, 0) // CB
    lane = lax.broadcasted_iota(jnp.int32, shape, 1)
    pick = (lane == lax.axis_index("slab") * (nz // CB) + level).astype(jnp.float32).astype(jnp.bfloat16)
    rows = jnp.concatenate(totals + [jnp.zeros_like(totals[0])], axis=0)
    pieces = jnp.concatenate(thirds(rows), axis=0).astype(jnp.bfloat16)
    found = jnp.dot(pieces, pick, preferred_element_type=jnp.float32)
    return found[0:4] + (found[4:8] + found[8:12])


def inner_kernel(vort, velo, visc, tiles_in, out, moments, tiles, sem):
    copy = pltpu.make_async_copy(tiles_in, tiles, sem)
    copy.start()
    own = by_level(interior_step(vort, velo, visc, out), moments.shape[1])
    copy.wait()
    moments[...] = tiles[...] + own


def inner(vort, velo, visc, tiles):
    return pl.pallas_call(
        inner_kernel,
        out_shape=(shaped(*vort.shape), shaped(*tiles.shape)),
        in_specs=[VMEM] * 3 + [ANY],
        out_specs=(VMEM,) * 2,
        scratch_shapes=[pltpu.VMEM(tiles.shape, jnp.float32), pltpu.SemaphoreType.DMA],
        compiler_params=PARAMS,
    )(vort, velo, visc, tiles)


def face_change(own, other, along, sign, c):
    stretch = (0.5 * sign) * own[along] * other[3 + c]
    diffuse = 0.5 * (own[6] + other[6]) * (other[c] - own[c])
    return TIME_STEP * (stretch + diffuse)


def edge_kernel(
    inside, moments, near, far, swap, other, near_in, far_in, swap_in, other_in, out, load_out, load, side_change, sem
):
    _, cx, cy, nz = out.shape
    even = lax.axis_index("pencil") % 2 == 0
    low, low_in = jnp.where(even, other[...], swap[...]), jnp.where(even, other_in[...], swap_in[...])
    high, high_in = jnp.where(even, swap[...], other[...]), jnp.where(even, swap_in[...], other_in[...])
    even = lax.axis_index("slab") % 2 == 0
    near_at, far_at = jnp.where(even, cx - 1, 0), jnp.where(even, 0, cx - 1)
    near_sign = jnp.where(even, 1.0, -1.0)
    totals = []
    for c in range(3):
        total = jnp.zeros((8, nz), jnp.float32)
        for own, came, at, sign in ((near, near_in, near_at, near_sign), (far, far_in, far_at, -near_sign)):
            change = face_change(own, came, 0, sign, c)
            out[c, at] = inside[c, at] + change
            total = total + jnp.sum(change.reshape(cy // 8, 8, nz), axis=0)
        for k, own, came, sign in ((0, low, low_in, -1.0), (1, high, high_in, 1.0)):
            change = face_change(own, came, 1, sign, c)
            side_change[k, c] = change
            total = total + change
        totals.append(jnp.sum(total, axis=0, keepdims=True))
    moment = moments[...] + by_level(totals, moments.shape[1])
    for k in range(load.shape[1] // 4):
        part = moment[:, k * LANES : (k + 1) * LANES]
        load[:, 4 * k : 4 * k + 4, :] = jnp.broadcast_to(part[None], (load.shape[0], 4, LANES))
    copy = pltpu.make_async_copy(load, load_out, sem)
    copy.start()
    for c in range(3):
        out[c, 1 : cx - 1] = inside[c, 1 : cx - 1]
        for k, at in ((0, 0), (1, cy - 1)):
            for x in range(cx):
                out[c, x, at : at + 1, :] = out[c, x, at : at + 1, :] + side_change[k, c, x : x + 1, :]
    copy.wait()


def edges(inside, moments, faces, halos, n_all):
    _, cx, _, nz = inside.shape
    load = shaped(n_all, 4 * moments.shape[1] // LANES, LANES)
    return pl.pallas_call(
        edge_kernel,
        out_shape=(shaped(*inside.shape), load),
        in_specs=[VMEM] * 10,
        out_specs=(VMEM, ANY),
        scratch_shapes=[
            pltpu.VMEM(load.shape, jnp.float32),
            pltpu.VMEM((2, 3, cx, nz), jnp.float32),
            pltpu.SemaphoreType.DMA,
        ],
        compiler_params=PARAMS,
    )(inside, moments, *faces, *halos)


def far_kernel(cx, cy, ncl, n_pencil, load, out):
    n_all = load.shape[0]
    n_slab = n_all // n_pencil
    slab = lax.axis_index("slab")
    pencil = lax.axis_index("pencil")
    shape = (ncl, n_slab * ncl)
    target = lax.broadcasted_iota(jnp.int32, shape, 0)
    source = lax.broadcasted_iota(jnp.int32, shape, 1)
    sigma = jnp.float32(cx * n_slab // 4)
    rel_x = ((slab - source // ncl) * cx).astype(jnp.float32)
    rel_z = ((target - source % ncl) * CB).astype(jnp.float32)
    flat = rel_x * rel_x + rel_z * rel_z + sigma * sigma
    turned = [jnp.zeros(shape, jnp.float32) for _ in range(3)]
    for p in range(n_pencil):
        total = load[p]
        for s in range(1, n_slab):
            total = total + load[s * n_pencil + p]
        moment = jnp.concatenate([total[4 * k : 4 * k + 4] for k in range(load.shape[1] // 4)], axis=1)
        first, second, third = moment[0:1], moment[1:2], moment[2:3]
        rel_y = ((pencil - p) * cy).astype(jnp.float32)
        inverse = lax.rsqrt(flat + rel_y * rel_y)
        weight = inverse * inverse * inverse
        turned[0] = turned[0] + weight * (rel_z * second - rel_y * third)
        turned[1] = turned[1] + weight * (rel_x * third - rel_z * first)
        turned[2] = turned[2] + weight * (rel_y * first - rel_x * second)
    ones = jnp.ones((8, shape[1]), jnp.float32)
    for c in range(3):
        row = lax.dot_general(
            ones,
            turned[c],
            (((1,), (1,)), ((), ())),
            precision=lax.Precision.HIGHEST,
            preferred_element_type=jnp.float32,
        )
        out[c, 0] = row[0:1]


def far(load, cx, cy, ncl, n_pencil):
    return pl.pallas_call(
        functools.partial(far_kernel, cx, cy, ncl, n_pencil),
        out_shape=shaped(3, 1, 1, ncl),
        in_specs=[VMEM],
        out_specs=VMEM,
        compiler_params=PARAMS,
    )(load)


def deposit_step(group, first, listed, load, order, acc, shape):
    cx, cy, nz = shape
    rows = cx * cy // 2
    wide = group * load.shape[2]

    def numbers(length):
        shape = (length // 16, 16, wide)
        return (lax.broadcasted_iota(jnp.int32, shape, 0) * 16 + lax.broadcasted_iota(jnp.int32, shape, 1)).astype(
            jnp.float32
        ).astype(jnp.bfloat16)

    def spread(row):
        return jnp.broadcast_to(row, (16, wide)).astype(jnp.bfloat16)[None]

    zero = jnp.zeros((), jnp.bfloat16)
    one = jnp.ones((), jnp.bfloat16)
    block = jnp.concatenate([load[order[first + k]] for k in range(group)], axis=1)
    live = lax.broadcasted_iota(jnp.int32, (1, wide), 1) // load.shape[2] < listed - first
    cell = block[3:4, :].astype(jnp.int32) % (cx * cy * nz)
    row = cell // nz
    half = row // rows
    at_row = numbers(rows) == spread(jnp.where(live, row % rows, -1).astype(jnp.float32))
    right = []
    for h in range(2):
        at_col = numbers(nz) == spread(jnp.where(half == h, cell % nz, -1).astype(jnp.float32))
        right.append(jnp.where(at_col, one, zero).reshape(nz, wide))
    left = []
    for piece in split(block):
        for c in range(3):
            left.append(jnp.where(at_row, spread(piece[c : c + 1, :]), zero).reshape(rows, wide))
    added = lax.dot_general(
        jnp.concatenate(left, axis=0),
        jnp.concatenate(right, axis=0),
        (((1,), (1,)), ((), ())),
        preferred_element_type=jnp.float32,
    )
    acc[...] += (added[: 3 * rows] + added[3 * rows :]).reshape(acc.shape)


def deposit_kernel(cap, inside, load, out, acc, order, sems):
    _, cx, cy, nz = out.shape
    shape = (cx, cy, nz)
    for h in range(2):
        acc[:, :, :, h * nz : (h + 1) * nz] = inside[:, h * (cx // 2) : (h + 1) * (cx // 2)]
    listed = jnp.int32(0)
    for d in range(load.shape[0] // cap):
        first = d * cap
        held = jnp.max(load[first, 3:4, :]).astype(jnp.int32) // (cx * cy * nz)
        for k in range(cap):
            order[listed + k] = first + k
        listed = listed + held
    for k in range(GROUP):
        order[listed + k] = 0
    rest = listed % GROUP
    whole = listed // GROUP + (rest > GROUP // 2).astype(jnp.int32)

    def step(g, carry):
        deposit_step(GROUP, g * GROUP, listed, load, order, acc, shape)
        return carry

    lax.fori_loop(0, whole, step, 0)

    @pl.when((rest > 0) & (rest <= GROUP // 2))
    def _():
        deposit_step(GROUP // 2, whole * GROUP, listed, load, order, acc, shape)

    copies = Copies(sems)
    for c in range(3):
        for h in range(2):
            part = acc.at[c, :, :, h * nz : (h + 1) * nz]
            copies.start(part, out.at[c, h * (cx // 2) : (h + 1) * (cx // 2)])
    copies.wait(0, 6)


def deposit(inside, load, cap):
    return pl.pallas_call(
        functools.partial(deposit_kernel, cap),
        out_shape=shaped(*inside.shape),
        in_specs=[VMEM] * 2,
        out_specs=ANY,
        scratch_shapes=[
            pltpu.VMEM((3, inside.shape[1] // 2, inside.shape[2], 2 * inside.shape[3]), jnp.float32),
            pltpu.SMEM((load.shape[0] + max(cap, GROUP),), jnp.int32),
            pltpu.SemaphoreType.DMA((6,)),
        ],
        compiler_params=PARAMS,
    )(inside, load)


def swapped(array, axis, first):
    up = [(i, i + 1) for i in range(first, lax.axis_size(axis) - 1, 2)]
    return lax.ppermute(array, axis, up + [(j, i) for i, j in up])


def per_device(vorticity, velocity, viscosity, tile_weights, tile_cells, tile_dest, tile_count):
    _, cx, cy, nz = vorticity.shape
    ncl = nz // CB
    n_slab = lax.axis_size("slab")
    n_pencil = lax.axis_size("pencil")
    cap = 2 * tile_weights.shape[0] // n_slab
    weights = jnp.transpose(tile_weights, (1, 0, 2))
    count = tile_count
    *faces, packets, tiles = to_send(
        vorticity, velocity, viscosity, weights, tile_cells, tile_dest.T, count, n_slab, cap
    )
    halos = [swapped(face, axis, k % 2) for k, (face, axis) in enumerate(zip(faces, SIDES))]
    order = outward(n_slab)
    arrived = lax.all_to_all(packets, "slab", 0, 0, axis_index_groups=[order], tiled=True)
    inside, moments = inner(vorticity, velocity, viscosity, tiles)
    advanced, load = edges(inside, moments, faces, halos, n_slab * n_pencil)
    everyone = [s * n_pencil + p for s in order for p in range(n_pencil)]
    load = lax.all_to_all(load, ("slab", "pencil"), 0, 0, axis_index_groups=[everyone], tiled=True)
    vorticity_out = deposit(advanced, arrived, cap)
    return (vorticity_out, far(load, cx, cy, ncl, n_pencil))


def solution(mesh):
    in_specs = (
        P(None, "slab", "pencil", None),
        P(None, "slab", "pencil", None),
        P("slab", "pencil", None),
        P(("slab", "pencil"), None, None),
        P(("slab", "pencil"), None),
        P(("slab", "pencil"), None),
        P(("slab", "pencil")),
    )
    out_specs = (P(None, "slab", "pencil", None), P(None, "slab", "pencil", None))
    return jax.shard_map(
        per_device, mesh=mesh, in_specs=in_specs, out_specs=out_specs, check_vma=False
    )
```
